32 devices in a mesh: wave: 8 (over z, y), lev: 4 (over x, core).
Axes of the slice: x: 2, y: 2, z: 4, core: 2. Of those that a mesh axis runs over, the one named last changes fastest.
Arguments:
- spectral: bfloat16 [1280, 256, 1280], P('wave', 'lev'), may hold values from -6 to 6
- legendre: bfloat16 [1280, 32, 1280], P('wave'), may hold values from -0.0034179688 to 0.0034179688
- wave_map: int32 [1280], replicated, may hold values from 0 to 1279, each once
- row_points: int32 [32], replicated, may hold values from 20 to 5136, as said below
- brackets: int32 [4], replicated, may hold values from 0 to 14, as said below
- lev_weight: float32 [4], replicated, may hold values from 0.05 to 0.95
- climatology: float32 [4, 64, 5248], P('lev', 'wave'), may hold values from 0.1 to 1
Outputs:
- anomaly: float32 [4, 64, 5248], P('lev', 'wave')
The draws below stay inside these ranges and needn't reach their ends.
Inputs may be any that keep to these rules, and one draw needn't show every extreme that they name: `wave_map`: each wavenumber once. `row_points`: each is 20 + 4 i for a whole number i below 1280; some row has 5136 points. `brackets`: pressure level p has its lower bracket level among the 4 model levels of band p (levels b * 4 to b * 4 + 3 for band b); some pressure level outside the last band takes the last level of its band; the last pressure level takes 16 - 2.
All inputs are finite; a program needn't handle non-finite values.
Results may differ from the reference program's by a relative error of at most 0.0003.
Values sent between devices are 32-bit elements; how exact they have to be, the bound alone decides.
No kernel may reach another device: no remote copies, remote signals or barrier semaphores. Data moves between devices by JAX's collectives and lax.ppermute only.
A program may use at most 256 MiB of HBM per device.

```python
import math
import jax
import jax.numpy as jnp
from jax import lax

M = 1280
NT = 1280
LEV_DEV = 4
PLEV_DEV = 1
STEPS = 4
FIELDS = 2
LEVELS = 16
PLEV = 4
COLS = 256
HALF = 32
LAT = 64
ROWPAD = 5248


def draw_row_points(key, part):
    key = jax.random.fold_in(key, 11)
    seed_draw, seed_place = jax.random.split(key)
    uniform_ids = jax.random.randint(seed_draw, (HALF,), 0, M)
    row_index = uniform_ids * uniform_ids // M
    chosen = jax.random.randint(seed_place, (), 0, HALF)
    row_index = jnp.where(jnp.arange(HALF) == chosen, M - 1, row_index)
    return (20 + 4 * row_index).astype(jnp.int32)


def draw_brackets(key, part):
    key = jax.random.fold_in(key, 57)
    seed_draw, seed_place = jax.random.split(key, 2)
    plev_ids = jnp.arange(PLEV, dtype=jnp.int32)
    band_ids = plev_ids // PLEV_DEV
    offsets = jax.random.randint(seed_draw, (PLEV,), 0, LEV_DEV)
    lower_ids = band_ids * LEV_DEV + offsets
    chosen = jax.random.randint(seed_place, (), 0, PLEV - PLEV_DEV)
    lower_ids = jnp.where(plev_ids == chosen, band_ids * LEV_DEV + LEV_DEV - 1, lower_ids)
    lower_ids = jnp.minimum(lower_ids, LEVELS - 2)
    lower_ids = jnp.where(plev_ids == PLEV - 1, LEVELS - 2, lower_ids)
    return lower_ids.astype(jnp.int32)


def levels(own_key, extent, pieces, least, top_value):
    gain = 1.0
    for axis_at, shards_of in pieces:
        heights = jax.random.uniform(jax.random.fold_in(jax.random.fold_in(own_key, 6), axis_at), (shards_of,), jnp.float32, least / len(pieces), top_value / len(pieces))
        gain = gain * jnp.repeat(jnp.exp(heights), extent[axis_at] // shards_of).reshape((-1,) + (1,) * (len(extent) - 1 - axis_at))
    return gain


def bell_draw(rng, shape, spread, limit, cuts=(), kind=jnp.bfloat16):
    array = spread * jax.random.normal(rng, shape, jnp.float32)
    if cuts:
        array = array * levels(rng, shape, cuts, -0.22, 0.18)
    return jnp.clip(array, -limit, limit).astype(kind)


def setup_inputs(seed: int = 0) -> dict:
    seeds = jax.random.split(jax.random.key(seed), 8)
    return {
        "spectral": bell_draw(seeds[0], (M, COLS, NT), 1.0, 6.0, ((0, 8), (1, 4))),
        "legendre": bell_draw(seeds[1], (M, HALF, NT), (2 * M * NT) ** -0.5, 0.0034179688, ((0, 8),)),
        "wave_map": jax.random.permutation(seeds[2], M).astype(jnp.int32),
        "row_points": draw_row_points(jax.random.fold_in(seeds[7], 71), 0),
        "brackets": draw_brackets(jax.random.fold_in(seeds[7], 71), 0),
        "lev_weight": jnp.clip(jax.random.uniform(seeds[5], (PLEV,), jnp.float32, 0.05, 0.95), 0.05, 0.95),
        "climatology": jnp.clip(0.1 + 0.9 * jax.random.uniform(seeds[6], (PLEV, LAT, ROWPAD), jnp.float32) ** levels(seeds[6], (PLEV, LAT, ROWPAD), ((0, 4), (1, 8)), -0.2, 0.2), 0.1, 1.0),
    }


TWO_PI = 2.0 * math.pi


def synthesize(coeffs, wave_map, points):
    wave_ids = wave_map.astype(jnp.int32)
    places = jnp.arange(ROWPAD, dtype=jnp.int32)
    phase_index = (wave_ids[:, None] * places[None, :]) % points
    angle_rad = phase_index.astype(jnp.float32) * (TWO_PI / points.astype(jnp.float32))
    live_mask = (wave_ids[:, None] <= (points - 1) // 2) & (places[None, :] < points)
    factor = jnp.where(wave_ids == 0, 1.0, 2.0).astype(jnp.float32)[:, None]
    cosine = jnp.where(live_mask, factor * jnp.cos(angle_rad), 0.0)
    sine_part = jnp.where(live_mask, -factor * jnp.sin(angle_rad), 0.0)
    basis_table = jnp.stack([cosine, sine_part], axis=1)
    return lax.dot_general(coeffs, basis_table, (((0, 2), (0, 1)), ((), ())),
                           precision=lax.Precision.HIGHEST, preferred_element_type=jnp.float32)


def kinetic(values):
    return 0.5 * jnp.mean(values[:, 0] * values[:, 0] + values[:, 1] * values[:, 1], axis=1)


def mixing_table(brackets, lev_weight, levels_all):
    level_ids = jnp.arange(levels_all, dtype=jnp.int32)
    lower_hit = (level_ids[None, :] == brackets[:, None]).astype(jnp.float32)
    upper_hit = (level_ids[None, :] == brackets[:, None] + 1).astype(jnp.float32)
    return lev_weight[:, None] * lower_hit + (1.0 - lev_weight[:, None]) * upper_hit


def reference(spectral, legendre, wave_map, row_points, brackets, lev_weight, climatology):
    mixing = mixing_table(brackets, lev_weight, LEVELS)
    degree = jnp.arange(NT, dtype=jnp.int32)
    width_q = FIELDS * STEPS * 2
    span_slots = 64

    def slot_block(first_slot):
        spec_part = lax.dynamic_slice_in_dim(spectral, first_slot, span_slots, 0)
        leg_part = lax.dynamic_slice_in_dim(legendre, first_slot, span_slots, 0).astype(jnp.float32)
        waves_part = lax.dynamic_slice_in_dim(wave_map, first_slot, span_slots, 0).astype(jnp.int32)
        kept_mask = degree[None, :] >= waves_part[:, None]
        parity = (1 - 2 * ((degree[None, :] + waves_part[:, None]) % 2)).astype(jnp.float32)
        plain_coeffs = jnp.where(kept_mask[:, None, :], spec_part.astype(jnp.float32), 0.0)
        signed = plain_coeffs * parity[:, None, :]
        north_part = jnp.einsum("scn,sjn->scj", plain_coeffs, leg_part, precision=lax.Precision.HIGHEST)
        south_part = jnp.einsum("scn,sjn->scj", signed, leg_part, precision=lax.Precision.HIGHEST)
        fourier = jnp.concatenate([north_part, south_part], axis=2).reshape(span_slots, LEVELS, width_q, LAT)
        return jnp.einsum("pl,slqr->rspq", mixing, fourier, precision=lax.Precision.HIGHEST)

    starts = jnp.arange(0, M, span_slots, dtype=jnp.int32)
    blocks_out = lax.map(slot_block, starts)
    coeffs = jnp.transpose(blocks_out, (1, 0, 2, 3, 4)).reshape(LAT, M, PLEV * FIELDS * STEPS, 2)
    points_all = jnp.concatenate([row_points, row_points]).astype(jnp.int32)

    def row_energy(row_input):
        row_coeffs, points = row_input
        grid_row = synthesize(row_coeffs, wave_map, points).reshape(PLEV, FIELDS, STEPS, ROWPAD)
        return kinetic(grid_row)

    energy = jnp.transpose(lax.map(row_energy, (coeffs, points_all)), (1, 0, 2))
    places = jnp.arange(ROWPAD, dtype=jnp.int32)
    inside = places[None, None, :] < points_all[None, :, None]
    return jnp.where(inside, energy - climatology, 0.0)
```

```python
import functools
import math

import jax
import jax.numpy as jnp
import numpy as np
from jax import lax
from jax.experimental import pallas as pl
from jax.experimental.pallas import tpu as pltpu
from jax.sharding import PartitionSpec as P

M = 1280
NT = 1280
LEV_DEV = 4
STEPS = 4
FIELDS = 2
ROWPAD = 5248

FS = FIELDS * STEPS
PART = 2 * FS
SQ = 8
HALF_M = M // 2
KPTS = 768
KBLK = 256
BUF = 1536
VMEM_LIMIT = 56 * 1024 * 1024
F32 = jnp.float32
BF16 = jnp.bfloat16


def iota(shape, dim):
    return lax.broadcasted_iota(jnp.int32, shape, dim)


def legendre_kernel(slots, wave_map, brackets, low_ref, up_ref, first_ref, leg_ref, weight_ref, own_ref, prev_ref):
    step = pl.program_id(0)
    groups = slots // SQ
    half = leg_ref.shape[2]
    wave = lax.axis_index("wave")
    lev = lax.axis_index("lev")
    degree = iota((16, NT), 1)
    sign = (1 - 2 * (degree % 2)).astype(F32).astype(BF16)
    row = iota((2 * half, 1), 0)
    lows, ups, firsts = [], [], []
    for sq in range(SQ):
        m = wave_map[wave * slots + sq * groups + step]
        kept = jnp.where(degree >= m, 1.0, 0.0).astype(BF16)
        leg = leg_ref[sq, 0]
        plain = jnp.concatenate([leg[i : i + 16] * kept for i in range(0, half, 16)], axis=0)
        signed = jnp.concatenate([plain[i : i + 16] * sign for i in range(0, half, 16)], axis=0)
        lhs = jnp.concatenate([plain, signed], axis=0)
        rhs = jnp.concatenate([low_ref[sq, 0], up_ref[sq, 0], first_ref[sq, 0]], axis=0)
        sums = lax.dot_general(lhs, rhs, (((1,), (1,)), ((), ())), preferred_element_type=F32)
        parity = (1 - 2 * (m % 2)).astype(F32)
        sums = sums * jnp.where(row < half, 1.0, parity)
        lows.append(sums[:, :PART])
        ups.append(sums[:, PART : 2 * PART])
        firsts.append(sums[:, 2 * PART :])
    lower = brackets[lev]
    has_upper = lower - lev * LEV_DEV < LEV_DEV - 1
    w = weight_ref[lev]
    upper_w = jnp.where(has_upper, 1.0 - w, 0.0)
    before = jnp.maximum(lev - 1, 0)
    crosses = (lev > 0) & (brackets[before] == lev * LEV_DEV - 1)
    first_w = jnp.where(crosses, 1.0 - weight_ref[before], 0.0)
    own_ref[0] = w * jnp.concatenate(lows, axis=1) + upper_w * jnp.concatenate(ups, axis=1)
    prev_ref[0] = first_w * jnp.concatenate(firsts, axis=1)


def legendre_sums(spectral, legendre, wave_map, brackets, lev_weight):
    slots, cols, _ = spectral.shape
    half = legendre.shape[1]
    groups = slots // SQ
    spec = spectral.reshape(SQ, groups, cols, NT)
    leg = legendre.reshape(SQ, groups, half, NT)

    def low_map(i, wm, br):
        lev = lax.axis_index("lev")
        return 0, i, br[lev] - lev * LEV_DEV, 0

    def up_map(i, wm, br):
        lev = lax.axis_index("lev")
        return 0, i, jnp.minimum(br[lev] - lev * LEV_DEV + 1, LEV_DEV - 1), 0

    spec_block = (SQ, 1, PART, NT)
    out = jax.ShapeDtypeStruct((groups, 2 * half, SQ * PART), F32)
    out_spec = pl.BlockSpec((1, 2 * half, SQ * PART), lambda i, wm, br: (i, 0, 0))
    return pl.pallas_call(
        functools.partial(legendre_kernel, slots),
        out_shape=[out, out],
        grid_spec=pltpu.PrefetchScalarGridSpec(
            num_scalar_prefetch=2,
            grid=(groups,),
            in_specs=[
                pl.BlockSpec(spec_block, low_map),
                pl.BlockSpec(spec_block, up_map),
                pl.BlockSpec(spec_block, lambda i, wm, br: (0, i, 0, 0)),
                pl.BlockSpec((SQ, 1, half, NT), lambda i, wm, br: (0, i, 0, 0)),
                pl.BlockSpec(memory_space=pltpu.SMEM),
            ],
            out_specs=[out_spec, out_spec],
        ),
        compiler_params=pltpu.CompilerParams(vmem_limit_bytes=VMEM_LIMIT),
        cost_estimate=pl.CostEstimate(flops=2 * slots * 2 * half * 48 * NT, bytes_accessed=slots * NT * 2 * (48 + half), transcendentals=0),
        name="legendre_sums",
    )(wave_map, brackets, spec, spec, spec, leg, lev_weight)


def unit_circle(product, quarter):
    turn = jnp.round(product * (1.0 / quarter))
    rest = product - turn * quarter
    x = rest * ((0.5 * math.pi) / quarter)
    x2 = x * x
    sine = x * (1.0 + x2 * (-1.0 / 6 + x2 * (1.0 / 120 + x2 * (-1.0 / 5040 + x2 * (1.0 / 362880)))))
    cosine = 1.0 + x2 * (-0.5 + x2 * (1.0 / 24 + x2 * (-1.0 / 720 + x2 * (1.0 / 40320))))
    quad = turn.astype(jnp.int32) & 3
    odd = (quad & 1) == 1
    c = jnp.where(odd, sine, cosine)
    s = jnp.where(odd, cosine, sine)
    c = jnp.where((quad == 1) | (quad == 2), -c, c)
    s = jnp.where(quad >= 2, -s, s)
    return c, s


def own_points(points_ref, r2):
    wave = lax.axis_index("wave")
    lev = lax.axis_index("lev")
    band = 2 * lax.axis_size("lev")
    row = wave * band + r2 * lax.axis_size("lev") + lev
    return points_ref[row % points_ref.shape[0]]


def table_kernel(points_ref, map_ref, hi_ref, lo_ref, perm_ref):
    r2 = pl.program_id(0)
    kb = pl.program_id(1)
    rows = hi_ref.shape[1]
    steps = pl.num_programs(1)
    quarter = (own_points(points_ref, r2) // 4).astype(F32)
    perm_rows = perm_ref.shape[0]
    order = (r2 * steps + kb) * perm_rows + iota((perm_rows, M), 0)
    wanted = jnp.where(order < HALF_M, 2 * order, 2 * (order - HALF_M) + 1)
    perm_ref[...] = jnp.where(map_ref[...] == wanted, 1.0, 0.0).astype(BF16)

    def put(tile, chunk, value):
        lanes = slice(tile * 128, tile * 128 + 128)
        hi = value.astype(BF16)
        hi_ref[0, pl.ds(chunk, 16), lanes] = hi
        lo_ref[0, pl.ds(chunk, 16), lanes] = (value - hi.astype(F32)).astype(BF16)

    def chunk_body(i, carry):
        chunk = pl.multiple_of(i * 16, 16)
        k = (kb * rows + chunk + iota((16, 128), 0)).astype(F32)
        lane = iota((16, 128), 1).astype(F32)
        c, s = unit_circle(2.0 * lane * k, quarter)
        c1, s1 = unit_circle(k, quarter)
        ct, st = unit_circle(256.0 * k, quarter)
        co = c * c1 - s * s1
        so = s * c1 + c * s1
        for t in range(HALF_M // 128):
            if t:
                c, s = c * ct - s * st, s * ct + c * st
                co, so = co * ct - so * st, so * ct + co * st
            put(t, chunk, c)
            put(5 + t, chunk, s)
            put(10 + t, chunk, co)
            put(15 + t, chunk, so)
        return carry

    lax.fori_loop(0, rows // 16, chunk_body, 0)


def tables(row_points, slot_map):
    steps = 8
    rows = KPTS // steps
    table = jax.ShapeDtypeStruct((2, KPTS, 2 * M), BF16)
    table_spec = pl.BlockSpec((1, rows, 2 * M), lambda r, k: (r, k, 0))
    return pl.pallas_call(
        table_kernel,
        out_shape=[table, table, jax.ShapeDtypeStruct((M, M), BF16)],
        grid=(2, steps),
        in_specs=[pl.BlockSpec(memory_space=pltpu.SMEM), pl.BlockSpec(memory_space=pltpu.VMEM)],
        out_specs=[table_spec, table_spec, pl.BlockSpec((M // (2 * steps), M), lambda r, k: (r * steps + k, 0))],
        compiler_params=pltpu.CompilerParams(vmem_limit_bytes=VMEM_LIMIT),
        cost_estimate=pl.CostEstimate(flops=2 * KPTS * 2 * M * 12, bytes_accessed=2 * KPTS * 2 * M * 4 + M * M * 2, transcendentals=0),
        name="fourier_tables",
    )(row_points, slot_map)


def pick_tables(plev):
    wide = plev * 2 * PART
    out = np.zeros((2, 4, 2 * wide, 2 * wide), np.float32)
    plans = (
        ((0, 1), (0, 1), (0, 1), (0, 1)),
        ((1, -1), (1, 1), (1, -1), (1, 1)),
        ((0, 1), (0, 1), (1, -1), (1, -1)),
        ((1, -1), (1, 1), (0, -1), (0, 1)),
    )
    for r2 in range(2):
        for kind, plan in enumerate(plans):
            for image, (part, sgn) in enumerate(plan):
                for hl in range(2):
                    for p in range(plev):
                        for q in range(FS):
                            src = hl * wide + p * 2 * PART + r2 * PART + q * 2 + part
                            dst = hl * wide + image * plev * FS + p * FS + q
                            out[r2, kind, src, dst] = sgn
    return out.astype(jnp.bfloat16)


def mean_table(plev):
    wide = plev * FS * 4
    out = np.zeros((2 * 4 * plev, 2 * wide), np.float32)
    for quarter in range(4):
        for p in range(plev):
            for part in range(2):
                image_quarter = (quarter + part) % 4
                start = (image_quarter * 2 + part) * plev * FS + p * FS
                out[part * 4 * plev + quarter * plev + p, start : start + FS] = 0.5 / STEPS
    return out.astype(jnp.bfloat16)


def flip_table():
    return np.fliplr(np.eye(KBLK, dtype=np.float32)).astype(jnp.bfloat16)


def split(x):
    hi = x.astype(BF16)
    return hi, (x - hi.astype(F32)).astype(BF16)


def nt_dot(a, b):
    return lax.dot_general(a, b, (((1,), (1,)), ((), ())), preferred_element_type=F32)


def nn_dot(a, b):
    return jnp.dot(a, b, preferred_element_type=F32)


def synth_kernel(points_ref, moved_ref, perm_ref, hi_ref, lo_ref, pick_ref, mean_ref, flip_ref, out_ref, mixed, coef, direct, mirror, line):
    r2 = pl.program_id(0)
    kb = pl.program_id(1)
    waves, plev, block_rows, _ = moved_ref.shape
    sub = block_rows // 2
    wide = plev * 2 * PART
    part_rows = waves * sub

    @pl.when((r2 == 0) & (kb == 0))
    def _():
        for base in range(0, plev * 2, 8):
            cur = []
            for g in range(base, base + 8):
                pieces = [moved_ref[w, g // 2, (g % 2) * sub : (g % 2 + 1) * sub, :] for w in range(waves)]
                cur.append(jnp.concatenate(pieces, axis=0))
            group = iota((part_rows, 128), 1) // PART
            for bit in (1, 2, 4):
                unset = (group & bit) == 0
                nxt = list(cur)
                for g in range(8):
                    if g & bit == 0:
                        a, b = cur[g], cur[g + bit]
                        nxt[g] = jnp.where(unset, a, pltpu.roll(b, bit * PART, 1))
                        nxt[g + bit] = jnp.where(unset, pltpu.roll(a, 128 - bit * PART, 1), b)
                cur = nxt
            for sq in range(SQ):
                hi, lo = split(cur[sq])
                lane = base * PART
                mixed[sq * part_rows : (sq + 1) * part_rows, lane : lane + 128] = hi
                mixed[sq * part_rows : (sq + 1) * part_rows, wide + lane : wide + lane + 128] = lo

        lane_row = (iota((1, 2 * wide), 1) // PART) % 2
        limit0 = (own_points(points_ref, 0) - 1) // 2
        limit1 = (own_points(points_ref, 1) - 1) // 2
        limit = jnp.where(lane_row == 0, limit0, limit1)
        place = iota((HALF_M, 1), 0)
        turned = (iota((1, 2 * wide), 1) % wide) // (plev * FS) >= 2
        flip_sign = jnp.where(turned & (place % 2 == 1), -1.0, 1.0).astype(BF16)
        for odd in range(2):
            ordered = nn_dot(perm_ref[odd * HALF_M : (odd + 1) * HALF_M, :], mixed[...])
            wave = 2 * place + odd
            factor = jnp.where(wave <= limit, jnp.where(wave == 0, 1.0, 2.0), 0.0)
            ordered = (ordered * factor).astype(BF16)
            for row in range(2):
                for part in range(2):
                    picked = nn_dot(ordered, pick_ref[row, odd * 2 + part]).astype(BF16)
                    coef[row, odd, part * HALF_M : (part + 1) * HALF_M, :] = picked * flip_sign
        direct[...] = jnp.zeros_like(direct)
        mirror[...] = jnp.zeros_like(mirror)

    def contraction(odd):
        lanes = slice(odd * M, (odd + 1) * M)
        both = nn_dot(hi_ref[0, :, lanes], coef[r2, odd])
        rest = nn_dot(lo_ref[0, :, lanes], coef[r2, odd, :, :wide])
        return both[:, :wide] + (both[:, wide:] + rest)

    even_sum = contraction(0)
    odd_sum = contraction(1)
    plus = even_sum + odd_sum
    minus = even_sum - odd_sum
    squares = jnp.concatenate([plus * plus, minus * minus], axis=1)
    sq_hi, sq_lo = split(squares)
    energy = nt_dot(mean_ref[...], sq_hi) + nt_dot(mean_ref[...], sq_lo)
    rows = 4 * plev
    direct[:, pl.ds(pl.multiple_of(kb * KBLK, KBLK), KBLK)] = energy[:rows]
    en_hi, en_lo = split(energy[rows:])
    back = KPTS // KBLK - 1 - kb
    mirror[:, pl.ds(pl.multiple_of(back * KBLK, KBLK), KBLK)] = nn_dot(en_hi, flip_ref[...]) + nn_dot(en_lo, flip_ref[...])

    @pl.when(kb == KPTS // KBLK - 1)
    def _():
        quarter = own_points(points_ref, r2) // 4
        lane = iota((rows, BUF), 1)
        shift = (quarter + (BUF - (KPTS - 1))) % BUF
        whole = jnp.where(lane <= quarter // 2, direct[...], pltpu.roll(mirror[...], shift, 1))
        direct[...] = whole
        line[...] = jnp.zeros_like(line)
        lane = iota((plev, BUF), 1)
        for b in range(4):
            start = quarter * b
            inner = start % 128
            base = pl.multiple_of(start - inner, 128)
            piece = pltpu.roll(direct[b * plev : (b + 1) * plev, :], inner, 1)
            old = line[:, pl.ds(base, BUF)]
            line[:, pl.ds(base, BUF)] = jnp.where((lane >= inner) & (lane < inner + quarter), piece, old)
        out_ref[:, pl.ds(r2, 1), :] = line[:, :ROWPAD].reshape(plev, 1, ROWPAD)


def synthesis(moved, perm, table_hi, table_lo, row_points):
    waves, plev, block_rows, _ = moved.shape
    wide = plev * 2 * PART
    steps = KPTS // KBLK
    table_spec = pl.BlockSpec((1, KBLK, 2 * M), lambda r, k: (r, k, 0))
    vmem = pl.BlockSpec(memory_space=pltpu.VMEM)
    return pl.pallas_call(
        synth_kernel,
        out_shape=jax.ShapeDtypeStruct((plev, 2, ROWPAD), F32),
        grid=(2, steps),
        in_specs=[pl.BlockSpec(memory_space=pltpu.SMEM), vmem, vmem, table_spec, table_spec, vmem, vmem, vmem],
        out_specs=vmem,
        scratch_shapes=[
            pltpu.VMEM((M, 2 * wide), BF16),
            pltpu.VMEM((2, 2, M, 2 * wide), BF16),
            pltpu.VMEM((4 * plev, BUF), F32),
            pltpu.VMEM((4 * plev, BUF), F32),
            pltpu.VMEM((plev, 3 * 1280 + BUF), F32),
        ],
        compiler_params=pltpu.CompilerParams(vmem_limit_bytes=VMEM_LIMIT),
        cost_estimate=pl.CostEstimate(flops=2 * 2 * KPTS * 2 * M * 384, bytes_accessed=2 * KPTS * 2 * M * 4 + M * M * 2, transcendentals=0),
        name="synthesis",
    )(row_points, moved, perm, table_hi, table_lo, pick_tables(plev), mean_table(plev), flip_table())


def local(spectral, legendre, wave_map, row_points, brackets, lev_weight, climatology):
    slots = spectral.shape[0]
    half = legendre.shape[1]
    groups = slots // SQ
    wave_count = lax.axis_size("wave")
    lev_count = lax.axis_size("lev")
    rows_dev = 2 * half // (wave_count * lev_count)
    own, prev = legendre_sums(spectral, legendre, wave_map, brackets, lev_weight)
    from_next = lax.ppermute(prev, "lev", [(d, d - 1) for d in range(1, lev_count)])
    sums = (own + from_next).reshape(groups, wave_count, rows_dev, lev_count, SQ * PART)
    sums = jnp.transpose(sums, (1, 3, 2, 0, 4)).reshape(wave_count * lev_count, rows_dev * groups, SQ * PART)
    moved = lax.all_to_all(sums, ("wave", "lev"), split_axis=0, concat_axis=0, tiled=True)
    moved = moved.reshape(wave_count, lev_count, rows_dev * groups, SQ * PART)
    slot_map = jnp.transpose(wave_map.reshape(wave_count, SQ, groups), (1, 0, 2)).reshape(1, M)
    table_hi, table_lo, perm = tables(row_points, slot_map)
    energy = synthesis(moved, perm, table_hi, table_lo, row_points)
    result = lax.all_to_all(energy, "lev", split_axis=0, concat_axis=0, tiled=True)
    result = jnp.transpose(result, (1, 0, 2)).reshape(1, rows_dev * lev_count, ROWPAD)
    points_all = jnp.concatenate([row_points, row_points])
    band_rows = rows_dev * lev_count
    out_points = lax.dynamic_slice_in_dim(points_all, lax.axis_index("wave") * band_rows, band_rows, 0)
    places = jnp.arange(ROWPAD, dtype=jnp.int32)
    inside = places[None, None, :] < out_points[None, :, None]
    return jnp.where(inside, result - climatology, 0.0)


def solution(mesh):
    placed = (
        P("wave", "lev", None),
        P("wave", None, None),
        P(),
        P(),
        P(),
        P(),
        P("lev", "wave", None),
    )
    return jax.shard_map(
        local, mesh=mesh, in_specs=placed, out_specs=P("lev", "wave", None), check_vma=False
    )
```

```python
import functools
import math

import jax
import jax.numpy as jnp
import numpy as np
from jax import lax
from jax.experimental import pallas as pl
from jax.experimental.pallas import tpu as pltpu
from jax.sharding import PartitionSpec as P

M = 1280
NT = 1280
LEV_DEV = 4
STEPS = 4
FIELDS = 2
ROWPAD = 5248

FS = FIELDS * STEPS
PART = 2 * FS
SQ = 8
STEP_SLOTS = 2
HALF_M = M // 2
KPTS = 768
KBLK = 256
BUF = 1536
VMEM_LIMIT = 56 * 1024 * 1024
F32 = jnp.float32
BF16 = jnp.bfloat16


def iota(shape, dim):
    return lax.broadcasted_iota(jnp.int32, shape, dim)


def legendre_kernel(slots, wave_map, brackets, low_ref, up_ref, first_ref, leg_ref, weight_ref, own_ref, prev_ref, legs):
    step = pl.program_id(0)
    groups = slots // SQ
    half = leg_ref.shape[2]
    width = STEP_SLOTS * 2 * half
    wave = lax.axis_index("wave")
    lev = lax.axis_index("lev")
    lower = brackets[lev]
    has_upper = lower - lev * LEV_DEV < LEV_DEV - 1
    w = weight_ref[lev]
    upper_w = jnp.where(has_upper, 1.0 - w, 0.0)
    before = jnp.maximum(lev - 1, 0)
    crosses = (lev > 0) & (brackets[before] == lev * LEV_DEV - 1)
    first_w = jnp.where(crosses, 1.0 - weight_ref[before], 0.0)
    degree = iota((16, NT), 1)
    sign = (1 - 2 * (degree % 2)).astype(F32).astype(BF16)
    lane = iota((1, width), 1)
    south = lane % (2 * half) >= half
    owns, firsts = [], []
    for pair in range(SQ // 2):
        orders = []
        for a in range(2):
            sq = 2 * pair + a
            for b in range(STEP_SLOTS):
                m = wave_map[wave * slots + sq * groups + step * STEP_SLOTS + b]
                orders.append(m)
                kept = jnp.where(degree >= m, 1.0, 0.0).astype(BF16)
                base = (a * STEP_SLOTS + b) * 2 * half
                for i in range(0, half, 16):
                    plain = leg_ref[sq, b, i : i + 16, :] * kept
                    legs[pair, base + i : base + i + 16, :] = plain
                    legs[pair, base + half + i : base + half + i + 16, :] = plain * sign
        columns = []
        for a in range(2):
            for b in range(STEP_SLOTS):
                columns += [ref[2 * pair + a, b] for ref in (low_ref, up_ref, first_ref)]
        sums = lax.dot_general(
            jnp.concatenate(columns, axis=0), legs[pair], (((1,), (1,)), ((), ())), preferred_element_type=F32
        )
        for a in range(2):
            own = jnp.zeros((PART, width), F32)
            first = jnp.zeros((PART, width), F32)
            for b in range(STEP_SLOTS):
                at = (a * STEP_SLOTS + b) * 3 * PART
                block = sums[at : at + 3 * PART, a * width : (a + 1) * width]
                parity = (1 - 2 * (orders[a * STEP_SLOTS + b] % 2)).astype(F32)
                factor = jnp.where(south, parity, 1.0)
                here = lane // (2 * half) == b
                mixed = block[:PART] * (factor * w) + block[PART : 2 * PART] * (factor * upper_w)
                own = jnp.where(here, mixed, own)
                first = jnp.where(here, block[2 * PART :] * (factor * first_w), first)
            owns.append(own)
            firsts.append(first)
    for ref, parts in ((own_ref, owns), (prev_ref, firsts)):
        stacked = jnp.concatenate(parts, axis=0)
        for t in range(width // 128):
            turned = stacked[:, t * 128 : (t + 1) * 128].T
            for at in range(t * 128, (t + 1) * 128, 2 * half if half < 64 else 128):
                rows = min(128, 2 * half)
                ref[at // (2 * half), at % (2 * half) : at % (2 * half) + rows, :] = turned[at - t * 128 : at - t * 128 + rows]


def legendre_sums(spectral, legendre, wave_map, brackets, lev_weight):
    slots, cols, _ = spectral.shape
    half = legendre.shape[1]
    groups = slots // SQ
    spec = spectral.reshape(SQ, groups, cols, NT)
    leg = legendre.reshape(SQ, groups, half, NT)

    def low_map(i, wm, br):
        lev = lax.axis_index("lev")
        return 0, i, br[lev] - lev * LEV_DEV, 0

    def up_map(i, wm, br):
        lev = lax.axis_index("lev")
        return 0, i, jnp.minimum(br[lev] - lev * LEV_DEV + 1, LEV_DEV - 1), 0

    spec_block = (SQ, STEP_SLOTS, PART, NT)
    out = jax.ShapeDtypeStruct((groups, 2 * half, SQ * PART), F32)
    out_spec = pl.BlockSpec((STEP_SLOTS, 2 * half, SQ * PART), lambda i, wm, br: (i, 0, 0))
    return pl.pallas_call(
        functools.partial(legendre_kernel, slots),
        out_shape=[out, out],
        grid_spec=pltpu.PrefetchScalarGridSpec(
            num_scalar_prefetch=2,
            grid=(groups // STEP_SLOTS,),
            in_specs=[
                pl.BlockSpec(spec_block, low_map),
                pl.BlockSpec(spec_block, up_map),
                pl.BlockSpec(spec_block, lambda i, wm, br: (0, i, 0, 0)),
                pl.BlockSpec((SQ, STEP_SLOTS, half, NT), lambda i, wm, br: (0, i, 0, 0)),
                pl.BlockSpec(memory_space=pltpu.SMEM),
            ],
            out_specs=[out_spec, out_spec],
            scratch_shapes=[pltpu.VMEM((SQ // 2, 2 * STEP_SLOTS * 2 * half, NT), BF16)],
        ),
        compiler_params=pltpu.CompilerParams(vmem_limit_bytes=VMEM_LIMIT),
        cost_estimate=pl.CostEstimate(flops=2 * slots * 2 * half * 48 * NT, bytes_accessed=slots * NT * 2 * (48 + half), transcendentals=0),
        name="legendre_sums",
    )(wave_map, brackets, spec, spec, spec, leg, lev_weight)


def unit_circle(product, quarter):
    turn = jnp.round(product * (1.0 / quarter))
    rest = product - turn * quarter
    x = rest * ((0.5 * math.pi) / quarter)
    x2 = x * x
    sine = x * (1.0 + x2 * (-1.0 / 6 + x2 * (1.0 / 120 + x2 * (-1.0 / 5040 + x2 * (1.0 / 362880)))))
    cosine = 1.0 + x2 * (-0.5 + x2 * (1.0 / 24 + x2 * (-1.0 / 720 + x2 * (1.0 / 40320))))
    quad = turn.astype(jnp.int32) & 3
    odd = (quad & 1) == 1
    c = jnp.where(odd, sine, cosine)
    s = jnp.where(odd, cosine, sine)
    c = jnp.where((quad == 1) | (quad == 2), -c, c)
    s = jnp.where(quad >= 2, -s, s)
    return c, s


def own_points(points_ref, r2):
    wave = lax.axis_index("wave")
    lev = lax.axis_index("lev")
    row = 2 * (wave * lax.axis_size("lev") + lev) + r2
    return points_ref[row % points_ref.shape[0]]


def table_kernel(points_ref, map_ref, hi_ref, lo_ref, perm_ref):
    r2 = pl.program_id(0)
    kb = pl.program_id(1)
    rows = hi_ref.shape[1]
    steps = pl.num_programs(1)
    quarter = (own_points(points_ref, r2) // 4).astype(F32)
    perm_rows = perm_ref.shape[0]
    order = (r2 * steps + kb) * perm_rows + iota((perm_rows, 1), 0)
    wanted = jnp.where(order < HALF_M, 2 * order, 2 * (order - HALF_M) + 1)
    perm_ref[...] = jnp.where(map_ref[...] == wanted, 1.0, 0.0).astype(BF16)

    def put(tile, chunk, value):
        lanes = slice(tile * 128, tile * 128 + 128)
        hi = value.astype(BF16)
        hi_ref[0, pl.ds(chunk, 16), lanes] = hi
        lo_ref[0, pl.ds(chunk, 16), lanes] = (value - hi.astype(F32)).astype(BF16)

    def chunk_body(i, carry):
        chunk = pl.multiple_of(i * 16, 16)
        k = (kb * rows + chunk + iota((16, 128), 0)).astype(F32)
        lane = iota((16, 128), 1).astype(F32)
        c, s = unit_circle(2.0 * lane * k, quarter)
        c1, s1 = unit_circle(k, quarter)
        ct, st = unit_circle(256.0 * k, quarter)
        co = c * c1 - s * s1
        so = s * c1 + c * s1
        for t in range(HALF_M // 128):
            if t:
                c, s = c * ct - s * st, s * ct + c * st
                co, so = co * ct - so * st, so * ct + co * st
            put(t, chunk, c)
            put(5 + t, chunk, s)
            put(10 + t, chunk, co)
            put(15 + t, chunk, so)
        return carry

    lax.fori_loop(0, rows // 16, chunk_body, 0, unroll=2)


def tables(row_points, slot_map):
    steps = 8
    rows = KPTS // steps
    table = jax.ShapeDtypeStruct((2, KPTS, 2 * M), BF16)
    table_spec = pl.BlockSpec((1, rows, 2 * M), lambda r, k: (r, k, 0))
    return pl.pallas_call(
        table_kernel,
        out_shape=[table, table, jax.ShapeDtypeStruct((M, M), BF16)],
        grid=(2, steps),
        in_specs=[pl.BlockSpec(memory_space=pltpu.SMEM), pl.BlockSpec(memory_space=pltpu.VMEM)],
        out_specs=[table_spec, table_spec, pl.BlockSpec((M // (2 * steps), M), lambda r, k: (r * steps + k, 0))],
        compiler_params=pltpu.CompilerParams(vmem_limit_bytes=VMEM_LIMIT),
        cost_estimate=pl.CostEstimate(flops=2 * KPTS * 2 * M * 12, bytes_accessed=2 * KPTS * 2 * M * 4 + M * M * 2, transcendentals=0),
        name="fourier_tables",
    )(row_points, slot_map)


def pick_tables(plev):
    wide = plev * 2 * PART
    out = np.zeros((2, 4, 2 * wide, 2 * wide), np.float32)
    plans = (
        ((0, 1), (0, 1), (0, 1), (0, 1)),
        ((1, -1), (1, 1), (1, -1), (1, 1)),
        ((0, 1), (0, 1), (1, -1), (1, -1)),
        ((1, -1), (1, 1), (0, -1), (0, 1)),
    )
    for r2 in range(2):
        for kind, plan in enumerate(plans):
            for image, (part, sgn) in enumerate(plan):
                for hl in range(2):
                    for p in range(plev):
                        for q in range(FS):
                            src = hl * wide + p * 2 * PART + r2 * PART + q * 2 + part
                            dst = hl * wide + image * plev * FS + p * FS + q
                            out[r2, kind, src, dst] = sgn
    return out.astype(jnp.bfloat16)


def mean_table(plev):
    wide = plev * FS * 4
    out = np.zeros((2 * 4 * plev, 2 * wide), np.float32)
    for quarter in range(4):
        for p in range(plev):
            for part in range(2):
                image_quarter = (quarter + part) % 4
                start = (image_quarter * 2 + part) * plev * FS + p * FS
                out[part * 4 * plev + quarter * plev + p, start : start + FS] = 0.5 / STEPS
    return out.astype(jnp.bfloat16)


def flip_table():
    return np.fliplr(np.eye(KBLK, dtype=np.float32)).astype(jnp.bfloat16)


def split(x):
    hi = x.astype(BF16)
    return hi, (x - hi.astype(F32)).astype(BF16)


def nt_dot(a, b):
    return lax.dot_general(a, b, (((1,), (1,)), ((), ())), preferred_element_type=F32)


def nn_dot(a, b):
    return jnp.dot(a, b, preferred_element_type=F32)


def synth_kernel(points_ref, moved_ref, perm_ref, hi_ref, lo_ref, pick_ref, mean_ref, flip_ref, out_ref, mixed, coef, direct, mirror, line):
    r2 = pl.program_id(0)
    kb = pl.program_id(1)
    waves, plev, block_rows, _ = moved_ref.shape
    sub = block_rows // 2
    wide = plev * 2 * PART
    part_rows = waves * sub

    @pl.when((r2 == 0) & (kb == 0))
    def _():
        for base in range(0, plev * 2, 8):
            cur = []
            for g in range(base, base + 8):
                pieces = [moved_ref[w, g // 2, (g % 2) * sub : (g % 2 + 1) * sub, :] for w in range(waves)]
                cur.append(jnp.concatenate(pieces, axis=0))
            group = iota((part_rows, 128), 1) // PART
            for bit in (1, 2, 4):
                unset = (group & bit) == 0
                nxt = list(cur)
                for g in range(8):
                    if g & bit == 0:
                        a, b = cur[g], cur[g + bit]
                        nxt[g] = jnp.where(unset, a, pltpu.roll(b, bit * PART, 1))
                        nxt[g + bit] = jnp.where(unset, pltpu.roll(a, 128 - bit * PART, 1), b)
                cur = nxt
            for sq in range(SQ):
                hi, lo = split(cur[sq])
                lane = base * PART
                mixed[sq * part_rows : (sq + 1) * part_rows, lane : lane + 128] = hi
                mixed[sq * part_rows : (sq + 1) * part_rows, wide + lane : wide + lane + 128] = lo

        lane_row = (iota((1, 2 * wide), 1) // PART) % 2
        limit0 = (own_points(points_ref, 0) - 1) // 2
        limit1 = (own_points(points_ref, 1) - 1) // 2
        limit = jnp.where(lane_row == 0, limit0, limit1)
        place = iota((HALF_M, 1), 0)
        turned = (iota((1, 2 * wide), 1) % wide) // (plev * FS) >= 2
        flip_sign = jnp.where(turned & (place % 2 == 1), -1.0, 1.0).astype(BF16)
        for odd in range(2):
            ordered = nn_dot(perm_ref[odd * HALF_M : (odd + 1) * HALF_M, :], mixed[...])
            wave = 2 * place + odd
            factor = jnp.where(wave <= limit, jnp.where(wave == 0, 1.0, 2.0), 0.0)
            ordered = (ordered * factor).astype(BF16)
            for row in range(2):
                for part in range(2):
                    picked = nn_dot(ordered, pick_ref[row, odd * 2 + part]).astype(BF16)
                    coef[row, odd, part * HALF_M : (part + 1) * HALF_M, :] = picked * flip_sign
        direct[...] = jnp.zeros_like(direct)
        mirror[...] = jnp.zeros_like(mirror)

    def contraction(odd):
        lanes = slice(odd * M, (odd + 1) * M)
        both = nn_dot(hi_ref[0, :, lanes], coef[r2, odd])
        rest = nn_dot(lo_ref[0, :, lanes], coef[r2, odd, :, :wide])
        return both[:, :wide] + (both[:, wide:] + rest)

    even_sum = contraction(0)
    odd_sum = contraction(1)
    plus = even_sum + odd_sum
    minus = even_sum - odd_sum
    squares = jnp.concatenate([plus * plus, minus * minus], axis=1)
    sq_hi, sq_lo = split(squares)
    energy = nt_dot(mean_ref[...], sq_hi) + nt_dot(mean_ref[...], sq_lo)
    rows = 4 * plev
    direct[:, pl.ds(pl.multiple_of(kb * KBLK, KBLK), KBLK)] = energy[:rows]
    en_hi, en_lo = split(energy[rows:])
    back = KPTS // KBLK - 1 - kb
    mirror[:, pl.ds(pl.multiple_of(back * KBLK, KBLK), KBLK)] = nn_dot(en_hi, flip_ref[...]) + nn_dot(en_lo, flip_ref[...])

    @pl.when(kb == KPTS // KBLK - 1)
    def _():
        quarter = own_points(points_ref, r2) // 4
        lane = iota((rows, BUF), 1)
        shift = (quarter + (BUF - (KPTS - 1))) % BUF
        whole = jnp.where(lane <= quarter // 2, direct[...], pltpu.roll(mirror[...], shift, 1))
        direct[...] = whole
        line[...] = jnp.zeros_like(line)
        lane = iota((plev, BUF), 1)
        for b in range(4):
            start = quarter * b
            inner = start % 128
            base = pl.multiple_of(start - inner, 128)
            piece = pltpu.roll(direct[b * plev : (b + 1) * plev, :], inner, 1)
            old = line[:, pl.ds(base, BUF)]
            line[:, pl.ds(base, BUF)] = jnp.where((lane >= inner) & (lane < inner + quarter), piece, old)
        out_ref[:, pl.ds(r2, 1), :] = line[:, :ROWPAD].reshape(plev, 1, ROWPAD)


def synthesis(moved, perm, table_hi, table_lo, row_points):
    waves, plev, block_rows, _ = moved.shape
    wide = plev * 2 * PART
    steps = KPTS // KBLK
    table_spec = pl.BlockSpec((1, KBLK, 2 * M), lambda r, k: (r, k, 0))
    vmem = pl.BlockSpec(memory_space=pltpu.VMEM)
    return pl.pallas_call(
        synth_kernel,
        out_shape=jax.ShapeDtypeStruct((plev, 2, ROWPAD), F32),
        grid=(2, steps),
        in_specs=[pl.BlockSpec(memory_space=pltpu.SMEM), vmem, vmem, table_spec, table_spec, vmem, vmem, vmem],
        out_specs=vmem,
        scratch_shapes=[
            pltpu.VMEM((M, 2 * wide), BF16),
            pltpu.VMEM((2, 2, M, 2 * wide), BF16),
            pltpu.VMEM((4 * plev, BUF), F32),
            pltpu.VMEM((4 * plev, BUF), F32),
            pltpu.VMEM((plev, 3 * 1280 + BUF), F32),
        ],
        compiler_params=pltpu.CompilerParams(vmem_limit_bytes=VMEM_LIMIT),
        cost_estimate=pl.CostEstimate(flops=2 * 2 * KPTS * 2 * M * 384, bytes_accessed=2 * KPTS * 2 * M * 4 + M * M * 2, transcendentals=0),
        name="synthesis",
    )(row_points, moved, perm, table_hi, table_lo, pick_tables(plev), mean_table(plev), flip_table())


def local(spectral, legendre, wave_map, row_points, brackets, lev_weight, climatology):
    slots = spectral.shape[0]
    half = legendre.shape[1]
    groups = slots // SQ
    wave_count = lax.axis_size("wave")
    lev_count = lax.axis_size("lev")
    rows_dev = 2 * half // (wave_count * lev_count)
    own, prev = legendre_sums(spectral, legendre, wave_map, brackets, lev_weight)
    from_next = lax.ppermute(prev, "lev", [(d, d - 1) for d in range(1, lev_count)])
    sums = jnp.transpose(own + from_next, (1, 0, 2))
    sums = sums.reshape(wave_count * lev_count, rows_dev * groups, SQ * PART)
    moved = lax.all_to_all(sums, ("wave", "lev"), split_axis=0, concat_axis=0, tiled=True)
    moved = moved.reshape(wave_count, lev_count, rows_dev * groups, SQ * PART)
    slot_map = jnp.transpose(wave_map.reshape(wave_count, SQ, groups), (1, 0, 2)).reshape(1, M)
    table_hi, table_lo, perm = tables(row_points, slot_map)
    energy = synthesis(moved, perm, table_hi, table_lo, row_points)
    result = lax.all_to_all(energy, "lev", split_axis=0, concat_axis=0, tiled=True)
    result = result.reshape(1, rows_dev * lev_count, ROWPAD)
    points_all = jnp.concatenate([row_points, row_points])
    band_rows = rows_dev * lev_count
    out_points = lax.dynamic_slice_in_dim(points_all, lax.axis_index("wave") * band_rows, band_rows, 0)
    places = jnp.arange(ROWPAD, dtype=jnp.int32)
    inside = places[None, None, :] < out_points[None, :, None]
    return jnp.where(inside, result - climatology, 0.0)


def solution(mesh):
    placed = (
        P("wave", "lev", None),
        P("wave", None, None),
        P(),
        P(),
        P(),
        P(),
        P("lev", "wave", None),
    )
    return jax.shard_map(
        local, mesh=mesh, in_specs=placed, out_specs=P("lev", "wave", None), check_vma=False
    )
```

```python
import functools
import math

import jax
import jax.numpy as jnp
import numpy as np
from jax import lax
from jax.experimental import pallas as pl
from jax.experimental.pallas import tpu as pltpu
from jax.sharding import PartitionSpec as P

M = 1280
NT = 1280
LEV_DEV = 4
STEPS = 4
FIELDS = 2
ROWPAD = 5248

FS = FIELDS * STEPS
PART = 2 * FS
SQ = 8
STEP_SLOTS = 2
HALF_M = M // 2
KPTS = 768
KBLK = 256
BUF = 1536
VMEM_LIMIT = 56 * 1024 * 1024
F32 = jnp.float32
BF16 = jnp.bfloat16


def iota(shape, dim):
    return lax.broadcasted_iota(jnp.int32, shape, dim)


def legendre_kernel(slots, wave_map, brackets, low_ref, up_ref, first_ref, leg_ref, weight_ref, own_ref, prev_ref, own_rows, prev_rows):
    step = pl.program_id(0)
    groups = slots // SQ
    half = leg_ref.shape[2]
    width = STEP_SLOTS * 2 * half
    wave = lax.axis_index("wave")
    lev = lax.axis_index("lev")
    lower = brackets[lev]
    has_upper = lower - lev * LEV_DEV < LEV_DEV - 1
    w = weight_ref[lev]
    upper_w = jnp.where(has_upper, 1.0 - w, 0.0)
    before = jnp.maximum(lev - 1, 0)
    crosses = (lev > 0) & (brackets[before] == lev * LEV_DEV - 1)
    first_w = jnp.where(crosses, 1.0 - weight_ref[before], 0.0)
    degree = iota((16, NT), 1)
    sign = (1 - 2 * (degree % 2)).astype(F32).astype(BF16)
    lane = iota((1, width), 1)
    south = lane % (2 * half) >= half
    owns, firsts = [], []
    for pair in range(SQ // 2):
        orders, values = [], []
        for a in range(2):
            sq = 2 * pair + a
            for b in range(STEP_SLOTS):
                m = wave_map[wave * slots + sq * groups + step * STEP_SLOTS + b]
                orders.append(m)
                kept = jnp.where(degree >= m, 1.0, 0.0).astype(BF16)
                plain = [leg_ref[sq, b, i : i + 16, :] * kept for i in range(0, half, 16)]
                values += plain + [x * sign for x in plain]
        columns = []
        for a in range(2):
            for b in range(STEP_SLOTS):
                columns += [ref[2 * pair + a, b] for ref in (low_ref, up_ref, first_ref)]
        sums = lax.dot_general(
            jnp.concatenate(columns, axis=0), jnp.concatenate(values, axis=0), (((1,), (1,)), ((), ())), preferred_element_type=F32
        )
        for a in range(2):
            own = jnp.zeros((PART, width), F32)
            first = jnp.zeros((PART, width), F32)
            for b in range(STEP_SLOTS):
                at = (a * STEP_SLOTS + b) * 3 * PART
                block = sums[at : at + 3 * PART, a * width : (a + 1) * width]
                parity = (1 - 2 * (orders[a * STEP_SLOTS + b] % 2)).astype(F32)
                factor = jnp.where(south, parity, 1.0)
                here = lane // (2 * half) == b
                mixed = block[:PART] * (factor * w) + block[PART : 2 * PART] * (factor * upper_w)
                own = jnp.where(here, mixed, own)
                first = jnp.where(here, block[2 * PART :] * (factor * first_w), first)
            owns.append(own)
            firsts.append(first)
    rows = 2 * half
    for ref, parts in ((own_rows, owns), (prev_rows, firsts)):
        stacked = jnp.concatenate(parts, axis=0)
        for t in range(width // 128):
            at = pl.multiple_of(step * width + t * 128, 128)
            ref[pl.ds(at, 128), :] = stacked[:, t * 128 : (t + 1) * 128].T

    @pl.when(step == pl.num_programs(0) - 1)
    def _():
        for rows_ref, ref in ((own_rows, own_ref), (prev_rows, prev_ref)):
            rows_dev = ref.shape[1] // groups
            for r in range(rows):
                ref[r // rows_dev, (r % rows_dev) * groups : (r % rows_dev + 1) * groups, :] = rows_ref[pl.ds(r, groups, stride=rows), :]


def legendre_sums(spectral, legendre, wave_map, brackets, lev_weight):
    slots, cols, _ = spectral.shape
    half = legendre.shape[1]
    groups = slots // SQ
    spec = spectral.reshape(SQ, groups, cols, NT)
    leg = legendre.reshape(SQ, groups, half, NT)

    def low_map(i, wm, br):
        lev = lax.axis_index("lev")
        return 0, i, br[lev] - lev * LEV_DEV, 0

    def up_map(i, wm, br):
        lev = lax.axis_index("lev")
        return 0, i, jnp.minimum(br[lev] - lev * LEV_DEV + 1, LEV_DEV - 1), 0

    spec_block = (SQ, STEP_SLOTS, PART, NT)
    devices = lax.axis_size("wave") * lax.axis_size("lev")
    out_shape = (devices, 2 * half // devices * groups, SQ * PART)
    out = jax.ShapeDtypeStruct(out_shape, F32)
    out_spec = pl.BlockSpec(out_shape, lambda i, wm, br: (0, 0, 0))
    return pl.pallas_call(
        functools.partial(legendre_kernel, slots),
        out_shape=[out, out],
        grid_spec=pltpu.PrefetchScalarGridSpec(
            num_scalar_prefetch=2,
            grid=(groups // STEP_SLOTS,),
            in_specs=[
                pl.BlockSpec(spec_block, low_map),
                pl.BlockSpec(spec_block, up_map),
                pl.BlockSpec(spec_block, lambda i, wm, br: (0, i, 0, 0)),
                pl.BlockSpec((SQ, STEP_SLOTS, half, NT), lambda i, wm, br: (0, i, 0, 0)),
                pl.BlockSpec(memory_space=pltpu.SMEM),
            ],
            out_specs=[out_spec, out_spec],
            scratch_shapes=[pltpu.VMEM((groups * 2 * half, SQ * PART), F32)] * 2,
        ),
        compiler_params=pltpu.CompilerParams(vmem_limit_bytes=VMEM_LIMIT),
        cost_estimate=pl.CostEstimate(flops=2 * slots * 2 * half * 48 * NT, bytes_accessed=slots * NT * 2 * (48 + half), transcendentals=0),
        name="legendre_sums",
    )(wave_map, brackets, spec, spec, spec, leg, lev_weight)


def unit_circle(product, quarter):
    turn = jnp.round(product * (1.0 / quarter))
    rest = product - turn * quarter
    x = rest * ((0.5 * math.pi) / quarter)
    x2 = x * x
    sine = x * (1.0 + x2 * (-1.0 / 6 + x2 * (1.0 / 120 + x2 * (-1.0 / 5040 + x2 * (1.0 / 362880)))))
    cosine = 1.0 + x2 * (-0.5 + x2 * (1.0 / 24 + x2 * (-1.0 / 720 + x2 * (1.0 / 40320))))
    quad = turn.astype(jnp.int32) & 3
    odd = (quad & 1) == 1
    c = jnp.where(odd, sine, cosine)
    s = jnp.where(odd, cosine, sine)
    c = jnp.where((quad == 1) | (quad == 2), -c, c)
    s = jnp.where(quad >= 2, -s, s)
    return c, s


def own_points(points_ref, r2):
    wave = lax.axis_index("wave")
    lev = lax.axis_index("lev")
    row = 2 * (wave * lax.axis_size("lev") + lev) + r2
    return points_ref[row % points_ref.shape[0]]


def table_kernel(points_ref, map_ref, hi_ref, lo_ref, perm_ref):
    r2 = pl.program_id(0)
    kb = pl.program_id(1)
    rows = hi_ref.shape[1]
    steps = pl.num_programs(1)
    quarter = (own_points(points_ref, r2) // 4).astype(F32)
    perm_rows = perm_ref.shape[0]
    order = (r2 * steps + kb) * perm_rows + iota((perm_rows, 1), 0)
    wanted = jnp.where(order < HALF_M, 2 * order, 2 * (order - HALF_M) + 1)
    perm_ref[...] = jnp.where(map_ref[...] == wanted, 1.0, 0.0).astype(BF16)

    def put(tile, chunk, value):
        lanes = slice(tile * 128, tile * 128 + 128)
        hi = value.astype(BF16)
        hi_ref[0, pl.ds(chunk, 16), lanes] = hi
        lo_ref[0, pl.ds(chunk, 16), lanes] = (value - hi.astype(F32)).astype(BF16)

    def chunk_body(i, carry):
        chunk = pl.multiple_of(i * 16, 16)
        k = (kb * rows + chunk + iota((16, 128), 0)).astype(F32)
        lane = iota((16, 128), 1).astype(F32)
        c, s = unit_circle(2.0 * lane * k, quarter)
        c1, s1 = unit_circle(k, quarter)
        ct, st = unit_circle(256.0 * k, quarter)
        co = c * c1 - s * s1
        so = s * c1 + c * s1
        for t in range(HALF_M // 128):
            if t:
                c, s = c * ct - s * st, s * ct + c * st
                co, so = co * ct - so * st, so * ct + co * st
            put(t, chunk, c)
            put(5 + t, chunk, s)
            put(10 + t, chunk, co)
            put(15 + t, chunk, so)
        return carry

    lax.fori_loop(0, rows // 16, chunk_body, 0, unroll=2)


def tables(row_points, slot_map):
    steps = 8
    rows = KPTS // steps
    table = jax.ShapeDtypeStruct((2, KPTS, 2 * M), BF16)
    table_spec = pl.BlockSpec((1, rows, 2 * M), lambda r, k: (r, k, 0))
    return pl.pallas_call(
        table_kernel,
        out_shape=[table, table, jax.ShapeDtypeStruct((M, M), BF16)],
        grid=(2, steps),
        in_specs=[pl.BlockSpec(memory_space=pltpu.SMEM), pl.BlockSpec(memory_space=pltpu.VMEM)],
        out_specs=[table_spec, table_spec, pl.BlockSpec((M // (2 * steps), M), lambda r, k: (r * steps + k, 0))],
        compiler_params=pltpu.CompilerParams(vmem_limit_bytes=VMEM_LIMIT),
        cost_estimate=pl.CostEstimate(flops=2 * KPTS * 2 * M * 12, bytes_accessed=2 * KPTS * 2 * M * 4 + M * M * 2, transcendentals=0),
        name="fourier_tables",
    )(row_points, slot_map)


def pick_tables(plev):
    wide = plev * 2 * PART
    out = np.zeros((2, 4, 2 * wide, 2 * wide), np.float32)
    plans = (
        ((0, 1), (0, 1), (0, 1), (0, 1)),
        ((1, -1), (1, 1), (1, -1), (1, 1)),
        ((0, 1), (0, 1), (1, -1), (1, -1)),
        ((1, -1), (1, 1), (0, -1), (0, 1)),
    )
    for r2 in range(2):
        for kind, plan in enumerate(plans):
            for image, (part, sgn) in enumerate(plan):
                for hl in range(2):
                    for p in range(plev):
                        for q in range(FS):
                            src = hl * wide + p * 2 * PART + r2 * PART + q * 2 + part
                            dst = hl * wide + image * plev * FS + p * FS + q
                            out[r2, kind, src, dst] = sgn
    return out.astype(jnp.bfloat16)


def mean_table(plev):
    wide = plev * FS * 4
    out = np.zeros((2 * 4 * plev, 2 * wide), np.float32)
    for quarter in range(4):
        for p in range(plev):
            for part in range(2):
                image_quarter = (quarter + part) % 4
                start = (image_quarter * 2 + part) * plev * FS + p * FS
                out[part * 4 * plev + quarter * plev + p, start : start + FS] = 0.5 / STEPS
    return out.astype(jnp.bfloat16)


def flip_table():
    return np.fliplr(np.eye(KBLK, dtype=np.float32)).astype(jnp.bfloat16)


def split(x):
    hi = x.astype(BF16)
    return hi, (x - hi.astype(F32)).astype(BF16)


def nt_dot(a, b):
    return lax.dot_general(a, b, (((1,), (1,)), ((), ())), preferred_element_type=F32)


def nn_dot(a, b):
    return jnp.dot(a, b, preferred_element_type=F32)


def synth_kernel(
    points_ref, moved_ref, pick_ref, mean_ref, flip_ref, perm_hbm, hi_hbm, lo_hbm, out_ref,
    perm_ref, hi_ref, lo_ref, mixed, coef, direct, mirror, line, sems,
):
    waves, plev, block_rows, _ = moved_ref.shape
    sub = block_rows // 2
    wide = plev * 2 * PART
    part_rows = waves * sub
    copies = [pltpu.make_async_copy(perm_hbm, perm_ref, sems.at[0])]
    for r2 in range(2):
        copies.append(pltpu.make_async_copy(hi_hbm.at[r2], hi_ref.at[r2], sems.at[1 + 2 * r2]))
        copies.append(pltpu.make_async_copy(lo_hbm.at[r2], lo_ref.at[r2], sems.at[2 + 2 * r2]))
    for copy in copies:
        copy.start()

    for base in range(0, plev * 2, 8):
        cur = []
        for g in range(base, base + 8):
            pieces = [moved_ref[w, g // 2, (g % 2) * sub : (g % 2 + 1) * sub, :] for w in range(waves)]
            cur.append(jnp.concatenate(pieces, axis=0))
        group = iota((part_rows, 128), 1) // PART
        for bit in (1, 2, 4):
            unset = (group & bit) == 0
            nxt = list(cur)
            for g in range(8):
                if g & bit == 0:
                    a, b = cur[g], cur[g + bit]
                    nxt[g] = jnp.where(unset, a, pltpu.roll(b, bit * PART, 1))
                    nxt[g + bit] = jnp.where(unset, pltpu.roll(a, 128 - bit * PART, 1), b)
            cur = nxt
        for sq in range(SQ):
            hi, lo = split(cur[sq])
            lane = base * PART
            mixed[sq * part_rows : (sq + 1) * part_rows, lane : lane + 128] = hi
            mixed[sq * part_rows : (sq + 1) * part_rows, wide + lane : wide + lane + 128] = lo

    lane_row = (iota((1, 2 * wide), 1) // PART) % 2
    limit0 = (own_points(points_ref, 0) - 1) // 2
    limit1 = (own_points(points_ref, 1) - 1) // 2
    limit = jnp.where(lane_row == 0, limit0, limit1)
    place = iota((HALF_M, 1), 0)
    turned = (iota((1, 2 * wide), 1) % wide) // (plev * FS) >= 2
    flip_sign = jnp.where(turned & (place % 2 == 1), -1.0, 1.0).astype(BF16)
    copies[0].wait()
    for odd in range(2):
        ordered = nn_dot(perm_ref[odd * HALF_M : (odd + 1) * HALF_M, :], mixed[...])
        wave = 2 * place + odd
        factor = jnp.where(wave <= limit, jnp.where(wave == 0, 1.0, 2.0), 0.0)
        ordered = (ordered * factor).astype(BF16)
        for row in range(2):
            for part in range(2):
                picked = nn_dot(ordered, pick_ref[row, odd * 2 + part]).astype(BF16)
                coef[row, odd, part * HALF_M : (part + 1) * HALF_M, :] = picked * flip_sign
    direct[...] = jnp.zeros_like(direct)
    mirror[...] = jnp.zeros_like(mirror)

    for r2 in range(2):
        copies[1 + 2 * r2].wait()
        copies[2 + 2 * r2].wait()

        def contraction(odd):
            lanes = slice(odd * M, (odd + 1) * M)
            both = nn_dot(hi_ref[r2, :, lanes], coef[r2, odd])
            rest = nn_dot(lo_ref[r2, :, lanes], coef[r2, odd, :, :wide])
            return both[:, :wide] + (both[:, wide:] + rest)

        even_sum = contraction(0)
        odd_sum = contraction(1)
        plus = even_sum + odd_sum
        minus = even_sum - odd_sum
        squares = jnp.concatenate([plus * plus, minus * minus], axis=1)
        sq_hi, sq_lo = split(squares)
        energy = nt_dot(mean_ref[...], sq_hi) + nt_dot(mean_ref[...], sq_lo)
        rows = 4 * plev
        direct[:, :KPTS] = energy[:rows]
        en_hi, en_lo = split(energy[rows:])
        for t in range(KPTS // KBLK):
            lanes = slice(t * KBLK, (t + 1) * KBLK)
            back = KPTS - (t + 1) * KBLK
            mirror[:, back : back + KBLK] = nn_dot(en_hi[:, lanes], flip_ref[...]) + nn_dot(en_lo[:, lanes], flip_ref[...])

        quarter = own_points(points_ref, r2) // 4
        lane = iota((rows, BUF), 1)
        shift = (quarter + (BUF - (KPTS - 1))) % BUF
        whole = jnp.where(lane <= quarter // 2, direct[...], pltpu.roll(mirror[...], shift, 1))
        direct[...] = whole
        line[...] = jnp.zeros_like(line)
        lane = iota((plev, BUF), 1)
        for b in range(4):
            start = quarter * b
            inner = start % 128
            base = pl.multiple_of(start - inner, 128)
            piece = pltpu.roll(direct[b * plev : (b + 1) * plev, :], inner, 1)
            old = line[:, pl.ds(base, BUF)]
            line[:, pl.ds(base, BUF)] = jnp.where((lane >= inner) & (lane < inner + quarter), piece, old)
        out_ref[:, pl.ds(r2, 1), :] = line[:, :ROWPAD].reshape(plev, 1, ROWPAD)


def synthesis(moved, perm, table_hi, table_lo, row_points):
    waves, plev, block_rows, _ = moved.shape
    wide = plev * 2 * PART
    vmem = pl.BlockSpec(memory_space=pltpu.VMEM)
    anywhere = pl.BlockSpec(memory_space=pl.ANY)
    return pl.pallas_call(
        synth_kernel,
        out_shape=jax.ShapeDtypeStruct((plev, 2, ROWPAD), F32),
        in_specs=[pl.BlockSpec(memory_space=pltpu.SMEM), vmem, vmem, vmem, vmem, anywhere, anywhere, anywhere],
        out_specs=vmem,
        scratch_shapes=[
            pltpu.VMEM((M, M), BF16),
            pltpu.VMEM((2, KPTS, 2 * M), BF16),
            pltpu.VMEM((2, KPTS, 2 * M), BF16),
            pltpu.VMEM((M, 2 * wide), BF16),
            pltpu.VMEM((2, 2, M, 2 * wide), BF16),
            pltpu.VMEM((4 * plev, BUF), F32),
            pltpu.VMEM((4 * plev, BUF), F32),
            pltpu.VMEM((plev, 3 * 1280 + BUF), F32),
            pltpu.SemaphoreType.DMA((5,)),
        ],
        compiler_params=pltpu.CompilerParams(vmem_limit_bytes=VMEM_LIMIT),
        cost_estimate=pl.CostEstimate(flops=2 * 2 * KPTS * 2 * M * 384, bytes_accessed=2 * KPTS * 2 * M * 4 + M * M * 2, transcendentals=0),
        name="synthesis",
    )(row_points, moved, pick_tables(plev), mean_table(plev), flip_table(), perm, table_hi, table_lo)


def local(spectral, legendre, wave_map, row_points, brackets, lev_weight, climatology):
    slots = spectral.shape[0]
    half = legendre.shape[1]
    groups = slots // SQ
    wave_count = lax.axis_size("wave")
    lev_count = lax.axis_size("lev")
    rows_dev = 2 * half // (wave_count * lev_count)
    own, prev = legendre_sums(spectral, legendre, wave_map, brackets, lev_weight)
    from_next = lax.ppermute(prev, "lev", [(d, d - 1) for d in range(1, lev_count)])
    moved = lax.all_to_all(own + from_next, ("wave", "lev"), split_axis=0, concat_axis=0, tiled=True)
    moved = moved.reshape(wave_count, lev_count, rows_dev * groups, SQ * PART)
    slot_map = jnp.transpose(wave_map.reshape(wave_count, SQ, groups), (1, 0, 2)).reshape(1, M)
    table_hi, table_lo, perm = tables(row_points, slot_map)
    energy = synthesis(moved, perm, table_hi, table_lo, row_points)
    result = lax.all_to_all(energy, "lev", split_axis=0, concat_axis=0, tiled=True)
    result = result.reshape(1, rows_dev * lev_count, ROWPAD)
    points_all = jnp.concatenate([row_points, row_points])
    band_rows = rows_dev * lev_count
    out_points = lax.dynamic_slice_in_dim(points_all, lax.axis_index("wave") * band_rows, band_rows, 0)
    places = jnp.arange(ROWPAD, dtype=jnp.int32)
    inside = places[None, None, :] < out_points[None, :, None]
    return jnp.where(inside, result - climatology, 0.0)


def solution(mesh):
    placed = (
        P("wave", "lev", None),
        P("wave", None, None),
        P(),
        P(),
        P(),
        P(),
        P("lev", "wave", None),
    )
    return jax.shard_map(
        local, mesh=mesh, in_specs=placed, out_specs=P("lev", "wave", None), check_vma=False
    )
```

```python
import functools
import math

import jax
import jax.numpy as jnp
import numpy as np
from jax import lax
from jax.experimental import pallas as pl
from jax.experimental.pallas import tpu as pltpu
from jax.sharding import PartitionSpec as P

M = 1280
NT = 1280
LEV_DEV = 4
STEPS = 4
FIELDS = 2
ROWPAD = 5248

FS = FIELDS * STEPS
PART = 2 * FS
SQ = 8
STEP_SLOTS = 2
DEPTH = 3
HALF_M = M // 2
KPTS = 768
KBLK = 256
BUF = 1536
VMEM_LIMIT = 56 * 1024 * 1024
F32 = jnp.float32
BF16 = jnp.bfloat16


def iota(shape, dim):
    return lax.broadcasted_iota(jnp.int32, shape, dim)


def legendre_kernel(
    wave_map, brackets, weight_ref, spec_hbm, leg_hbm, own_ref, prev_ref,
    low_buf, up_buf, first_buf, leg_buf, own_rows, prev_rows, sems,
):
    groups = spec_hbm.shape[1]
    slots = SQ * groups
    steps = groups // STEP_SLOTS
    half = leg_hbm.shape[2]
    width = STEP_SLOTS * 2 * half
    wave = lax.axis_index("wave")
    lev = lax.axis_index("lev")
    lower = brackets[lev] - lev * LEV_DEV
    has_upper = lower < LEV_DEV - 1
    w = weight_ref[lev]
    upper_w = jnp.where(has_upper, 1.0 - w, 0.0)
    before = jnp.maximum(lev - 1, 0)
    crosses = (lev > 0) & (brackets[before] == lev * LEV_DEV - 1)
    first_w = jnp.where(crosses, 1.0 - weight_ref[before], 0.0)
    degree = iota((16, NT), 1)
    sign = (1 - 2 * (degree % 2)).astype(F32).astype(BF16)
    lane = iota((1, width), 1)
    south = lane % (2 * half) >= half

    def columns_copy(step, level, buf, kind):
        slot = step % DEPTH
        rows = pl.ds(pl.multiple_of(level * PART, PART), PART)
        src = spec_hbm.at[:, pl.ds(step * STEP_SLOTS, STEP_SLOTS), rows, :]
        return pltpu.make_async_copy(src, buf.at[slot], sems.at[slot, kind])

    def values_copy(step):
        slot = step % DEPTH
        return pltpu.make_async_copy(leg_hbm.at[:, pl.ds(step * STEP_SLOTS, STEP_SLOTS)], leg_buf.at[slot], sems.at[slot, 3])

    def fetch(step):
        values_copy(step).start()
        columns_copy(step, lower, low_buf, 0).start()

        @pl.when(has_upper)
        def _():
            columns_copy(step, lower + 1, up_buf, 1).start()

        @pl.when(crosses)
        def _():
            columns_copy(step, 0, first_buf, 2).start()

    def await_step(step):
        values_copy(step).wait()
        columns_copy(step, lower, low_buf, 0).wait()

        @pl.when(has_upper)
        def _():
            columns_copy(step, lower + 1, up_buf, 1).wait()

        @pl.when(crosses)
        def _():
            columns_copy(step, 0, first_buf, 2).wait()

    for step in range(DEPTH - 1):
        fetch(step)

    @pl.when(jnp.logical_not(has_upper))
    def _():
        up_buf[...] = jnp.zeros_like(up_buf)

    @pl.when(jnp.logical_not(crosses))
    def _():
        first_buf[...] = jnp.zeros_like(first_buf)

    def step_body(step, carry):
        slot = step % DEPTH
        await_step(step)

        @pl.when(step + DEPTH - 1 < steps)
        def _():
            fetch(step + DEPTH - 1)

        owns, firsts = [], []
        for pair in range(SQ // 2):
            orders, values, columns = [], [], []
            for a in range(2):
                sq = 2 * pair + a
                for b in range(STEP_SLOTS):
                    m = wave_map[wave * slots + sq * groups + step * STEP_SLOTS + b]
                    orders.append(m)
                    kept = jnp.where(degree >= m, 1.0, 0.0).astype(BF16)
                    plain = [leg_buf[slot, sq, b, i : i + 16, :] * kept for i in range(0, half, 16)]
                    values += plain + [x * sign for x in plain]
                    columns += [buf[slot, sq, b] for buf in (low_buf, up_buf, first_buf)]
            sums = nt_dot(jnp.concatenate(columns, axis=0), jnp.concatenate(values, axis=0))
            for a in range(2):
                own = jnp.zeros((PART, width), F32)
                first = jnp.zeros((PART, width), F32)
                for b in range(STEP_SLOTS):
                    at = (a * STEP_SLOTS + b) * 3 * PART
                    block = sums[at : at + 3 * PART, a * width : (a + 1) * width]
                    parity = (1 - 2 * (orders[a * STEP_SLOTS + b] % 2)).astype(F32)
                    factor = jnp.where(south, parity, 1.0)
                    here = lane // (2 * half) == b
                    mixed = block[:PART] * (factor * w) + block[PART : 2 * PART] * (factor * upper_w)
                    own = jnp.where(here, mixed, own)
                    first = jnp.where(here, block[2 * PART :] * (factor * first_w), first)
                owns.append(own)
                firsts.append(first)
        for ref, parts in ((own_rows, owns), (prev_rows, firsts)):
            stacked = jnp.concatenate(parts, axis=0)
            for t in range(width // 128):
                at = pl.multiple_of(step * width + t * 128, 128)
                ref[pl.ds(at, 128), :] = stacked[:, t * 128 : (t + 1) * 128].T
        return carry

    lax.fori_loop(0, steps, step_body, 0)
    rows = 2 * half
    for rows_ref, ref in ((own_rows, own_ref), (prev_rows, prev_ref)):
        rows_dev = ref.shape[1] // groups
        for r in range(rows):
            ref[r // rows_dev, (r % rows_dev) * groups : (r % rows_dev + 1) * groups, :] = rows_ref[pl.ds(r, groups, stride=rows), :]


def legendre_sums(spectral, legendre, wave_map, brackets, lev_weight):
    slots, cols, _ = spectral.shape
    half = legendre.shape[1]
    groups = slots // SQ
    spec = spectral.reshape(SQ, groups, cols, NT)
    leg = legendre.reshape(SQ, groups, half, NT)
    devices = lax.axis_size("wave") * lax.axis_size("lev")
    out = jax.ShapeDtypeStruct((devices, 2 * half // devices * groups, SQ * PART), F32)
    smem = pl.BlockSpec(memory_space=pltpu.SMEM)
    vmem = pl.BlockSpec(memory_space=pltpu.VMEM)
    anywhere = pl.BlockSpec(memory_space=pl.ANY)
    return pl.pallas_call(
        legendre_kernel,
        out_shape=[out, out],
        in_specs=[smem, smem, smem, anywhere, anywhere],
        out_specs=[vmem, vmem],
        scratch_shapes=[pltpu.VMEM((DEPTH, SQ, STEP_SLOTS, PART, NT), BF16)] * 3
        + [pltpu.VMEM((DEPTH, SQ, STEP_SLOTS, half, NT), BF16)]
        + [pltpu.VMEM((groups * 2 * half, SQ * PART), F32)] * 2
        + [pltpu.SemaphoreType.DMA((DEPTH, 4))],
        compiler_params=pltpu.CompilerParams(vmem_limit_bytes=VMEM_LIMIT),
        cost_estimate=pl.CostEstimate(flops=2 * slots * 2 * half * 48 * NT, bytes_accessed=slots * NT * 2 * (48 + half), transcendentals=0),
        name="legendre_sums",
    )(wave_map, brackets, lev_weight, spec, leg)


def unit_circle(product, quarter):
    turn = jnp.round(product * (1.0 / quarter))
    rest = product - turn * quarter
    x = rest * ((0.5 * math.pi) / quarter)
    x2 = x * x
    sine = x * (1.0 + x2 * (-1.0 / 6 + x2 * (1.0 / 120 + x2 * (-1.0 / 5040 + x2 * (1.0 / 362880)))))
    cosine = 1.0 + x2 * (-0.5 + x2 * (1.0 / 24 + x2 * (-1.0 / 720 + x2 * (1.0 / 40320))))
    quad = turn.astype(jnp.int32) & 3
    odd = (quad & 1) == 1
    c = jnp.where(odd, sine, cosine)
    s = jnp.where(odd, cosine, sine)
    c = jnp.where((quad == 1) | (quad == 2), -c, c)
    s = jnp.where(quad >= 2, -s, s)
    return c, s


def own_points(points_ref, r2):
    wave = lax.axis_index("wave")
    lev = lax.axis_index("lev")
    row = 2 * (wave * lax.axis_size("lev") + lev) + r2
    return points_ref[row % points_ref.shape[0]]


def table_kernel(points_ref, map_ref, hi_ref, lo_ref, perm_ref):
    r2 = pl.program_id(0)
    kb = pl.program_id(1)
    rows = hi_ref.shape[1]
    steps = pl.num_programs(1)
    quarter = (own_points(points_ref, r2) // 4).astype(F32)
    perm_rows = perm_ref.shape[0]
    order = (r2 * steps + kb) * perm_rows + iota((perm_rows, 1), 0)
    wanted = jnp.where(order < HALF_M, 2 * order, 2 * (order - HALF_M) + 1)
    perm_ref[...] = jnp.where(map_ref[...] == wanted, 1.0, 0.0).astype(BF16)

    def put(tile, chunk, value):
        lanes = slice(tile * 128, tile * 128 + 128)
        hi = value.astype(BF16)
        hi_ref[0, pl.ds(chunk, 16), lanes] = hi
        lo_ref[0, pl.ds(chunk, 16), lanes] = (value - hi.astype(F32)).astype(BF16)

    def chunk_body(i, carry):
        chunk = pl.multiple_of(i * 16, 16)
        k = (kb * rows + chunk + iota((16, 128), 0)).astype(F32)
        lane = iota((16, 128), 1).astype(F32)
        c, s = unit_circle(2.0 * lane * k, quarter)
        c1, s1 = unit_circle(k, quarter)
        ct, st = unit_circle(256.0 * k, quarter)
        co = c * c1 - s * s1
        so = s * c1 + c * s1
        for t in range(HALF_M // 128):
            if t:
                c, s = c * ct - s * st, s * ct + c * st
                co, so = co * ct - so * st, so * ct + co * st
            put(t, chunk, c)
            put(5 + t, chunk, s)
            put(10 + t, chunk, co)
            put(15 + t, chunk, so)
        return carry

    lax.fori_loop(0, rows // 16, chunk_body, 0, unroll=2)


def tables(row_points, slot_map):
    steps = 8
    rows = KPTS // steps
    table = jax.ShapeDtypeStruct((2, KPTS, 2 * M), BF16)
    table_spec = pl.BlockSpec((1, rows, 2 * M), lambda r, k: (r, k, 0))
    return pl.pallas_call(
        table_kernel,
        out_shape=[table, table, jax.ShapeDtypeStruct((M, M), BF16)],
        grid=(2, steps),
        in_specs=[pl.BlockSpec(memory_space=pltpu.SMEM), pl.BlockSpec(memory_space=pltpu.VMEM)],
        out_specs=[table_spec, table_spec, pl.BlockSpec((M // (2 * steps), M), lambda r, k: (r * steps + k, 0))],
        compiler_params=pltpu.CompilerParams(vmem_limit_bytes=VMEM_LIMIT),
        cost_estimate=pl.CostEstimate(flops=2 * KPTS * 2 * M * 12, bytes_accessed=2 * KPTS * 2 * M * 4 + M * M * 2, transcendentals=0),
        name="fourier_tables",
    )(row_points, slot_map)


def pick_tables(plev):
    wide = plev * 2 * PART
    out = np.zeros((2, 4, 2 * wide, 2 * wide), np.float32)
    plans = (
        ((0, 1), (0, 1), (0, 1), (0, 1)),
        ((1, -1), (1, 1), (1, -1), (1, 1)),
        ((0, 1), (0, 1), (1, -1), (1, -1)),
        ((1, -1), (1, 1), (0, -1), (0, 1)),
    )
    for r2 in range(2):
        for kind, plan in enumerate(plans):
            for image, (part, sgn) in enumerate(plan):
                for hl in range(2):
                    for p in range(plev):
                        for q in range(FS):
                            src = hl * wide + p * 2 * PART + r2 * PART + q * 2 + part
                            dst = hl * wide + image * plev * FS + p * FS + q
                            out[r2, kind, src, dst] = sgn
    return out.astype(jnp.bfloat16)


def mean_table(plev):
    wide = plev * FS * 4
    out = np.zeros((2 * 4 * plev, 2 * wide), np.float32)
    for quarter in range(4):
        for p in range(plev):
            for part in range(2):
                image_quarter = (quarter + part) % 4
                start = (image_quarter * 2 + part) * plev * FS + p * FS
                out[part * 4 * plev + quarter * plev + p, start : start + FS] = 0.5 / STEPS
    return out.astype(jnp.bfloat16)


def flip_table():
    return np.fliplr(np.eye(KBLK, dtype=np.float32)).astype(jnp.bfloat16)


def split(x):
    hi = x.astype(BF16)
    return hi, (x - hi.astype(F32)).astype(BF16)


def nt_dot(a, b):
    return lax.dot_general(a, b, (((1,), (1,)), ((), ())), preferred_element_type=F32)


def nn_dot(a, b):
    return jnp.dot(a, b, preferred_element_type=F32)


def synth_kernel(
    points_ref, moved_ref, pick_ref, mean_ref, flip_ref, perm_hbm, hi_hbm, lo_hbm, out_ref,
    perm_ref, hi_ref, lo_ref, mixed, coef, direct, mirror, line, sems,
):
    waves, plev, block_rows, _ = moved_ref.shape
    sub = block_rows // 2
    wide = plev * 2 * PART
    part_rows = waves * sub
    copies = [pltpu.make_async_copy(perm_hbm, perm_ref, sems.at[0])]
    for r2 in range(2):
        copies.append(pltpu.make_async_copy(hi_hbm.at[r2], hi_ref.at[r2], sems.at[1 + 2 * r2]))
        copies.append(pltpu.make_async_copy(lo_hbm.at[r2], lo_ref.at[r2], sems.at[2 + 2 * r2]))
    for copy in copies:
        copy.start()

    for base in range(0, plev * 2, 8):
        cur = []
        for g in range(base, base + 8):
            pieces = [moved_ref[w, g // 2, (g % 2) * sub : (g % 2 + 1) * sub, :] for w in range(waves)]
            cur.append(jnp.concatenate(pieces, axis=0))
        group = iota((part_rows, 128), 1) // PART
        for bit in (1, 2, 4):
            unset = (group & bit) == 0
            nxt = list(cur)
            for g in range(8):
                if g & bit == 0:
                    a, b = cur[g], cur[g + bit]
                    nxt[g] = jnp.where(unset, a, pltpu.roll(b, bit * PART, 1))
                    nxt[g + bit] = jnp.where(unset, pltpu.roll(a, 128 - bit * PART, 1), b)
            cur = nxt
        for sq in range(SQ):
            hi, lo = split(cur[sq])
            lane = base * PART
            mixed[sq * part_rows : (sq + 1) * part_rows, lane : lane + 128] = hi
            mixed[sq * part_rows : (sq + 1) * part_rows, wide + lane : wide + lane + 128] = lo

    lane_row = (iota((1, 2 * wide), 1) // PART) % 2
    limit0 = (own_points(points_ref, 0) - 1) // 2
    limit1 = (own_points(points_ref, 1) - 1) // 2
    limit = jnp.where(lane_row == 0, limit0, limit1)
    place = iota((HALF_M, 1), 0)
    turned = (iota((1, 2 * wide), 1) % wide) // (plev * FS) >= 2
    flip_sign = jnp.where(turned & (place % 2 == 1), -1.0, 1.0).astype(BF16)
    copies[0].wait()
    for odd in range(2):
        ordered = nn_dot(perm_ref[odd * HALF_M : (odd + 1) * HALF_M, :], mixed[...])
        wave = 2 * place + odd
        factor = jnp.where(wave <= limit, jnp.where(wave == 0, 1.0, 2.0), 0.0)
        ordered = (ordered * factor).astype(BF16)
        for row in range(2):
            for part in range(2):
                picked = nn_dot(ordered, pick_ref[row, odd * 2 + part]).astype(BF16)
                coef[row, odd, part * HALF_M : (part + 1) * HALF_M, :] = picked * flip_sign
    direct[...] = jnp.zeros_like(direct)
    mirror[...] = jnp.zeros_like(mirror)

    for r2 in range(2):
        copies[1 + 2 * r2].wait()
        copies[2 + 2 * r2].wait()

        def contraction(odd):
            lanes = slice(odd * M, (odd + 1) * M)
            both = nn_dot(hi_ref[r2, :, lanes], coef[r2, odd])
            rest = nn_dot(lo_ref[r2, :, lanes], coef[r2, odd, :, :wide])
            return both[:, :wide] + (both[:, wide:] + rest)

        even_sum = contraction(0)
        odd_sum = contraction(1)
        plus = even_sum + odd_sum
        minus = even_sum - odd_sum
        squares = jnp.concatenate([plus * plus, minus * minus], axis=1)
        sq_hi, sq_lo = split(squares)
        energy = nt_dot(mean_ref[...], sq_hi) + nt_dot(mean_ref[...], sq_lo)
        rows = 4 * plev
        direct[:, :KPTS] = energy[:rows]
        en_hi, en_lo = split(energy[rows:])
        for t in range(KPTS // KBLK):
            lanes = slice(t * KBLK, (t + 1) * KBLK)
            back = KPTS - (t + 1) * KBLK
            mirror[:, back : back + KBLK] = nn_dot(en_hi[:, lanes], flip_ref[...]) + nn_dot(en_lo[:, lanes], flip_ref[...])

        quarter = own_points(points_ref, r2) // 4
        lane = iota((rows, BUF), 1)
        shift = (quarter + (BUF - (KPTS - 1))) % BUF
        whole = jnp.where(lane <= quarter // 2, direct[...], pltpu.roll(mirror[...], shift, 1))
        direct[...] = whole
        line[...] = jnp.zeros_like(line)
        lane = iota((plev, BUF), 1)
        for b in range(4):
            start = quarter * b
            inner = start % 128
            base = pl.multiple_of(start - inner, 128)
            piece = pltpu.roll(direct[b * plev : (b + 1) * plev, :], inner, 1)
            old = line[:, pl.ds(base, BUF)]
            line[:, pl.ds(base, BUF)] = jnp.where((lane >= inner) & (lane < inner + quarter), piece, old)
        out_ref[:, pl.ds(r2, 1), :] = line[:, :ROWPAD].reshape(plev, 1, ROWPAD)


def synthesis(moved, perm, table_hi, table_lo, row_points):
    waves, plev, block_rows, _ = moved.shape
    wide = plev * 2 * PART
    vmem = pl.BlockSpec(memory_space=pltpu.VMEM)
    anywhere = pl.BlockSpec(memory_space=pl.ANY)
    return pl.pallas_call(
        synth_kernel,
        out_shape=jax.ShapeDtypeStruct((plev, 2, ROWPAD), F32),
        in_specs=[pl.BlockSpec(memory_space=pltpu.SMEM), vmem, vmem, vmem, vmem, anywhere, anywhere, anywhere],
        out_specs=vmem,
        scratch_shapes=[
            pltpu.VMEM((M, M), BF16),
            pltpu.VMEM((2, KPTS, 2 * M), BF16),
            pltpu.VMEM((2, KPTS, 2 * M), BF16),
            pltpu.VMEM((M, 2 * wide), BF16),
            pltpu.VMEM((2, 2, M, 2 * wide), BF16),
            pltpu.VMEM((4 * plev, BUF), F32),
            pltpu.VMEM((4 * plev, BUF), F32),
            pltpu.VMEM((plev, 3 * 1280 + BUF), F32),
            pltpu.SemaphoreType.DMA((5,)),
        ],
        compiler_params=pltpu.CompilerParams(vmem_limit_bytes=VMEM_LIMIT),
        cost_estimate=pl.CostEstimate(flops=2 * 2 * KPTS * 2 * M * 384, bytes_accessed=2 * KPTS * 2 * M * 4 + M * M * 2, transcendentals=0),
        name="synthesis",
    )(row_points, moved, pick_tables(plev), mean_table(plev), flip_table(), perm, table_hi, table_lo)


def local(spectral, legendre, wave_map, row_points, brackets, lev_weight, climatology):
    slots = spectral.shape[0]
    half = legendre.shape[1]
    groups = slots // SQ
    wave_count = lax.axis_size("wave")
    lev_count = lax.axis_size("lev")
    rows_dev = 2 * half // (wave_count * lev_count)
    own, prev = legendre_sums(spectral, legendre, wave_map, brackets, lev_weight)
    from_next = lax.ppermute(prev, "lev", [(d, d - 1) for d in range(1, lev_count)])
    moved = lax.all_to_all(own + from_next, ("wave", "lev"), split_axis=0, concat_axis=0, tiled=True)
    moved = moved.reshape(wave_count, lev_count, rows_dev * groups, SQ * PART)
    slot_map = jnp.transpose(wave_map.reshape(wave_count, SQ, groups), (1, 0, 2)).reshape(1, M)
    table_hi, table_lo, perm = tables(row_points, slot_map)
    energy = synthesis(moved, perm, table_hi, table_lo, row_points)
    result = lax.all_to_all(energy, "lev", split_axis=0, concat_axis=0, tiled=True)
    result = result.reshape(1, rows_dev * lev_count, ROWPAD)
    points_all = jnp.concatenate([row_points, row_points])
    band_rows = rows_dev * lev_count
    out_points = lax.dynamic_slice_in_dim(points_all, lax.axis_index("wave") * band_rows, band_rows, 0)
    places = jnp.arange(ROWPAD, dtype=jnp.int32)
    inside = places[None, None, :] < out_points[None, :, None]
    return jnp.where(inside, result - climatology, 0.0)


def solution(mesh):
    placed = (
        P("wave", "lev", None),
        P("wave", None, None),
        P(),
        P(),
        P(),
        P(),
        P("lev", "wave", None),
    )
    return jax.shard_map(
        local, mesh=mesh, in_specs=placed, out_specs=P("lev", "wave", None), check_vma=False
    )
```

```python
import functools
import math

import jax
import jax.numpy as jnp
import numpy as np
from jax import lax
from jax.experimental import pallas as pl
from jax.experimental.pallas import tpu as pltpu
from jax.sharding import PartitionSpec as P

M = 1280
NT = 1280
LEV_DEV = 4
STEPS = 4
FIELDS = 2
ROWPAD = 5248

FS = FIELDS * STEPS
PART = 2 * FS
SQ = 8
STEP_SLOTS = 2
DEPTH = 3
HALF_M = M // 2
KPTS = 672
KPAD = 768
KBLK = 256
TABLE_STEPS = 7
PERM_ROWS = 128
BUF = 1536
MIB = 1024 * 1024
F32 = jnp.float32
BF16 = jnp.bfloat16


def iota(shape, dim):
    return lax.broadcasted_iota(jnp.int32, shape, dim)


def legendre_kernel(
    first_group, count, wave_map, brackets, weight_ref, spec_hbm, leg_hbm, own_ref, prev_ref,
    low_buf, up_buf, first_buf, leg_buf, own_rows, prev_rows, sems,
):
    groups = spec_hbm.shape[1]
    slots = SQ * groups
    steps = count // STEP_SLOTS
    half = leg_hbm.shape[2]
    width = STEP_SLOTS * 2 * half
    wave = lax.axis_index("wave")
    lev = lax.axis_index("lev")
    lower = brackets[lev] - lev * LEV_DEV
    has_upper = lower < LEV_DEV - 1
    w = weight_ref[lev]
    upper_w = jnp.where(has_upper, 1.0 - w, 0.0)
    before = jnp.maximum(lev - 1, 0)
    crosses = (lev > 0) & (brackets[before] == lev * LEV_DEV - 1)
    first_w = jnp.where(crosses, 1.0 - weight_ref[before], 0.0)
    degree = iota((16, NT), 1)
    sign = (1 - 2 * (degree % 2)).astype(F32).astype(BF16)
    lane = iota((1, width), 1)
    south = lane % (2 * half) >= half

    def columns_copy(step, level, buf, kind):
        slot = step % DEPTH
        rows = pl.ds(pl.multiple_of(level * PART, PART), PART)
        src = spec_hbm.at[:, pl.ds(first_group + step * STEP_SLOTS, STEP_SLOTS), rows, :]
        return pltpu.make_async_copy(src, buf.at[slot], sems.at[slot, kind])

    def values_copy(step):
        slot = step % DEPTH
        src = leg_hbm.at[:, pl.ds(first_group + step * STEP_SLOTS, STEP_SLOTS)]
        return pltpu.make_async_copy(src, leg_buf.at[slot], sems.at[slot, 3])

    def fetch(step):
        values_copy(step).start()
        columns_copy(step, lower, low_buf, 0).start()

        @pl.when(has_upper)
        def _():
            columns_copy(step, lower + 1, up_buf, 1).start()

        @pl.when(crosses)
        def _():
            columns_copy(step, 0, first_buf, 2).start()

    def await_step(step):
        values_copy(step).wait()
        columns_copy(step, lower, low_buf, 0).wait()

        @pl.when(has_upper)
        def _():
            columns_copy(step, lower + 1, up_buf, 1).wait()

        @pl.when(crosses)
        def _():
            columns_copy(step, 0, first_buf, 2).wait()

    for step in range(DEPTH - 1):
        fetch(step)

    @pl.when(jnp.logical_not(has_upper))
    def _():
        up_buf[...] = jnp.zeros_like(up_buf)

    @pl.when(jnp.logical_not(crosses))
    def _():
        first_buf[...] = jnp.zeros_like(first_buf)

    def step_body(step, carry):
        slot = step % DEPTH
        await_step(step)

        @pl.when(step + DEPTH - 1 < steps)
        def _():
            fetch(step + DEPTH - 1)

        owns, firsts = [], []
        for pair in range(SQ // 2):
            orders, values, columns = [], [], []
            for a in range(2):
                sq = 2 * pair + a
                for b in range(STEP_SLOTS):
                    m = wave_map[wave * slots + sq * groups + first_group + step * STEP_SLOTS + b]
                    orders.append(m)
                    kept = jnp.where(degree >= m, 1.0, 0.0).astype(BF16)
                    plain = [leg_buf[slot, sq, b, i : i + 16, :] * kept for i in range(0, half, 16)]
                    values += plain + [x * sign for x in plain]
                    columns += [buf[slot, sq, b] for buf in (low_buf, up_buf, first_buf)]
            sums = nt_dot(jnp.concatenate(columns, axis=0), jnp.concatenate(values, axis=0))
            for a in range(2):
                own = jnp.zeros((PART, width), F32)
                first = jnp.zeros((PART, width), F32)
                for b in range(STEP_SLOTS):
                    at = (a * STEP_SLOTS + b) * 3 * PART
                    block = sums[at : at + 3 * PART, a * width : (a + 1) * width]
                    parity = (1 - 2 * (orders[a * STEP_SLOTS + b] % 2)).astype(F32)
                    factor = jnp.where(south, parity, 1.0)
                    here = lane // (2 * half) == b
                    mixed = block[:PART] * (factor * w) + block[PART : 2 * PART] * (factor * upper_w)
                    own = jnp.where(here, mixed, own)
                    first = jnp.where(here, block[2 * PART :] * (factor * first_w), first)
                owns.append(own)
                firsts.append(first)
        for ref, parts in ((own_rows, owns), (prev_rows, firsts)):
            stacked = jnp.concatenate(parts, axis=0)
            for t in range(width // 128):
                at = pl.multiple_of(step * width + t * 128, 128)
                ref[pl.ds(at, 128), :] = stacked[:, t * 128 : (t + 1) * 128].T
        return carry

    lax.fori_loop(0, steps, step_body, 0)
    rows = 2 * half
    for rows_ref, ref in ((own_rows, own_ref), (prev_rows, prev_ref)):
        rows_dev = ref.shape[1] // count
        for r in range(rows):
            at = (r % rows_dev) * count
            ref[r // rows_dev, at : at + count, :] = rows_ref[pl.ds(r, count, stride=rows), :]


def legendre_sums(first_group, count, spectral, legendre, wave_map, brackets, lev_weight):
    slots, cols, _ = spectral.shape
    half = legendre.shape[1]
    groups = slots // SQ
    spec = spectral.reshape(SQ, groups, cols, NT)
    leg = legendre.reshape(SQ, groups, half, NT)
    devices = lax.axis_size("wave") * lax.axis_size("lev")
    out = jax.ShapeDtypeStruct((devices, 2 * half // devices * count, SQ * PART), F32)
    smem = pl.BlockSpec(memory_space=pltpu.SMEM)
    vmem = pl.BlockSpec(memory_space=pltpu.VMEM)
    anywhere = pl.BlockSpec(memory_space=pltpu.HBM)
    return pl.pallas_call(
        functools.partial(legendre_kernel, first_group, count),
        out_shape=[out, out],
        in_specs=[smem, smem, smem, anywhere, anywhere],
        out_specs=[vmem, vmem],
        scratch_shapes=[pltpu.VMEM((DEPTH, SQ, STEP_SLOTS, PART, NT), BF16)] * 3
        + [pltpu.VMEM((DEPTH, SQ, STEP_SLOTS, half, NT), BF16)]
        + [pltpu.VMEM((count * 2 * half, SQ * PART), F32)] * 2
        + [pltpu.SemaphoreType.DMA((DEPTH, 4))],
        compiler_params=pltpu.CompilerParams(vmem_limit_bytes=(24 if half < 64 else 40) * MIB),
        cost_estimate=pl.CostEstimate(
            flops=2 * SQ * count * 2 * half * 48 * NT, bytes_accessed=SQ * count * NT * 2 * (48 + half), transcendentals=0
        ),
        name="legendre_sums",
    )(
        wave_map, brackets, lev_weight,
        pltpu.with_memory_space_constraint(spec, pltpu.HBM), pltpu.with_memory_space_constraint(leg, pltpu.HBM),
    )


def unit_circle(product, points, inverse):
    big = 12582912.0
    turn = (product * inverse + big) - big
    x = (product - turn * points) * (math.pi * inverse)
    x2 = x * x
    sine = 0.0
    cosine = 0.0
    for power in (11, 9, 7, 5, 3, 1):
        sine = sine * x2 + (-1) ** (power // 2) / math.factorial(power)
    for power in (12, 10, 8, 6, 4, 2, 0):
        cosine = cosine * x2 + (-1) ** (power // 2) / math.factorial(power)
    sine = sine * x
    twice = sine + sine
    return 1.0 - twice * sine, twice * cosine


def own_points(points_ref, r2):
    wave = lax.axis_index("wave")
    lev = lax.axis_index("lev")
    row = 2 * (wave * lax.axis_size("lev") + lev) + r2
    return points_ref[row % points_ref.shape[0]]


def table_kernel(points_ref, map_ref, hi_ref, lo_ref, perm_ref):
    r2 = pl.program_id(0)
    kb = pl.program_id(1)
    rows = hi_ref.shape[1]
    points = own_points(points_ref, r2).astype(F32)
    inverse = 1.0 / points
    part = r2 * pl.num_programs(1) + kb

    @pl.when(part < M // PERM_ROWS)
    def _():
        order = part * PERM_ROWS + iota((PERM_ROWS, 1), 0)
        wanted = jnp.where(order < HALF_M, 2 * order, 2 * (order - HALF_M) + 1)
        perm_ref[...] = jnp.where(map_ref[...] == wanted, 1.0, 0.0).astype(BF16)

    lane = iota((16, 128), 1).astype(F32)

    def chunk_body(i, carry):
        chunk = pl.multiple_of(i * 16, 16)

        def put(tile, value):
            lanes = slice(tile * 128, tile * 128 + 128)
            hi = value.astype(BF16)
            hi_ref[0, pl.ds(chunk, 16), lanes] = hi
            lo_ref[0, pl.ds(chunk, 16), lanes] = (value - hi.astype(F32)).astype(BF16)

        k = (kb * rows + chunk + iota((16, 128), 0)).astype(F32)
        c, s = unit_circle(2.0 * lane * k, points, inverse)
        c1, s1 = unit_circle(k, points, inverse)
        ct, st = unit_circle(256.0 * k, points, inverse)
        co = c * c1 - s * s1
        so = s * c1 + c * s1
        for t in range(HALF_M // 128):
            if t:
                c, s = c * ct - s * st, s * ct + c * st
                co, so = co * ct - so * st, so * ct + co * st
            put(t, c)
            put(5 + t, s)
            put(10 + t, co)
            put(15 + t, so)
        return carry

    lax.fori_loop(0, rows // 16, chunk_body, 0, unroll=True)


def tables(row_points, slot_map):
    rows = KPTS // TABLE_STEPS
    table = jax.ShapeDtypeStruct((2, KPTS, 2 * M), BF16)
    table_spec = pl.BlockSpec((1, rows, 2 * M), lambda r, k: (r, k, 0))
    perm_spec = pl.BlockSpec((PERM_ROWS, M), lambda r, k: (jnp.minimum(r * TABLE_STEPS + k, M // PERM_ROWS - 1), 0))
    return pl.pallas_call(
        table_kernel,
        out_shape=[table, table, jax.ShapeDtypeStruct((M, M), BF16)],
        grid=(2, TABLE_STEPS),
        in_specs=[pl.BlockSpec(memory_space=pltpu.SMEM), pl.BlockSpec(memory_space=pltpu.VMEM)],
        out_specs=[table_spec, table_spec, perm_spec],
        compiler_params=pltpu.CompilerParams(vmem_limit_bytes=16 * MIB),
        cost_estimate=pl.CostEstimate(flops=2 * KPTS * 2 * M * 12, bytes_accessed=2 * KPTS * 2 * M * 4 + M * M * 2, transcendentals=0),
        name="fourier_tables",
    )(row_points, slot_map)


def pick_tables(plev):
    wide = plev * 2 * PART
    out = np.zeros((2, 4, 2 * wide, 2 * wide), np.float32)
    plans = (
        ((0, 1), (0, 1), (0, 1), (0, 1)),
        ((1, -1), (1, 1), (1, -1), (1, 1)),
        ((0, 1), (0, 1), (1, -1), (1, -1)),
        ((1, -1), (1, 1), (0, -1), (0, 1)),
    )
    for r2 in range(2):
        for kind, plan in enumerate(plans):
            for image, (part, sgn) in enumerate(plan):
                for hl in range(2):
                    for p in range(plev):
                        for q in range(FS):
                            src = hl * wide + p * 2 * PART + r2 * PART + q * 2 + part
                            dst = hl * wide + image * plev * FS + p * FS + q
                            out[r2, kind, src, dst] = sgn
    return out.astype(jnp.bfloat16)


def mean_table(plev):
    wide = plev * FS * 4
    out = np.zeros((2 * 4 * plev, 2 * wide), np.float32)
    for quarter in range(4):
        for p in range(plev):
            for part in range(2):
                image_quarter = (quarter + part) % 4
                start = (image_quarter * 2 + part) * plev * FS + p * FS
                out[part * 4 * plev + quarter * plev + p, start : start + FS] = 0.5 / STEPS
    return out.astype(jnp.bfloat16)


def flip_table():
    return np.fliplr(np.eye(KBLK, dtype=np.float32)).astype(jnp.bfloat16)


def split(x):
    hi = x.astype(BF16)
    return hi, (x - hi.astype(F32)).astype(BF16)


def nt_dot(a, b):
    return lax.dot_general(a, b, (((1,), (1,)), ((), ())), preferred_element_type=F32)


def nn_dot(a, b):
    return jnp.dot(a, b, preferred_element_type=F32)


def synth_kernel(parts, points_ref, *refs):
    moved_refs = refs[:parts]
    pick_ref, mean_ref, flip_ref, perm_ref, hi_ref, lo_ref, out_ref = refs[parts : parts + 7]
    mixed, coef, flat, mirror, line = refs[parts + 7 :]
    waves, plev, _, _ = moved_refs[0].shape
    wide = plev * 2 * PART
    part_rows = M // SQ
    for base in range(0, plev * 2, 8):
        cur = []
        for g in range(base, base + 8):
            pieces = []
            for ref in moved_refs:
                sub = ref.shape[2] // 2
                pieces += [ref[w, g // 2, (g % 2) * sub : (g % 2 + 1) * sub, :] for w in range(waves)]
            cur.append(jnp.concatenate(pieces, axis=0))
        group = iota((part_rows, 128), 1) // PART
        for bit in (1, 2, 4):
            unset = (group & bit) == 0
            nxt = list(cur)
            for g in range(8):
                if g & bit == 0:
                    a, b = cur[g], cur[g + bit]
                    nxt[g] = jnp.where(unset, a, pltpu.roll(b, bit * PART, 1))
                    nxt[g + bit] = jnp.where(unset, pltpu.roll(a, 128 - bit * PART, 1), b)
            cur = nxt
        for sq in range(SQ):
            hi, lo = split(cur[sq])
            lane = base * PART
            mixed[sq * part_rows : (sq + 1) * part_rows, lane : lane + 128] = hi
            mixed[sq * part_rows : (sq + 1) * part_rows, wide + lane : wide + lane + 128] = lo

    lane_row = (iota((1, 2 * wide), 1) // PART) % 2
    limit0 = (own_points(points_ref, 0) - 1) // 2
    limit1 = (own_points(points_ref, 1) - 1) // 2
    limit = jnp.where(lane_row == 0, limit0, limit1)
    place = iota((HALF_M, 1), 0)
    turned = (iota((1, 2 * wide), 1) % wide) // (plev * FS) >= 2
    flip_sign = jnp.where(turned & (place % 2 == 1), -1.0, 1.0).astype(BF16)
    for odd in range(2):
        ordered = nn_dot(perm_ref[odd * HALF_M : (odd + 1) * HALF_M, :], mixed[...])
        wave = 2 * place + odd
        factor = jnp.where(wave <= limit, jnp.where(wave == 0, 1.0, 2.0), 0.0)
        ordered = (ordered * factor).astype(BF16)
        for row in range(2):
            for part in range(2):
                picked = nn_dot(ordered, pick_ref[row, odd * 2 + part]).astype(BF16)
                coef[row, odd, part * HALF_M : (part + 1) * HALF_M, :] = picked * flip_sign
    flat[...] = jnp.zeros_like(flat)
    mirror[...] = jnp.zeros_like(mirror)

    for r2 in range(2):
        def contraction(odd):
            lanes = slice(odd * M, (odd + 1) * M)
            both = nn_dot(hi_ref[r2, :, lanes], coef[r2, odd])
            rest = nn_dot(lo_ref[r2, :, lanes], coef[r2, odd, :, :wide])
            return both[:, :wide] + (both[:, wide:] + rest)

        even_sum = contraction(0)
        odd_sum = contraction(1)
        plus = even_sum + odd_sum
        minus = even_sum - odd_sum
        squares = jnp.concatenate([plus * plus, minus * minus], axis=1)
        sq_hi, sq_lo = split(squares)
        energy = nt_dot(mean_ref[...], sq_hi) + nt_dot(mean_ref[...], sq_lo)
        rows = 4 * plev
        flat[:, :KPTS] = energy
        en_hi, en_lo = split(flat[rows:, :KPAD])
        for t in range(KPAD // KBLK):
            lanes = slice(t * KBLK, (t + 1) * KBLK)
            back = KPAD - (t + 1) * KBLK
            mirror[:, back : back + KBLK] = nn_dot(en_hi[:, lanes], flip_ref[...]) + nn_dot(en_lo[:, lanes], flip_ref[...])

        quarter = own_points(points_ref, r2) // 4
        lane = iota((rows, BUF), 1)
        shift = (quarter + (BUF - (KPAD - 1))) % BUF
        flat[:rows, :] = jnp.where(lane <= quarter // 2, flat[:rows, :], pltpu.roll(mirror[...], shift, 1))
        line[...] = jnp.zeros_like(line)
        lane = iota((plev, BUF), 1)
        for b in range(4):
            start = quarter * b
            inner = start % 128
            base = pl.multiple_of(start - inner, 128)
            piece = pltpu.roll(flat[b * plev : (b + 1) * plev, :], inner, 1)
            old = line[:, pl.ds(base, BUF)]
            line[:, pl.ds(base, BUF)] = jnp.where((lane >= inner) & (lane < inner + quarter), piece, old)
        out_ref[:, pl.ds(r2, 1), :] = line[:, :ROWPAD].reshape(plev, 1, ROWPAD)


def synthesis(moved, perm, table_hi, table_lo, row_points):
    plev = moved[0].shape[1]
    wide = plev * 2 * PART
    vmem = pl.BlockSpec(memory_space=pltpu.VMEM)
    return pl.pallas_call(
        functools.partial(synth_kernel, len(moved)),
        out_shape=jax.ShapeDtypeStruct((plev, 2, ROWPAD), F32),
        in_specs=[pl.BlockSpec(memory_space=pltpu.SMEM)] + [vmem] * (len(moved) + 6),
        out_specs=vmem,
        scratch_shapes=[
            pltpu.VMEM((M, 2 * wide), BF16),
            pltpu.VMEM((2, 2, M, 2 * wide), BF16),
            pltpu.VMEM((8 * plev, BUF), F32),
            pltpu.VMEM((4 * plev, BUF), F32),
            pltpu.VMEM((plev, 3 * 1280 + BUF), F32),
        ],
        compiler_params=pltpu.CompilerParams(vmem_limit_bytes=(20 if plev <= 4 else 32) * MIB),
        cost_estimate=pl.CostEstimate(flops=2 * 2 * KPTS * 2 * M * 384, bytes_accessed=2 * KPTS * 2 * M * 4 + M * M * 2, transcendentals=0),
        name="synthesis",
    )(row_points, *moved, pick_tables(plev), mean_table(plev), flip_table(), perm, table_hi, table_lo)


def local(spectral, legendre, wave_map, row_points, brackets, lev_weight, climatology):
    slots = spectral.shape[0]
    half = legendre.shape[1]
    groups = slots // SQ
    wave_count = lax.axis_size("wave")
    lev_count = lax.axis_size("lev")
    rows_dev = 2 * half // (wave_count * lev_count)
    cuts = (0, 12, groups) if groups >= 16 else (0, groups)
    own_maps = wave_map.reshape(wave_count, SQ, groups)
    moved, maps, sent = [], [], []
    order = wave_map
    for start, stop in zip(cuts[:-1], cuts[1:]):
        own, prev = legendre_sums(start, stop - start, spectral, legendre, order, brackets, lev_weight)
        order, prev = lax.optimization_barrier((wave_map, prev))
        if sent:
            prev, _ = lax.optimization_barrier((prev, sent[-1]))
        from_next = lax.ppermute(prev, "lev", [(d, d - 1) for d in range(1, lev_count)])
        sent.append(own + from_next)
        part = lax.all_to_all(sent[-1], ("wave", "lev"), split_axis=0, concat_axis=0, tiled=True)
        moved.append(part.reshape(wave_count, lev_count, rows_dev * (stop - start), SQ * PART))
        maps.append(jnp.transpose(own_maps[:, :, start:stop], (1, 0, 2)).reshape(SQ, wave_count * (stop - start)))
    slot_map = jnp.concatenate(maps, axis=1).reshape(1, M)
    table_points, _ = lax.optimization_barrier((row_points, sent))
    table_hi, table_lo, perm = tables(table_points, slot_map)
    energy = synthesis(moved, perm, table_hi, table_lo, row_points)
    result = lax.all_to_all(energy, "lev", split_axis=0, concat_axis=0, tiled=True)
    result = result.reshape(1, rows_dev * lev_count, ROWPAD)
    points_all = jnp.concatenate([row_points, row_points])
    band_rows = rows_dev * lev_count
    out_points = lax.dynamic_slice_in_dim(points_all, lax.axis_index("wave") * band_rows, band_rows, 0)
    places = jnp.arange(ROWPAD, dtype=jnp.int32)
    inside = places[None, None, :] < out_points[None, :, None]
    return jnp.where(inside, result - climatology, 0.0)


def solution(mesh):
    placed = (
        P("wave", "lev", None),
        P("wave", None, None),
        P(),
        P(),
        P(),
        P(),
        P("lev", "wave", None),
    )
    return jax.shard_map(
        local, mesh=mesh, in_specs=placed, out_specs=P("lev", "wave", None), check_vma=False
    )
```

```python
import functools
import math

import jax
import jax.numpy as jnp
import numpy as np
from jax import lax
from jax.experimental import pallas as pl
from jax.experimental.pallas import tpu as pltpu
from jax.sharding import PartitionSpec as P

M = 1280
NT = 1280
LEV_DEV = 4
STEPS = 4
FIELDS = 2
ROWPAD = 5248

FS = FIELDS * STEPS
PART = 2 * FS
SQ = 8
STEP_SLOTS = 2
DEPTH = 3
HALF_M = M // 2
KPTS = 672
KPAD = 768
KBLK = 256
TABLE_STEPS = 7
PERM_ROWS = 128
BUF = 1536
MIB = 1024 * 1024
F32 = jnp.float32
BF16 = jnp.bfloat16


def iota(shape, dim):
    return lax.broadcasted_iota(jnp.int32, shape, dim)


def legendre_kernel(
    first_group, count, wave_map, brackets, weight_ref, spec_hbm, leg_hbm, own_ref, prev_ref,
    low_buf, up_buf, first_buf, leg_buf, own_rows, prev_rows, sems,
):
    groups = spec_hbm.shape[1]
    slots = SQ * groups
    steps = count // STEP_SLOTS
    half = leg_hbm.shape[2]
    width = STEP_SLOTS * 2 * half
    wave = lax.axis_index("wave")
    lev = lax.axis_index("lev")
    lower = brackets[lev] - lev * LEV_DEV
    has_upper = lower < LEV_DEV - 1
    w = weight_ref[lev]
    upper_w = jnp.where(has_upper, 1.0 - w, 0.0)
    before = jnp.maximum(lev - 1, 0)
    crosses = (lev > 0) & (brackets[before] == lev * LEV_DEV - 1)
    first_w = jnp.where(crosses, 1.0 - weight_ref[before], 0.0)
    degree = iota((16, NT), 1)
    sign = (1 - 2 * (degree % 2)).astype(F32).astype(BF16)
    lane = iota((1, width), 1)
    south = lane % (2 * half) >= half

    def columns_copy(step, pair, level, buf, kind):
        slot = step % DEPTH
        rows = pl.ds(pl.multiple_of(level * PART, PART), PART)
        here = pl.ds(first_group + step * STEP_SLOTS, STEP_SLOTS)
        src = spec_hbm.at[pl.ds(2 * pair, 2), here, rows, :]
        return pltpu.make_async_copy(src, buf.at[slot, pl.ds(2 * pair, 2)], sems.at[slot, pair, kind])

    def values_copy(step, pair):
        slot = step % DEPTH
        here = pl.ds(first_group + step * STEP_SLOTS, STEP_SLOTS)
        src = leg_hbm.at[pl.ds(2 * pair, 2), here]
        return pltpu.make_async_copy(src, leg_buf.at[slot, pl.ds(2 * pair, 2)], sems.at[slot, pair, 3])

    def fetch(step):
        for pair in range(SQ // 2):
            values_copy(step, pair).start()
            columns_copy(step, pair, lower, low_buf, 0).start()

        @pl.when(has_upper)
        def _():
            for pair in range(SQ // 2):
                columns_copy(step, pair, lower + 1, up_buf, 1).start()

        @pl.when(crosses)
        def _():
            for pair in range(SQ // 2):
                columns_copy(step, pair, 0, first_buf, 2).start()

    def await_pair(step, pair):
        values_copy(step, pair).wait()
        columns_copy(step, pair, lower, low_buf, 0).wait()

        @pl.when(has_upper)
        def _():
            columns_copy(step, pair, lower + 1, up_buf, 1).wait()

        @pl.when(crosses)
        def _():
            columns_copy(step, pair, 0, first_buf, 2).wait()

    for step in range(DEPTH - 1):
        fetch(step)

    @pl.when(jnp.logical_not(has_upper))
    def _():
        up_buf[...] = jnp.zeros_like(up_buf)

    @pl.when(jnp.logical_not(crosses))
    def _():
        first_buf[...] = jnp.zeros_like(first_buf)

    def step_body(step, carry):
        slot = step % DEPTH

        @pl.when(step + DEPTH - 1 < steps)
        def _():
            fetch(step + DEPTH - 1)

        for pair in range(SQ // 2):
            await_pair(step, pair)
        owns, firsts = [], []
        for pair in range(SQ // 2):
            orders, values, columns = [], [], []
            for a in range(2):
                sq = 2 * pair + a
                for b in range(STEP_SLOTS):
                    m = wave_map[wave * slots + sq * groups + first_group + step * STEP_SLOTS + b]
                    orders.append(m)
                    kept = jnp.where(degree >= m, 1.0, 0.0).astype(BF16)
                    plain = [leg_buf[slot, sq, b, i : i + 16, :] * kept for i in range(0, half, 16)]
                    values += plain + [x * sign for x in plain]
                    columns += [buf[slot, sq, b] for buf in (low_buf, up_buf, first_buf)]
            sums = nt_dot(jnp.concatenate(columns, axis=0), jnp.concatenate(values, axis=0))
            for a in range(2):
                own = jnp.zeros((PART, width), F32)
                first = jnp.zeros((PART, width), F32)
                for b in range(STEP_SLOTS):
                    at = (a * STEP_SLOTS + b) * 3 * PART
                    block = sums[at : at + 3 * PART, a * width : (a + 1) * width]
                    parity = (1 - 2 * (orders[a * STEP_SLOTS + b] % 2)).astype(F32)
                    factor = jnp.where(south, parity, 1.0)
                    here = lane // (2 * half) == b
                    mixed = block[:PART] * (factor * w) + block[PART : 2 * PART] * (factor * upper_w)
                    own = jnp.where(here, mixed, own)
                    first = jnp.where(here, block[2 * PART :] * (factor * first_w), first)
                owns.append(own)
                firsts.append(first)
        for ref, parts in ((own_rows, owns), (prev_rows, firsts)):
            stacked = jnp.concatenate(parts, axis=0)
            for t in range(width // 128):
                at = pl.multiple_of(step * width + t * 128, 128)
                ref[pl.ds(at, 128), :] = stacked[:, t * 128 : (t + 1) * 128].T
        return carry

    lax.fori_loop(0, steps, step_body, 0)
    rows = 2 * half
    for rows_ref, ref in ((own_rows, own_ref), (prev_rows, prev_ref)):
        rows_dev = ref.shape[1] // count
        for r in range(rows):
            at = (r % rows_dev) * count
            ref[r // rows_dev, at : at + count, :] = rows_ref[pl.ds(r, count, stride=rows), :]


def legendre_sums(first_group, count, spectral, legendre, wave_map, brackets, lev_weight):
    slots, cols, _ = spectral.shape
    half = legendre.shape[1]
    groups = slots // SQ
    spec = spectral.reshape(SQ, groups, cols, NT)
    leg = legendre.reshape(SQ, groups, half, NT)
    devices = lax.axis_size("wave") * lax.axis_size("lev")
    out = pltpu.VMEM((devices, 2 * half // devices * count, SQ * PART), F32)
    smem = pl.BlockSpec(memory_space=pltpu.SMEM)
    vmem = pl.BlockSpec(memory_space=pltpu.VMEM)
    anywhere = pl.BlockSpec(memory_space=pltpu.HBM)
    return pl.pallas_call(
        functools.partial(legendre_kernel, first_group, count),
        out_shape=[out, out],
        in_specs=[smem, smem, smem, anywhere, anywhere],
        out_specs=[vmem, vmem],
        scratch_shapes=[pltpu.VMEM((DEPTH, SQ, STEP_SLOTS, PART, NT), BF16)] * 3
        + [pltpu.VMEM((DEPTH, SQ, STEP_SLOTS, half, NT), BF16)]
        + [pltpu.VMEM((count * 2 * half, SQ * PART), F32)] * 2
        + [pltpu.SemaphoreType.DMA((DEPTH, SQ // 2, 4))],
        compiler_params=pltpu.CompilerParams(vmem_limit_bytes=48 * MIB),
        cost_estimate=pl.CostEstimate(
            flops=2 * SQ * count * 2 * half * 48 * NT, bytes_accessed=SQ * count * NT * 2 * (48 + half), transcendentals=0
        ),
        name="legendre_sums",
    )(
        *[pltpu.with_memory_space_constraint(x, pltpu.HBM) for x in (wave_map, brackets, lev_weight, spec, leg)]
    )


def unit_circle(product, points, inverse):
    big = 12582912.0
    turn = (product * inverse + big) - big
    x = (product - turn * points) * (math.pi * inverse)
    x2 = x * x
    sine = 0.0
    cosine = 0.0
    for power in (11, 9, 7, 5, 3, 1):
        sine = sine * x2 + (-1) ** (power // 2) / math.factorial(power)
    for power in (12, 10, 8, 6, 4, 2, 0):
        cosine = cosine * x2 + (-1) ** (power // 2) / math.factorial(power)
    sine = sine * x
    twice = sine + sine
    return 1.0 - twice * sine, twice * cosine


def own_points(points_ref, r2):
    wave = lax.axis_index("wave")
    lev = lax.axis_index("lev")
    row = 2 * (wave * lax.axis_size("lev") + lev) + r2
    return points_ref[row % points_ref.shape[0]]


def table_kernel(points_ref, map_ref, hi_ref, lo_ref, perm_ref):
    r2 = pl.program_id(0)
    kb = pl.program_id(1)
    rows = hi_ref.shape[1]
    points = own_points(points_ref, r2).astype(F32)
    inverse = 1.0 / points
    part = r2 * pl.num_programs(1) + kb

    @pl.when(part < M // PERM_ROWS)
    def _():
        order = part * PERM_ROWS + iota((PERM_ROWS, 1), 0)
        wanted = jnp.where(order < HALF_M, 2 * order, 2 * (order - HALF_M) + 1)
        perm_ref[...] = jnp.where(map_ref[...] == wanted, 1.0, 0.0).astype(BF16)

    lane = iota((16, 128), 1).astype(F32)

    def chunk_body(i, carry):
        chunk = pl.multiple_of(i * 16, 16)

        def put(tile, value):
            lanes = slice(tile * 128, tile * 128 + 128)
            hi = value.astype(BF16)
            hi_ref[0, pl.ds(chunk, 16), lanes] = hi
            lo_ref[0, pl.ds(chunk, 16), lanes] = (value - hi.astype(F32)).astype(BF16)

        k = (kb * rows + chunk + iota((16, 128), 0)).astype(F32)
        c, s = unit_circle(2.0 * lane * k, points, inverse)
        c1, s1 = unit_circle(k, points, inverse)
        ct, st = unit_circle(256.0 * k, points, inverse)
        co = c * c1 - s * s1
        so = s * c1 + c * s1
        for t in range(HALF_M // 128):
            if t:
                c, s = c * ct - s * st, s * ct + c * st
                co, so = co * ct - so * st, so * ct + co * st
            put(t, c)
            put(5 + t, s)
            put(10 + t, co)
            put(15 + t, so)
        return carry

    lax.fori_loop(0, rows // 16, chunk_body, 0, unroll=True)


def tables(row_points, slot_map):
    rows = KPTS // TABLE_STEPS
    table = pltpu.HBM((2, KPTS, 2 * M), BF16)
    table_spec = pl.BlockSpec((1, rows, 2 * M), lambda r, k: (r, k, 0))
    perm_spec = pl.BlockSpec((PERM_ROWS, M), lambda r, k: (jnp.minimum(r * TABLE_STEPS + k, M // PERM_ROWS - 1), 0))
    return pl.pallas_call(
        table_kernel,
        out_shape=[table, table, pltpu.HBM((M, M), BF16)],
        grid=(2, TABLE_STEPS),
        in_specs=[pl.BlockSpec(memory_space=pltpu.SMEM), pl.BlockSpec(memory_space=pltpu.VMEM)],
        out_specs=[table_spec, table_spec, perm_spec],
        compiler_params=pltpu.CompilerParams(vmem_limit_bytes=48 * MIB),
        cost_estimate=pl.CostEstimate(flops=2 * KPTS * 2 * M * 12, bytes_accessed=2 * KPTS * 2 * M * 4 + M * M * 2, transcendentals=0),
        name="fourier_tables",
    )(pltpu.with_memory_space_constraint(row_points, pltpu.HBM), slot_map)


def pick_tables(plev):
    wide = plev * 2 * PART
    out = np.zeros((2, 4, 2 * wide, 2 * wide), np.float32)
    plans = (
        ((0, 1), (0, 1), (0, 1), (0, 1)),
        ((1, -1), (1, 1), (1, -1), (1, 1)),
        ((0, 1), (0, 1), (1, -1), (1, -1)),
        ((1, -1), (1, 1), (0, -1), (0, 1)),
    )
    for r2 in range(2):
        for kind, plan in enumerate(plans):
            for image, (part, sgn) in enumerate(plan):
                for hl in range(2):
                    for p in range(plev):
                        for q in range(FS):
                            src = hl * wide + p * 2 * PART + r2 * PART + q * 2 + part
                            dst = hl * wide + image * plev * FS + p * FS + q
                            out[r2, kind, src, dst] = sgn
    return out.astype(jnp.bfloat16)


def mean_table(plev):
    wide = plev * FS * 4
    out = np.zeros((2 * 4 * plev, 2 * wide), np.float32)
    for quarter in range(4):
        for p in range(plev):
            for part in range(2):
                image_quarter = (quarter + part) % 4
                start = (image_quarter * 2 + part) * plev * FS + p * FS
                out[part * 4 * plev + quarter * plev + p, start : start + FS] = 0.5 / STEPS
    return out.astype(jnp.bfloat16)


def flip_table():
    return np.fliplr(np.eye(KBLK, dtype=np.float32)).astype(jnp.bfloat16)


def split(x):
    hi = x.astype(BF16)
    return hi, (x - hi.astype(F32)).astype(BF16)


def nt_dot(a, b):
    return lax.dot_general(a, b, (((1,), (1,)), ((), ())), preferred_element_type=F32)


def nn_dot(a, b):
    return jnp.dot(a, b, preferred_element_type=F32)


def synth_kernel(parts, points_ref, *refs):
    moved_refs = refs[:parts]
    pick_ref, mean_ref, flip_ref, perm_hbm, hi_hbm, lo_hbm, out_ref = refs[parts : parts + 7]
    perm_ref, hi_ref, lo_ref, mixed, coef, flat, mirror, line, sems = refs[parts + 7 :]
    waves, plev, _, _ = moved_refs[0].shape
    wide = plev * 2 * PART
    part_rows = M // SQ
    copies = [pltpu.make_async_copy(perm_hbm, perm_ref, sems.at[0])]
    for r2 in range(2):
        copies.append(pltpu.make_async_copy(hi_hbm.at[r2], hi_ref.at[r2], sems.at[1 + 2 * r2]))
        copies.append(pltpu.make_async_copy(lo_hbm.at[r2], lo_ref.at[r2], sems.at[2 + 2 * r2]))
    for copy in copies:
        copy.start()

    for base in range(0, plev * 2, 8):
        cur = []
        for g in range(base, base + 8):
            pieces = []
            for ref in moved_refs:
                sub = ref.shape[2] // 2
                pieces += [ref[w, g // 2, (g % 2) * sub : (g % 2 + 1) * sub, :] for w in range(waves)]
            cur.append(jnp.concatenate(pieces, axis=0))
        group = iota((part_rows, 128), 1) // PART
        for bit in (1, 2, 4):
            unset = (group & bit) == 0
            nxt = list(cur)
            for g in range(8):
                if g & bit == 0:
                    a, b = cur[g], cur[g + bit]
                    nxt[g] = jnp.where(unset, a, pltpu.roll(b, bit * PART, 1))
                    nxt[g + bit] = jnp.where(unset, pltpu.roll(a, 128 - bit * PART, 1), b)
            cur = nxt
        for sq in range(SQ):
            hi, lo = split(cur[sq])
            lane = base * PART
            mixed[sq * part_rows : (sq + 1) * part_rows, lane : lane + 128] = hi
            mixed[sq * part_rows : (sq + 1) * part_rows, wide + lane : wide + lane + 128] = lo

    lane_row = (iota((1, 2 * wide), 1) // PART) % 2
    limit0 = (own_points(points_ref, 0) - 1) // 2
    limit1 = (own_points(points_ref, 1) - 1) // 2
    limit = jnp.where(lane_row == 0, limit0, limit1)
    place = iota((HALF_M, 1), 0)
    turned = (iota((1, 2 * wide), 1) % wide) // (plev * FS) >= 2
    flip_sign = jnp.where(turned & (place % 2 == 1), -1.0, 1.0).astype(BF16)
    copies[0].wait()
    for odd in range(2):
        ordered = nn_dot(perm_ref[odd * HALF_M : (odd + 1) * HALF_M, :], mixed[...])
        wave = 2 * place + odd
        factor = jnp.where(wave <= limit, jnp.where(wave == 0, 1.0, 2.0), 0.0)
        ordered = (ordered * factor).astype(BF16)
        for row in range(2):
            for part in range(2):
                picked = nn_dot(ordered, pick_ref[row, odd * 2 + part]).astype(BF16)
                coef[row, odd, part * HALF_M : (part + 1) * HALF_M, :] = picked * flip_sign
    flat[...] = jnp.zeros_like(flat)
    mirror[...] = jnp.zeros_like(mirror)

    for r2 in range(2):
        copies[1 + 2 * r2].wait()
        copies[2 + 2 * r2].wait()

        def contraction(odd):
            lanes = slice(odd * M, (odd + 1) * M)
            both = nn_dot(hi_ref[r2, :, lanes], coef[r2, odd])
            rest = nn_dot(lo_ref[r2, :, lanes], coef[r2, odd, :, :wide])
            return both[:, :wide] + (both[:, wide:] + rest)

        even_sum = contraction(0)
        odd_sum = contraction(1)
        plus = even_sum + odd_sum
        minus = even_sum - odd_sum
        squares = jnp.concatenate([plus * plus, minus * minus], axis=1)
        sq_hi, sq_lo = split(squares)
        energy = nt_dot(mean_ref[...], sq_hi) + nt_dot(mean_ref[...], sq_lo)
        rows = 4 * plev
        flat[:, :KPTS] = energy
        en_hi, en_lo = split(flat[rows:, :KPAD])
        for t in range(KPAD // KBLK):
            lanes = slice(t * KBLK, (t + 1) * KBLK)
            back = KPAD - (t + 1) * KBLK
            mirror[:, back : back + KBLK] = nn_dot(en_hi[:, lanes], flip_ref[...]) + nn_dot(en_lo[:, lanes], flip_ref[...])

        quarter = own_points(points_ref, r2) // 4
        lane = iota((rows, BUF), 1)
        shift = (quarter + (BUF - (KPAD - 1))) % BUF
        flat[:rows, :] = jnp.where(lane <= quarter // 2, flat[:rows, :], pltpu.roll(mirror[...], shift, 1))
        line[...] = jnp.zeros_like(line)
        lane = iota((plev, BUF), 1)
        for b in range(4):
            start = quarter * b
            inner = start % 128
            base = pl.multiple_of(start - inner, 128)
            piece = pltpu.roll(flat[b * plev : (b + 1) * plev, :], inner, 1)
            old = line[:, pl.ds(base, BUF)]
            line[:, pl.ds(base, BUF)] = jnp.where((lane >= inner) & (lane < inner + quarter), piece, old)
        out_ref[:, pl.ds(r2, 1), :] = line[:, :ROWPAD].reshape(plev, 1, ROWPAD)


def synthesis(moved, perm, table_hi, table_lo, row_points):
    plev = moved[0].shape[1]
    wide = plev * 2 * PART
    vmem = pl.BlockSpec(memory_space=pltpu.VMEM)
    return pl.pallas_call(
        functools.partial(synth_kernel, len(moved)),
        out_shape=jax.ShapeDtypeStruct((plev, 2, ROWPAD), F32),
        in_specs=[pl.BlockSpec(memory_space=pltpu.SMEM)] + [vmem] * (len(moved) + 3) + [pl.BlockSpec(memory_space=pltpu.HBM)] * 3,
        out_specs=vmem,
        scratch_shapes=[
            pltpu.VMEM((M, M), BF16),
            pltpu.VMEM((2, KPTS, 2 * M), BF16),
            pltpu.VMEM((2, KPTS, 2 * M), BF16),
            pltpu.VMEM((M, 2 * wide), BF16),
            pltpu.VMEM((2, 2, M, 2 * wide), BF16),
            pltpu.VMEM((8 * plev, BUF), F32),
            pltpu.VMEM((4 * plev, BUF), F32),
            pltpu.VMEM((plev, 3 * 1280 + BUF), F32),
            pltpu.SemaphoreType.DMA((5,)),
        ],
        compiler_params=pltpu.CompilerParams(vmem_limit_bytes=48 * MIB),
        cost_estimate=pl.CostEstimate(flops=2 * 2 * KPTS * 2 * M * 384, bytes_accessed=2 * KPTS * 2 * M * 4 + M * M * 2, transcendentals=0),
        name="synthesis",
    )(
        pltpu.with_memory_space_constraint(row_points, pltpu.HBM),
        *[pltpu.with_memory_space_constraint(x, pltpu.VMEM) for x in moved],
        pick_tables(plev), mean_table(plev), flip_table(),
        *[pltpu.with_memory_space_constraint(x, pltpu.HBM) for x in (perm, table_hi, table_lo)],
    )


def local(spectral, legendre, wave_map, row_points, brackets, lev_weight, climatology):
    slots = spectral.shape[0]
    half = legendre.shape[1]
    groups = slots // SQ
    wave_count = lax.axis_size("wave")
    lev_count = lax.axis_size("lev")
    rows_dev = 2 * half // (wave_count * lev_count)
    cuts = (0, 12, groups) if groups >= 16 else (0, groups)
    own_maps = wave_map.reshape(wave_count, SQ, groups)
    pairs = [(d, d - 1) for d in range(1, lev_count)]
    parts = list(zip(cuts[:-1], cuts[1:]))
    owns, prevs, sent = [], [], []
    order = wave_map
    for start, stop in parts:
        own, prev = legendre_sums(start, stop - start, spectral, legendre, order, brackets, lev_weight)
        order, prev = lax.optimization_barrier((wave_map, prev))
        owns.append(own)
        prevs.append(prev)
    for i in range(len(parts)):
        prev = prevs[i]
        if i:
            prev, _ = lax.optimization_barrier((prev, sent[-1]))
        whole = owns[i] + lax.ppermute(prev, "lev", pairs)
        whole, _ = lax.optimization_barrier((whole, owns[-1]))
        sent.append(whole)
    moved, maps = [], []
    for (start, stop), whole in zip(parts, sent):
        part = lax.all_to_all(whole, ("wave", "lev"), split_axis=0, concat_axis=0, tiled=True)
        moved.append(part.reshape(wave_count, lev_count, rows_dev * (stop - start), SQ * PART))
        maps.append(jnp.transpose(own_maps[:, :, start:stop], (1, 0, 2)).reshape(SQ, wave_count * (stop - start)))
    slot_map = jnp.concatenate(maps, axis=1).reshape(1, M)
    table_points, _ = lax.optimization_barrier((row_points, sent))
    table_hi, table_lo, perm = tables(table_points, slot_map)
    energy = synthesis(moved, perm, table_hi, table_lo, row_points)
    result = lax.all_to_all(energy, "lev", split_axis=0, concat_axis=0, tiled=True)
    result = result.reshape(1, rows_dev * lev_count, ROWPAD)
    points_all = jnp.concatenate([row_points, row_points])
    band_rows = rows_dev * lev_count
    out_points = lax.dynamic_slice_in_dim(points_all, lax.axis_index("wave") * band_rows, band_rows, 0)
    places = jnp.arange(ROWPAD, dtype=jnp.int32)
    inside = places[None, None, :] < out_points[None, :, None]
    return jnp.where(inside, result - climatology, 0.0)


def solution(mesh):
    placed = (
        P("wave", "lev", None),
        P("wave", None, None),
        P(),
        P(),
        P(),
        P(),
        P("lev", "wave", None),
    )
    return jax.shard_map(
        local, mesh=mesh, in_specs=placed, out_specs=P("lev", "wave", None), check_vma=False
    )
```

```python
import functools
import math

import jax
import jax.numpy as jnp
import numpy as np
from jax import lax
from jax.experimental import pallas as pl
from jax.experimental.pallas import tpu as pltpu
from jax.sharding import PartitionSpec as P

M = 1280
NT = 1280
LEV_DEV = 4
STEPS = 4
FIELDS = 2
ROWPAD = 5248

FS = FIELDS * STEPS
PART = 2 * FS
SQ = 8
STEP_SLOTS = 2
DEPTH = 3
HALF_M = M // 2
KPTS = 672
KPAD = 768
KBLK = 256
BUF = 1536
MIB = 1024 * 1024
F32 = jnp.float32
BF16 = jnp.bfloat16


def iota(shape, dim):
    return lax.broadcasted_iota(jnp.int32, shape, dim)


def legendre_kernel(
    first_group, count, wave_map, brackets, weight_ref, spec_hbm, leg_hbm, own_ref, prev_ref,
    low_buf, up_buf, first_buf, leg_buf, own_rows, prev_rows, sems,
):
    groups = spec_hbm.shape[1]
    slots = SQ * groups
    steps = count // STEP_SLOTS
    half = leg_hbm.shape[2]
    width = STEP_SLOTS * 2 * half
    wave = lax.axis_index("wave")
    lev = lax.axis_index("lev")
    lower = brackets[lev] - lev * LEV_DEV
    has_upper = lower < LEV_DEV - 1
    w = weight_ref[lev]
    upper_w = jnp.where(has_upper, 1.0 - w, 0.0)
    before = jnp.maximum(lev - 1, 0)
    crosses = (lev > 0) & (brackets[before] == lev * LEV_DEV - 1)
    first_w = jnp.where(crosses, 1.0 - weight_ref[before], 0.0)
    degree = iota((16, NT), 1).astype(jnp.int16)
    sign = (1 - 2 * (iota((16, NT), 1) % 2)).astype(F32).astype(BF16)
    lane = iota((1, width), 1)
    south = lane % (2 * half) >= half

    def columns_copy(step, level, buf, kind):
        slot = step % DEPTH
        rows = pl.ds(pl.multiple_of(level * PART, PART), PART)
        src = spec_hbm.at[:, pl.ds(first_group + step * STEP_SLOTS, STEP_SLOTS), rows, :]
        return pltpu.make_async_copy(src, buf.at[slot], sems.at[slot, kind])

    def values_copy(step):
        slot = step % DEPTH
        src = leg_hbm.at[:, pl.ds(first_group + step * STEP_SLOTS, STEP_SLOTS)]
        return pltpu.make_async_copy(src, leg_buf.at[slot], sems.at[slot, 3])

    def fetch(step):
        values_copy(step).start()
        columns_copy(step, lower, low_buf, 0).start()

        @pl.when(has_upper)
        def _():
            columns_copy(step, lower + 1, up_buf, 1).start()

        @pl.when(crosses)
        def _():
            columns_copy(step, 0, first_buf, 2).start()

    def await_step(step):
        values_copy(step).wait()
        columns_copy(step, lower, low_buf, 0).wait()

        @pl.when(has_upper)
        def _():
            columns_copy(step, lower + 1, up_buf, 1).wait()

        @pl.when(crosses)
        def _():
            columns_copy(step, 0, first_buf, 2).wait()

    for step in range(DEPTH - 1):
        fetch(step)

    @pl.when(jnp.logical_not(has_upper))
    def _():
        up_buf[...] = jnp.zeros_like(up_buf)

    @pl.when(jnp.logical_not(crosses))
    def _():
        first_buf[...] = jnp.zeros_like(first_buf)

    def step_body(step, carry):
        slot = step % DEPTH
        await_step(step)

        @pl.when(step + DEPTH - 1 < steps)
        def _():
            fetch(step + DEPTH - 1)

        owns, firsts = [], []
        for pair in range(SQ // 2):
            orders, values, columns = [], [], []
            for a in range(2):
                sq = 2 * pair + a
                for b in range(STEP_SLOTS):
                    m = wave_map[wave * slots + sq * groups + first_group + step * STEP_SLOTS + b]
                    orders.append(m)
                    kept = degree >= m.astype(jnp.int16)
                    plain = [jnp.where(kept, leg_buf[slot, sq, b, i : i + 16, :], 0) for i in range(0, half, 16)]
                    values += plain + [x * sign for x in plain]
                    columns += [buf[slot, sq, b] for buf in (low_buf, up_buf, first_buf)]
            sums = nt_dot(jnp.concatenate(columns, axis=0), jnp.concatenate(values, axis=0))
            for a in range(2):
                own = jnp.zeros((PART, width), F32)
                first = jnp.zeros((PART, width), F32)
                for b in range(STEP_SLOTS):
                    at = (a * STEP_SLOTS + b) * 3 * PART
                    block = sums[at : at + 3 * PART, a * width : (a + 1) * width]
                    parity = (1 - 2 * (orders[a * STEP_SLOTS + b] % 2)).astype(F32)
                    factor = jnp.where(south, parity, 1.0)
                    here = lane // (2 * half) == b
                    mixed = block[:PART] * (factor * w) + block[PART : 2 * PART] * (factor * upper_w)
                    own = jnp.where(here, mixed, own)
                    first = jnp.where(here, block[2 * PART :] * (factor * first_w), first)
                owns.append(own)
                firsts.append(first)
        for ref, parts in ((own_rows, owns), (prev_rows, firsts)):
            stacked = jnp.concatenate(parts, axis=0)
            for t in range(width // 128):
                at = pl.multiple_of(step * width + t * 128, 128)
                ref[pl.ds(at, 128), :] = stacked[:, t * 128 : (t + 1) * 128].T
        return carry

    lax.fori_loop(0, steps, step_body, 0)
    rows = 2 * half
    for rows_ref, ref in ((own_rows, own_ref), (prev_rows, prev_ref)):
        rows_dev = ref.shape[1] // count
        for r in range(rows):
            at = (r % rows_dev) * count
            ref[r // rows_dev, at : at + count, :] = rows_ref[pl.ds(r, count, stride=rows), :]


def legendre_sums(first_group, count, spectral, legendre, wave_map, brackets, lev_weight):
    slots, cols, _ = spectral.shape
    half = legendre.shape[1]
    groups = slots // SQ
    spec = spectral.reshape(SQ, groups, cols, NT)
    leg = legendre.reshape(SQ, groups, half, NT)
    devices = lax.axis_size("wave") * lax.axis_size("lev")
    out = pltpu.VMEM((devices, 2 * half // devices * count, SQ * PART), F32)
    smem = pl.BlockSpec(memory_space=pltpu.SMEM)
    vmem = pl.BlockSpec(memory_space=pltpu.VMEM)
    anywhere = pl.BlockSpec(memory_space=pltpu.HBM)
    return pl.pallas_call(
        functools.partial(legendre_kernel, first_group, count),
        out_shape=[out, out],
        in_specs=[smem, smem, smem, anywhere, anywhere],
        out_specs=[vmem, vmem],
        scratch_shapes=[pltpu.VMEM((DEPTH, SQ, STEP_SLOTS, PART, NT), BF16)] * 3
        + [pltpu.VMEM((DEPTH, SQ, STEP_SLOTS, half, NT), BF16)]
        + [pltpu.VMEM((count * 2 * half, SQ * PART), F32)] * 2
        + [pltpu.SemaphoreType.DMA((DEPTH, 4))],
        compiler_params=pltpu.CompilerParams(vmem_limit_bytes=48 * MIB),
        cost_estimate=pl.CostEstimate(
            flops=2 * SQ * count * 2 * half * 48 * NT, bytes_accessed=SQ * count * NT * 2 * (48 + half), transcendentals=0
        ),
        name="legendre_sums",
    )(
        *[pltpu.with_memory_space_constraint(x, pltpu.HBM) for x in (wave_map, brackets, lev_weight, spec, leg)]
    )


def unit_circle(product, points, inverse):
    big = 12582912.0
    turn = (product * inverse + big) - big
    x = (product - turn * points) * (math.pi * inverse)
    x2 = x * x
    sine = 0.0
    cosine = 0.0
    for power in (11, 9, 7, 5, 3, 1):
        sine = sine * x2 + (-1) ** (power // 2) / math.factorial(power)
    for power in (12, 10, 8, 6, 4, 2, 0):
        cosine = cosine * x2 + (-1) ** (power // 2) / math.factorial(power)
    sine = sine * x
    twice = sine + sine
    return 1.0 - twice * sine, twice * cosine


def own_points(points_ref, r2):
    wave = lax.axis_index("wave")
    lev = lax.axis_index("lev")
    row = 2 * (wave * lax.axis_size("lev") + lev) + r2
    return points_ref[row % points_ref.shape[0]]


def table_kernel(points_ref, map_ref, hi_ref, lo_ref, perm_ref):
    lane = iota((16, 128), 1).astype(F32)

    def perm_body(i, carry):
        row = pl.multiple_of(i * 16, 16)
        order = row + iota((16, 1), 0)
        wanted = jnp.where(order < HALF_M, 2 * order, 2 * (order - HALF_M) + 1)
        perm_ref[pl.ds(row, 16), :] = jnp.where(map_ref[...] == wanted, 1.0, 0.0).astype(BF16)
        return carry

    lax.fori_loop(0, M // 16, perm_body, 0, unroll=4)
    for r2 in range(2):
        points = own_points(points_ref, r2).astype(F32)
        inverse = 1.0 / points

        def chunk_body(i, carry):
            chunk = pl.multiple_of(i * 16, 16)

            def put(tile, value):
                lanes = slice(tile * 128, tile * 128 + 128)
                hi = value.astype(BF16)
                hi_ref[r2, pl.ds(chunk, 16), lanes] = hi
                lo_ref[r2, pl.ds(chunk, 16), lanes] = (value - hi.astype(F32)).astype(BF16)

            k = (chunk + iota((16, 128), 0)).astype(F32)
            c, s = unit_circle(2.0 * lane * k, points, inverse)
            c1, s1 = unit_circle(k, points, inverse)
            ct, st = unit_circle(256.0 * k, points, inverse)
            co = c * c1 - s * s1
            so = s * c1 + c * s1
            for t in range(HALF_M // 128):
                if t:
                    c, s = c * ct - s * st, s * ct + c * st
                    co, so = co * ct - so * st, so * ct + co * st
                put(t, c)
                put(5 + t, s)
                put(10 + t, co)
                put(15 + t, so)
            return carry

        lax.fori_loop(0, KPTS // 16, chunk_body, 0, unroll=6)


def tables(row_points, slot_map):
    table = pltpu.VMEM((2, KPTS, 2 * M), BF16)
    vmem = pl.BlockSpec(memory_space=pltpu.VMEM)
    return pl.pallas_call(
        table_kernel,
        out_shape=[table, table, pltpu.VMEM((M, M), BF16)],
        in_specs=[pl.BlockSpec(memory_space=pltpu.SMEM), vmem],
        out_specs=[vmem] * 3,
        compiler_params=pltpu.CompilerParams(vmem_limit_bytes=20 * MIB),
        cost_estimate=pl.CostEstimate(flops=2 * KPTS * 2 * M * 12, bytes_accessed=2 * KPTS * 2 * M * 4 + M * M * 2, transcendentals=0),
        name="fourier_tables",
    )(pltpu.with_memory_space_constraint(row_points, pltpu.HBM), slot_map)


def pick_tables(plev):
    wide = plev * 2 * PART
    out = np.zeros((2, 4, 2 * wide, 2 * wide), np.float32)
    plans = (
        ((0, 1), (0, 1), (0, 1), (0, 1)),
        ((1, -1), (1, 1), (1, -1), (1, 1)),
        ((0, 1), (0, 1), (1, -1), (1, -1)),
        ((1, -1), (1, 1), (0, -1), (0, 1)),
    )
    for r2 in range(2):
        for kind, plan in enumerate(plans):
            for image, (part, sgn) in enumerate(plan):
                for hl in range(2):
                    for p in range(plev):
                        for q in range(FS):
                            src = hl * wide + p * 2 * PART + r2 * PART + q * 2 + part
                            dst = hl * wide + image * plev * FS + p * FS + q
                            out[r2, kind, src, dst] = sgn
    return out.astype(jnp.bfloat16)


def mean_table(plev):
    wide = plev * FS * 4
    out = np.zeros((2 * 4 * plev, 2 * wide), np.float32)
    for quarter in range(4):
        for p in range(plev):
            for part in range(2):
                image_quarter = (quarter + part) % 4
                start = (image_quarter * 2 + part) * plev * FS + p * FS
                out[part * 4 * plev + quarter * plev + p, start : start + FS] = 0.5 / STEPS
    return out.astype(jnp.bfloat16)


def flip_table():
    return np.fliplr(np.eye(KBLK, dtype=np.float32)).astype(jnp.bfloat16)


def split(x):
    hi = x.astype(BF16)
    return hi, (x - hi.astype(F32)).astype(BF16)


def nt_dot(a, b):
    return lax.dot_general(a, b, (((1,), (1,)), ((), ())), preferred_element_type=F32)


def nn_dot(a, b):
    return jnp.dot(a, b, preferred_element_type=F32)


def synth_kernel(parts, points_ref, *refs):
    moved_ref, pick_ref, mean_ref, flip_ref, perm_ref, hi_ref, lo_ref, out_ref, mixed, coef, flat, mirror, line = refs
    waves, plev, _, _ = moved_ref.shape
    wide = plev * 2 * PART
    part_rows = M // SQ
    for base in range(0, plev * 2, 8):
        cur = []
        for g in range(base, base + 8):
            pieces = []
            for start, stop in parts:
                first = 2 * start + (g % 2) * (stop - start)
                pieces += [moved_ref[w, g // 2, first : first + stop - start, :] for w in range(waves)]
            cur.append(jnp.concatenate(pieces, axis=0))
        group = iota((part_rows, 128), 1) // PART
        for bit in (1, 2, 4):
            unset = (group & bit) == 0
            nxt = list(cur)
            for g in range(8):
                if g & bit == 0:
                    a, b = cur[g], cur[g + bit]
                    nxt[g] = jnp.where(unset, a, pltpu.roll(b, bit * PART, 1))
                    nxt[g + bit] = jnp.where(unset, pltpu.roll(a, 128 - bit * PART, 1), b)
            cur = nxt
        for sq in range(SQ):
            hi, lo = split(cur[sq])
            lane = base * PART
            mixed[sq * part_rows : (sq + 1) * part_rows, lane : lane + 128] = hi
            mixed[sq * part_rows : (sq + 1) * part_rows, wide + lane : wide + lane + 128] = lo

    lane_row = (iota((1, 2 * wide), 1) // PART) % 2
    limit0 = (own_points(points_ref, 0) - 1) // 2
    limit1 = (own_points(points_ref, 1) - 1) // 2
    limit = jnp.where(lane_row == 0, limit0, limit1)
    place = iota((HALF_M, 1), 0)
    turned = (iota((1, 2 * wide), 1) % wide) // (plev * FS) >= 2
    flip_sign = jnp.where(turned & (place % 2 == 1), -1.0, 1.0).astype(BF16)
    for odd in range(2):
        ordered = nn_dot(perm_ref[odd * HALF_M : (odd + 1) * HALF_M, :], mixed[...])
        wave = 2 * place + odd
        factor = jnp.where(wave <= limit, jnp.where(wave == 0, 1.0, 2.0), 0.0)
        ordered = (ordered * factor).astype(BF16)
        for row in range(2):
            for part in range(2):
                picked = nn_dot(ordered, pick_ref[row, odd * 2 + part]).astype(BF16)
                coef[row, odd, part * HALF_M : (part + 1) * HALF_M, :] = picked * flip_sign
    flat[...] = jnp.zeros_like(flat)
    mirror[...] = jnp.zeros_like(mirror)

    for r2 in range(2):

        def contraction(odd):
            lanes = slice(odd * M, (odd + 1) * M)
            both = nn_dot(hi_ref[r2, :, lanes], coef[r2, odd])
            rest = nn_dot(lo_ref[r2, :, lanes], coef[r2, odd, :, :wide])
            return both[:, :wide] + (both[:, wide:] + rest)

        even_sum = contraction(0)
        odd_sum = contraction(1)
        plus = even_sum + odd_sum
        minus = even_sum - odd_sum
        squares = jnp.concatenate([plus * plus, minus * minus], axis=1)
        sq_hi, sq_lo = split(squares)
        energy = nt_dot(mean_ref[...], sq_hi) + nt_dot(mean_ref[...], sq_lo)
        rows = 4 * plev
        flat[:, :KPTS] = energy
        en_hi, en_lo = split(flat[rows:, :KPAD])
        for t in range(KPAD // KBLK):
            lanes = slice(t * KBLK, (t + 1) * KBLK)
            back = KPAD - (t + 1) * KBLK
            mirror[:, back : back + KBLK] = nn_dot(en_hi[:, lanes], flip_ref[...]) + nn_dot(en_lo[:, lanes], flip_ref[...])

        quarter = own_points(points_ref, r2) // 4
        lane = iota((rows, BUF), 1)
        shift = (quarter + (BUF - (KPAD - 1))) % BUF
        flat[:rows, :] = jnp.where(lane <= quarter // 2, flat[:rows, :], pltpu.roll(mirror[...], shift, 1))
        line[...] = jnp.zeros_like(line)
        lane = iota((plev, BUF), 1)
        for b in range(4):
            start = quarter * b
            inner = start % 128
            base = pl.multiple_of(start - inner, 128)
            piece = pltpu.roll(flat[b * plev : (b + 1) * plev, :], inner, 1)
            old = line[:, pl.ds(base, BUF)]
            line[:, pl.ds(base, BUF)] = jnp.where((lane >= inner) & (lane < inner + quarter), piece, old)
        out_ref[:, pl.ds(r2, 1), :] = line[:, :ROWPAD].reshape(plev, 1, ROWPAD)


def synthesis(parts, moved, perm, table_hi, table_lo, row_points):
    plev = moved.shape[1]
    wide = plev * 2 * PART
    vmem = pl.BlockSpec(memory_space=pltpu.VMEM)
    return pl.pallas_call(
        functools.partial(synth_kernel, parts),
        out_shape=jax.ShapeDtypeStruct((plev, 2, ROWPAD), F32),
        in_specs=[pl.BlockSpec(memory_space=pltpu.SMEM)] + [vmem] * 7,
        out_specs=vmem,
        scratch_shapes=[
            pltpu.VMEM((M, 2 * wide), BF16),
            pltpu.VMEM((2, 2, M, 2 * wide), BF16),
            pltpu.VMEM((8 * plev, BUF), F32),
            pltpu.VMEM((4 * plev, BUF), F32),
            pltpu.VMEM((plev, 3 * 1280 + BUF), F32),
        ],
        compiler_params=pltpu.CompilerParams(vmem_limit_bytes=(24 if plev <= 4 else 36) * MIB),
        cost_estimate=pl.CostEstimate(flops=2 * 2 * KPTS * 2 * M * 384, bytes_accessed=2 * KPTS * 2 * M * 4 + M * M * 2, transcendentals=0),
        name="synthesis",
    )(
        pltpu.with_memory_space_constraint(row_points, pltpu.HBM),
        pltpu.with_memory_space_constraint(moved, pltpu.VMEM),
        pick_tables(plev), mean_table(plev), flip_table(),
        *[pltpu.with_memory_space_constraint(x, pltpu.VMEM) for x in (perm, table_hi, table_lo)],
    )


def join_kernel(*refs):
    parts = (len(refs) - 1) // 2
    at = 0
    for own_ref, other_ref in zip(refs[:parts], refs[parts:-1]):
        rows = own_ref.shape[1]
        refs[-1][:, at : at + rows, :] = own_ref[...] + other_ref[...]
        at += rows


def join(owns, others):
    rows = sum(x.shape[1] for x in owns)
    vmem = pl.BlockSpec(memory_space=pltpu.VMEM)
    return pl.pallas_call(
        join_kernel,
        out_shape=jax.ShapeDtypeStruct((owns[0].shape[0], rows, SQ * PART), F32),
        in_specs=[vmem] * (2 * len(owns)),
        out_specs=vmem,
        compiler_params=pltpu.CompilerParams(vmem_limit_bytes=32 * MIB),
        name="join",
    )(*[pltpu.with_memory_space_constraint(x, pltpu.VMEM) for x in owns + others])


def local(spectral, legendre, wave_map, row_points, brackets, lev_weight, climatology):
    slots = spectral.shape[0]
    half = legendre.shape[1]
    groups = slots // SQ
    wave_count = lax.axis_size("wave")
    lev_count = lax.axis_size("lev")
    rows_dev = 2 * half // (wave_count * lev_count)
    cuts = (0, 12, groups) if groups >= 16 else (0, groups)
    own_maps = wave_map.reshape(wave_count, SQ, groups)
    pairs = [(d, d - 1) for d in range(1, lev_count)]
    parts = list(zip(cuts[:-1], cuts[1:]))
    owns, others, maps = [], [], []
    order = wave_map
    for start, stop in parts:
        own, prev = legendre_sums(start, stop - start, spectral, legendre, order, brackets, lev_weight)
        order, prev = lax.optimization_barrier((wave_map, prev))
        if others:
            prev, _ = lax.optimization_barrier((prev, others[-1]))
        owns.append(own)
        others.append(lax.ppermute(prev, "lev", pairs))
        maps.append(jnp.transpose(own_maps[:, :, start:stop], (1, 0, 2)).reshape(SQ, wave_count * (stop - start)))
    sent = join(owns, others)
    moved = lax.all_to_all(sent, ("wave", "lev"), split_axis=0, concat_axis=0, tiled=True)
    moved = moved.reshape(wave_count, lev_count, rows_dev * groups, SQ * PART)
    slot_map = jnp.concatenate(maps, axis=1).reshape(1, M)
    table_points, _ = lax.optimization_barrier((row_points, sent))
    table_hi, table_lo, perm = tables(table_points, slot_map)
    energy = synthesis(parts, moved, perm, table_hi, table_lo, row_points)
    result = lax.all_to_all(energy, "lev", split_axis=0, concat_axis=0, tiled=True)
    result = result.reshape(1, rows_dev * lev_count, ROWPAD)
    points_all = jnp.concatenate([row_points, row_points])
    band_rows = rows_dev * lev_count
    out_points = lax.dynamic_slice_in_dim(points_all, lax.axis_index("wave") * band_rows, band_rows, 0)
    places = jnp.arange(ROWPAD, dtype=jnp.int32)
    inside = places[None, None, :] < out_points[None, :, None]
    return jnp.where(inside, result - climatology, 0.0)


def solution(mesh):
    placed = (
        P("wave", "lev", None),
        P("wave", None, None),
        P(),
        P(),
        P(),
        P(),
        P("lev", "wave", None),
    )
    return jax.shard_map(
        local, mesh=mesh, in_specs=placed, out_specs=P("lev", "wave", None), check_vma=False
    )
```

```python
import functools
import math

import jax
import jax.numpy as jnp
import numpy as np
from jax import lax
from jax.experimental import pallas as pl
from jax.experimental.pallas import tpu as pltpu
from jax.sharding import PartitionSpec as P

M = 1280
NT = 1280
LEV_DEV = 4
STEPS = 4
FIELDS = 2
ROWPAD = 5248

FS = FIELDS * STEPS
PART = 2 * FS
SQ = 8
STEP_SLOTS = 2
DEPTH = 3
HALF_M = M // 2
KPTS = 672
KPAD = 768
KBLK = 256
TABLE_STEPS = 7
PERM_ROWS = 128
BUF = 1536
MIB = 1024 * 1024
F32 = jnp.float32
BF16 = jnp.bfloat16


def iota(shape, dim):
    return lax.broadcasted_iota(jnp.int32, shape, dim)


def legendre_kernel(
    first_group, count, wave_map, brackets, weight_ref, spec_hbm, leg_hbm, own_ref, prev_ref,
    low_buf, up_buf, first_buf, leg_buf, own_rows, prev_rows, sems,
):
    groups = spec_hbm.shape[1]
    slots = SQ * groups
    steps = count // STEP_SLOTS
    half = leg_hbm.shape[2]
    wave = lax.axis_index("wave")
    lev = lax.axis_index("lev")
    lower = brackets[lev] - lev * LEV_DEV
    has_upper = lower < LEV_DEV - 1
    w = weight_ref[lev]
    upper_w = jnp.where(has_upper, 1.0 - w, 0.0)
    before = jnp.maximum(lev - 1, 0)
    crosses = (lev > 0) & (brackets[before] == lev * LEV_DEV - 1)
    first_w = jnp.where(crosses, 1.0 - weight_ref[before], 0.0)
    degree = iota((16, NT), 1).astype(jnp.int16)
    sign = (1 - 2 * (iota((16, NT), 1) % 2)).astype(F32).astype(BF16)
    lane_group = iota((1, 2 * SQ * PART), 1) % 64 // PART
    left = iota((1, SQ * PART), 1) < 64
    south = iota((2 * half, 1), 0) >= half

    def columns_copy(step, level, buf, kind):
        slot = step % DEPTH
        rows = pl.ds(pl.multiple_of(level * PART, PART), PART)
        src = spec_hbm.at[:, pl.ds(first_group + step * STEP_SLOTS, STEP_SLOTS), rows, :]
        return pltpu.make_async_copy(src, buf.at[slot], sems.at[slot, kind])

    def values_copy(step):
        slot = step % DEPTH
        src = leg_hbm.at[:, pl.ds(first_group + step * STEP_SLOTS, STEP_SLOTS)]
        return pltpu.make_async_copy(src, leg_buf.at[slot], sems.at[slot, 3])

    def fetch(step):
        values_copy(step).start()
        columns_copy(step, lower, low_buf, 0).start()

        @pl.when(has_upper)
        def _():
            columns_copy(step, lower + 1, up_buf, 1).start()

        @pl.when(crosses)
        def _():
            columns_copy(step, 0, first_buf, 2).start()

    def await_step(step):
        values_copy(step).wait()
        columns_copy(step, lower, low_buf, 0).wait()

        @pl.when(has_upper)
        def _():
            columns_copy(step, lower + 1, up_buf, 1).wait()

        @pl.when(crosses)
        def _():
            columns_copy(step, 0, first_buf, 2).wait()

    for step in range(DEPTH - 1):
        fetch(step)

    @pl.when(jnp.logical_not(has_upper))
    def _():
        up_buf[...] = jnp.zeros_like(up_buf)

    @pl.when(jnp.logical_not(crosses))
    def _():
        first_buf[...] = jnp.zeros_like(first_buf)

    def step_body(step, carry):
        slot = step % DEPTH
        await_step(step)

        @pl.when(step + DEPTH - 1 < steps)
        def _():
            fetch(step + DEPTH - 1)

        for b in range(STEP_SLOTS):
            owns, firsts = [], []
            for quad in range(2):
                values, factors = [], []
                for sq in range(4 * quad, 4 * quad + 4):
                    m = wave_map[wave * slots + sq * groups + first_group + step * STEP_SLOTS + b]
                    kept = degree >= m.astype(jnp.int16)
                    plain = [jnp.where(kept, leg_buf[slot, sq, b, i : i + 16, :], 0) for i in range(0, half, 16)]
                    values += plain + [x * sign for x in plain]
                    factors.append(jnp.where(south, (1 - 2 * (m % 2)).astype(F32), 1.0))
                bufs = (low_buf, up_buf, first_buf) if quad == 0 else (up_buf, low_buf, first_buf)
                columns = [buf[slot, sq, b] for buf in bufs for sq in range(4 * quad, 4 * quad + 4)]
                sums = nt_dot(jnp.concatenate(values, axis=0), jnp.concatenate(columns, axis=0))
                kept_sums = sums[: 2 * half] * factors[0]
                for a in range(1, 4):
                    block = sums[2 * half * a : 2 * half * (a + 1)] * factors[a]
                    kept_sums = jnp.where(lane_group[:, :192] == a, block, kept_sums)
                both = kept_sums[:, :128]
                other = pltpu.roll(both, 64, 1)
                owns.append(both * w + other * upper_w)
                firsts.append(jnp.concatenate([kept_sums[:, 128:]] * 2, axis=1))
            at = pl.multiple_of((step * STEP_SLOTS + b) * 2 * half, 2 * half)
            own_rows[pl.ds(at, 2 * half), :] = jnp.where(left, owns[0], owns[1])
            prev_rows[pl.ds(at, 2 * half), :] = jnp.where(left, firsts[0], firsts[1]) * first_w
        return carry

    lax.fori_loop(0, steps, step_body, 0)
    rows = 2 * half
    for rows_ref, ref in ((own_rows, own_ref), (prev_rows, prev_ref)):
        rows_dev = ref.shape[1] // count
        for r in range(rows):
            at = (r % rows_dev) * count
            ref[r // rows_dev, at : at + count, :] = rows_ref[pl.ds(r, count, stride=rows), :]


def legendre_sums(first_group, count, spectral, legendre, wave_map, brackets, lev_weight):
    slots, cols, _ = spectral.shape
    half = legendre.shape[1]
    groups = slots // SQ
    spec = spectral.reshape(SQ, groups, cols, NT)
    leg = legendre.reshape(SQ, groups, half, NT)
    devices = lax.axis_size("wave") * lax.axis_size("lev")
    out = pltpu.VMEM((devices, 2 * half // devices * count, SQ * PART), F32)
    smem = pl.BlockSpec(memory_space=pltpu.SMEM)
    vmem = pl.BlockSpec(memory_space=pltpu.VMEM)
    anywhere = pl.BlockSpec(memory_space=pltpu.HBM)
    return pl.pallas_call(
        functools.partial(legendre_kernel, first_group, count),
        out_shape=[out, out],
        in_specs=[smem, smem, smem, anywhere, anywhere],
        out_specs=[vmem, vmem],
        scratch_shapes=[pltpu.VMEM((DEPTH, SQ, STEP_SLOTS, PART, NT), BF16)] * 3
        + [pltpu.VMEM((DEPTH, SQ, STEP_SLOTS, half, NT), BF16)]
        + [pltpu.VMEM((count * 2 * half, SQ * PART), F32)] * 2
        + [pltpu.SemaphoreType.DMA((DEPTH, 4))],
        compiler_params=pltpu.CompilerParams(vmem_limit_bytes=48 * MIB),
        cost_estimate=pl.CostEstimate(
            flops=2 * SQ * count * 2 * half * 48 * NT, bytes_accessed=SQ * count * NT * 2 * (48 + half), transcendentals=0
        ),
        name="legendre_sums",
    )(
        *[pltpu.with_memory_space_constraint(x, pltpu.HBM) for x in (wave_map, brackets, lev_weight, spec, leg)]
    )


def unit_circle(product, points, inverse):
    big = 12582912.0
    turn = (product * inverse + big) - big
    x = (product - turn * points) * (math.pi * inverse)
    x2 = x * x
    sine = 0.0
    cosine = 0.0
    for power in (11, 9, 7, 5, 3, 1):
        sine = sine * x2 + (-1) ** (power // 2) / math.factorial(power)
    for power in (12, 10, 8, 6, 4, 2, 0):
        cosine = cosine * x2 + (-1) ** (power // 2) / math.factorial(power)
    sine = sine * x
    twice = sine + sine
    return 1.0 - twice * sine, twice * cosine


def own_points(points_ref, r2):
    wave = lax.axis_index("wave")
    lev = lax.axis_index("lev")
    row = 2 * (wave * lax.axis_size("lev") + lev) + r2
    return points_ref[row % points_ref.shape[0]]


def table_kernel(points_ref, map_ref, hi_ref, lo_ref, perm_ref):
    r2 = pl.program_id(0)
    kb = pl.program_id(1)
    rows = hi_ref.shape[1]
    points = own_points(points_ref, r2).astype(F32)
    inverse = 1.0 / points
    part = r2 * pl.num_programs(1) + kb

    @pl.when(part < M // PERM_ROWS)
    def _():
        order = part * PERM_ROWS + iota((PERM_ROWS, 1), 0)
        wanted = jnp.where(order < HALF_M, 2 * order, 2 * (order - HALF_M) + 1)
        perm_ref[...] = jnp.where(map_ref[...] == wanted, 1.0, 0.0).astype(BF16)

    lane = iota((16, 128), 1).astype(F32)

    def chunk_body(i, carry):
        chunk = pl.multiple_of(i * 16, 16)

        def put(tile, value):
            lanes = slice(tile * 128, tile * 128 + 128)
            hi = value.astype(BF16)
            hi_ref[0, pl.ds(chunk, 16), lanes] = hi
            lo_ref[0, pl.ds(chunk, 16), lanes] = (value - hi.astype(F32)).astype(BF16)

        k = (kb * rows + chunk + iota((16, 128), 0)).astype(F32)
        c, s = unit_circle(2.0 * lane * k, points, inverse)
        c1, s1 = unit_circle(k, points, inverse)
        ct, st = unit_circle(256.0 * k, points, inverse)
        co = c * c1 - s * s1
        so = s * c1 + c * s1
        for t in range(HALF_M // 128):
            if t:
                c, s = c * ct - s * st, s * ct + c * st
                co, so = co * ct - so * st, so * ct + co * st
            put(t, c)
            put(5 + t, s)
            put(10 + t, co)
            put(15 + t, so)
        return carry

    lax.fori_loop(0, rows // 16, chunk_body, 0, unroll=True)


def tables(row_points, slot_map):
    rows = KPTS // TABLE_STEPS
    table = pltpu.HBM((2, KPTS, 2 * M), BF16)
    table_spec = pl.BlockSpec((1, rows, 2 * M), lambda r, k: (r, k, 0))
    perm_spec = pl.BlockSpec((PERM_ROWS, M), lambda r, k: (jnp.minimum(r * TABLE_STEPS + k, M // PERM_ROWS - 1), 0))
    return pl.pallas_call(
        table_kernel,
        out_shape=[table, table, pltpu.HBM((M, M), BF16)],
        grid=(2, TABLE_STEPS),
        in_specs=[pl.BlockSpec(memory_space=pltpu.SMEM), pl.BlockSpec(memory_space=pltpu.VMEM)],
        out_specs=[table_spec, table_spec, perm_spec],
        compiler_params=pltpu.CompilerParams(vmem_limit_bytes=48 * MIB),
        cost_estimate=pl.CostEstimate(flops=2 * KPTS * 2 * M * 12, bytes_accessed=2 * KPTS * 2 * M * 4 + M * M * 2, transcendentals=0),
        name="fourier_tables",
    )(pltpu.with_memory_space_constraint(row_points, pltpu.HBM), slot_map)


def pick_tables(plev):
    wide = plev * 2 * PART
    out = np.zeros((2, 4, 2 * wide, 2 * wide), np.float32)
    plans = (
        ((0, 1), (0, 1), (0, 1), (0, 1)),
        ((1, -1), (1, 1), (1, -1), (1, 1)),
        ((0, 1), (0, 1), (1, -1), (1, -1)),
        ((1, -1), (1, 1), (0, -1), (0, 1)),
    )
    for r2 in range(2):
        for kind, plan in enumerate(plans):
            for image, (part, sgn) in enumerate(plan):
                for hl in range(2):
                    for p in range(plev):
                        for q in range(FS):
                            src = hl * wide + p * 2 * PART + r2 * PART + q * 2 + part
                            dst = hl * wide + image * plev * FS + p * FS + q
                            out[r2, kind, src, dst] = sgn
    return out.astype(jnp.bfloat16)


def mean_table(plev):
    wide = plev * FS * 4
    out = np.zeros((2 * 4 * plev, 2 * wide), np.float32)
    for quarter in range(4):
        for p in range(plev):
            for part in range(2):
                image_quarter = (quarter + part) % 4
                start = (image_quarter * 2 + part) * plev * FS + p * FS
                out[part * 4 * plev + quarter * plev + p, start : start + FS] = 0.5 / STEPS
    return out.astype(jnp.bfloat16)


def flip_table():
    return np.fliplr(np.eye(KBLK, dtype=np.float32)).astype(jnp.bfloat16)


def split(x):
    hi = x.astype(BF16)
    return hi, (x - hi.astype(F32)).astype(BF16)


def nt_dot(a, b):
    return lax.dot_general(a, b, (((1,), (1,)), ((), ())), preferred_element_type=F32)


def nn_dot(a, b):
    return jnp.dot(a, b, preferred_element_type=F32)


def synth_kernel(parts, points_ref, *refs):
    moved_ref, pick_ref, mean_ref, flip_ref, perm_hbm, hi_hbm, lo_hbm, out_ref = refs[:8]
    perm_ref, hi_ref, lo_ref, mixed, coef, flat, mirror, line, sems = refs[8:]
    perm_copy = pltpu.make_async_copy(perm_hbm, perm_ref, sems.at[0])
    table_copies = [
        [pltpu.make_async_copy(src.at[r2], dst.at[r2], sems.at[1 + 2 * r2 + i]) for i, (src, dst) in enumerate(((hi_hbm, hi_ref), (lo_hbm, lo_ref)))]
        for r2 in range(2)
    ]
    perm_copy.start()
    waves, plev, _, _ = moved_ref.shape
    wide = plev * 2 * PART
    part_rows = M // SQ
    for base in range(0, plev * 2, 8):
        cur = []
        for g in range(base, base + 8):
            pieces = []
            for start, stop in parts:
                first = 2 * start + (g % 2) * (stop - start)
                pieces += [moved_ref[w, g // 2, first : first + stop - start, :] for w in range(waves)]
            cur.append(jnp.concatenate(pieces, axis=0))
        group = iota((part_rows, 128), 1) // PART
        for bit in (1, 2, 4):
            unset = (group & bit) == 0
            nxt = list(cur)
            for g in range(8):
                if g & bit == 0:
                    a, b = cur[g], cur[g + bit]
                    nxt[g] = jnp.where(unset, a, pltpu.roll(b, bit * PART, 1))
                    nxt[g + bit] = jnp.where(unset, pltpu.roll(a, 128 - bit * PART, 1), b)
            cur = nxt
        for sq in range(SQ):
            hi, lo = split(cur[sq])
            lane = base * PART
            mixed[sq * part_rows : (sq + 1) * part_rows, lane : lane + 128] = hi
            mixed[sq * part_rows : (sq + 1) * part_rows, wide + lane : wide + lane + 128] = lo

    lane_row = (iota((1, 2 * wide), 1) // PART) % 2
    limit0 = (own_points(points_ref, 0) - 1) // 2
    limit1 = (own_points(points_ref, 1) - 1) // 2
    limit = jnp.where(lane_row == 0, limit0, limit1)
    place = iota((HALF_M, 1), 0)
    turned = (iota((1, 2 * wide), 1) % wide) // (plev * FS) >= 2
    flip_sign = jnp.where(turned & (place % 2 == 1), -1.0, 1.0).astype(BF16)
    perm_copy.wait()
    for copy in table_copies[0]:
        copy.start()
    for odd in range(2):
        ordered = nn_dot(perm_ref[odd * HALF_M : (odd + 1) * HALF_M, :], mixed[...])
        wave = 2 * place + odd
        factor = jnp.where(wave <= limit, jnp.where(wave == 0, 1.0, 2.0), 0.0)
        ordered = (ordered * factor).astype(BF16)
        for row in range(2):
            for part in range(2):
                picked = nn_dot(ordered, pick_ref[row, odd * 2 + part]).astype(BF16)
                coef[row, odd, part * HALF_M : (part + 1) * HALF_M, :] = picked * flip_sign
    flat[...] = jnp.zeros_like(flat)
    mirror[...] = jnp.zeros_like(mirror)

    for r2 in range(2):
        for copy in table_copies[r2]:
            copy.wait()
        for copy in table_copies[1] if r2 == 0 else []:
            copy.start()

        def contraction(odd):
            lanes = slice(odd * M, (odd + 1) * M)
            both = nn_dot(hi_ref[r2, :, lanes], coef[r2, odd])
            rest = nn_dot(lo_ref[r2, :, lanes], coef[r2, odd, :, :wide])
            return both[:, :wide] + (both[:, wide:] + rest)

        even_sum = contraction(0)
        odd_sum = contraction(1)
        plus = even_sum + odd_sum
        minus = even_sum - odd_sum
        squares = jnp.concatenate([plus * plus, minus * minus], axis=1)
        sq_hi, sq_lo = split(squares)
        energy = nt_dot(mean_ref[...], sq_hi) + nt_dot(mean_ref[...], sq_lo)
        rows = 4 * plev
        flat[:, :KPTS] = energy
        en_hi, en_lo = split(flat[rows:, :KPAD])
        for t in range(KPAD // KBLK):
            lanes = slice(t * KBLK, (t + 1) * KBLK)
            back = KPAD - (t + 1) * KBLK
            mirror[:, back : back + KBLK] = nn_dot(en_hi[:, lanes], flip_ref[...]) + nn_dot(en_lo[:, lanes], flip_ref[...])

        quarter = own_points(points_ref, r2) // 4
        lane = iota((rows, BUF), 1)
        shift = (quarter + (BUF - (KPAD - 1))) % BUF
        flat[:rows, :] = jnp.where(lane <= quarter // 2, flat[:rows, :], pltpu.roll(mirror[...], shift, 1))
        line[...] = jnp.zeros_like(line)
        lane = iota((plev, BUF), 1)
        for b in range(4):
            start = quarter * b
            inner = start % 128
            base = pl.multiple_of(start - inner, 128)
            piece = pltpu.roll(flat[b * plev : (b + 1) * plev, :], inner, 1)
            old = line[:, pl.ds(base, BUF)]
            line[:, pl.ds(base, BUF)] = jnp.where((lane >= inner) & (lane < inner + quarter), piece, old)
        out_ref[:, pl.ds(r2, 1), :] = line[:, :ROWPAD].reshape(plev, 1, ROWPAD)


def synthesis(parts, moved, perm, table_hi, table_lo, row_points):
    plev = moved.shape[1]
    wide = plev * 2 * PART
    vmem = pl.BlockSpec(memory_space=pltpu.VMEM)
    return pl.pallas_call(
        functools.partial(synth_kernel, parts),
        out_shape=jax.ShapeDtypeStruct((plev, 2, ROWPAD), F32),
        in_specs=[pl.BlockSpec(memory_space=pltpu.SMEM)] + [vmem] * 4 + [pl.BlockSpec(memory_space=pltpu.HBM)] * 3,
        out_specs=vmem,
        scratch_shapes=[
            pltpu.VMEM((M, M), BF16),
            pltpu.VMEM((2, KPTS, 2 * M), BF16),
            pltpu.VMEM((2, KPTS, 2 * M), BF16),
            pltpu.VMEM((M, 2 * wide), BF16),
            pltpu.VMEM((2, 2, M, 2 * wide), BF16),
            pltpu.VMEM((8 * plev, BUF), F32),
            pltpu.VMEM((4 * plev, BUF), F32),
            pltpu.VMEM((plev, 3 * 1280 + BUF), F32),
            pltpu.SemaphoreType.DMA((5,)),
        ],
        compiler_params=pltpu.CompilerParams(vmem_limit_bytes=44 * MIB),
        cost_estimate=pl.CostEstimate(flops=2 * 2 * KPTS * 2 * M * 384, bytes_accessed=2 * KPTS * 2 * M * 4 + M * M * 2, transcendentals=0),
        name="synthesis",
    )(
        pltpu.with_memory_space_constraint(row_points, pltpu.HBM),
        pltpu.with_memory_space_constraint(moved, pltpu.VMEM),
        pick_tables(plev), mean_table(plev), flip_table(),
        *[pltpu.with_memory_space_constraint(x, pltpu.HBM) for x in (perm, table_hi, table_lo)],
    )


def join_kernel(*refs):
    parts = (len(refs) - 1) // 2
    at = 0
    for own_ref, other_ref in zip(refs[:parts], refs[parts:-1]):
        rows = own_ref.shape[1]
        refs[-1][:, at : at + rows, :] = own_ref[...] + other_ref[...]
        at += rows


def join(owns, others):
    rows = sum(x.shape[1] for x in owns)
    vmem = pl.BlockSpec(memory_space=pltpu.VMEM)
    return pl.pallas_call(
        join_kernel,
        out_shape=jax.ShapeDtypeStruct((owns[0].shape[0], rows, SQ * PART), F32),
        in_specs=[vmem] * (2 * len(owns)),
        out_specs=vmem,
        compiler_params=pltpu.CompilerParams(vmem_limit_bytes=32 * MIB),
        name="join",
    )(*[pltpu.with_memory_space_constraint(x, pltpu.VMEM) for x in owns + others])


def local(spectral, legendre, wave_map, row_points, brackets, lev_weight, climatology):
    slots = spectral.shape[0]
    half = legendre.shape[1]
    groups = slots // SQ
    wave_count = lax.axis_size("wave")
    lev_count = lax.axis_size("lev")
    rows_dev = 2 * half // (wave_count * lev_count)
    cuts = (0, groups)
    own_maps = wave_map.reshape(wave_count, SQ, groups)
    pairs = [(d, d - 1) for d in range(1, lev_count)]
    parts = list(zip(cuts[:-1], cuts[1:]))
    owns, others, maps = [], [], []
    order = wave_map
    for start, stop in parts:
        own, prev = legendre_sums(start, stop - start, spectral, legendre, order, brackets, lev_weight)
        order, prev = lax.optimization_barrier((wave_map, prev))
        if others:
            prev, _ = lax.optimization_barrier((prev, others[-1]))
        owns.append(own)
        others.append(lax.ppermute(prev, "lev", pairs))
        maps.append(jnp.transpose(own_maps[:, :, start:stop], (1, 0, 2)).reshape(SQ, wave_count * (stop - start)))
    sent = join(owns, others)
    moved = lax.all_to_all(sent, ("wave", "lev"), split_axis=0, concat_axis=0, tiled=True)
    moved = moved.reshape(wave_count, lev_count, rows_dev * groups, SQ * PART)
    slot_map = jnp.concatenate(maps, axis=1).reshape(1, M)
    table_points, _ = lax.optimization_barrier((row_points, sent))
    table_hi, table_lo, perm = tables(table_points, slot_map)
    energy = synthesis(parts, moved, perm, table_hi, table_lo, row_points)
    result = lax.all_to_all(energy, "lev", split_axis=0, concat_axis=0, tiled=True)
    result = result.reshape(1, rows_dev * lev_count, ROWPAD)
    points_all = jnp.concatenate([row_points, row_points])
    band_rows = rows_dev * lev_count
    out_points = lax.dynamic_slice_in_dim(points_all, lax.axis_index("wave") * band_rows, band_rows, 0)
    places = jnp.arange(ROWPAD, dtype=jnp.int32)
    inside = places[None, None, :] < out_points[None, :, None]
    return jnp.where(inside, result - climatology, 0.0)


def solution(mesh):
    placed = (
        P("wave", "lev", None),
        P("wave", None, None),
        P(),
        P(),
        P(),
        P(),
        P("lev", "wave", None),
    )
    return jax.shard_map(
        local, mesh=mesh, in_specs=placed, out_specs=P("lev", "wave", None), check_vma=False
    )
```

```python
import functools
import math

import jax
import jax.numpy as jnp
import numpy as np
from jax import lax
from jax.experimental import pallas as pl
from jax.experimental.pallas import tpu as pltpu
from jax.sharding import PartitionSpec as P

M = 1280
NT = 1280
LEV_DEV = 4
STEPS = 4
FIELDS = 2
ROWPAD = 5248

FS = FIELDS * STEPS
PART = 2 * FS
SQ = 8
STEP_SLOTS = 2
DEPTH = 3
HALF_M = M // 2
KPTS = 672
KPAD = 768
KBLK = 256
TABLE_STEPS = 7
PERM_ROWS = 128
BUF = 1536
MIB = 1024 * 1024
F32 = jnp.float32
BF16 = jnp.bfloat16


def iota(shape, dim):
    return lax.broadcasted_iota(jnp.int32, shape, dim)


def legendre_kernel(
    first_group, count, wave_map, brackets, weight_ref, spec_hbm, leg_hbm, own_ref, prev_ref,
    low_buf, up_buf, first_buf, leg_buf, own_rows, prev_rows, sems,
):
    groups = spec_hbm.shape[1]
    slots = SQ * groups
    steps = count // STEP_SLOTS
    half = leg_hbm.shape[2]
    wave = lax.axis_index("wave")
    lev = lax.axis_index("lev")
    lower = brackets[lev] - lev * LEV_DEV
    has_upper = lower < LEV_DEV - 1
    w = weight_ref[lev]
    upper_w = jnp.where(has_upper, 1.0 - w, 0.0)
    before = jnp.maximum(lev - 1, 0)
    crosses = (lev > 0) & (brackets[before] == lev * LEV_DEV - 1)
    first_w = jnp.where(crosses, 1.0 - weight_ref[before], 0.0)
    degree = iota((16, NT), 1).astype(jnp.int16)
    sign = (1 - 2 * (iota((16, NT), 1) % 2)).astype(F32).astype(BF16)
    lane_group = iota((1, 2 * SQ * PART), 1) % 64 // PART
    left = iota((1, SQ * PART), 1) < 64
    south = iota((2 * half, 1), 0) >= half

    def columns_copy(step, level, buf, kind):
        slot = step % DEPTH
        rows = pl.ds(pl.multiple_of(level * PART, PART), PART)
        src = spec_hbm.at[:, pl.ds(first_group + step * STEP_SLOTS, STEP_SLOTS), rows, :]
        return pltpu.make_async_copy(src, buf.at[slot], sems.at[slot, kind])

    def values_copy(step):
        slot = step % DEPTH
        src = leg_hbm.at[:, pl.ds(first_group + step * STEP_SLOTS, STEP_SLOTS)]
        return pltpu.make_async_copy(src, leg_buf.at[slot], sems.at[slot, 3])

    def fetch(step):
        values_copy(step).start()
        columns_copy(step, lower, low_buf, 0).start()

        @pl.when(has_upper)
        def _():
            columns_copy(step, lower + 1, up_buf, 1).start()

        @pl.when(crosses)
        def _():
            columns_copy(step, 0, first_buf, 2).start()

    def await_step(step):
        values_copy(step).wait()
        columns_copy(step, lower, low_buf, 0).wait()

        @pl.when(has_upper)
        def _():
            columns_copy(step, lower + 1, up_buf, 1).wait()

        @pl.when(crosses)
        def _():
            columns_copy(step, 0, first_buf, 2).wait()

    for step in range(DEPTH - 1):
        fetch(step)

    @pl.when(jnp.logical_not(has_upper))
    def _():
        up_buf[...] = jnp.zeros_like(up_buf)

    @pl.when(jnp.logical_not(crosses))
    def _():
        first_buf[...] = jnp.zeros_like(first_buf)

    def step_body(step, carry):
        slot = step % DEPTH
        await_step(step)

        @pl.when(step + DEPTH - 1 < steps)
        def _():
            fetch(step + DEPTH - 1)

        for b in range(STEP_SLOTS):
            owns, firsts = [], []
            for quad in range(2):
                values, factors = [], []
                for sq in range(4 * quad, 4 * quad + 4):
                    m = wave_map[wave * slots + sq * groups + first_group + step * STEP_SLOTS + b]
                    kept = degree >= m.astype(jnp.int16)
                    plain = [jnp.where(kept, leg_buf[slot, sq, b, i : i + 16, :], 0) for i in range(0, half, 16)]
                    values += plain + [x * sign for x in plain]
                    factors.append(jnp.where(south, (1 - 2 * (m % 2)).astype(F32), 1.0))
                bufs = (low_buf, up_buf, first_buf) if quad == 0 else (up_buf, low_buf, first_buf)
                columns = [buf[slot, sq, b] for buf in bufs for sq in range(4 * quad, 4 * quad + 4)]
                sums = nt_dot(jnp.concatenate(values, axis=0), jnp.concatenate(columns, axis=0))
                kept_sums = sums[: 2 * half] * factors[0]
                for a in range(1, 4):
                    block = sums[2 * half * a : 2 * half * (a + 1)] * factors[a]
                    kept_sums = jnp.where(lane_group[:, :192] == a, block, kept_sums)
                both = kept_sums[:, :128]
                other = pltpu.roll(both, 64, 1)
                owns.append(both * w + other * upper_w)
                firsts.append(jnp.concatenate([kept_sums[:, 128:]] * 2, axis=1))
            at = pl.multiple_of((step * STEP_SLOTS + b) * 2 * half, 2 * half)
            own_rows[pl.ds(at, 2 * half), :] = jnp.where(left, owns[0], owns[1])
            prev_rows[pl.ds(at, 2 * half), :] = jnp.where(left, firsts[0], firsts[1]) * first_w
        return carry

    lax.fori_loop(0, steps, step_body, 0)
    rows = 2 * half
    for rows_ref, ref in ((own_rows, own_ref), (prev_rows, prev_ref)):
        rows_dev = ref.shape[1] // count
        for r in range(rows):
            at = (r % rows_dev) * count
            ref[r // rows_dev, at : at + count, :] = rows_ref[pl.ds(r, count, stride=rows), :]


def legendre_sums(first_group, count, spectral, legendre, wave_map, brackets, lev_weight):
    slots, cols, _ = spectral.shape
    half = legendre.shape[1]
    groups = slots // SQ
    spec = spectral.reshape(SQ, groups, cols, NT)
    leg = legendre.reshape(SQ, groups, half, NT)
    devices = lax.axis_size("wave") * lax.axis_size("lev")
    out = pltpu.VMEM((devices, 2 * half // devices * count, SQ * PART), F32)
    smem = pl.BlockSpec(memory_space=pltpu.SMEM)
    vmem = pl.BlockSpec(memory_space=pltpu.VMEM)
    anywhere = pl.BlockSpec(memory_space=pltpu.HBM)
    return pl.pallas_call(
        functools.partial(legendre_kernel, first_group, count),
        out_shape=[out, out],
        in_specs=[smem, smem, smem, anywhere, anywhere],
        out_specs=[vmem, vmem],
        scratch_shapes=[pltpu.VMEM((DEPTH, SQ, STEP_SLOTS, PART, NT), BF16)] * 3
        + [pltpu.VMEM((DEPTH, SQ, STEP_SLOTS, half, NT), BF16)]
        + [pltpu.VMEM((count * 2 * half, SQ * PART), F32)] * 2
        + [pltpu.SemaphoreType.DMA((DEPTH, 4))],
        compiler_params=pltpu.CompilerParams(vmem_limit_bytes=48 * MIB),
        cost_estimate=pl.CostEstimate(
            flops=2 * SQ * count * 2 * half * 48 * NT, bytes_accessed=SQ * count * NT * 2 * (48 + half), transcendentals=0
        ),
        name="legendre_sums",
    )(
        *[pltpu.with_memory_space_constraint(x, pltpu.HBM) for x in (wave_map, brackets, lev_weight, spec, leg)]
    )


def unit_circle(product, points, inverse):
    big = 12582912.0
    turn = (product * inverse + big) - big
    x = (product - turn * points) * (math.pi * inverse)
    x2 = x * x
    sine = 0.0
    cosine = 0.0
    for power in (11, 9, 7, 5, 3, 1):
        sine = sine * x2 + (-1) ** (power // 2) / math.factorial(power)
    for power in (12, 10, 8, 6, 4, 2, 0):
        cosine = cosine * x2 + (-1) ** (power // 2) / math.factorial(power)
    sine = sine * x
    twice = sine + sine
    return 1.0 - twice * sine, twice * cosine


def own_points(points_ref, r2):
    wave = lax.axis_index("wave")
    lev = lax.axis_index("lev")
    row = 2 * (wave * lax.axis_size("lev") + lev) + r2
    return points_ref[row % points_ref.shape[0]]


def table_kernel(points_ref, map_ref, hi_ref, lo_ref, perm_ref):
    r2 = pl.program_id(0)
    kb = pl.program_id(1)
    rows = hi_ref.shape[1]
    points = own_points(points_ref, r2).astype(F32)
    inverse = 1.0 / points
    part = r2 * pl.num_programs(1) + kb

    @pl.when(part < M // PERM_ROWS)
    def _():
        order = part * PERM_ROWS + iota((PERM_ROWS, 1), 0)
        wanted = jnp.where(order < HALF_M, 2 * order, 2 * (order - HALF_M) + 1)
        here = pl.ds(pl.multiple_of(part * PERM_ROWS, PERM_ROWS), PERM_ROWS)
        perm_ref[here, :] = jnp.where(map_ref[...] == wanted, 1.0, 0.0).astype(BF16)

    lane = iota((16, 128), 1).astype(F32)

    def chunk_body(i, carry):
        chunk = pl.multiple_of(i * 16, 16)

        def put(tile, value):
            lanes = slice(tile * 128, tile * 128 + 128)
            hi = value.astype(BF16)
            hi_ref[0, pl.ds(chunk, 16), lanes] = hi
            lo_ref[0, pl.ds(chunk, 16), lanes] = (value - hi.astype(F32)).astype(BF16)

        k = (kb * rows + chunk + iota((16, 128), 0)).astype(F32)
        c, s = unit_circle(2.0 * lane * k, points, inverse)
        c1, s1 = unit_circle(k, points, inverse)
        ct, st = unit_circle(256.0 * k, points, inverse)
        co = c * c1 - s * s1
        so = s * c1 + c * s1
        for t in range(HALF_M // 128):
            if t:
                c, s = c * ct - s * st, s * ct + c * st
                co, so = co * ct - so * st, so * ct + co * st
            put(t, c)
            put(5 + t, s)
            put(10 + t, co)
            put(15 + t, so)
        return carry

    lax.fori_loop(0, rows // 16, chunk_body, 0, unroll=True)


def tables(row_points, slot_map):
    rows = KPTS // TABLE_STEPS
    table = pltpu.HBM((2, KPTS, 2 * M), BF16)
    table_spec = pl.BlockSpec((1, rows, 2 * M), lambda r, k: (r, k, 0))
    perm_spec = pl.BlockSpec(memory_space=pltpu.VMEM)
    return pl.pallas_call(
        table_kernel,
        out_shape=[table, table, pltpu.VMEM((M, M), BF16)],
        grid=(2, TABLE_STEPS),
        in_specs=[pl.BlockSpec(memory_space=pltpu.SMEM), pl.BlockSpec(memory_space=pltpu.VMEM)],
        out_specs=[table_spec, table_spec, perm_spec],
        compiler_params=pltpu.CompilerParams(vmem_limit_bytes=48 * MIB),
        cost_estimate=pl.CostEstimate(flops=2 * KPTS * 2 * M * 12, bytes_accessed=2 * KPTS * 2 * M * 4 + M * M * 2, transcendentals=0),
        name="fourier_tables",
    )(pltpu.with_memory_space_constraint(row_points, pltpu.HBM), slot_map)


def pick_tables(plev):
    wide = plev * 2 * PART
    out = np.zeros((2, 4, 2 * wide, 2 * wide), np.float32)
    plans = (
        ((0, 1), (0, 1), (0, 1), (0, 1)),
        ((1, -1), (1, 1), (1, -1), (1, 1)),
        ((0, 1), (0, 1), (1, -1), (1, -1)),
        ((1, -1), (1, 1), (0, -1), (0, 1)),
    )
    for r2 in range(2):
        for kind, plan in enumerate(plans):
            for image, (part, sgn) in enumerate(plan):
                for hl in range(2):
                    for p in range(plev):
                        for q in range(FS):
                            src = hl * wide + p * 2 * PART + r2 * PART + q * 2 + part
                            dst = hl * wide + image * plev * FS + p * FS + q
                            out[r2, kind, src, dst] = sgn
    return out.astype(jnp.bfloat16)


def mean_table(plev):
    wide = plev * FS * 4
    out = np.zeros((2 * 4 * plev, 2 * wide), np.float32)
    for quarter in range(4):
        for p in range(plev):
            for part in range(2):
                image_quarter = (quarter + part) % 4
                start = (image_quarter * 2 + part) * plev * FS + p * FS
                out[part * 4 * plev + quarter * plev + p, start : start + FS] = 0.5 / STEPS
    return out.astype(jnp.bfloat16)


def flip_table():
    return np.fliplr(np.eye(KBLK, dtype=np.float32)).astype(jnp.bfloat16)


def split(x):
    hi = x.astype(BF16)
    return hi, (x - hi.astype(F32)).astype(BF16)


def nt_dot(a, b):
    return lax.dot_general(a, b, (((1,), (1,)), ((), ())), preferred_element_type=F32)


def nn_dot(a, b):
    return jnp.dot(a, b, preferred_element_type=F32)


def synth_kernel(parts, points_ref, *refs):
    moved_ref, pick_ref, mean_ref, flip_ref, perm_ref, hi_hbm, lo_hbm, out_ref = refs[:8]
    hi_ref, lo_ref, mixed, coef, flat, mirror, line, sems = refs[8:]
    table_copies = []
    for r2 in range(2):
        table_copies.append([])
        for i, (src, dst) in enumerate(((hi_hbm, hi_ref), (lo_hbm, lo_ref))):
            for c in range(2):
                rows = pl.ds(c * (KPTS // 2), KPTS // 2)
                table_copies[r2].append(pltpu.make_async_copy(src.at[r2, rows], dst.at[r2, rows], sems.at[r2, i, c]))
    for copy in table_copies[0]:
        copy.start()
    waves, plev, _, _ = moved_ref.shape
    wide = plev * 2 * PART
    part_rows = M // SQ
    for base in range(0, plev * 2, 8):
        cur = []
        for g in range(base, base + 8):
            pieces = []
            for start, stop in parts:
                first = 2 * start + (g % 2) * (stop - start)
                pieces += [moved_ref[w, g // 2, first : first + stop - start, :] for w in range(waves)]
            cur.append(jnp.concatenate(pieces, axis=0))
        group = iota((part_rows, 128), 1) // PART
        for bit in (1, 2, 4):
            unset = (group & bit) == 0
            nxt = list(cur)
            for g in range(8):
                if g & bit == 0:
                    a, b = cur[g], cur[g + bit]
                    nxt[g] = jnp.where(unset, a, pltpu.roll(b, bit * PART, 1))
                    nxt[g + bit] = jnp.where(unset, pltpu.roll(a, 128 - bit * PART, 1), b)
            cur = nxt
        for sq in range(SQ):
            hi, lo = split(cur[sq])
            lane = base * PART
            mixed[sq * part_rows : (sq + 1) * part_rows, lane : lane + 128] = hi
            mixed[sq * part_rows : (sq + 1) * part_rows, wide + lane : wide + lane + 128] = lo

    lane_row = (iota((1, 2 * wide), 1) // PART) % 2
    limit0 = (own_points(points_ref, 0) - 1) // 2
    limit1 = (own_points(points_ref, 1) - 1) // 2
    limit = jnp.where(lane_row == 0, limit0, limit1)
    place = iota((HALF_M, 1), 0)
    turned = (iota((1, 2 * wide), 1) % wide) // (plev * FS) >= 2
    flip_sign = jnp.where(turned & (place % 2 == 1), -1.0, 1.0).astype(BF16)
    for odd in range(2):
        ordered = nn_dot(perm_ref[odd * HALF_M : (odd + 1) * HALF_M, :], mixed[...])
        wave = 2 * place + odd
        factor = jnp.where(wave <= limit, jnp.where(wave == 0, 1.0, 2.0), 0.0)
        ordered = (ordered * factor).astype(BF16)
        for row in range(2):
            for part in range(2):
                picked = nn_dot(ordered, pick_ref[row, odd * 2 + part]).astype(BF16)
                coef[row, odd, part * HALF_M : (part + 1) * HALF_M, :] = picked * flip_sign
    flat[...] = jnp.zeros_like(flat)
    mirror[...] = jnp.zeros_like(mirror)

    for r2 in range(2):
        for copy in table_copies[r2]:
            copy.wait()
        for copy in table_copies[1] if r2 == 0 else []:
            copy.start()

        def contraction(odd):
            lanes = slice(odd * M, (odd + 1) * M)
            both = nn_dot(hi_ref[r2, :, lanes], coef[r2, odd])
            rest = nn_dot(lo_ref[r2, :, lanes], coef[r2, odd, :, :wide])
            return both[:, :wide] + (both[:, wide:] + rest)

        even_sum = contraction(0)
        odd_sum = contraction(1)
        plus = even_sum + odd_sum
        minus = even_sum - odd_sum
        squares = jnp.concatenate([plus * plus, minus * minus], axis=1)
        sq_hi, sq_lo = split(squares)
        energy = nt_dot(mean_ref[...], sq_hi) + nt_dot(mean_ref[...], sq_lo)
        rows = 4 * plev
        flat[:, :KPTS] = energy
        en_hi, en_lo = split(flat[rows:, :KPAD])
        for t in range(KPAD // KBLK):
            lanes = slice(t * KBLK, (t + 1) * KBLK)
            back = KPAD - (t + 1) * KBLK
            mirror[:, back : back + KBLK] = nn_dot(en_hi[:, lanes], flip_ref[...]) + nn_dot(en_lo[:, lanes], flip_ref[...])

        quarter = own_points(points_ref, r2) // 4
        lane = iota((rows, BUF), 1)
        shift = (quarter + (BUF - (KPAD - 1))) % BUF
        flat[:rows, :] = jnp.where(lane <= quarter // 2, flat[:rows, :], pltpu.roll(mirror[...], shift, 1))
        line[...] = jnp.zeros_like(line)
        lane = iota((plev, BUF), 1)
        for b in range(4):
            start = quarter * b
            inner = start % 128
            base = pl.multiple_of(start - inner, 128)
            piece = pltpu.roll(flat[b * plev : (b + 1) * plev, :], inner, 1)
            old = line[:, pl.ds(base, BUF)]
            line[:, pl.ds(base, BUF)] = jnp.where((lane >= inner) & (lane < inner + quarter), piece, old)
        out_ref[:, pl.ds(r2, 1), :] = line[:, :ROWPAD].reshape(plev, 1, ROWPAD)


def synthesis(parts, moved, perm, table_hi, table_lo, row_points):
    plev = moved.shape[1]
    wide = plev * 2 * PART
    vmem = pl.BlockSpec(memory_space=pltpu.VMEM)
    return pl.pallas_call(
        functools.partial(synth_kernel, parts),
        out_shape=jax.ShapeDtypeStruct((plev, 2, ROWPAD), F32),
        in_specs=[pl.BlockSpec(memory_space=pltpu.SMEM)] + [vmem] * 5 + [pl.BlockSpec(memory_space=pltpu.HBM)] * 2,
        out_specs=vmem,
        scratch_shapes=[
            pltpu.VMEM((2, KPTS, 2 * M), BF16),
            pltpu.VMEM((2, KPTS, 2 * M), BF16),
            pltpu.VMEM((M, 2 * wide), BF16),
            pltpu.VMEM((2, 2, M, 2 * wide), BF16),
            pltpu.VMEM((8 * plev, BUF), F32),
            pltpu.VMEM((4 * plev, BUF), F32),
            pltpu.VMEM((plev, 3 * 1280 + BUF), F32),
            pltpu.SemaphoreType.DMA((2, 2, 2)),
        ],
        compiler_params=pltpu.CompilerParams(vmem_limit_bytes=44 * MIB),
        cost_estimate=pl.CostEstimate(flops=2 * 2 * KPTS * 2 * M * 384, bytes_accessed=2 * KPTS * 2 * M * 4 + M * M * 2, transcendentals=0),
        name="synthesis",
    )(
        pltpu.with_memory_space_constraint(row_points, pltpu.HBM),
        pltpu.with_memory_space_constraint(moved, pltpu.VMEM),
        pick_tables(plev), mean_table(plev), flip_table(),
        pltpu.with_memory_space_constraint(perm, pltpu.VMEM),
        *[pltpu.with_memory_space_constraint(x, pltpu.HBM) for x in (table_hi, table_lo)],
    )


def join_kernel(*refs):
    parts = (len(refs) - 1) // 2
    at = 0
    for own_ref, other_ref in zip(refs[:parts], refs[parts:-1]):
        rows = own_ref.shape[1]
        refs[-1][:, at : at + rows, :] = own_ref[...] + other_ref[...]
        at += rows


def join(owns, others):
    rows = sum(x.shape[1] for x in owns)
    vmem = pl.BlockSpec(memory_space=pltpu.VMEM)
    return pl.pallas_call(
        join_kernel,
        out_shape=jax.ShapeDtypeStruct((owns[0].shape[0], rows, SQ * PART), F32),
        in_specs=[vmem] * (2 * len(owns)),
        out_specs=vmem,
        compiler_params=pltpu.CompilerParams(vmem_limit_bytes=32 * MIB),
        name="join",
    )(*[pltpu.with_memory_space_constraint(x, pltpu.VMEM) for x in owns + others])


def local(spectral, legendre, wave_map, row_points, brackets, lev_weight, climatology):
    slots = spectral.shape[0]
    half = legendre.shape[1]
    groups = slots // SQ
    wave_count = lax.axis_size("wave")
    lev_count = lax.axis_size("lev")
    rows_dev = 2 * half // (wave_count * lev_count)
    cuts = (0, groups)
    own_maps = wave_map.reshape(wave_count, SQ, groups)
    pairs = [(d, d - 1) for d in range(1, lev_count)]
    parts = list(zip(cuts[:-1], cuts[1:]))
    owns, others, maps = [], [], []
    order = wave_map
    between_chips = jnp.any(brackets[1:-1:2] == jnp.arange(2, lev_count, 2) * LEV_DEV - 1)
    for start, stop in parts:
        own, prev = legendre_sums(start, stop - start, spectral, legendre, order, brackets, lev_weight)
        order, prev = lax.optimization_barrier((wave_map, prev))
        if others:
            prev, _ = lax.optimization_barrier((prev, others[-1]))
        owns.append(own)
        others.append(
            lax.cond(
                between_chips,
                lambda x: lax.ppermute(x, "lev", pairs),
                lambda x: lax.ppermute(x, "lev", pairs[::2]),
                prev,
            )
        )
        maps.append(jnp.transpose(own_maps[:, :, start:stop], (1, 0, 2)).reshape(SQ, wave_count * (stop - start)))
    sent = join(owns, others)
    moved = lax.all_to_all(sent, ("wave", "lev"), split_axis=0, concat_axis=0, tiled=True)
    moved = moved.reshape(wave_count, lev_count, rows_dev * groups, SQ * PART)
    slot_map = jnp.concatenate(maps, axis=1).reshape(1, M)
    table_points, _ = lax.optimization_barrier((row_points, sent))
    table_hi, table_lo, perm = tables(table_points, slot_map)
    energy = synthesis(parts, moved, perm, table_hi, table_lo, row_points)
    result = lax.all_to_all(energy, "lev", split_axis=0, concat_axis=0, tiled=True)
    result = result.reshape(1, rows_dev * lev_count, ROWPAD)
    points_all = jnp.concatenate([row_points, row_points])
    band_rows = rows_dev * lev_count
    out_points = lax.dynamic_slice_in_dim(points_all, lax.axis_index("wave") * band_rows, band_rows, 0)
    places = jnp.arange(ROWPAD, dtype=jnp.int32)
    inside = places[None, None, :] < out_points[None, :, None]
    return jnp.where(inside, result - climatology, 0.0)


def solution(mesh):
    placed = (
        P("wave", "lev", None),
        P("wave", None, None),
        P(),
        P(),
        P(),
        P(),
        P("lev", "wave", None),
    )
    return jax.shard_map(
        local, mesh=mesh, in_specs=placed, out_specs=P("lev", "wave", None), check_vma=False
    )
```

```python
import functools
import math

import jax
import jax.numpy as jnp
import numpy as np
from jax import lax
from jax.experimental import pallas as pl
from jax.experimental.pallas import tpu as pltpu
from jax.sharding import PartitionSpec as P

M = 1280
NT = 1280
LEV_DEV = 4
STEPS = 4
FIELDS = 2
ROWPAD = 5248

FS = FIELDS * STEPS
PART = 2 * FS
SQ = 8
STEP_SLOTS = 1
DEPTH = 5
HALF_M = M // 2
KPTS = 672
KPAD = 768
KBLK = 256
TABLE_STEPS = 7
TABLE_CUTS = 3
BUF = 1536
MIB = 1024 * 1024
F32 = jnp.float32
BF16 = jnp.bfloat16


def iota(shape, dim):
    return lax.broadcasted_iota(jnp.int32, shape, dim)


def legendre_kernel(
    first_group, count, wave_map, brackets, weight_ref, spec_hbm, leg_hbm, own_ref, prev_ref,
    low_buf, up_buf, first_buf, leg_buf, own_rows, prev_rows, sems,
):
    groups = spec_hbm.shape[1]
    slots = SQ * groups
    steps = count // STEP_SLOTS
    half = leg_hbm.shape[2]
    wave = lax.axis_index("wave")
    lev = lax.axis_index("lev")
    lower = brackets[lev] - lev * LEV_DEV
    has_upper = lower < LEV_DEV - 1
    w = weight_ref[lev]
    upper_w = jnp.where(has_upper, 1.0 - w, 0.0)
    before = jnp.maximum(lev - 1, 0)
    crosses = (lev > 0) & (brackets[before] == lev * LEV_DEV - 1)
    first_w = jnp.where(crosses, 1.0 - weight_ref[before], 0.0)
    degree = iota((16, NT), 1).astype(jnp.int16)
    sign = (1 - 2 * (iota((16, NT), 1) % 2)).astype(F32).astype(BF16)
    lane_group = iota((1, 2 * SQ * PART), 1) % 64 // PART
    left = iota((1, SQ * PART), 1) < 64
    south = iota((2 * half, 1), 0) >= half

    def columns_copy(step, level, buf, kind):
        slot = step % DEPTH
        rows = pl.ds(pl.multiple_of(level * PART, PART), PART)
        src = spec_hbm.at[:, pl.ds(first_group + step * STEP_SLOTS, STEP_SLOTS), rows, :]
        return pltpu.make_async_copy(src, buf.at[slot], sems.at[slot, kind])

    def values_copy(step):
        slot = step % DEPTH
        src = leg_hbm.at[:, pl.ds(first_group + step * STEP_SLOTS, STEP_SLOTS)]
        return pltpu.make_async_copy(src, leg_buf.at[slot], sems.at[slot, 3])

    def fetch(step):
        values_copy(step).start()
        columns_copy(step, lower, low_buf, 0).start()

        @pl.when(has_upper)
        def _():
            columns_copy(step, lower + 1, up_buf, 1).start()

        @pl.when(crosses)
        def _():
            columns_copy(step, 0, first_buf, 2).start()

    def await_step(step):
        values_copy(step).wait()
        columns_copy(step, lower, low_buf, 0).wait()

        @pl.when(has_upper)
        def _():
            columns_copy(step, lower + 1, up_buf, 1).wait()

        @pl.when(crosses)
        def _():
            columns_copy(step, 0, first_buf, 2).wait()

    for step in range(DEPTH - 1):
        fetch(step)

    @pl.when(jnp.logical_not(has_upper))
    def _():
        up_buf[...] = jnp.zeros_like(up_buf)

    @pl.when(jnp.logical_not(crosses))
    def _():
        first_buf[...] = jnp.zeros_like(first_buf)

    def step_body(step, carry):
        slot = step % DEPTH
        await_step(step)

        @pl.when(step + DEPTH - 1 < steps)
        def _():
            fetch(step + DEPTH - 1)

        for b in range(STEP_SLOTS):
            owns, firsts = [], []
            for quad in range(2):
                values, factors = [], []
                for sq in range(4 * quad, 4 * quad + 4):
                    m = wave_map[wave * slots + sq * groups + first_group + step * STEP_SLOTS + b]
                    kept = degree >= m.astype(jnp.int16)
                    plain = [jnp.where(kept, leg_buf[slot, sq, b, i : i + 16, :], 0) for i in range(0, half, 16)]
                    values += plain + [x * sign for x in plain]
                    factors.append(jnp.where(south, (1 - 2 * (m % 2)).astype(F32), 1.0))
                bufs = (low_buf, up_buf, first_buf) if quad == 0 else (up_buf, low_buf, first_buf)
                columns = [buf[slot, sq, b] for buf in bufs for sq in range(4 * quad, 4 * quad + 4)]
                sums = nt_dot(jnp.concatenate(values, axis=0), jnp.concatenate(columns, axis=0))
                kept_sums = sums[: 2 * half] * factors[0]
                for a in range(1, 4):
                    block = sums[2 * half * a : 2 * half * (a + 1)] * factors[a]
                    kept_sums = jnp.where(lane_group[:, :192] == a, block, kept_sums)
                both = kept_sums[:, :128]
                other = pltpu.roll(both, 64, 1)
                owns.append(both * w + other * upper_w)
                firsts.append(jnp.concatenate([kept_sums[:, 128:]] * 2, axis=1))
            at = pl.multiple_of((step * STEP_SLOTS + b) * 2 * half, 2 * half)
            own_rows[pl.ds(at, 2 * half), :] = jnp.where(left, owns[0], owns[1])
            prev_rows[pl.ds(at, 2 * half), :] = jnp.where(left, firsts[0], firsts[1]) * first_w
        return carry

    lax.fori_loop(0, steps, step_body, 0)
    rows = 2 * half
    for rows_ref, ref in ((own_rows, own_ref), (prev_rows, prev_ref)):
        rows_dev = ref.shape[1] // count
        for r in range(rows):
            at = (r % rows_dev) * count
            ref[r // rows_dev, at : at + count, :] = rows_ref[pl.ds(r, count, stride=rows), :]


def legendre_sums(first_group, count, spectral, legendre, wave_map, brackets, lev_weight):
    slots, cols, _ = spectral.shape
    half = legendre.shape[1]
    groups = slots // SQ
    spec = spectral.reshape(SQ, groups, cols, NT)
    leg = legendre.reshape(SQ, groups, half, NT)
    devices = lax.axis_size("wave") * lax.axis_size("lev")
    out = pltpu.VMEM((devices, 2 * half // devices * count, SQ * PART), F32)
    smem = pl.BlockSpec(memory_space=pltpu.SMEM)
    vmem = pl.BlockSpec(memory_space=pltpu.VMEM)
    anywhere = pl.BlockSpec(memory_space=pltpu.HBM)
    return pl.pallas_call(
        functools.partial(legendre_kernel, first_group, count),
        out_shape=[out, out],
        in_specs=[smem, smem, smem, anywhere, anywhere],
        out_specs=[vmem, vmem],
        scratch_shapes=[pltpu.VMEM((DEPTH, SQ, STEP_SLOTS, PART, NT), BF16)] * 3
        + [pltpu.VMEM((DEPTH, SQ, STEP_SLOTS, half, NT), BF16)]
        + [pltpu.VMEM((count * 2 * half, SQ * PART), F32)] * 2
        + [pltpu.SemaphoreType.DMA((DEPTH, 4))],
        compiler_params=pltpu.CompilerParams(vmem_limit_bytes=48 * MIB),
        cost_estimate=pl.CostEstimate(
            flops=2 * SQ * count * 2 * half * 48 * NT, bytes_accessed=SQ * count * NT * 2 * (48 + half), transcendentals=0
        ),
        name="legendre_sums",
    )(
        *[pltpu.with_memory_space_constraint(x, pltpu.HBM) for x in (wave_map, brackets, lev_weight, spec, leg)]
    )


def unit_circle(product, points, inverse):
    big = 12582912.0
    turn = (product * inverse + big) - big
    x = (product - turn * points) * (math.pi * inverse)
    x2 = x * x
    sine = 0.0
    cosine = 0.0
    for power in (11, 9, 7, 5, 3, 1):
        sine = sine * x2 + (-1) ** (power // 2) / math.factorial(power)
    for power in (12, 10, 8, 6, 4, 2, 0):
        cosine = cosine * x2 + (-1) ** (power // 2) / math.factorial(power)
    sine = sine * x
    twice = sine + sine
    return 1.0 - twice * sine, twice * cosine


def own_points(points_ref, r2):
    wave = lax.axis_index("wave")
    lev = lax.axis_index("lev")
    row = 2 * (wave * lax.axis_size("lev") + lev) + r2
    return points_ref[row % points_ref.shape[0]]


def table_kernel(points_ref, hi_ref, lo_ref):
    r2 = pl.program_id(0)
    kb = pl.program_id(1)
    rows = hi_ref.shape[1]
    points = own_points(points_ref, r2).astype(F32)
    inverse = 1.0 / points

    lane = iota((16, 128), 1).astype(F32)

    def chunk_body(i, carry):
        chunk = pl.multiple_of(i * 16, 16)

        def put(tile, value):
            lanes = slice(tile * 128, tile * 128 + 128)
            hi = value.astype(BF16)
            hi_ref[0, pl.ds(chunk, 16), lanes] = hi
            lo_ref[0, pl.ds(chunk, 16), lanes] = (value - hi.astype(F32)).astype(BF16)

        k = (kb * rows + chunk + iota((16, 128), 0)).astype(F32)
        c, s = unit_circle(2.0 * lane * k, points, inverse)
        c1, s1 = unit_circle(k, points, inverse)
        ct, st = unit_circle(256.0 * k, points, inverse)
        co = c * c1 - s * s1
        so = s * c1 + c * s1
        for t in range(HALF_M // 128):
            if t:
                c, s = c * ct - s * st, s * ct + c * st
                co, so = co * ct - so * st, so * ct + co * st
            put(t, c)
            put(5 + t, s)
            put(10 + t, co)
            put(15 + t, so)
        return carry

    lax.fori_loop(0, rows // 16, chunk_body, 0, unroll=True)


def tables(row_points):
    rows = KPTS // TABLE_STEPS
    table = pltpu.HBM((2, KPTS, 2 * M), BF16)
    table_spec = pl.BlockSpec((1, rows, 2 * M), lambda r, k: (r, k, 0))
    return pl.pallas_call(
        table_kernel,
        out_shape=[table, table],
        grid=(2, TABLE_STEPS),
        in_specs=[pl.BlockSpec(memory_space=pltpu.SMEM)],
        out_specs=[table_spec, table_spec],
        compiler_params=pltpu.CompilerParams(vmem_limit_bytes=48 * MIB),
        cost_estimate=pl.CostEstimate(flops=2 * KPTS * 2 * M * 12, bytes_accessed=2 * KPTS * 2 * M * 4, transcendentals=0),
        name="fourier_tables",
    )(pltpu.with_memory_space_constraint(row_points, pltpu.HBM))


def pick_tables(plev):
    wide = plev * 2 * PART
    out = np.zeros((2, 4, 2 * wide, 2 * wide), np.float32)
    plans = (
        ((0, 1), (0, 1), (0, 1), (0, 1)),
        ((1, -1), (1, 1), (1, -1), (1, 1)),
        ((0, 1), (0, 1), (1, -1), (1, -1)),
        ((1, -1), (1, 1), (0, -1), (0, 1)),
    )
    for r2 in range(2):
        for kind, plan in enumerate(plans):
            for image, (part, sgn) in enumerate(plan):
                for hl in range(2):
                    for p in range(plev):
                        for q in range(FS):
                            src = hl * wide + p * 2 * PART + r2 * PART + q * 2 + part
                            dst = hl * wide + image * plev * FS + p * FS + q
                            out[r2, kind, src, dst] = sgn
    return out.astype(jnp.bfloat16)


def mean_table(plev):
    wide = plev * FS * 4
    out = np.zeros((2 * 4 * plev, 2 * wide), np.float32)
    for quarter in range(4):
        for p in range(plev):
            for part in range(2):
                image_quarter = (quarter + part) % 4
                start = (image_quarter * 2 + part) * plev * FS + p * FS
                out[part * 4 * plev + quarter * plev + p, start : start + FS] = 0.5 / STEPS
    return out.astype(jnp.bfloat16)


def flip_table():
    return np.fliplr(np.eye(KBLK, dtype=np.float32)).astype(jnp.bfloat16)


def split(x):
    hi = x.astype(BF16)
    return hi, (x - hi.astype(F32)).astype(BF16)


def nt_dot(a, b):
    return lax.dot_general(a, b, (((1,), (1,)), ((), ())), preferred_element_type=F32)


def nn_dot(a, b):
    return jnp.dot(a, b, preferred_element_type=F32)


def synth_kernel(parts, points_ref, *refs):
    moved_ref, map_ref, pick_ref, mean_ref, flip_ref, hi_hbm, lo_hbm, out_ref = refs[:8]
    perm_ref, hi_ref, lo_ref, mixed, coef, flat, mirror, line, sems = refs[8:]
    table_copies = []
    for r2 in range(2):
        table_copies.append([])
        for i, (src, dst) in enumerate(((hi_hbm, hi_ref), (lo_hbm, lo_ref))):
            for c in range(TABLE_CUTS):
                rows = pl.ds(c * (KPTS // TABLE_CUTS), KPTS // TABLE_CUTS)
                table_copies[r2].append(pltpu.make_async_copy(src.at[r2, rows], dst.at[r2, rows], sems.at[r2, i, c]))
    for copy in table_copies[0]:
        copy.start()

    slot_waves = jnp.broadcast_to(map_ref[...], (16, M)).astype(jnp.int16)

    def perm_body(i, carry):
        row = pl.multiple_of(i * 16, 16)
        order = row + iota((16, M), 0)
        wanted = jnp.where(row < HALF_M, 2 * order, 2 * (order - HALF_M) + 1).astype(jnp.int16)
        perm_ref[pl.ds(row, 16), :] = jnp.where(slot_waves == wanted, 1.0, 0.0).astype(BF16)
        return carry

    lax.fori_loop(0, M // 16, perm_body, 0, unroll=4)
    waves, plev, _, _ = moved_ref.shape
    wide = plev * 2 * PART
    part_rows = M // SQ
    for base in range(0, plev * 2, 8):
        cur = []
        for g in range(base, base + 8):
            pieces = []
            for start, stop in parts:
                first = 2 * start + (g % 2) * (stop - start)
                pieces += [moved_ref[w, g // 2, first : first + stop - start, :] for w in range(waves)]
            cur.append(jnp.concatenate(pieces, axis=0))
        group = iota((part_rows, 128), 1) // PART
        for bit in (1, 2, 4):
            unset = (group & bit) == 0
            nxt = list(cur)
            for g in range(8):
                if g & bit == 0:
                    a, b = cur[g], cur[g + bit]
                    nxt[g] = jnp.where(unset, a, pltpu.roll(b, bit * PART, 1))
                    nxt[g + bit] = jnp.where(unset, pltpu.roll(a, 128 - bit * PART, 1), b)
            cur = nxt
        for sq in range(SQ):
            hi, lo = split(cur[sq])
            lane = base * PART
            mixed[sq * part_rows : (sq + 1) * part_rows, lane : lane + 128] = hi
            mixed[sq * part_rows : (sq + 1) * part_rows, wide + lane : wide + lane + 128] = lo

    lane_row = (iota((1, 2 * wide), 1) // PART) % 2
    limit0 = (own_points(points_ref, 0) - 1) // 2
    limit1 = (own_points(points_ref, 1) - 1) // 2
    limit = jnp.where(lane_row == 0, limit0, limit1)
    place = iota((HALF_M, 1), 0)
    turned = (iota((1, 2 * wide), 1) % wide) // (plev * FS) >= 2
    flip_sign = jnp.where(turned & (place % 2 == 1), -1.0, 1.0).astype(BF16)
    for odd in range(2):
        ordered = nn_dot(perm_ref[odd * HALF_M : (odd + 1) * HALF_M, :], mixed[...])
        wave = 2 * place + odd
        factor = jnp.where(wave <= limit, jnp.where(wave == 0, 1.0, 2.0), 0.0)
        ordered = (ordered * factor).astype(BF16)
        for row in range(2):
            for part in range(2):
                picked = nn_dot(ordered, pick_ref[row, odd * 2 + part]).astype(BF16)
                coef[row, odd, part * HALF_M : (part + 1) * HALF_M, :] = picked * flip_sign
    flat[...] = jnp.zeros_like(flat)
    mirror[...] = jnp.zeros_like(mirror)

    for r2 in range(2):
        for copy in table_copies[r2]:
            copy.wait()
        for copy in table_copies[1] if r2 == 0 else []:
            copy.start()

        def contraction(odd):
            lanes = slice(odd * M, (odd + 1) * M)
            both = nn_dot(hi_ref[r2, :, lanes], coef[r2, odd])
            rest = nn_dot(lo_ref[r2, :, lanes], coef[r2, odd, :, :wide])
            return both[:, :wide] + (both[:, wide:] + rest)

        even_sum = contraction(0)
        odd_sum = contraction(1)
        plus = even_sum + odd_sum
        minus = even_sum - odd_sum
        squares = jnp.concatenate([plus * plus, minus * minus], axis=1)
        sq_hi, sq_lo = split(squares)
        energy = nt_dot(mean_ref[...], sq_hi) + nt_dot(mean_ref[...], sq_lo)
        rows = 4 * plev
        flat[:, :KPTS] = energy
        en_hi, en_lo = split(flat[rows:, :KPAD])
        for t in range(KPAD // KBLK):
            lanes = slice(t * KBLK, (t + 1) * KBLK)
            back = KPAD - (t + 1) * KBLK
            mirror[:, back : back + KBLK] = nn_dot(en_hi[:, lanes], flip_ref[...]) + nn_dot(en_lo[:, lanes], flip_ref[...])

        quarter = own_points(points_ref, r2) // 4
        lane = iota((rows, BUF), 1)
        shift = (quarter + (BUF - (KPAD - 1))) % BUF
        flat[:rows, :] = jnp.where(lane <= quarter // 2, flat[:rows, :], pltpu.roll(mirror[...], shift, 1))
        line[...] = jnp.zeros_like(line)
        lane = iota((plev, BUF), 1)
        for b in range(4):
            start = quarter * b
            inner = start % 128
            base = pl.multiple_of(start - inner, 128)
            piece = pltpu.roll(flat[b * plev : (b + 1) * plev, :], inner, 1)
            old = line[:, pl.ds(base, BUF)]
            line[:, pl.ds(base, BUF)] = jnp.where((lane >= inner) & (lane < inner + quarter), piece, old)
        out_ref[:, pl.ds(r2, 1), :] = line[:, :ROWPAD].reshape(plev, 1, ROWPAD)


def synthesis(parts, moved, slot_map, table_hi, table_lo, row_points):
    plev = moved.shape[1]
    wide = plev * 2 * PART
    vmem = pl.BlockSpec(memory_space=pltpu.VMEM)
    return pl.pallas_call(
        functools.partial(synth_kernel, parts),
        out_shape=jax.ShapeDtypeStruct((plev, 2, ROWPAD), F32),
        in_specs=[pl.BlockSpec(memory_space=pltpu.SMEM)] + [vmem] * 5 + [pl.BlockSpec(memory_space=pltpu.HBM)] * 2,
        out_specs=vmem,
        scratch_shapes=[
            pltpu.VMEM((M, M), BF16),
            pltpu.VMEM((2, KPTS, 2 * M), BF16),
            pltpu.VMEM((2, KPTS, 2 * M), BF16),
            pltpu.VMEM((M, 2 * wide), BF16),
            pltpu.VMEM((2, 2, M, 2 * wide), BF16),
            pltpu.VMEM((8 * plev, BUF), F32),
            pltpu.VMEM((4 * plev, BUF), F32),
            pltpu.VMEM((plev, 3 * 1280 + BUF), F32),
            pltpu.SemaphoreType.DMA((2, 2, TABLE_CUTS)),
        ],
        compiler_params=pltpu.CompilerParams(vmem_limit_bytes=44 * MIB),
        cost_estimate=pl.CostEstimate(flops=2 * 2 * KPTS * 2 * M * 384, bytes_accessed=2 * KPTS * 2 * M * 4 + M * M * 2, transcendentals=0),
        name="synthesis",
    )(
        pltpu.with_memory_space_constraint(row_points, pltpu.HBM),
        pltpu.with_memory_space_constraint(moved, pltpu.VMEM), slot_map,
        pick_tables(plev), mean_table(plev), flip_table(),
        *[pltpu.with_memory_space_constraint(x, pltpu.HBM) for x in (table_hi, table_lo)],
    )


def join_kernel(*refs):
    parts = (len(refs) - 1) // 2
    at = 0
    for own_ref, other_ref in zip(refs[:parts], refs[parts:-1]):
        rows = own_ref.shape[1]
        refs[-1][:, at : at + rows, :] = own_ref[...] + other_ref[...]
        at += rows


def join(owns, others):
    rows = sum(x.shape[1] for x in owns)
    vmem = pl.BlockSpec(memory_space=pltpu.VMEM)
    return pl.pallas_call(
        join_kernel,
        out_shape=jax.ShapeDtypeStruct((owns[0].shape[0], rows, SQ * PART), F32),
        in_specs=[vmem] * (2 * len(owns)),
        out_specs=vmem,
        compiler_params=pltpu.CompilerParams(vmem_limit_bytes=32 * MIB),
        name="join",
    )(*[pltpu.with_memory_space_constraint(x, pltpu.VMEM) for x in owns + others])


def local(spectral, legendre, wave_map, row_points, brackets, lev_weight, climatology):
    slots = spectral.shape[0]
    half = legendre.shape[1]
    groups = slots // SQ
    wave_count = lax.axis_size("wave")
    lev_count = lax.axis_size("lev")
    rows_dev = 2 * half // (wave_count * lev_count)
    cuts = (0, groups)
    own_maps = wave_map.reshape(wave_count, SQ, groups)
    pairs = [(d, d - 1) for d in range(1, lev_count)]
    parts = list(zip(cuts[:-1], cuts[1:]))
    owns, others, maps = [], [], []
    order = wave_map
    last_levels = np.array([(p + 1) * LEV_DEV - 1 if p % 2 and p + 1 < lev_count else -1 for p in range(lev_count)], np.int32)
    between_chips = jnp.max((brackets == last_levels).astype(jnp.int32)) > 0
    for start, stop in parts:
        own, prev = legendre_sums(start, stop - start, spectral, legendre, order, brackets, lev_weight)
        order, prev = lax.optimization_barrier((wave_map, prev))
        owns.append(own)
        others.append(prev)
        maps.append(jnp.transpose(own_maps[:, :, start:stop], (1, 0, 2)).reshape(SQ, wave_count * (stop - start)))
    sent = lax.cond(
        between_chips,
        lambda mine, theirs: join(mine, [lax.ppermute(x, "lev", pairs) for x in theirs]),
        lambda mine, theirs: join(mine, [lax.ppermute(x, "lev", pairs[::2]) for x in theirs]),
        owns,
        others,
    )
    moved = lax.all_to_all(sent, ("wave", "lev"), split_axis=0, concat_axis=0, tiled=True)
    moved = moved.reshape(wave_count, lev_count, rows_dev * groups, SQ * PART)
    slot_map = jnp.concatenate(maps, axis=1).reshape(1, M)
    table_points, _ = lax.optimization_barrier((row_points, sent))
    table_hi, table_lo = tables(table_points)
    energy = synthesis(parts, moved, slot_map, table_hi, table_lo, row_points)
    result = lax.all_to_all(energy, "lev", split_axis=0, concat_axis=0, tiled=True)
    result = result.reshape(1, rows_dev * lev_count, ROWPAD)
    points_all = jnp.concatenate([row_points, row_points])
    band_rows = rows_dev * lev_count
    out_points = lax.dynamic_slice_in_dim(points_all, lax.axis_index("wave") * band_rows, band_rows, 0)
    places = jnp.arange(ROWPAD, dtype=jnp.int32)
    inside = places[None, None, :] < out_points[None, :, None]
    return jnp.where(inside, result - climatology, 0.0)


def solution(mesh):
    placed = (
        P("wave", "lev", None),
        P("wave", None, None),
        P(),
        P(),
        P(),
        P(),
        P("lev", "wave", None),
    )
    return jax.shard_map(
        local, mesh=mesh, in_specs=placed, out_specs=P("lev", "wave", None), check_vma=False
    )
```

```python
import functools
import math

import jax
import jax.numpy as jnp
import numpy as np
from jax import lax
from jax.experimental import pallas as pl
from jax.experimental.pallas import tpu as pltpu
from jax.sharding import PartitionSpec as P

M = 1280
NT = 1280
LEV_DEV = 4
STEPS = 4
FIELDS = 2
ROWPAD = 5248

FS = FIELDS * STEPS
PART = 2 * FS
SQ = 8
DEPTH = 3
HALF_M = M // 2
KPTS = 672
KPAD = 768
KBLK = 256
TABLE_STEPS = 7
TABLE_CUTS = 3
BUF = 1536
MIB = 1024 * 1024
F32 = jnp.float32
BF16 = jnp.bfloat16


def iota(shape, dim):
    return lax.broadcasted_iota(jnp.int32, shape, dim)


def legendre_kernel(
    first_group, count, wave_map, brackets, weight_ref, spec_hbm, leg_hbm, own_ref, prev_ref, between_ref,
    low_buf, up_buf, first_buf, leg_buf, own_rows, prev_rows, sems,
):
    groups = spec_hbm.shape[1]
    slots = SQ * groups
    step_slots = low_buf.shape[2]
    steps = count // step_slots
    half = leg_hbm.shape[2]
    wave = lax.axis_index("wave")
    lev = lax.axis_index("lev")
    lower = brackets[lev] - lev * LEV_DEV
    has_upper = lower < LEV_DEV - 1
    w = weight_ref[lev]
    upper_w = jnp.where(has_upper, 1.0 - w, 0.0)
    before = jnp.maximum(lev - 1, 0)
    crosses = (lev > 0) & (brackets[before] == lev * LEV_DEV - 1)
    first_w = jnp.where(crosses, 1.0 - weight_ref[before], 0.0)
    degree = iota((16, NT), 1).astype(jnp.int16)
    sign = (1 - 2 * (iota((16, NT), 1) % 2)).astype(F32).astype(BF16)
    lane_group = iota((1, 2 * SQ * PART), 1) % 64 // PART
    left = iota((1, SQ * PART), 1) < 64
    south = iota((2 * half, 1), 0) >= half

    def columns_copy(step, level, buf, kind):
        slot = step % DEPTH
        rows = pl.ds(pl.multiple_of(level * PART, PART), PART)
        src = spec_hbm.at[:, pl.ds(first_group + step * step_slots, step_slots), rows, :]
        return pltpu.make_async_copy(src, buf.at[slot], sems.at[slot, kind])

    def values_copy(step):
        slot = step % DEPTH
        src = leg_hbm.at[:, pl.ds(first_group + step * step_slots, step_slots)]
        return pltpu.make_async_copy(src, leg_buf.at[slot], sems.at[slot, 3])

    upper = jnp.minimum(lower + 1, LEV_DEV - 1)

    def copies(step):
        return [
            values_copy(step),
            columns_copy(step, lower, low_buf, 0),
            columns_copy(step, upper, up_buf, 1),
            columns_copy(step, 0, first_buf, 2),
        ]

    def fetch(step):
        for copy in copies(step):
            copy.start()

    for step in range(DEPTH - 1):
        fetch(step)
    between = jnp.int32(0)
    for p in range(1, brackets.shape[0] - 1, 2):
        between = between | (brackets[p] == (p + 1) * LEV_DEV - 1).astype(jnp.int32)
    between_ref[0] = between

    def step_body(step, carry):
        slot = step % DEPTH
        for copy in copies(step):
            copy.wait()

        @pl.when(step + DEPTH - 1 < steps)
        def _():
            fetch(step + DEPTH - 1)

        for b in range(step_slots):
            owns, firsts = [], []
            for quad in range(2):
                values, factors = [], []
                for sq in range(4 * quad, 4 * quad + 4):
                    m = wave_map[wave * slots + sq * groups + first_group + step * step_slots + b]
                    kept = degree >= m.astype(jnp.int16)
                    plain = [jnp.where(kept, leg_buf[slot, sq, b, i : i + 16, :], 0) for i in range(0, half, 16)]
                    values += plain + [x * sign for x in plain]
                    factors.append(jnp.where(south, (1 - 2 * (m % 2)).astype(F32), 1.0))
                bufs = (low_buf, up_buf, first_buf) if quad == 0 else (up_buf, low_buf, first_buf)
                columns = [buf[slot, sq, b] for buf in bufs for sq in range(4 * quad, 4 * quad + 4)]
                sums = nt_dot(jnp.concatenate(values, axis=0), jnp.concatenate(columns, axis=0))
                kept_sums = sums[: 2 * half] * factors[0]
                for a in range(1, 4):
                    block = sums[2 * half * a : 2 * half * (a + 1)] * factors[a]
                    kept_sums = jnp.where(lane_group[:, :192] == a, block, kept_sums)
                both = kept_sums[:, :128]
                other = pltpu.roll(both, 64, 1)
                owns.append(both * w + other * upper_w)
                firsts.append(jnp.concatenate([kept_sums[:, 128:]] * 2, axis=1))
            at = pl.multiple_of((step * step_slots + b) * 2 * half, 2 * half)
            own_rows[pl.ds(at, 2 * half), :] = jnp.where(left, owns[0], owns[1])
            prev_rows[pl.ds(at, 2 * half), :] = jnp.where(left, firsts[0], firsts[1]) * first_w
        return carry

    lax.fori_loop(0, steps, step_body, 0)
    rows = 2 * half
    for rows_ref, ref in ((own_rows, own_ref), (prev_rows, prev_ref)):
        rows_dev = ref.shape[1] // count
        for r in range(rows):
            at = (r % rows_dev) * count
            ref[r // rows_dev, at : at + count, :] = rows_ref[pl.ds(r, count, stride=rows), :]


def legendre_sums(first_group, count, spectral, legendre, wave_map, brackets, lev_weight):
    slots, cols, _ = spectral.shape
    half = legendre.shape[1]
    groups = slots // SQ
    step_slots = 4 if count % 4 == 0 else 2
    spec = spectral.reshape(SQ, groups, cols, NT)
    leg = legendre.reshape(SQ, groups, half, NT)
    devices = lax.axis_size("wave") * lax.axis_size("lev")
    out = pltpu.VMEM((devices, 2 * half // devices * count, SQ * PART), F32)
    smem = pl.BlockSpec(memory_space=pltpu.SMEM)
    vmem = pl.BlockSpec(memory_space=pltpu.VMEM)
    anywhere = pl.BlockSpec(memory_space=pltpu.HBM)
    return pl.pallas_call(
        functools.partial(legendre_kernel, first_group, count),
        out_shape=[out, out, jax.ShapeDtypeStruct((1,), jnp.int32)],
        in_specs=[smem, smem, smem, anywhere, anywhere],
        out_specs=[vmem, vmem, smem],
        scratch_shapes=[pltpu.VMEM((DEPTH, SQ, step_slots, PART, NT), BF16)] * 3
        + [pltpu.VMEM((DEPTH, SQ, step_slots, half, NT), BF16)]
        + [pltpu.VMEM((count * 2 * half, SQ * PART), F32)] * 2
        + [pltpu.SemaphoreType.DMA((DEPTH, 4))],
        compiler_params=pltpu.CompilerParams(vmem_limit_bytes=48 * MIB),
        cost_estimate=pl.CostEstimate(
            flops=2 * SQ * count * 2 * half * 48 * NT, bytes_accessed=SQ * count * NT * 2 * (48 + half), transcendentals=0
        ),
        name="legendre_sums",
    )(
        *[pltpu.with_memory_space_constraint(x, pltpu.HBM) for x in (wave_map, brackets, lev_weight, spec, leg)]
    )


def unit_circle(product, points, inverse):
    big = 12582912.0
    turn = (product * inverse + big) - big
    x = (product - turn * points) * (math.pi * inverse)
    x2 = x * x
    sine = 0.0
    cosine = 0.0
    for power in (11, 9, 7, 5, 3, 1):
        sine = sine * x2 + (-1) ** (power // 2) / math.factorial(power)
    for power in (12, 10, 8, 6, 4, 2, 0):
        cosine = cosine * x2 + (-1) ** (power // 2) / math.factorial(power)
    sine = sine * x
    twice = sine + sine
    return 1.0 - twice * sine, twice * cosine


def own_points(points_ref, r2):
    wave = lax.axis_index("wave")
    lev = lax.axis_index("lev")
    row = 2 * (wave * lax.axis_size("lev") + lev) + r2
    return points_ref[row % points_ref.shape[0]]


def table_kernel(points_ref, hi_ref, lo_ref):
    r2 = pl.program_id(0)
    kb = pl.program_id(1)
    rows = hi_ref.shape[1]
    points = own_points(points_ref, r2).astype(F32)
    inverse = 1.0 / points

    lane = iota((16, 128), 1).astype(F32)

    def chunk_body(i, carry):
        chunk = pl.multiple_of(i * 16, 16)

        def put(tile, value):
            lanes = slice(tile * 128, tile * 128 + 128)
            hi = value.astype(BF16)
            hi_ref[0, pl.ds(chunk, 16), lanes] = hi
            lo_ref[0, pl.ds(chunk, 16), lanes] = (value - hi.astype(F32)).astype(BF16)

        k = (kb * rows + chunk + iota((16, 128), 0)).astype(F32)
        c, s = unit_circle(2.0 * lane * k, points, inverse)
        c1, s1 = unit_circle(k, points, inverse)
        ct, st = unit_circle(256.0 * k, points, inverse)
        co = c * c1 - s * s1
        so = s * c1 + c * s1
        for t in range(HALF_M // 128):
            if t:
                c, s = c * ct - s * st, s * ct + c * st
                co, so = co * ct - so * st, so * ct + co * st
            put(t, c)
            put(5 + t, s)
            put(10 + t, co)
            put(15 + t, so)
        return carry

    lax.fori_loop(0, rows // 16, chunk_body, 0, unroll=True)


def tables(row_points):
    rows = KPTS // TABLE_STEPS
    table = pltpu.HBM((2, KPTS, 2 * M), BF16)
    table_spec = pl.BlockSpec((1, rows, 2 * M), lambda r, k: (r, k, 0))
    return pl.pallas_call(
        table_kernel,
        out_shape=[table, table],
        grid=(2, TABLE_STEPS),
        in_specs=[pl.BlockSpec(memory_space=pltpu.SMEM)],
        out_specs=[table_spec, table_spec],
        compiler_params=pltpu.CompilerParams(vmem_limit_bytes=48 * MIB),
        cost_estimate=pl.CostEstimate(flops=2 * KPTS * 2 * M * 12, bytes_accessed=2 * KPTS * 2 * M * 4, transcendentals=0),
        name="fourier_tables",
    )(pltpu.with_memory_space_constraint(row_points, pltpu.HBM))


def pick_tables(plev):
    wide = plev * 2 * PART
    out = np.zeros((2, 4, 2 * wide, 2 * wide), np.float32)
    plans = (
        ((0, 1), (0, 1), (0, 1), (0, 1)),
        ((1, -1), (1, 1), (1, -1), (1, 1)),
        ((0, 1), (0, 1), (1, -1), (1, -1)),
        ((1, -1), (1, 1), (0, -1), (0, 1)),
    )
    for r2 in range(2):
        for kind, plan in enumerate(plans):
            for image, (part, sgn) in enumerate(plan):
                for hl in range(2):
                    for p in range(plev):
                        for q in range(FS):
                            src = hl * wide + p * 2 * PART + r2 * PART + q * 2 + part
                            dst = hl * wide + image * plev * FS + p * FS + q
                            out[r2, kind, src, dst] = sgn
    return out.astype(jnp.bfloat16)


def mean_table(plev):
    wide = plev * FS * 4
    out = np.zeros((2 * 4 * plev, 2 * wide), np.float32)
    for quarter in range(4):
        for p in range(plev):
            for part in range(2):
                image_quarter = (quarter + part) % 4
                start = (image_quarter * 2 + part) * plev * FS + p * FS
                out[part * 4 * plev + quarter * plev + p, start : start + FS] = 0.5 / STEPS
    return out.astype(jnp.bfloat16)


def flip_table():
    return np.fliplr(np.eye(KBLK, dtype=np.float32)).astype(jnp.bfloat16)


def split(x):
    hi = x.astype(BF16)
    return hi, (x - hi.astype(F32)).astype(BF16)


def nt_dot(a, b):
    return lax.dot_general(a, b, (((1,), (1,)), ((), ())), preferred_element_type=F32)


def nn_dot(a, b):
    return jnp.dot(a, b, preferred_element_type=F32)


def synth_kernel(parts, points_ref, *refs):
    moved_ref, map_ref, pick_ref, mean_ref, flip_ref, hi_hbm, lo_hbm, out_ref = refs[:8]
    perm_ref, hi_ref, lo_ref, mixed, coef, flat, mirror, line, sems = refs[8:]
    table_copies = []
    for r2 in range(2):
        table_copies.append([])
        for i, (src, dst) in enumerate(((hi_hbm, hi_ref), (lo_hbm, lo_ref))):
            for c in range(TABLE_CUTS):
                rows = pl.ds(c * (KPTS // TABLE_CUTS), KPTS // TABLE_CUTS)
                table_copies[r2].append(pltpu.make_async_copy(src.at[r2, rows], dst.at[r2, rows], sems.at[r2, i, c]))
    for copy in table_copies[0]:
        copy.start()

    slot_waves = jnp.broadcast_to(map_ref[...], (16, M)).astype(jnp.int16)

    def perm_body(i, carry):
        row = pl.multiple_of(i * 16, 16)
        order = row + iota((16, M), 0)
        wanted = jnp.where(row < HALF_M, 2 * order, 2 * (order - HALF_M) + 1).astype(jnp.int16)
        perm_ref[pl.ds(row, 16), :] = jnp.where(slot_waves == wanted, 1.0, 0.0).astype(BF16)
        return carry

    lax.fori_loop(0, M // 16, perm_body, 0, unroll=4)
    waves, plev, _, _ = moved_ref.shape
    wide = plev * 2 * PART
    part_rows = M // SQ
    for base in range(0, plev * 2, 8):
        cur = []
        for g in range(base, base + 8):
            pieces = []
            for start, stop in parts:
                first = 2 * start + (g % 2) * (stop - start)
                pieces += [moved_ref[w, g // 2, first : first + stop - start, :] for w in range(waves)]
            cur.append(jnp.concatenate(pieces, axis=0))
        group = iota((part_rows, 128), 1) // PART
        for bit in (1, 2, 4):
            unset = (group & bit) == 0
            nxt = list(cur)
            for g in range(8):
                if g & bit == 0:
                    a, b = cur[g], cur[g + bit]
                    nxt[g] = jnp.where(unset, a, pltpu.roll(b, bit * PART, 1))
                    nxt[g + bit] = jnp.where(unset, pltpu.roll(a, 128 - bit * PART, 1), b)
            cur = nxt
        for sq in range(SQ):
            hi, lo = split(cur[sq])
            lane = base * PART
            mixed[sq * part_rows : (sq + 1) * part_rows, lane : lane + 128] = hi
            mixed[sq * part_rows : (sq + 1) * part_rows, wide + lane : wide + lane + 128] = lo

    lane_row = (iota((1, 2 * wide), 1) // PART) % 2
    limit0 = (own_points(points_ref, 0) - 1) // 2
    limit1 = (own_points(points_ref, 1) - 1) // 2
    limit = jnp.where(lane_row == 0, limit0, limit1)
    place = iota((HALF_M, 1), 0)
    turned = (iota((1, 2 * wide), 1) % wide) // (plev * FS) >= 2
    flip_sign = jnp.where(turned & (place % 2 == 1), -1.0, 1.0).astype(BF16)
    for odd in range(2):
        ordered = nn_dot(perm_ref[odd * HALF_M : (odd + 1) * HALF_M, :], mixed[...])
        wave = 2 * place + odd
        factor = jnp.where(wave <= limit, jnp.where(wave == 0, 1.0, 2.0), 0.0)
        ordered = (ordered * factor).astype(BF16)
        for row in range(2):
            for part in range(2):
                picked = nn_dot(ordered, pick_ref[row, odd * 2 + part]).astype(BF16)
                coef[row, odd, part * HALF_M : (part + 1) * HALF_M, :] = picked * flip_sign
    flat[...] = jnp.zeros_like(flat)
    mirror[...] = jnp.zeros_like(mirror)

    for r2 in range(2):
        for copy in table_copies[r2]:
            copy.wait()
        for copy in table_copies[1] if r2 == 0 else []:
            copy.start()

        def contraction(odd):
            lanes = slice(odd * M, (odd + 1) * M)
            both = nn_dot(hi_ref[r2, :, lanes], coef[r2, odd])
            rest = nn_dot(lo_ref[r2, :, lanes], coef[r2, odd, :, :wide])
            return both[:, :wide] + (both[:, wide:] + rest)

        even_sum = contraction(0)
        odd_sum = contraction(1)
        plus = even_sum + odd_sum
        minus = even_sum - odd_sum
        squares = jnp.concatenate([plus * plus, minus * minus], axis=1)
        sq_hi, sq_lo = split(squares)
        energy = nt_dot(mean_ref[...], sq_hi) + nt_dot(mean_ref[...], sq_lo)
        rows = 4 * plev
        flat[:, :KPTS] = energy
        en_hi, en_lo = split(flat[rows:, :KPAD])
        for t in range(KPAD // KBLK):
            lanes = slice(t * KBLK, (t + 1) * KBLK)
            back = KPAD - (t + 1) * KBLK
            mirror[:, back : back + KBLK] = nn_dot(en_hi[:, lanes], flip_ref[...]) + nn_dot(en_lo[:, lanes], flip_ref[...])

        quarter = own_points(points_ref, r2) // 4
        lane = iota((rows, BUF), 1)
        shift = (quarter + (BUF - (KPAD - 1))) % BUF
        flat[:rows, :] = jnp.where(lane <= quarter // 2, flat[:rows, :], pltpu.roll(mirror[...], shift, 1))
        line[...] = jnp.zeros_like(line)
        lane = iota((plev, BUF), 1)
        for b in range(4):
            start = quarter * b
            inner = start % 128
            base = pl.multiple_of(start - inner, 128)
            piece = pltpu.roll(flat[b * plev : (b + 1) * plev, :], inner, 1)
            old = line[:, pl.ds(base, BUF)]
            line[:, pl.ds(base, BUF)] = jnp.where((lane >= inner) & (lane < inner + quarter), piece, old)
        out_ref[:, pl.ds(r2, 1), :] = line[:, :ROWPAD].reshape(plev, 1, ROWPAD)


def synthesis(parts, moved, slot_map, table_hi, table_lo, row_points):
    plev = moved.shape[1]
    wide = plev * 2 * PART
    vmem = pl.BlockSpec(memory_space=pltpu.VMEM)
    return pl.pallas_call(
        functools.partial(synth_kernel, parts),
        out_shape=jax.ShapeDtypeStruct((plev, 2, ROWPAD), F32),
        in_specs=[pl.BlockSpec(memory_space=pltpu.SMEM)] + [vmem] * 5 + [pl.BlockSpec(memory_space=pltpu.HBM)] * 2,
        out_specs=vmem,
        scratch_shapes=[
            pltpu.VMEM((M, M), BF16),
            pltpu.VMEM((2, KPTS, 2 * M), BF16),
            pltpu.VMEM((2, KPTS, 2 * M), BF16),
            pltpu.VMEM((M, 2 * wide), BF16),
            pltpu.VMEM((2, 2, M, 2 * wide), BF16),
            pltpu.VMEM((8 * plev, BUF), F32),
            pltpu.VMEM((4 * plev, BUF), F32),
            pltpu.VMEM((plev, 3 * 1280 + BUF), F32),
            pltpu.SemaphoreType.DMA((2, 2, TABLE_CUTS)),
        ],
        compiler_params=pltpu.CompilerParams(vmem_limit_bytes=44 * MIB),
        cost_estimate=pl.CostEstimate(flops=2 * 2 * KPTS * 2 * M * 384, bytes_accessed=2 * KPTS * 2 * M * 4 + M * M * 2, transcendentals=0),
        name="synthesis",
    )(
        pltpu.with_memory_space_constraint(row_points, pltpu.HBM),
        pltpu.with_memory_space_constraint(moved, pltpu.VMEM), slot_map,
        pick_tables(plev), mean_table(plev), flip_table(),
        *[pltpu.with_memory_space_constraint(x, pltpu.HBM) for x in (table_hi, table_lo)],
    )


def join_kernel(*refs):
    parts = (len(refs) - 1) // 2
    at = 0
    for own_ref, other_ref in zip(refs[:parts], refs[parts:-1]):
        rows = own_ref.shape[1]
        refs[-1][:, at : at + rows, :] = own_ref[...] + other_ref[...]
        at += rows


def join(owns, others):
    rows = sum(x.shape[1] for x in owns)
    vmem = pl.BlockSpec(memory_space=pltpu.VMEM)
    return pl.pallas_call(
        join_kernel,
        out_shape=jax.ShapeDtypeStruct((owns[0].shape[0], rows, SQ * PART), F32),
        in_specs=[vmem] * (2 * len(owns)),
        out_specs=vmem,
        compiler_params=pltpu.CompilerParams(vmem_limit_bytes=32 * MIB),
        name="join",
    )(*[pltpu.with_memory_space_constraint(x, pltpu.VMEM) for x in owns + others])


def local(spectral, legendre, wave_map, row_points, brackets, lev_weight, climatology):
    slots = spectral.shape[0]
    half = legendre.shape[1]
    groups = slots // SQ
    wave_count = lax.axis_size("wave")
    lev_count = lax.axis_size("lev")
    rows_dev = 2 * half // (wave_count * lev_count)
    cuts = (0, groups)
    own_maps = wave_map.reshape(wave_count, SQ, groups)
    pairs = [(d, d - 1) for d in range(1, lev_count)]
    parts = list(zip(cuts[:-1], cuts[1:]))
    owns, others, maps = [], [], []
    order = wave_map
    for start, stop in parts:
        own, prev, between = legendre_sums(start, stop - start, spectral, legendre, order, brackets, lev_weight)
        order, prev = lax.optimization_barrier((wave_map, prev))
        owns.append(own)
        others.append(prev)
        maps.append(jnp.transpose(own_maps[:, :, start:stop], (1, 0, 2)).reshape(SQ, wave_count * (stop - start)))
    sent = lax.cond(
        between[0] > 0,
        lambda mine, theirs: join(mine, [lax.ppermute(x, "lev", pairs) for x in theirs]),
        lambda mine, theirs: join(mine, [lax.ppermute(x, "lev", pairs[::2]) for x in theirs]),
        owns,
        others,
    )
    moved = lax.all_to_all(sent, ("wave", "lev"), split_axis=0, concat_axis=0, tiled=True)
    moved = moved.reshape(wave_count, lev_count, rows_dev * groups, SQ * PART)
    slot_map = jnp.concatenate(maps, axis=1).reshape(1, M)
    table_points, _ = lax.optimization_barrier((row_points, sent))
    table_hi, table_lo = tables(table_points)
    energy = synthesis(parts, moved, slot_map, table_hi, table_lo, row_points)
    result = lax.all_to_all(energy, "lev", split_axis=0, concat_axis=0, tiled=True)
    result = result.reshape(1, rows_dev * lev_count, ROWPAD)
    points_all = jnp.concatenate([row_points, row_points])
    band_rows = rows_dev * lev_count
    out_points = lax.dynamic_slice_in_dim(points_all, lax.axis_index("wave") * band_rows, band_rows, 0)
    places = jnp.arange(ROWPAD, dtype=jnp.int32)
    inside = places[None, None, :] < out_points[None, :, None]
    return jnp.where(inside, result - climatology, 0.0)


def solution(mesh):
    placed = (
        P("wave", "lev", None),
        P("wave", None, None),
        P(),
        P(),
        P(),
        P(),
        P("lev", "wave", None),
    )
    return jax.shard_map(
        local, mesh=mesh, in_specs=placed, out_specs=P("lev", "wave", None), check_vma=False
    )
```

```python
import functools
import math

import jax
import jax.numpy as jnp
import numpy as np
from jax import lax
from jax.experimental import pallas as pl
from jax.experimental.pallas import tpu as pltpu
from jax.sharding import PartitionSpec as P

M = 1280
NT = 1280
LEV_DEV = 4
STEPS = 4
FIELDS = 2
ROWPAD = 5248

FS = FIELDS * STEPS
PART = 2 * FS
SQ = 8
STEP = 16
CHUNK = 256
DEPTH = 3
HALF_M = M // 2
KPTS = 672
KPAD = 768
KBLK = 256
TABLE_STEPS = 7
TABLE_CUTS = 3
BUF = 1536
MIB = 1024 * 1024
F32 = jnp.float32
BF16 = jnp.bfloat16


def iota(shape, dim):
    return lax.broadcasted_iota(jnp.int32, shape, dim)


def waves_of(map_ref, wave, slots):
    start = wave * slots
    row = start // 128
    last = map_ref.shape[0] - 1
    pair = jnp.concatenate([map_ref[pl.ds(row, 1), :], map_ref[pl.ds(jnp.minimum(row + 1, last), 1), :]], axis=1)
    pair = jnp.broadcast_to(pair, (8, 256)).astype(F32)
    turned = pltpu.roll(pair, (256 - start % 128) % 256, 1)
    return jnp.where(iota((8, 256), 1) < slots, turned, 4096.0)[:1]


def ranks_of(waves):
    across = jnp.broadcast_to(waves, (256, 256))
    down = across.T
    rank = jnp.sum(jnp.where(across < down, 1.0, 0.0), axis=1, keepdims=True)
    return rank, down


def legendre_kernel(
    brackets, weight_ref, map_ref, spec_hbm, leg_hbm, own_ref, prev_ref, between_ref,
    pair_buf, first_buf, leg_buf, own_rows, prev_rows, order_vmem, order, order_sem, sems,
):
    slots, half, _ = leg_hbm.shape
    groups = slots // SQ
    steps = slots // STEP
    wave = lax.axis_index("wave")
    lev = lax.axis_index("lev")
    lower = brackets[lev] - lev * LEV_DEV
    has_upper = lower < LEV_DEV - 1
    w = weight_ref[lev]
    low_w = jnp.where(has_upper, w, 0.0)
    upper_w = jnp.where(has_upper, 1.0 - w, w)
    pair_row = jnp.minimum(lower, LEV_DEV - 2) * PART
    before = jnp.maximum(lev - 1, 0)
    crosses = (lev > 0) & (brackets[before] == lev * LEV_DEV - 1)
    first_w = jnp.where(crosses, 1.0 - weight_ref[before], 0.0)
    degree = iota((16, NT), 1).astype(jnp.int16)
    sign = (1 - 2 * (iota((16, NT), 1) % 2)).astype(F32).astype(BF16)
    lane_group = iota((1, 192), 1) % 64 // PART
    left = iota((1, SQ * PART), 1) < 64
    south = iota((2 * half, 1), 0) >= half

    rank, down = ranks_of(waves_of(map_ref, wave, slots))
    hit = rank == iota((256, 256), 1).astype(F32)
    slot_at = jnp.sum(jnp.where(hit, iota((256, 256), 0).astype(F32), 0.0), axis=0, keepdims=True)
    wave_at = jnp.sum(jnp.where(hit, down, 0.0), axis=0, keepdims=True)
    order_vmem[0:1, :] = slot_at.astype(jnp.int32)
    order_vmem[1:2, :] = wave_at.astype(jnp.int32)
    to_smem = pltpu.make_async_copy(order_vmem, order, order_sem)
    to_smem.start()
    to_smem.wait()

    def buffers(slot, c):
        lanes = pl.ds(c * CHUNK, NT - c * CHUNK)
        return [
            (leg_hbm.at[:, :, lanes], leg_buf.at[slot, :, :, lanes], sems.at[slot, 0]),
            (spec_hbm.at[:, pl.ds(pl.multiple_of(pair_row, PART), 2 * PART), lanes], pair_buf.at[slot, :, :, lanes], sems.at[slot, 1]),
            (spec_hbm.at[:, pl.ds(0, PART), lanes], first_buf.at[slot, :, :, lanes], sems.at[slot, 2]),
        ]

    def fetch(step):
        chunk = order[1, step * STEP] // CHUNK
        for c in range(NT // CHUNK):

            @pl.when(chunk == c)
            def _():
                for i in range(STEP):
                    at = order[0, step * STEP + i]
                    for src, dst, sem in buffers(step % DEPTH, c):
                        pltpu.make_async_copy(src.at[at], dst.at[i], sem).start()

    for step in range(DEPTH - 1):
        fetch(step)
    between = jnp.int32(0)
    for p in range(1, brackets.shape[0] - 1, 2):
        between = between | (brackets[p] == (p + 1) * LEV_DEV - 1).astype(jnp.int32)
    between_ref[0] = between

    def multiply(step, c):
        slot = step % DEPTH
        lanes = slice(c * CHUNK, NT)
        for src, dst, sem in buffers(slot, c):
            pltpu.make_async_copy(src.at[pl.ds(0, STEP)], dst, sem).wait()
        for b in range(STEP // SQ):
            owns, firsts = [], []
            for quad in range(2):
                values, factors, columns = [], [], [[], [], []]
                for i in range(b * SQ + 4 * quad, b * SQ + 4 * quad + 4):
                    m = order[1, step * STEP + i]
                    kept = degree[:, lanes] >= m.astype(jnp.int16)
                    plain = [jnp.where(kept, leg_buf[slot, i, r : r + 16, lanes], 0) for r in range(0, half, 16)]
                    values += plain + [x * sign[:, lanes] for x in plain]
                    factors.append(jnp.where(south, (1 - 2 * (m % 2)).astype(F32), 1.0))
                    columns[quad].append(pair_buf[slot, i, :PART, lanes])
                    columns[1 - quad].append(pair_buf[slot, i, PART:, lanes])
                    columns[2].append(first_buf[slot, i, :, lanes])
                sums = nt_dot(jnp.concatenate(values, axis=0), jnp.concatenate(columns[0] + columns[1] + columns[2], axis=0))
                kept_sums = sums[: 2 * half] * factors[0]
                for a in range(1, 4):
                    block = sums[2 * half * a : 2 * half * (a + 1)] * factors[a]
                    kept_sums = jnp.where(lane_group == a, block, kept_sums)
                both = kept_sums[:, :128]
                owns.append(both * low_w + pltpu.roll(both, 64, 1) * upper_w)
                firsts.append(jnp.concatenate([kept_sums[:, 128:]] * 2, axis=1))
            at = pl.multiple_of((step * (STEP // SQ) + b) * 2 * half, 2 * half)
            own_rows[pl.ds(at, 2 * half), :] = jnp.where(left, owns[0], owns[1])
            prev_rows[pl.ds(at, 2 * half), :] = jnp.where(left, firsts[0], firsts[1]) * first_w

    def step_body(step, carry):
        @pl.when(step + DEPTH - 1 < steps)
        def _():
            fetch(step + DEPTH - 1)

        chunk = order[1, step * STEP] // CHUNK
        for c in range(NT // CHUNK):
            pl.when(chunk == c)(functools.partial(multiply, step, c))
        return carry

    lax.fori_loop(0, steps, step_body, 0)
    rows = 2 * half
    for rows_ref, ref in ((own_rows, own_ref), (prev_rows, prev_ref)):
        rows_dev = ref.shape[1] // groups
        for r in range(rows):
            at = (r % rows_dev) * groups
            ref[r // rows_dev, at : at + groups, :] = rows_ref[pl.ds(r, groups, stride=rows), :]


def legendre_sums(spectral, legendre, map_rows, brackets, lev_weight):
    slots = spectral.shape[0]
    half = legendre.shape[1]
    groups = slots // SQ
    devices = lax.axis_size("wave") * lax.axis_size("lev")
    out = pltpu.VMEM((devices, 2 * half // devices * groups, SQ * PART), F32)
    smem = pl.BlockSpec(memory_space=pltpu.SMEM)
    vmem = pl.BlockSpec(memory_space=pltpu.VMEM)
    hbm = pl.BlockSpec(memory_space=pltpu.HBM)
    return pl.pallas_call(
        legendre_kernel,
        out_shape=[out, out, jax.ShapeDtypeStruct((1,), jnp.int32)],
        in_specs=[smem, smem, vmem, hbm, hbm],
        out_specs=[vmem, vmem, smem],
        scratch_shapes=[
            pltpu.VMEM((DEPTH, STEP, 2 * PART, NT), BF16),
            pltpu.VMEM((DEPTH, STEP, PART, NT), BF16),
            pltpu.VMEM((DEPTH, STEP, half, NT), BF16),
            pltpu.VMEM((groups * 2 * half, SQ * PART), F32),
            pltpu.VMEM((groups * 2 * half, SQ * PART), F32),
            pltpu.VMEM((2, 256), jnp.int32),
            pltpu.SMEM((2, 256), jnp.int32),
            pltpu.SemaphoreType.DMA,
            pltpu.SemaphoreType.DMA((DEPTH, 3)),
        ],
        compiler_params=pltpu.CompilerParams(vmem_limit_bytes=48 * MIB),
        cost_estimate=pl.CostEstimate(flops=2 * slots * 2 * half * 48 * NT, bytes_accessed=slots * NT * 2 * (48 + half), transcendentals=0),
        name="legendre_sums",
    )(*[pltpu.with_memory_space_constraint(x, pltpu.HBM) for x in (brackets, lev_weight, map_rows, spectral, legendre)])


def unit_circle(product, points, inverse):
    big = 12582912.0
    turn = (product * inverse + big) - big
    x = (product - turn * points) * (math.pi * inverse)
    x2 = x * x
    sine = 0.0
    cosine = 0.0
    for power in (11, 9, 7, 5, 3, 1):
        sine = sine * x2 + (-1) ** (power // 2) / math.factorial(power)
    for power in (12, 10, 8, 6, 4, 2, 0):
        cosine = cosine * x2 + (-1) ** (power // 2) / math.factorial(power)
    sine = sine * x
    twice = sine + sine
    return 1.0 - twice * sine, twice * cosine


def own_points(points_ref, r2):
    wave = lax.axis_index("wave")
    lev = lax.axis_index("lev")
    row = 2 * (wave * lax.axis_size("lev") + lev) + r2
    return points_ref[row % points_ref.shape[0]]


def table_kernel(points_ref, map_ref, hi_ref, lo_ref, sorted_ref):
    r2 = pl.program_id(0)
    kb = pl.program_id(1)
    rows = hi_ref.shape[1]
    points = own_points(points_ref, r2).astype(F32)
    inverse = 1.0 / points

    @pl.when((r2 == 0) & (kb == 0))
    def _():
        waves, slots = sorted_ref.shape
        for wave in range(waves):
            rank, down = ranks_of(waves_of(map_ref, wave, slots))
            whole = jnp.floor((rank + 0.5) * (1.0 / SQ))
            place = (rank - whole * SQ) * (slots // SQ) + whole
            hit = (place == iota((256, 256), 1).astype(F32)) & (rank < slots)
            row = jnp.sum(jnp.where(hit, down, 0.0), axis=0, keepdims=True)
            sorted_ref[wave : wave + 1, :] = row[:, :slots].astype(jnp.int32)

    lane = iota((16, 128), 1).astype(F32)

    def chunk_body(i, carry):
        chunk = pl.multiple_of(i * 16, 16)

        def put(tile, value):
            lanes = slice(tile * 128, tile * 128 + 128)
            hi = value.astype(BF16)
            hi_ref[0, pl.ds(chunk, 16), lanes] = hi
            lo_ref[0, pl.ds(chunk, 16), lanes] = (value - hi.astype(F32)).astype(BF16)

        k = (kb * rows + chunk + iota((16, 128), 0)).astype(F32)
        c, s = unit_circle(2.0 * lane * k, points, inverse)
        c1, s1 = unit_circle(k, points, inverse)
        ct, st = unit_circle(256.0 * k, points, inverse)
        co = c * c1 - s * s1
        so = s * c1 + c * s1
        for t in range(HALF_M // 128):
            if t:
                c, s = c * ct - s * st, s * ct + c * st
                co, so = co * ct - so * st, so * ct + co * st
            put(t, c)
            put(5 + t, s)
            put(10 + t, co)
            put(15 + t, so)
        return carry

    lax.fori_loop(0, rows // 16, chunk_body, 0, unroll=True)


def tables(row_points, map_rows):
    waves = lax.axis_size("wave")
    rows = KPTS // TABLE_STEPS
    table = pltpu.HBM((2, KPTS, 2 * M), BF16)
    table_spec = pl.BlockSpec((1, rows, 2 * M), lambda r, k: (r, k, 0))
    return pl.pallas_call(
        table_kernel,
        out_shape=[table, table, jax.ShapeDtypeStruct((waves, M // waves), jnp.int32)],
        grid=(2, TABLE_STEPS),
        in_specs=[pl.BlockSpec(memory_space=pltpu.SMEM), pl.BlockSpec(memory_space=pltpu.VMEM)],
        out_specs=[table_spec, table_spec, pl.BlockSpec(memory_space=pltpu.VMEM)],
        compiler_params=pltpu.CompilerParams(vmem_limit_bytes=48 * MIB),
        cost_estimate=pl.CostEstimate(flops=2 * KPTS * 2 * M * 12, bytes_accessed=2 * KPTS * 2 * M * 4, transcendentals=0),
        name="fourier_tables",
    )(*[pltpu.with_memory_space_constraint(x, pltpu.HBM) for x in (row_points, map_rows)])


def pick_tables(plev):
    wide = plev * 2 * PART
    out = np.zeros((2, 4, 2 * wide, 2 * wide), np.float32)
    plans = (
        ((0, 1), (0, 1), (0, 1), (0, 1)),
        ((1, -1), (1, 1), (1, -1), (1, 1)),
        ((0, 1), (0, 1), (1, -1), (1, -1)),
        ((1, -1), (1, 1), (0, -1), (0, 1)),
    )
    for r2 in range(2):
        for kind, plan in enumerate(plans):
            for image, (part, sgn) in enumerate(plan):
                for hl in range(2):
                    for p in range(plev):
                        for q in range(FS):
                            src = hl * wide + p * 2 * PART + r2 * PART + q * 2 + part
                            dst = hl * wide + image * plev * FS + p * FS + q
                            out[r2, kind, src, dst] = sgn
    return out.astype(jnp.bfloat16)


def mean_table(plev):
    wide = plev * FS * 4
    out = np.zeros((2 * 4 * plev, 2 * wide), np.float32)
    for quarter in range(4):
        for p in range(plev):
            for part in range(2):
                image_quarter = (quarter + part) % 4
                start = (image_quarter * 2 + part) * plev * FS + p * FS
                out[part * 4 * plev + quarter * plev + p, start : start + FS] = 0.5 / STEPS
    return out.astype(jnp.bfloat16)


def flip_table():
    return np.fliplr(np.eye(KBLK, dtype=np.float32)).astype(jnp.bfloat16)


def split(x):
    hi = x.astype(BF16)
    return hi, (x - hi.astype(F32)).astype(BF16)


def nt_dot(a, b):
    return lax.dot_general(a, b, (((1,), (1,)), ((), ())), preferred_element_type=F32)


def nn_dot(a, b):
    return jnp.dot(a, b, preferred_element_type=F32)


def synth_kernel(points_ref, *refs):
    moved_ref, map_ref, pick_ref, mean_ref, flip_ref, hi_hbm, lo_hbm, out_ref = refs[:8]
    perm_ref, hi_ref, lo_ref, mixed, coef, flat, mirror, line, sems = refs[8:]
    table_copies = []
    for r2 in range(2):
        table_copies.append([])
        for i, (src, dst) in enumerate(((hi_hbm, hi_ref), (lo_hbm, lo_ref))):
            for c in range(TABLE_CUTS):
                rows = pl.ds(c * (KPTS // TABLE_CUTS), KPTS // TABLE_CUTS)
                table_copies[r2].append(pltpu.make_async_copy(src.at[r2, rows], dst.at[r2, rows], sems.at[r2, i, c]))
    for copy in table_copies[0]:
        copy.start()

    slot_waves = jnp.broadcast_to(map_ref[...], (16, M)).astype(jnp.int16)

    def perm_body(i, carry):
        row = pl.multiple_of(i * 16, 16)
        order = row + iota((16, M), 0)
        wanted = jnp.where(row < HALF_M, 2 * order, 2 * (order - HALF_M) + 1).astype(jnp.int16)
        perm_ref[pl.ds(row, 16), :] = jnp.where(slot_waves == wanted, 1.0, 0.0).astype(BF16)
        return carry

    lax.fori_loop(0, M // 16, perm_body, 0, unroll=4)
    waves, plev, _, _ = moved_ref.shape
    wide = plev * 2 * PART
    part_rows = M // SQ
    for base in range(0, plev * 2, 8):
        cur = []
        for g in range(base, base + 8):
            sub = moved_ref.shape[2] // 2
            pieces = [moved_ref[w, g // 2, (g % 2) * sub : (g % 2 + 1) * sub, :] for w in range(waves)]
            cur.append(jnp.concatenate(pieces, axis=0))
        group = iota((part_rows, 128), 1) // PART
        for bit in (1, 2, 4):
            unset = (group & bit) == 0
            nxt = list(cur)
            for g in range(8):
                if g & bit == 0:
                    a, b = cur[g], cur[g + bit]
                    nxt[g] = jnp.where(unset, a, pltpu.roll(b, bit * PART, 1))
                    nxt[g + bit] = jnp.where(unset, pltpu.roll(a, 128 - bit * PART, 1), b)
            cur = nxt
        for sq in range(SQ):
            hi, lo = split(cur[sq])
            lane = base * PART
            mixed[sq * part_rows : (sq + 1) * part_rows, lane : lane + 128] = hi
            mixed[sq * part_rows : (sq + 1) * part_rows, wide + lane : wide + lane + 128] = lo

    lane_row = (iota((1, 2 * wide), 1) // PART) % 2
    limit0 = (own_points(points_ref, 0) - 1) // 2
    limit1 = (own_points(points_ref, 1) - 1) // 2
    limit = jnp.where(lane_row == 0, limit0, limit1)
    place = iota((HALF_M, 1), 0)
    turned = (iota((1, 2 * wide), 1) % wide) // (plev * FS) >= 2
    flip_sign = jnp.where(turned & (place % 2 == 1), -1.0, 1.0).astype(BF16)
    for odd in range(2):
        ordered = nn_dot(perm_ref[odd * HALF_M : (odd + 1) * HALF_M, :], mixed[...])
        wave = 2 * place + odd
        factor = jnp.where(wave <= limit, jnp.where(wave == 0, 1.0, 2.0), 0.0)
        ordered = (ordered * factor).astype(BF16)
        for row in range(2):
            for part in range(2):
                picked = nn_dot(ordered, pick_ref[row, odd * 2 + part]).astype(BF16)
                coef[row, odd, part * HALF_M : (part + 1) * HALF_M, :] = picked * flip_sign
    flat[...] = jnp.zeros_like(flat)
    mirror[...] = jnp.zeros_like(mirror)

    row_sums = []
    for r2 in range(2):
        for copy in table_copies[r2]:
            copy.wait()
        for copy in table_copies[1] if r2 == 0 else []:
            copy.start()

        def contraction(odd):
            lanes = slice(odd * M, (odd + 1) * M)
            both = nn_dot(hi_ref[r2, :, lanes], coef[r2, odd])
            rest = nn_dot(lo_ref[r2, :, lanes], coef[r2, odd, :, :wide])
            return both[:, :wide] + (both[:, wide:] + rest)

        row_sums.append((contraction(0), contraction(1)))

    for r2 in range(2):
        even_sum, odd_sum = row_sums[r2]
        plus = even_sum + odd_sum
        minus = even_sum - odd_sum
        squares = jnp.concatenate([plus * plus, minus * minus], axis=1)
        sq_hi, sq_lo = split(squares)
        energy = nt_dot(mean_ref[...], sq_hi) + nt_dot(mean_ref[...], sq_lo)
        rows = 4 * plev
        flat[:, :KPTS] = energy
        en_hi, en_lo = split(flat[rows:, :KPAD])
        for t in range(KPAD // KBLK):
            lanes = slice(t * KBLK, (t + 1) * KBLK)
            back = KPAD - (t + 1) * KBLK
            mirror[:, back : back + KBLK] = nn_dot(en_hi[:, lanes], flip_ref[...]) + nn_dot(en_lo[:, lanes], flip_ref[...])

        quarter = own_points(points_ref, r2) // 4
        lane = iota((rows, BUF), 1)
        shift = (quarter + (BUF - (KPAD - 1))) % BUF
        flat[:rows, :] = jnp.where(lane <= quarter // 2, flat[:rows, :], pltpu.roll(mirror[...], shift, 1))
        line[...] = jnp.zeros_like(line)
        lane = iota((plev, BUF), 1)
        for b in range(4):
            start = quarter * b
            inner = start % 128
            base = pl.multiple_of(start - inner, 128)
            piece = pltpu.roll(flat[b * plev : (b + 1) * plev, :], inner, 1)
            old = line[:, pl.ds(base, BUF)]
            line[:, pl.ds(base, BUF)] = jnp.where((lane >= inner) & (lane < inner + quarter), piece, old)
        out_ref[:, pl.ds(r2, 1), :] = line[:, :ROWPAD].reshape(plev, 1, ROWPAD)


def synthesis(moved, slot_map, table_hi, table_lo, row_points):
    plev = moved.shape[1]
    wide = plev * 2 * PART
    vmem = pl.BlockSpec(memory_space=pltpu.VMEM)
    return pl.pallas_call(
        synth_kernel,
        out_shape=jax.ShapeDtypeStruct((plev, 2, ROWPAD), F32),
        in_specs=[pl.BlockSpec(memory_space=pltpu.SMEM)] + [vmem] * 5 + [pl.BlockSpec(memory_space=pltpu.HBM)] * 2,
        out_specs=vmem,
        scratch_shapes=[
            pltpu.VMEM((M, M), BF16),
            pltpu.VMEM((2, KPTS, 2 * M), BF16),
            pltpu.VMEM((2, KPTS, 2 * M), BF16),
            pltpu.VMEM((M, 2 * wide), BF16),
            pltpu.VMEM((2, 2, M, 2 * wide), BF16),
            pltpu.VMEM((8 * plev, BUF), F32),
            pltpu.VMEM((4 * plev, BUF), F32),
            pltpu.VMEM((plev, 3 * 1280 + BUF), F32),
            pltpu.SemaphoreType.DMA((2, 2, TABLE_CUTS)),
        ],
        compiler_params=pltpu.CompilerParams(vmem_limit_bytes=44 * MIB),
        cost_estimate=pl.CostEstimate(flops=2 * 2 * KPTS * 2 * M * 384, bytes_accessed=2 * KPTS * 2 * M * 4 + M * M * 2, transcendentals=0),
        name="synthesis",
    )(
        pltpu.with_memory_space_constraint(row_points, pltpu.HBM),
        pltpu.with_memory_space_constraint(moved, pltpu.VMEM), slot_map,
        pick_tables(plev), mean_table(plev), flip_table(),
        *[pltpu.with_memory_space_constraint(x, pltpu.HBM) for x in (table_hi, table_lo)],
    )


def join_kernel(*refs):
    parts = (len(refs) - 1) // 2
    at = 0
    for own_ref, other_ref in zip(refs[:parts], refs[parts:-1]):
        rows = own_ref.shape[1]
        refs[-1][:, at : at + rows, :] = own_ref[...] + other_ref[...]
        at += rows


def join(owns, others):
    rows = sum(x.shape[1] for x in owns)
    vmem = pl.BlockSpec(memory_space=pltpu.VMEM)
    return pl.pallas_call(
        join_kernel,
        out_shape=jax.ShapeDtypeStruct((owns[0].shape[0], rows, SQ * PART), F32),
        in_specs=[vmem] * (2 * len(owns)),
        out_specs=vmem,
        compiler_params=pltpu.CompilerParams(vmem_limit_bytes=32 * MIB),
        name="join",
    )(*[pltpu.with_memory_space_constraint(x, pltpu.VMEM) for x in owns + others])


def local(spectral, legendre, wave_map, row_points, brackets, lev_weight, climatology):
    slots = spectral.shape[0]
    half = legendre.shape[1]
    groups = slots // SQ
    wave_count = lax.axis_size("wave")
    lev_count = lax.axis_size("lev")
    rows_dev = 2 * half // (wave_count * lev_count)
    pairs = [(d, d - 1) for d in range(1, lev_count)]
    map_rows = wave_map.reshape(M // 128, 128)
    own, prev, between = legendre_sums(spectral, legendre, map_rows, brackets, lev_weight)
    sent = lax.cond(
        between[0] > 0,
        lambda mine, theirs: join([mine], [lax.ppermute(theirs, "lev", pairs)]),
        lambda mine, theirs: join([mine], [lax.ppermute(theirs, "lev", pairs[::2])]),
        own,
        prev,
    )
    moved = lax.all_to_all(sent, ("wave", "lev"), split_axis=0, concat_axis=0, tiled=True)
    moved = moved.reshape(wave_count, lev_count, rows_dev * groups, SQ * PART)
    table_points, _ = lax.optimization_barrier((row_points, sent))
    table_hi, table_lo, sorted_map = tables(table_points, map_rows)
    slot_map = jnp.transpose(sorted_map.reshape(wave_count, SQ, groups), (1, 0, 2)).reshape(1, M)
    energy = synthesis(moved, slot_map, table_hi, table_lo, row_points)
    result = lax.all_to_all(energy, "lev", split_axis=0, concat_axis=0, tiled=True)
    result = result.reshape(1, rows_dev * lev_count, ROWPAD)
    points_all = jnp.concatenate([row_points, row_points])
    band_rows = rows_dev * lev_count
    out_points = lax.dynamic_slice_in_dim(points_all, lax.axis_index("wave") * band_rows, band_rows, 0)
    places = jnp.arange(ROWPAD, dtype=jnp.int32)
    inside = places[None, None, :] < out_points[None, :, None]
    return jnp.where(inside, result - climatology, 0.0)


def solution(mesh):
    placed = (
        P("wave", "lev", None),
        P("wave", None, None),
        P(),
        P(),
        P(),
        P(),
        P("lev", "wave", None),
    )
    return jax.shard_map(
        local, mesh=mesh, in_specs=placed, out_specs=P("lev", "wave", None), check_vma=False
    )
```

```python
import functools
import math

import jax
import jax.numpy as jnp
import numpy as np
from jax import lax
from jax.experimental import pallas as pl
from jax.experimental.pallas import tpu as pltpu
from jax.sharding import PartitionSpec as P

M = 1280
NT = 1280
LEV_DEV = 4
STEPS = 4
FIELDS = 2
ROWPAD = 5248

FS = FIELDS * STEPS
PART = 2 * FS
SQ = 8
STEP = 16
CHUNK = 256
DEPTH = 3
HALF_M = M // 2
KPTS = 672
KPAD = 768
KBLK = 256
TABLE_STEPS = 7
TABLE_CUTS = 3
BUF = 1536
MIB = 1024 * 1024
F32 = jnp.float32
BF16 = jnp.bfloat16
FP8 = jnp.float8_e4m3fn
REST_SCALE = 256.0


def iota(shape, dim):
    return lax.broadcasted_iota(jnp.int32, shape, dim)


def waves_of(map_ref, wave, slots):
    start = wave * slots
    row = start // 128
    last = map_ref.shape[0] - 1
    pair = jnp.concatenate([map_ref[pl.ds(row, 1), :], map_ref[pl.ds(jnp.minimum(row + 1, last), 1), :]], axis=1)
    pair = jnp.broadcast_to(pair, (8, 256)).astype(F32)
    turned = pltpu.roll(pair, (256 - start % 128) % 256, 1)
    return jnp.where(iota((8, 256), 1) < slots, turned, 4096.0)[:1]


def ranks_of(waves):
    across = jnp.broadcast_to(waves, (256, 256))
    down = across.T
    rank = jnp.sum(jnp.where(across < down, 1.0, 0.0), axis=1, keepdims=True)
    return rank, down


def legendre_kernel(
    brackets, weight_ref, map_ref, spec_hbm, leg_hbm, own_ref, prev_ref, between_ref,
    pair_buf, first_buf, leg_buf, own_rows, prev_rows, order_vmem, order, order_sem, sems,
):
    slots, half, _ = leg_hbm.shape
    groups = slots // SQ
    steps = slots // STEP
    wave = lax.axis_index("wave")
    lev = lax.axis_index("lev")
    lower = brackets[lev] - lev * LEV_DEV
    has_upper = lower < LEV_DEV - 1
    w = weight_ref[lev]
    low_w = jnp.where(has_upper, w, 0.0)
    upper_w = jnp.where(has_upper, 1.0 - w, w)
    pair_row = jnp.minimum(lower, LEV_DEV - 2) * PART
    before = jnp.maximum(lev - 1, 0)
    crosses = (lev > 0) & (brackets[before] == lev * LEV_DEV - 1)
    first_w = jnp.where(crosses, 1.0 - weight_ref[before], 0.0)
    degree = iota((16, NT), 1).astype(jnp.int16)
    sign = (1 - 2 * (iota((16, NT), 1) % 2)).astype(F32).astype(BF16)
    lane_group = iota((1, 192), 1) % 64 // PART
    left = iota((1, SQ * PART), 1) < 64
    south = iota((2 * half, 1), 0) >= half

    rank, down = ranks_of(waves_of(map_ref, wave, slots))
    hit = rank == iota((256, 256), 1).astype(F32)
    slot_at = jnp.sum(jnp.where(hit, iota((256, 256), 0).astype(F32), 0.0), axis=0, keepdims=True)
    wave_at = jnp.sum(jnp.where(hit, down, 0.0), axis=0, keepdims=True)
    order_vmem[0:1, :] = slot_at.astype(jnp.int32)
    order_vmem[1:2, :] = wave_at.astype(jnp.int32)
    to_smem = pltpu.make_async_copy(order_vmem, order, order_sem)
    to_smem.start()
    to_smem.wait()

    def buffers(slot, c):
        lanes = pl.ds(c * CHUNK, NT - c * CHUNK)
        return [
            (leg_hbm.at[:, :, lanes], leg_buf.at[slot, :, :, lanes], sems.at[slot, 0]),
            (spec_hbm.at[:, pl.ds(pl.multiple_of(pair_row, PART), 2 * PART), lanes], pair_buf.at[slot, :, :, lanes], sems.at[slot, 1]),
            (spec_hbm.at[:, pl.ds(0, PART), lanes], first_buf.at[slot, :, :, lanes], sems.at[slot, 2]),
        ]

    def fetch(step):
        chunk = order[1, step * STEP] // CHUNK
        for c in range(NT // CHUNK):

            @pl.when(chunk == c)
            def _():
                for i in range(STEP):
                    at = order[0, step * STEP + i]
                    for src, dst, sem in buffers(step % DEPTH, c):
                        pltpu.make_async_copy(src.at[at], dst.at[i], sem).start()

    for step in range(DEPTH - 1):
        fetch(step)
    between = jnp.int32(0)
    for p in range(1, brackets.shape[0] - 1, 2):
        between = between | (brackets[p] == (p + 1) * LEV_DEV - 1).astype(jnp.int32)
    between_ref[0] = between

    def multiply(step, c):
        slot = step % DEPTH
        lanes = slice(c * CHUNK, NT)
        for src, dst, sem in buffers(slot, c):
            pltpu.make_async_copy(src.at[pl.ds(0, STEP)], dst, sem).wait()
        for b in range(STEP // SQ):
            owns, firsts = [], []
            for quad in range(2):
                values, factors, columns = [], [], [[], [], []]
                for i in range(b * SQ + 4 * quad, b * SQ + 4 * quad + 4):
                    m = order[1, step * STEP + i]
                    kept = degree[:, lanes] >= m.astype(jnp.int16)
                    plain = [jnp.where(kept, leg_buf[slot, i, r : r + 16, lanes], 0) for r in range(0, half, 16)]
                    values += plain + [x * sign[:, lanes] for x in plain]
                    factors.append(jnp.where(south, (1 - 2 * (m % 2)).astype(F32), 1.0))
                    columns[quad].append(pair_buf[slot, i, :PART, lanes])
                    columns[1 - quad].append(pair_buf[slot, i, PART:, lanes])
                    columns[2].append(first_buf[slot, i, :, lanes])
                sums = nt_dot(jnp.concatenate(values, axis=0), jnp.concatenate(columns[0] + columns[1] + columns[2], axis=0))
                kept_sums = sums[: 2 * half] * factors[0]
                for a in range(1, 4):
                    block = sums[2 * half * a : 2 * half * (a + 1)] * factors[a]
                    kept_sums = jnp.where(lane_group == a, block, kept_sums)
                both = kept_sums[:, :128]
                owns.append(both * low_w + pltpu.roll(both, 64, 1) * upper_w)
                firsts.append(jnp.concatenate([kept_sums[:, 128:]] * 2, axis=1))
            at = pl.multiple_of((step * (STEP // SQ) + b) * 2 * half, 2 * half)
            own_rows[pl.ds(at, 2 * half), :] = jnp.where(left, owns[0], owns[1])
            prev_rows[pl.ds(at, 2 * half), :] = jnp.where(left, firsts[0], firsts[1]) * first_w

    def step_body(step, carry):
        @pl.when(step + DEPTH - 1 < steps)
        def _():
            fetch(step + DEPTH - 1)

        chunk = order[1, step * STEP] // CHUNK
        for c in range(NT // CHUNK):
            pl.when(chunk == c)(functools.partial(multiply, step, c))
        return carry

    lax.fori_loop(0, steps, step_body, 0)
    rows = 2 * half
    for rows_ref, ref in ((own_rows, own_ref), (prev_rows, prev_ref)):
        rows_dev = ref.shape[1] // groups
        for r in range(rows):
            at = (r % rows_dev) * groups
            ref[r // rows_dev, at : at + groups, :] = rows_ref[pl.ds(r, groups, stride=rows), :]


def legendre_sums(spectral, legendre, map_rows, brackets, lev_weight):
    slots = spectral.shape[0]
    half = legendre.shape[1]
    groups = slots // SQ
    devices = lax.axis_size("wave") * lax.axis_size("lev")
    out = pltpu.VMEM((devices, 2 * half // devices * groups, SQ * PART), F32)
    smem = pl.BlockSpec(memory_space=pltpu.SMEM)
    vmem = pl.BlockSpec(memory_space=pltpu.VMEM)
    hbm = pl.BlockSpec(memory_space=pltpu.HBM)
    return pl.pallas_call(
        legendre_kernel,
        out_shape=[out, out, jax.ShapeDtypeStruct((1,), jnp.int32)],
        in_specs=[smem, smem, vmem, hbm, hbm],
        out_specs=[vmem, vmem, smem],
        scratch_shapes=[
            pltpu.VMEM((DEPTH, STEP, 2 * PART, NT), BF16),
            pltpu.VMEM((DEPTH, STEP, PART, NT), BF16),
            pltpu.VMEM((DEPTH, STEP, half, NT), BF16),
            pltpu.VMEM((groups * 2 * half, SQ * PART), F32),
            pltpu.VMEM((groups * 2 * half, SQ * PART), F32),
            pltpu.VMEM((2, 256), jnp.int32),
            pltpu.SMEM((2, 256), jnp.int32),
            pltpu.SemaphoreType.DMA,
            pltpu.SemaphoreType.DMA((DEPTH, 3)),
        ],
        compiler_params=pltpu.CompilerParams(vmem_limit_bytes=48 * MIB),
        cost_estimate=pl.CostEstimate(flops=2 * slots * 2 * half * 48 * NT, bytes_accessed=slots * NT * 2 * (48 + half), transcendentals=0),
        name="legendre_sums",
    )(*[pltpu.with_memory_space_constraint(x, pltpu.HBM) for x in (brackets, lev_weight, map_rows, spectral, legendre)])


def unit_circle(product, points, inverse):
    big = 12582912.0
    turn = (product * inverse + big) - big
    x = (product - turn * points) * (math.pi * inverse)
    x2 = x * x
    sine = 0.0
    cosine = 0.0
    for power in (11, 9, 7, 5, 3, 1):
        sine = sine * x2 + (-1) ** (power // 2) / math.factorial(power)
    for power in (12, 10, 8, 6, 4, 2, 0):
        cosine = cosine * x2 + (-1) ** (power // 2) / math.factorial(power)
    sine = sine * x
    twice = sine + sine
    return 1.0 - twice * sine, twice * cosine


def own_points(points_ref, r2):
    wave = lax.axis_index("wave")
    lev = lax.axis_index("lev")
    row = 2 * (wave * lax.axis_size("lev") + lev) + r2
    return points_ref[row % points_ref.shape[0]]


def table_kernel(points_ref, map_ref, hi_ref, lo_ref, sorted_ref):
    r2 = pl.program_id(0)
    kb = pl.program_id(1)
    rows = hi_ref.shape[1]
    points = own_points(points_ref, r2).astype(F32)
    inverse = 1.0 / points

    @pl.when((r2 == 0) & (kb == 0))
    def _():
        waves, slots = sorted_ref.shape
        for wave in range(waves):
            rank, down = ranks_of(waves_of(map_ref, wave, slots))
            whole = jnp.floor((rank + 0.5) * (1.0 / SQ))
            place = (rank - whole * SQ) * (slots // SQ) + whole
            hit = (place == iota((256, 256), 1).astype(F32)) & (rank < slots)
            row = jnp.sum(jnp.where(hit, down, 0.0), axis=0, keepdims=True)
            sorted_ref[wave : wave + 1, :] = row[:, :slots].astype(jnp.int32)

    lane = iota((32, 128), 1).astype(F32)

    def chunk_body(i, carry):
        chunk = pl.multiple_of(i * 32, 32)

        def put(tile, value):
            lanes = slice(tile * 128, tile * 128 + 128)
            hi = value.astype(BF16)
            hi_ref[0, pl.ds(chunk, 32), lanes] = hi
            lo_ref[0, pl.ds(chunk, 32), lanes] = ((value - hi.astype(F32)) * REST_SCALE).astype(FP8)

        k = (kb * rows + chunk + iota((32, 128), 0)).astype(F32)
        c, s = unit_circle(2.0 * lane * k, points, inverse)
        c1, s1 = unit_circle(k, points, inverse)
        ct, st = unit_circle(256.0 * k, points, inverse)
        co = c * c1 - s * s1
        so = s * c1 + c * s1
        for t in range(HALF_M // 128):
            if t:
                c, s = c * ct - s * st, s * ct + c * st
                co, so = co * ct - so * st, so * ct + co * st
            put(t, c)
            put(5 + t, s)
            put(10 + t, co)
            put(15 + t, so)
        return carry

    lax.fori_loop(0, rows // 32, chunk_body, 0, unroll=True)


def tables(row_points, map_rows):
    waves = lax.axis_size("wave")
    rows = KPTS // TABLE_STEPS
    table = pltpu.HBM((2, KPTS, 2 * M), BF16)
    table_spec = pl.BlockSpec((1, rows, 2 * M), lambda r, k: (r, k, 0))
    return pl.pallas_call(
        table_kernel,
        out_shape=[table, pltpu.HBM((2, KPTS, 2 * M), FP8), jax.ShapeDtypeStruct((waves, M // waves), jnp.int32)],
        grid=(2, TABLE_STEPS),
        in_specs=[pl.BlockSpec(memory_space=pltpu.SMEM), pl.BlockSpec(memory_space=pltpu.VMEM)],
        out_specs=[table_spec, table_spec, pl.BlockSpec(memory_space=pltpu.VMEM)],
        compiler_params=pltpu.CompilerParams(vmem_limit_bytes=48 * MIB),
        cost_estimate=pl.CostEstimate(flops=2 * KPTS * 2 * M * 12, bytes_accessed=2 * KPTS * 2 * M * 4, transcendentals=0),
        name="fourier_tables",
    )(*[pltpu.with_memory_space_constraint(x, pltpu.HBM) for x in (row_points, map_rows)])


def pick_tables(plev):
    wide = plev * 2 * PART
    out = np.zeros((2, 4, 2 * wide, 2 * wide), np.float32)
    plans = (
        ((0, 1), (0, 1), (0, 1), (0, 1)),
        ((1, -1), (1, 1), (1, -1), (1, 1)),
        ((0, 1), (0, 1), (1, -1), (1, -1)),
        ((1, -1), (1, 1), (0, -1), (0, 1)),
    )
    for r2 in range(2):
        for kind, plan in enumerate(plans):
            for image, (part, sgn) in enumerate(plan):
                for hl in range(2):
                    for p in range(plev):
                        for q in range(FS):
                            src = hl * wide + p * 2 * PART + r2 * PART + q * 2 + part
                            dst = hl * wide + image * plev * FS + p * FS + q
                            out[r2, kind, src, dst] = sgn
    return out.astype(jnp.bfloat16)


def mean_table(plev):
    wide = plev * FS * 4
    out = np.zeros((2 * 4 * plev, 2 * wide), np.float32)
    for quarter in range(4):
        for p in range(plev):
            for part in range(2):
                image_quarter = (quarter + part) % 4
                start = (image_quarter * 2 + part) * plev * FS + p * FS
                out[part * 4 * plev + quarter * plev + p, start : start + FS] = 0.5 / STEPS
    return out.astype(jnp.bfloat16)


def flip_table():
    return np.fliplr(np.eye(KBLK, dtype=np.float32)).astype(jnp.bfloat16)


def split(x):
    hi = x.astype(BF16)
    return hi, (x - hi.astype(F32)).astype(BF16)


def nt_dot(a, b):
    return lax.dot_general(a, b, (((1,), (1,)), ((), ())), preferred_element_type=F32)


def nn_dot(a, b):
    return jnp.dot(a, b, preferred_element_type=F32)


def synth_kernel(points_ref, *refs):
    moved_ref, map_ref, pick_ref, mean_ref, flip_ref, hi_hbm, lo_hbm, out_ref = refs[:8]
    perm_ref, hi_ref, lo_ref, mixed, coef, coef8, flat, mirror, line, sems = refs[8:]
    table_copies = []
    for r2 in range(2):
        table_copies.append([])
        for i, (src, dst) in enumerate(((hi_hbm, hi_ref), (lo_hbm, lo_ref))):
            for c in range(TABLE_CUTS):
                rows = pl.ds(c * (KPTS // TABLE_CUTS), KPTS // TABLE_CUTS)
                table_copies[r2].append(pltpu.make_async_copy(src.at[r2, rows], dst.at[r2, rows], sems.at[r2, i, c]))
    for copy in table_copies[0] + table_copies[1]:
        copy.start()

    slot_waves = jnp.broadcast_to(map_ref[...], (16, M)).astype(jnp.int16)

    def perm_body(i, carry):
        row = pl.multiple_of(i * 16, 16)
        order = row + iota((16, M), 0)
        wanted = jnp.where(row < HALF_M, 2 * order, 2 * (order - HALF_M) + 1).astype(jnp.int16)
        perm_ref[pl.ds(row, 16), :] = jnp.where(slot_waves == wanted, 1.0, 0.0).astype(BF16)
        return carry

    lax.fori_loop(0, M // 16, perm_body, 0, unroll=4)
    waves, plev, _, _ = moved_ref.shape
    wide = plev * 2 * PART
    part_rows = M // SQ
    for base in range(0, plev * 2, 8):
        cur = []
        for g in range(base, base + 8):
            sub = moved_ref.shape[2] // 2
            pieces = [moved_ref[w, g // 2, (g % 2) * sub : (g % 2 + 1) * sub, :] for w in range(waves)]
            cur.append(jnp.concatenate(pieces, axis=0))
        group = iota((part_rows, 128), 1) // PART
        for bit in (1, 2, 4):
            unset = (group & bit) == 0
            nxt = list(cur)
            for g in range(8):
                if g & bit == 0:
                    a, b = cur[g], cur[g + bit]
                    nxt[g] = jnp.where(unset, a, pltpu.roll(b, bit * PART, 1))
                    nxt[g + bit] = jnp.where(unset, pltpu.roll(a, 128 - bit * PART, 1), b)
            cur = nxt
        for sq in range(SQ):
            hi, lo = split(cur[sq])
            lane = base * PART
            mixed[sq * part_rows : (sq + 1) * part_rows, lane : lane + 128] = hi
            mixed[sq * part_rows : (sq + 1) * part_rows, wide + lane : wide + lane + 128] = lo

    lane_row = (iota((1, 2 * wide), 1) // PART) % 2
    limit0 = (own_points(points_ref, 0) - 1) // 2
    limit1 = (own_points(points_ref, 1) - 1) // 2
    limit = jnp.where(lane_row == 0, limit0, limit1)
    place = iota((HALF_M, 1), 0)
    turned = (iota((1, 2 * wide), 1) % wide) // (plev * FS) >= 2
    flip_sign = jnp.where(turned & (place % 2 == 1), -1.0, 1.0).astype(BF16)
    for odd in range(2):
        ordered = nn_dot(perm_ref[odd * HALF_M : (odd + 1) * HALF_M, :], mixed[...])
        wave = 2 * place + odd
        factor = jnp.where(wave <= limit, jnp.where(wave == 0, 1.0, 2.0), 0.0)
        ordered = (ordered * factor).astype(BF16)
        for row in range(2):
            for part in range(2):
                picked = nn_dot(ordered, pick_ref[row, odd * 2 + part]).astype(BF16)
                picked = picked * flip_sign
                coef[row, odd, part * HALF_M : (part + 1) * HALF_M, :] = picked
                coef8[row, odd, part * HALF_M : (part + 1) * HALF_M, :] = picked[:, :wide].astype(F32).astype(FP8)
    flat[...] = jnp.zeros_like(flat)
    mirror[...] = jnp.zeros_like(mirror)

    row_sums = []
    for r2 in range(2):
        for copy in table_copies[r2]:
            copy.wait()

        def contraction(odd):
            lanes = slice(odd * M, (odd + 1) * M)
            both = nn_dot(hi_ref[r2, :, lanes], coef[r2, odd])
            rest = nn_dot(lo_ref[r2, :, lanes], coef8[r2, odd])
            return both[:, :wide] + (both[:, wide:] + rest * (1.0 / REST_SCALE))

        row_sums.append((contraction(0), contraction(1)))

    for r2 in range(2):
        even_sum, odd_sum = row_sums[r2]
        plus = even_sum + odd_sum
        minus = even_sum - odd_sum
        squares = jnp.concatenate([plus * plus, minus * minus], axis=1)
        sq_hi, sq_lo = split(squares)
        energy = nt_dot(mean_ref[...], sq_hi) + nt_dot(mean_ref[...], sq_lo)
        rows = 4 * plev
        flat[:, :KPTS] = energy
        en_hi, en_lo = split(flat[rows:, :KPAD])
        for t in range(KPAD // KBLK):
            lanes = slice(t * KBLK, (t + 1) * KBLK)
            back = KPAD - (t + 1) * KBLK
            mirror[:, back : back + KBLK] = nn_dot(en_hi[:, lanes], flip_ref[...]) + nn_dot(en_lo[:, lanes], flip_ref[...])

        quarter = own_points(points_ref, r2) // 4
        lane = iota((rows, BUF), 1)
        shift = (quarter + (BUF - (KPAD - 1))) % BUF
        flat[:rows, :] = jnp.where(lane <= quarter // 2, flat[:rows, :], pltpu.roll(mirror[...], shift, 1))
        line[...] = jnp.zeros_like(line)
        lane = iota((plev, BUF), 1)
        for b in range(4):
            start = quarter * b
            inner = start % 128
            base = pl.multiple_of(start - inner, 128)
            piece = pltpu.roll(flat[b * plev : (b + 1) * plev, :], inner, 1)
            old = line[:, pl.ds(base, BUF)]
            line[:, pl.ds(base, BUF)] = jnp.where((lane >= inner) & (lane < inner + quarter), piece, old)
        out_ref[:, pl.ds(r2, 1), :] = line[:, :ROWPAD].reshape(plev, 1, ROWPAD)


def synthesis(moved, slot_map, table_hi, table_lo, row_points):
    plev = moved.shape[1]
    wide = plev * 2 * PART
    vmem = pl.BlockSpec(memory_space=pltpu.VMEM)
    return pl.pallas_call(
        synth_kernel,
        out_shape=jax.ShapeDtypeStruct((plev, 2, ROWPAD), F32),
        in_specs=[pl.BlockSpec(memory_space=pltpu.SMEM)] + [vmem] * 5 + [pl.BlockSpec(memory_space=pltpu.HBM)] * 2,
        out_specs=vmem,
        scratch_shapes=[
            pltpu.VMEM((M, M), BF16),
            pltpu.VMEM((2, KPTS, 2 * M), BF16),
            pltpu.VMEM((2, KPTS, 2 * M), FP8),
            pltpu.VMEM((M, 2 * wide), BF16),
            pltpu.VMEM((2, 2, M, 2 * wide), BF16),
            pltpu.VMEM((2, 2, M, wide), FP8),
            pltpu.VMEM((8 * plev, BUF), F32),
            pltpu.VMEM((4 * plev, BUF), F32),
            pltpu.VMEM((plev, 3 * 1280 + BUF), F32),
            pltpu.SemaphoreType.DMA((2, 2, TABLE_CUTS)),
        ],
        compiler_params=pltpu.CompilerParams(vmem_limit_bytes=44 * MIB),
        cost_estimate=pl.CostEstimate(flops=2 * 2 * KPTS * 2 * M * 384, bytes_accessed=2 * KPTS * 2 * M * 4 + M * M * 2, transcendentals=0),
        name="synthesis",
    )(
        pltpu.with_memory_space_constraint(row_points, pltpu.HBM),
        pltpu.with_memory_space_constraint(moved, pltpu.VMEM), slot_map,
        pick_tables(plev), mean_table(plev), flip_table(),
        *[pltpu.with_memory_space_constraint(x, pltpu.HBM) for x in (table_hi, table_lo)],
    )


def join_kernel(*refs):
    parts = (len(refs) - 1) // 2
    at = 0
    for own_ref, other_ref in zip(refs[:parts], refs[parts:-1]):
        rows = own_ref.shape[1]
        refs[-1][:, at : at + rows, :] = own_ref[...] + other_ref[...]
        at += rows


def join(owns, others):
    rows = sum(x.shape[1] for x in owns)
    vmem = pl.BlockSpec(memory_space=pltpu.VMEM)
    return pl.pallas_call(
        join_kernel,
        out_shape=jax.ShapeDtypeStruct((owns[0].shape[0], rows, SQ * PART), F32),
        in_specs=[vmem] * (2 * len(owns)),
        out_specs=vmem,
        compiler_params=pltpu.CompilerParams(vmem_limit_bytes=32 * MIB),
        name="join",
    )(*[pltpu.with_memory_space_constraint(x, pltpu.VMEM) for x in owns + others])


def local(spectral, legendre, wave_map, row_points, brackets, lev_weight, climatology):
    slots = spectral.shape[0]
    half = legendre.shape[1]
    groups = slots // SQ
    wave_count = lax.axis_size("wave")
    lev_count = lax.axis_size("lev")
    rows_dev = 2 * half // (wave_count * lev_count)
    pairs = [(d, d - 1) for d in range(1, lev_count)]
    map_rows = wave_map.reshape(M // 128, 128)
    own, prev, between = legendre_sums(spectral, legendre, map_rows, brackets, lev_weight)
    sent = lax.cond(
        between[0] > 0,
        lambda mine, theirs: join([mine], [lax.ppermute(theirs, "lev", pairs)]),
        lambda mine, theirs: join([mine], [lax.ppermute(theirs, "lev", pairs[::2])]),
        own,
        prev,
    )
    moved = lax.all_to_all(sent, ("wave", "lev"), split_axis=0, concat_axis=0, tiled=True)
    moved = moved.reshape(wave_count, lev_count, rows_dev * groups, SQ * PART)
    table_points, _ = lax.optimization_barrier((row_points, sent))
    table_hi, table_lo, sorted_map = tables(table_points, map_rows)
    slot_map = jnp.transpose(sorted_map.reshape(wave_count, SQ, groups), (1, 0, 2)).reshape(1, M)
    energy = synthesis(moved, slot_map, table_hi, table_lo, row_points)
    result = lax.all_to_all(energy, "lev", split_axis=0, concat_axis=0, tiled=True)
    result = result.reshape(1, rows_dev * lev_count, ROWPAD)
    points_all = jnp.concatenate([row_points, row_points])
    band_rows = rows_dev * lev_count
    out_points = lax.dynamic_slice_in_dim(points_all, lax.axis_index("wave") * band_rows, band_rows, 0)
    places = jnp.arange(ROWPAD, dtype=jnp.int32)
    inside = places[None, None, :] < out_points[None, :, None]
    return jnp.where(inside, result - climatology, 0.0)


def solution(mesh):
    placed = (
        P("wave", "lev", None),
        P("wave", None, None),
        P(),
        P(),
        P(),
        P(),
        P("lev", "wave", None),
    )
    return jax.shard_map(
        local, mesh=mesh, in_specs=placed, out_specs=P("lev", "wave", None), check_vma=False
    )
```

```python
import functools
import math

import jax
import jax.numpy as jnp
import numpy as np
from jax import lax
from jax.experimental import pallas as pl
from jax.experimental.pallas import tpu as pltpu
from jax.sharding import PartitionSpec as P

M = 1280
NT = 1280
LEV_DEV = 4
STEPS = 4
FIELDS = 2
ROWPAD = 5248

FS = FIELDS * STEPS
PART = 2 * FS
SQ = 8
STEP = 16
CHUNK = 256
DEPTH = 3
HALF_M = M // 2
KPTS = 672
KPAD = 768
KBLK = 256
TABLE_STEPS = 7
TABLE_CUTS = 3
BUF = 1536
MIB = 1024 * 1024
F32 = jnp.float32
BF16 = jnp.bfloat16
FP8 = jnp.float8_e4m3fn
REST_SCALE = 256.0


def iota(shape, dim):
    return lax.broadcasted_iota(jnp.int32, shape, dim)


def waves_of(map_ref, wave, slots):
    start = wave * slots
    row = start // 128
    last = map_ref.shape[0] - 1
    pair = jnp.concatenate([map_ref[pl.ds(row, 1), :], map_ref[pl.ds(jnp.minimum(row + 1, last), 1), :]], axis=1)
    pair = jnp.broadcast_to(pair, (8, 256)).astype(F32)
    turned = pltpu.roll(pair, (256 - start % 128) % 256, 1)
    return jnp.where(iota((8, 256), 1) < slots, turned, 4096.0)[:1]


def ranks_of(waves):
    across = jnp.broadcast_to(waves, (256, 256))
    down = across.T
    rank = jnp.sum(jnp.where(across < down, 1.0, 0.0), axis=1, keepdims=True)
    return rank, down


def legendre_kernel(
    brackets, weight_ref, map_ref, spec_hbm, leg_hbm, own_ref, prev_ref, between_ref,
    pair_buf, first_buf, leg_buf, own_rows, prev_rows, order_vmem, order, order_sem, sems,
):
    slots, half, _ = leg_hbm.shape
    groups = slots // SQ
    steps = slots // STEP
    wave = lax.axis_index("wave")
    lev = lax.axis_index("lev")
    lower = brackets[lev] - lev * LEV_DEV
    has_upper = lower < LEV_DEV - 1
    w = weight_ref[lev]
    low_w = jnp.where(has_upper, w, 0.0)
    upper_w = jnp.where(has_upper, 1.0 - w, w)
    pair_row = jnp.minimum(lower, LEV_DEV - 2) * PART
    before = jnp.maximum(lev - 1, 0)
    crosses = (lev > 0) & (brackets[before] == lev * LEV_DEV - 1)
    first_w = jnp.where(crosses, 1.0 - weight_ref[before], 0.0)
    degree = iota((16, NT), 1).astype(jnp.int16)
    sign = (1 - 2 * (iota((16, NT), 1) % 2)).astype(F32).astype(BF16)
    lane_group = iota((1, 192), 1) % 64 // PART
    left = iota((1, SQ * PART), 1) < 64
    south = iota((2 * half, 1), 0) >= half

    rank, down = ranks_of(waves_of(map_ref, wave, slots))
    hit = rank == iota((256, 256), 1).astype(F32)
    slot_at = jnp.sum(jnp.where(hit, iota((256, 256), 0).astype(F32), 0.0), axis=0, keepdims=True)
    wave_at = jnp.sum(jnp.where(hit, down, 0.0), axis=0, keepdims=True)
    order_vmem[0:1, :] = slot_at.astype(jnp.int32)
    order_vmem[1:2, :] = wave_at.astype(jnp.int32)
    to_smem = pltpu.make_async_copy(order_vmem, order, order_sem)
    to_smem.start()
    to_smem.wait()

    def buffers(slot, c):
        lanes = pl.ds(c * CHUNK, NT - c * CHUNK)
        return [
            (leg_hbm.at[:, :, lanes], leg_buf.at[slot, :, :, lanes], sems.at[slot, 0]),
            (spec_hbm.at[:, pl.ds(pl.multiple_of(pair_row, PART), 2 * PART), lanes], pair_buf.at[slot, :, :, lanes], sems.at[slot, 1]),
            (spec_hbm.at[:, pl.ds(0, PART), lanes], first_buf.at[slot, :, :, lanes], sems.at[slot, 2]),
        ]

    def wave_chunk(step):
        return order[1, step * STEP] // CHUNK

    def fetch(step, place, c, ranks):
        for i in ranks:
            at = order[0, step * STEP + i]
            for src, dst, sem in buffers(place % DEPTH, c):
                pltpu.make_async_copy(src.at[at], dst.at[i], sem).start()

    def await_copies(place, c):
        for src, dst, sem in buffers(place % DEPTH, c):
            pltpu.make_async_copy(src.at[pl.ds(0, STEP)], dst, sem).wait()

    for step in range(DEPTH - 1):
        for c in range(NT // CHUNK):
            pl.when(wave_chunk(step) == c)(functools.partial(fetch, step, step, c, range(STEP)))
    between = jnp.int32(0)
    for p in range(1, brackets.shape[0] - 1, 2):
        between = between | (brackets[p] == (p + 1) * LEV_DEV - 1).astype(jnp.int32)
    between_ref[0] = between

    def multiply(step, c, later_c):
        slot = step % DEPTH
        lanes = slice(c * CHUNK, NT)
        later = jnp.minimum(step + DEPTH - 1, steps - 1)
        await_copies(step, c)
        for b in range(STEP // SQ):
            owns, firsts = [], []
            for quad in range(2):
                first_rank = b * SQ + 4 * quad
                fetch(later, step + DEPTH - 1, later_c, range(first_rank, first_rank + 4))
                values, factors, columns = [], [], [[], [], []]
                for i in range(b * SQ + 4 * quad, b * SQ + 4 * quad + 4):
                    m = order[1, step * STEP + i]
                    kept = degree[:, lanes] >= m.astype(jnp.int16)
                    plain = [jnp.where(kept, leg_buf[slot, i, r : r + 16, lanes], 0) for r in range(0, half, 16)]
                    values += plain + [x * sign[:, lanes] for x in plain]
                    factors.append(jnp.where(south, (1 - 2 * (m % 2)).astype(F32), 1.0))
                    columns[quad].append(pair_buf[slot, i, :PART, lanes])
                    columns[1 - quad].append(pair_buf[slot, i, PART:, lanes])
                    columns[2].append(first_buf[slot, i, :, lanes])
                sums = nt_dot(jnp.concatenate(values, axis=0), jnp.concatenate(columns[0] + columns[1] + columns[2], axis=0))
                kept_sums = sums[: 2 * half] * factors[0]
                for a in range(1, 4):
                    block = sums[2 * half * a : 2 * half * (a + 1)] * factors[a]
                    kept_sums = jnp.where(lane_group == a, block, kept_sums)
                both = kept_sums[:, :128]
                owns.append(both * low_w + pltpu.roll(both, 64, 1) * upper_w)
                firsts.append(jnp.concatenate([kept_sums[:, 128:]] * 2, axis=1))
            at = pl.multiple_of((step * (STEP // SQ) + b) * 2 * half, 2 * half)
            own_rows[pl.ds(at, 2 * half), :] = jnp.where(left, owns[0], owns[1])
            prev_rows[pl.ds(at, 2 * half), :] = jnp.where(left, firsts[0], firsts[1]) * first_w

    def step_body(step, held):
        now = held[0]
        later = jnp.minimum(wave_chunk(jnp.minimum(step + DEPTH - 1, steps - 1)), now + 1)
        for c in range(NT // CHUNK):
            for later_c in range(c, min(c + 2, NT // CHUNK)):
                pl.when((now == c) & (later == later_c))(functools.partial(multiply, step, c, later_c))
        return (*held[1:], later)

    held = lax.fori_loop(0, steps, step_body, tuple(wave_chunk(step) for step in range(DEPTH - 1)))
    for i in range(DEPTH - 1):
        for c in range(NT // CHUNK):
            pl.when(held[i] == c)(functools.partial(await_copies, steps + i, c))
    rows = 2 * half
    for rows_ref, ref in ((own_rows, own_ref), (prev_rows, prev_ref)):
        rows_dev = ref.shape[1] // groups
        for r in range(rows):
            at = (r % rows_dev) * groups
            ref[r // rows_dev, at : at + groups, :] = rows_ref[pl.ds(r, groups, stride=rows), :]


def legendre_sums(spectral, legendre, map_rows, brackets, lev_weight):
    slots = spectral.shape[0]
    half = legendre.shape[1]
    groups = slots // SQ
    devices = lax.axis_size("wave") * lax.axis_size("lev")
    out = pltpu.VMEM((devices, 2 * half // devices * groups, SQ * PART), F32)
    smem = pl.BlockSpec(memory_space=pltpu.SMEM)
    vmem = pl.BlockSpec(memory_space=pltpu.VMEM)
    hbm = pl.BlockSpec(memory_space=pltpu.HBM)
    return pl.pallas_call(
        legendre_kernel,
        out_shape=[out, out, jax.ShapeDtypeStruct((1,), jnp.int32)],
        in_specs=[smem, smem, vmem, hbm, hbm],
        out_specs=[vmem, vmem, smem],
        scratch_shapes=[
            pltpu.VMEM((DEPTH, STEP, 2 * PART, NT), BF16),
            pltpu.VMEM((DEPTH, STEP, PART, NT), BF16),
            pltpu.VMEM((DEPTH, STEP, half, NT), BF16),
            pltpu.VMEM((groups * 2 * half, SQ * PART), F32),
            pltpu.VMEM((groups * 2 * half, SQ * PART), F32),
            pltpu.VMEM((2, 256), jnp.int32),
            pltpu.SMEM((2, 256), jnp.int32),
            pltpu.SemaphoreType.DMA,
            pltpu.SemaphoreType.DMA((DEPTH, 3)),
        ],
        compiler_params=pltpu.CompilerParams(vmem_limit_bytes=48 * MIB),
        cost_estimate=pl.CostEstimate(flops=2 * slots * 2 * half * 48 * NT, bytes_accessed=slots * NT * 2 * (48 + half), transcendentals=0),
        name="legendre_sums",
    )(*[pltpu.with_memory_space_constraint(x, pltpu.HBM) for x in (brackets, lev_weight, map_rows, spectral, legendre)])


def unit_circle(product, points, inverse):
    big = 12582912.0
    turn = (product * inverse + big) - big
    x = (product - turn * points) * (math.pi * inverse)
    x2 = x * x
    sine = 0.0
    cosine = 0.0
    for power in (11, 9, 7, 5, 3, 1):
        sine = sine * x2 + (-1) ** (power // 2) / math.factorial(power)
    for power in (12, 10, 8, 6, 4, 2, 0):
        cosine = cosine * x2 + (-1) ** (power // 2) / math.factorial(power)
    sine = sine * x
    twice = sine + sine
    return 1.0 - twice * sine, twice * cosine


def own_points(points_ref, r2):
    wave = lax.axis_index("wave")
    lev = lax.axis_index("lev")
    row = 2 * (wave * lax.axis_size("lev") + lev) + r2
    return points_ref[row % points_ref.shape[0]]


def table_kernel(points_ref, map_ref, hi_ref, lo_ref, sorted_ref):
    r2 = pl.program_id(0)
    kb = pl.program_id(1)
    rows = hi_ref.shape[1]
    points = own_points(points_ref, r2).astype(F32)
    inverse = 1.0 / points

    @pl.when((r2 == 0) & (kb == 0))
    def _():
        waves, slots = sorted_ref.shape
        for wave in range(waves):
            rank, down = ranks_of(waves_of(map_ref, wave, slots))
            whole = jnp.floor((rank + 0.5) * (1.0 / SQ))
            place = (rank - whole * SQ) * (slots // SQ) + whole
            hit = (place == iota((256, 256), 1).astype(F32)) & (rank < slots)
            row = jnp.sum(jnp.where(hit, down, 0.0), axis=0, keepdims=True)
            sorted_ref[wave : wave + 1, :] = row[:, :slots].astype(jnp.int32)

    lane = iota((32, 128), 1).astype(F32)

    def chunk_body(i, carry):
        chunk = pl.multiple_of(i * 32, 32)

        def put(tile, value):
            lanes = slice(tile * 128, tile * 128 + 128)
            hi = value.astype(BF16)
            hi_ref[0, pl.ds(chunk, 32), lanes] = hi
            lo_ref[0, pl.ds(chunk, 32), lanes] = ((value - hi.astype(F32)) * REST_SCALE).astype(FP8)

        k = (kb * rows + chunk + iota((32, 128), 0)).astype(F32)
        c, s = unit_circle(2.0 * lane * k, points, inverse)
        c1, s1 = unit_circle(k, points, inverse)
        ct, st = unit_circle(256.0 * k, points, inverse)
        co = c * c1 - s * s1
        so = s * c1 + c * s1
        for t in range(HALF_M // 128):
            if t:
                c, s = c * ct - s * st, s * ct + c * st
                co, so = co * ct - so * st, so * ct + co * st
            put(t, c)
            put(5 + t, s)
            put(10 + t, co)
            put(15 + t, so)
        return carry

    lax.fori_loop(0, rows // 32, chunk_body, 0, unroll=True)


def tables(row_points, map_rows):
    waves = lax.axis_size("wave")
    rows = KPTS // TABLE_STEPS
    table = pltpu.HBM((2, KPTS, 2 * M), BF16)
    table_spec = pl.BlockSpec((1, rows, 2 * M), lambda r, k: (r, k, 0))
    return pl.pallas_call(
        table_kernel,
        out_shape=[table, pltpu.HBM((2, KPTS, 2 * M), FP8), jax.ShapeDtypeStruct((waves, M // waves), jnp.int32)],
        grid=(2, TABLE_STEPS),
        in_specs=[pl.BlockSpec(memory_space=pltpu.SMEM), pl.BlockSpec(memory_space=pltpu.VMEM)],
        out_specs=[table_spec, table_spec, pl.BlockSpec(memory_space=pltpu.VMEM)],
        compiler_params=pltpu.CompilerParams(vmem_limit_bytes=48 * MIB),
        cost_estimate=pl.CostEstimate(flops=2 * KPTS * 2 * M * 12, bytes_accessed=2 * KPTS * 2 * M * 4, transcendentals=0),
        name="fourier_tables",
    )(*[pltpu.with_memory_space_constraint(x, pltpu.HBM) for x in (row_points, map_rows)])


def pick_tables(plev):
    wide = plev * 2 * PART
    out = np.zeros((2, 4, 2 * wide, 2 * wide), np.float32)
    plans = (
        ((0, 1), (0, 1), (0, 1), (0, 1)),
        ((1, -1), (1, 1), (1, -1), (1, 1)),
        ((0, 1), (0, 1), (1, -1), (1, -1)),
        ((1, -1), (1, 1), (0, -1), (0, 1)),
    )
    for r2 in range(2):
        for kind, plan in enumerate(plans):
            for image, (part, sgn) in enumerate(plan):
                for hl in range(2):
                    for p in range(plev):
                        for q in range(FS):
                            src = hl * wide + p * 2 * PART + r2 * PART + q * 2 + part
                            dst = hl * wide + image * plev * FS + p * FS + q
                            out[r2, kind, src, dst] = sgn
    return out.astype(jnp.bfloat16)


def mean_table(plev):
    wide = plev * FS * 4
    out = np.zeros((2 * 4 * plev, 2 * wide), np.float32)
    for quarter in range(4):
        for p in range(plev):
            for part in range(2):
                image_quarter = (quarter + part) % 4
                start = (image_quarter * 2 + part) * plev * FS + p * FS
                out[part * 4 * plev + quarter * plev + p, start : start + FS] = 0.5 / STEPS
    return out.astype(jnp.bfloat16)


def flip_table():
    return np.fliplr(np.eye(KBLK, dtype=np.float32)).astype(jnp.bfloat16)


def split(x):
    hi = x.astype(BF16)
    return hi, (x - hi.astype(F32)).astype(BF16)


def nt_dot(a, b):
    return lax.dot_general(a, b, (((1,), (1,)), ((), ())), preferred_element_type=F32)


def nn_dot(a, b):
    return jnp.dot(a, b, preferred_element_type=F32)


def synth_kernel(points_ref, *refs):
    moved_ref, map_ref, pick_ref, mean_ref, flip_ref, hi_hbm, lo_hbm, out_ref = refs[:8]
    perm_ref, hi_ref, lo_ref, mixed, coef, coef8, flat, mirror, line, sems = refs[8:]
    table_copies = []
    for r2 in range(2):
        table_copies.append([])
        for i, (src, dst) in enumerate(((hi_hbm, hi_ref), (lo_hbm, lo_ref))):
            for c in range(TABLE_CUTS):
                rows = pl.ds(c * (KPTS // TABLE_CUTS), KPTS // TABLE_CUTS)
                table_copies[r2].append(pltpu.make_async_copy(src.at[r2, rows], dst.at[r2, rows], sems.at[r2, i, c]))
    for copy in table_copies[0] + table_copies[1]:
        copy.start()

    slot_waves = jnp.broadcast_to(map_ref[...], (16, M)).astype(jnp.int16)

    def perm_body(i, carry):
        row = pl.multiple_of(i * 16, 16)
        order = row + iota((16, M), 0)
        wanted = jnp.where(row < HALF_M, 2 * order, 2 * (order - HALF_M) + 1).astype(jnp.int16)
        perm_ref[pl.ds(row, 16), :] = jnp.where(slot_waves == wanted, 1.0, 0.0).astype(BF16)
        return carry

    lax.fori_loop(0, M // 16, perm_body, 0, unroll=4)
    waves, plev, _, _ = moved_ref.shape
    wide = plev * 2 * PART
    part_rows = M // SQ
    for base in range(0, plev * 2, 8):
        cur = []
        for g in range(base, base + 8):
            sub = moved_ref.shape[2] // 2
            pieces = [moved_ref[w, g // 2, (g % 2) * sub : (g % 2 + 1) * sub, :] for w in range(waves)]
            cur.append(jnp.concatenate(pieces, axis=0))
        group = iota((part_rows, 128), 1) // PART
        for bit in (1, 2, 4):
            unset = (group & bit) == 0
            nxt = list(cur)
            for g in range(8):
                if g & bit == 0:
                    a, b = cur[g], cur[g + bit]
                    nxt[g] = jnp.where(unset, a, pltpu.roll(b, bit * PART, 1))
                    nxt[g + bit] = jnp.where(unset, pltpu.roll(a, 128 - bit * PART, 1), b)
            cur = nxt
        for sq in range(SQ):
            hi, lo = split(cur[sq])
            lane = base * PART
            mixed[sq * part_rows : (sq + 1) * part_rows, lane : lane + 128] = hi
            mixed[sq * part_rows : (sq + 1) * part_rows, wide + lane : wide + lane + 128] = lo

    lane_row = (iota((1, 2 * wide), 1) // PART) % 2
    limit0 = (own_points(points_ref, 0) - 1) // 2
    limit1 = (own_points(points_ref, 1) - 1) // 2
    limit = jnp.where(lane_row == 0, limit0, limit1)
    place = iota((HALF_M, 1), 0)
    turned = (iota((1, 2 * wide), 1) % wide) // (plev * FS) >= 2
    flip_sign = jnp.where(turned & (place % 2 == 1), -1.0, 1.0).astype(BF16)
    for odd in range(2):
        ordered = nn_dot(perm_ref[odd * HALF_M : (odd + 1) * HALF_M, :], mixed[...])
        wave = 2 * place + odd
        factor = jnp.where(wave <= limit, jnp.where(wave == 0, 1.0, 2.0), 0.0)
        ordered = (ordered * factor).astype(BF16)
        for row in range(2):
            for part in range(2):
                picked = nn_dot(ordered, pick_ref[row, odd * 2 + part]).astype(BF16)
                picked = picked * flip_sign
                coef[row, odd, part * HALF_M : (part + 1) * HALF_M, :] = picked
                coef8[row, odd, part * HALF_M : (part + 1) * HALF_M, :] = picked[:, :wide].astype(F32).astype(FP8)
    flat[...] = jnp.zeros_like(flat)
    mirror[...] = jnp.zeros_like(mirror)

    row_sums = []
    for r2 in range(2):
        for copy in table_copies[r2]:
            copy.wait()

        def contraction(odd):
            lanes = slice(odd * M, (odd + 1) * M)
            both = nn_dot(hi_ref[r2, :, lanes], coef[r2, odd])
            rest = nn_dot(lo_ref[r2, :, lanes], coef8[r2, odd])
            return both[:, :wide] + (both[:, wide:] + rest * (1.0 / REST_SCALE))

        row_sums.append((contraction(0), contraction(1)))

    for r2 in range(2):
        even_sum, odd_sum = row_sums[r2]
        plus = even_sum + odd_sum
        minus = even_sum - odd_sum
        squares = jnp.concatenate([plus * plus, minus * minus], axis=1)
        sq_hi, sq_lo = split(squares)
        energy = nt_dot(mean_ref[...], sq_hi) + nt_dot(mean_ref[...], sq_lo)
        rows = 4 * plev
        flat[:, :KPTS] = energy
        en_hi, en_lo = split(flat[rows:, :KPAD])
        for t in range(KPAD // KBLK):
            lanes = slice(t * KBLK, (t + 1) * KBLK)
            back = KPAD - (t + 1) * KBLK
            mirror[:, back : back + KBLK] = nn_dot(en_hi[:, lanes], flip_ref[...]) + nn_dot(en_lo[:, lanes], flip_ref[...])

        quarter = own_points(points_ref, r2) // 4
        lane = iota((rows, BUF), 1)
        shift = (quarter + (BUF - (KPAD - 1))) % BUF
        flat[:rows, :] = jnp.where(lane <= quarter // 2, flat[:rows, :], pltpu.roll(mirror[...], shift, 1))
        line[...] = jnp.zeros_like(line)
        lane = iota((plev, BUF), 1)
        for b in range(4):
            start = quarter * b
            inner = start % 128
            base = pl.multiple_of(start - inner, 128)
            piece = pltpu.roll(flat[b * plev : (b + 1) * plev, :], inner, 1)
            old = line[:, pl.ds(base, BUF)]
            line[:, pl.ds(base, BUF)] = jnp.where((lane >= inner) & (lane < inner + quarter), piece, old)
        out_ref[:, pl.ds(r2, 1), :] = line[:, :ROWPAD].reshape(plev, 1, ROWPAD)


def synthesis(moved, slot_map, table_hi, table_lo, row_points):
    plev = moved.shape[1]
    wide = plev * 2 * PART
    vmem = pl.BlockSpec(memory_space=pltpu.VMEM)
    return pl.pallas_call(
        synth_kernel,
        out_shape=jax.ShapeDtypeStruct((plev, 2, ROWPAD), F32),
        in_specs=[pl.BlockSpec(memory_space=pltpu.SMEM)] + [vmem] * 5 + [pl.BlockSpec(memory_space=pltpu.HBM)] * 2,
        out_specs=vmem,
        scratch_shapes=[
            pltpu.VMEM((M, M), BF16),
            pltpu.VMEM((2, KPTS, 2 * M), BF16),
            pltpu.VMEM((2, KPTS, 2 * M), FP8),
            pltpu.VMEM((M, 2 * wide), BF16),
            pltpu.VMEM((2, 2, M, 2 * wide), BF16),
            pltpu.VMEM((2, 2, M, wide), FP8),
            pltpu.VMEM((8 * plev, BUF), F32),
            pltpu.VMEM((4 * plev, BUF), F32),
            pltpu.VMEM((plev, 3 * 1280 + BUF), F32),
            pltpu.SemaphoreType.DMA((2, 2, TABLE_CUTS)),
        ],
        compiler_params=pltpu.CompilerParams(vmem_limit_bytes=44 * MIB),
        cost_estimate=pl.CostEstimate(flops=2 * 2 * KPTS * 2 * M * 384, bytes_accessed=2 * KPTS * 2 * M * 4 + M * M * 2, transcendentals=0),
        name="synthesis",
    )(
        pltpu.with_memory_space_constraint(row_points, pltpu.HBM),
        pltpu.with_memory_space_constraint(moved, pltpu.VMEM), slot_map,
        pick_tables(plev), mean_table(plev), flip_table(),
        *[pltpu.with_memory_space_constraint(x, pltpu.HBM) for x in (table_hi, table_lo)],
    )


def join_kernel(*refs):
    parts = (len(refs) - 1) // 2
    at = 0
    for own_ref, other_ref in zip(refs[:parts], refs[parts:-1]):
        rows = own_ref.shape[1]
        refs[-1][:, at : at + rows, :] = own_ref[...] + other_ref[...]
        at += rows


def join(owns, others):
    rows = sum(x.shape[1] for x in owns)
    vmem = pl.BlockSpec(memory_space=pltpu.VMEM)
    return pl.pallas_call(
        join_kernel,
        out_shape=jax.ShapeDtypeStruct((owns[0].shape[0], rows, SQ * PART), F32),
        in_specs=[vmem] * (2 * len(owns)),
        out_specs=vmem,
        compiler_params=pltpu.CompilerParams(vmem_limit_bytes=32 * MIB),
        name="join",
    )(*[pltpu.with_memory_space_constraint(x, pltpu.VMEM) for x in owns + others])


def local(spectral, legendre, wave_map, row_points, brackets, lev_weight, climatology):
    slots = spectral.shape[0]
    half = legendre.shape[1]
    groups = slots // SQ
    wave_count = lax.axis_size("wave")
    lev_count = lax.axis_size("lev")
    rows_dev = 2 * half // (wave_count * lev_count)
    pairs = [(d, d - 1) for d in range(1, lev_count)]
    map_rows = wave_map.reshape(M // 128, 128)
    own, prev, between = legendre_sums(spectral, legendre, map_rows, brackets, lev_weight)
    sent = lax.cond(
        between[0] > 0,
        lambda mine, theirs: join([mine], [lax.ppermute(theirs, "lev", pairs)]),
        lambda mine, theirs: join([mine], [lax.ppermute(theirs, "lev", pairs[::2])]),
        own,
        prev,
    )
    moved = lax.all_to_all(sent, ("wave", "lev"), split_axis=0, concat_axis=0, tiled=True)
    moved = moved.reshape(wave_count, lev_count, rows_dev * groups, SQ * PART)
    table_points, _ = lax.optimization_barrier((row_points, sent))
    table_hi, table_lo, sorted_map = tables(table_points, map_rows)
    slot_map = jnp.transpose(sorted_map.reshape(wave_count, SQ, groups), (1, 0, 2)).reshape(1, M)
    energy = synthesis(moved, slot_map, table_hi, table_lo, row_points)
    result = lax.all_to_all(energy, "lev", split_axis=0, concat_axis=0, tiled=True)
    result = result.reshape(1, rows_dev * lev_count, ROWPAD)
    points_all = jnp.concatenate([row_points, row_points])
    band_rows = rows_dev * lev_count
    out_points = lax.dynamic_slice_in_dim(points_all, lax.axis_index("wave") * band_rows, band_rows, 0)
    places = jnp.arange(ROWPAD, dtype=jnp.int32)
    inside = places[None, None, :] < out_points[None, :, None]
    return jnp.where(inside, result - climatology, 0.0)


def solution(mesh):
    placed = (
        P("wave", "lev", None),
        P("wave", None, None),
        P(),
        P(),
        P(),
        P(),
        P("lev", "wave", None),
    )
    return jax.shard_map(
        local, mesh=mesh, in_specs=placed, out_specs=P("lev", "wave", None), check_vma=False
    )
```

```python
import functools
import math

import jax
import jax.numpy as jnp
import numpy as np
from jax import lax
from jax.experimental import pallas as pl
from jax.experimental.pallas import tpu as pltpu
from jax.sharding import PartitionSpec as P

M = 1280
NT = 1280
LEV_DEV = 4
STEPS = 4
FIELDS = 2
ROWPAD = 5248

FS = FIELDS * STEPS
PART = 2 * FS
SQ = 8
STEP = 16
CHUNK = 256
DEPTH = 3
HALF_M = M // 2
KPTS = 672
KPAD = 768
KBLK = 256
TABLE_STEPS = 7
TABLE_CUTS = 3
BUF = 1536
MIB = 1024 * 1024
F32 = jnp.float32
BF16 = jnp.bfloat16
FP8 = jnp.float8_e4m3fn
REST_SCALE = 256.0


def iota(shape, dim):
    return lax.broadcasted_iota(jnp.int32, shape, dim)


def waves_of(map_ref, wave, slots):
    start = wave * slots
    row = start // 128
    last = map_ref.shape[0] - 1
    pair = jnp.concatenate([map_ref[pl.ds(row, 1), :], map_ref[pl.ds(jnp.minimum(row + 1, last), 1), :]], axis=1)
    pair = jnp.broadcast_to(pair, (8, 256)).astype(F32)
    turned = pltpu.roll(pair, (256 - start % 128) % 256, 1)
    return jnp.where(iota((8, 256), 1) < slots, turned, 4096.0)[:1]


def ranks_of(waves):
    across = jnp.broadcast_to(waves, (256, 256))
    down = across.T
    rank = jnp.sum(jnp.where(across < down, 1.0, 0.0), axis=1, keepdims=True)
    return rank, down


def legendre_kernel(
    brackets, weight_ref, map_ref, spec_hbm, leg_hbm, own_ref, prev_ref, between_ref,
    spec_buf, leg_buf, own_rows, prev_rows, order_vmem, order, order_sem, sems,
):
    slots, half, _ = leg_hbm.shape
    groups = slots // SQ
    steps = slots // STEP
    wave = lax.axis_index("wave")
    lev = lax.axis_index("lev")
    lower = brackets[lev] - lev * LEV_DEV
    has_upper = lower < LEV_DEV - 1
    w = weight_ref[lev]
    upper_w = jnp.where(has_upper, 1.0 - w, 0.0)
    low_rows = pl.ds(pl.multiple_of(lower * PART, PART), PART)
    up_rows = pl.ds(pl.multiple_of(jnp.minimum(lower + 1, LEV_DEV - 1) * PART, PART), PART)
    before = jnp.maximum(lev - 1, 0)
    crosses = (lev > 0) & (brackets[before] == lev * LEV_DEV - 1)
    first_w = jnp.where(crosses, 1.0 - weight_ref[before], 0.0)
    degree = iota((16, NT), 1).astype(jnp.int16)
    sign = (1 - 2 * (iota((16, NT), 1) % 2)).astype(F32).astype(BF16)
    lane_group = iota((1, 192), 1) % 64 // PART
    left = iota((1, SQ * PART), 1) < 64
    south = iota((2 * half, 1), 0) >= half

    rank, down = ranks_of(waves_of(map_ref, wave, slots))
    hit = rank == iota((256, 256), 1).astype(F32)
    slot_at = jnp.sum(jnp.where(hit, iota((256, 256), 0).astype(F32), 0.0), axis=0, keepdims=True)
    wave_at = jnp.sum(jnp.where(hit, down, 0.0), axis=0, keepdims=True)
    order_vmem[0:1, :] = slot_at.astype(jnp.int32)
    order_vmem[1:2, :] = wave_at.astype(jnp.int32)
    to_smem = pltpu.make_async_copy(order_vmem, order, order_sem)
    to_smem.start()
    to_smem.wait()

    def buffers(slot, c):
        lanes = pl.ds(c * CHUNK, NT - c * CHUNK)
        return [
            (leg_hbm.at[:, :, lanes], leg_buf.at[slot, :, :, lanes], sems.at[slot, 0]),
            (spec_hbm.at[:, :, lanes], spec_buf.at[slot, :, :, lanes], sems.at[slot, 1]),
        ]

    def fetch(step):
        chunk = order[1, step * STEP] // CHUNK
        for c in range(NT // CHUNK):

            @pl.when(chunk == c)
            def _():
                for i in range(STEP):
                    at = order[0, step * STEP + i]
                    for src, dst, sem in buffers(step % DEPTH, c):
                        pltpu.make_async_copy(src.at[at], dst.at[i], sem).start()

    for step in range(DEPTH - 1):
        fetch(step)
    between = jnp.int32(0)
    for p in range(1, brackets.shape[0] - 1, 2):
        between = between | (brackets[p] == (p + 1) * LEV_DEV - 1).astype(jnp.int32)
    between_ref[0] = between

    def multiply(step, c):
        slot = step % DEPTH
        lanes = slice(c * CHUNK, NT)
        for src, dst, sem in buffers(slot, c):
            pltpu.make_async_copy(src.at[pl.ds(0, STEP)], dst, sem).wait()
        for b in range(STEP // SQ):
            owns, firsts = [], []
            for quad in range(2):
                values, factors, columns = [], [], [[], [], []]
                for i in range(b * SQ + 4 * quad, b * SQ + 4 * quad + 4):
                    m = order[1, step * STEP + i]
                    kept = degree[:, lanes] >= m.astype(jnp.int16)
                    plain = [jnp.where(kept, leg_buf[slot, i, r : r + 16, lanes], 0) for r in range(0, half, 16)]
                    values += plain + [x * sign[:, lanes] for x in plain]
                    factors.append(jnp.where(south, (1 - 2 * (m % 2)).astype(F32), 1.0))
                    columns[quad].append(spec_buf[slot, i, low_rows, lanes])
                    columns[1 - quad].append(spec_buf[slot, i, up_rows, lanes])
                    columns[2].append(spec_buf[slot, i, :PART, lanes])
                sums = nt_dot(jnp.concatenate(values, axis=0), jnp.concatenate(columns[0] + columns[1] + columns[2], axis=0))
                kept_sums = sums[: 2 * half] * factors[0]
                for a in range(1, 4):
                    block = sums[2 * half * a : 2 * half * (a + 1)] * factors[a]
                    kept_sums = jnp.where(lane_group == a, block, kept_sums)
                both = kept_sums[:, :128]
                owns.append(both * w + pltpu.roll(both, 64, 1) * upper_w)
                firsts.append(jnp.concatenate([kept_sums[:, 128:]] * 2, axis=1))
            at = pl.multiple_of((step * (STEP // SQ) + b) * 2 * half, 2 * half)
            own_rows[pl.ds(at, 2 * half), :] = jnp.where(left, owns[0], owns[1])
            prev_rows[pl.ds(at, 2 * half), :] = jnp.where(left, firsts[0], firsts[1]) * first_w

    def step_body(step, carry):
        @pl.when(step + DEPTH - 1 < steps)
        def _():
            fetch(step + DEPTH - 1)

        chunk = order[1, step * STEP] // CHUNK
        for c in range(NT // CHUNK):
            pl.when(chunk == c)(functools.partial(multiply, step, c))
        return carry

    lax.fori_loop(0, steps, step_body, 0)
    rows = 2 * half
    for rows_ref, ref in ((own_rows, own_ref), (prev_rows, prev_ref)):
        rows_dev = ref.shape[1] // groups
        for r in range(rows):
            at = (r % rows_dev) * groups
            ref[r // rows_dev, at : at + groups, :] = rows_ref[pl.ds(r, groups, stride=rows), :]


def legendre_sums(spectral, legendre, map_rows, brackets, lev_weight):
    slots = spectral.shape[0]
    half = legendre.shape[1]
    groups = slots // SQ
    devices = lax.axis_size("wave") * lax.axis_size("lev")
    out = pltpu.VMEM((devices, 2 * half // devices * groups, SQ * PART), F32)
    smem = pl.BlockSpec(memory_space=pltpu.SMEM)
    vmem = pl.BlockSpec(memory_space=pltpu.VMEM)
    hbm = pl.BlockSpec(memory_space=pltpu.HBM)
    return pl.pallas_call(
        legendre_kernel,
        out_shape=[out, out, jax.ShapeDtypeStruct((1,), jnp.int32)],
        in_specs=[smem, smem, vmem, hbm, hbm],
        out_specs=[vmem, vmem, smem],
        scratch_shapes=[
            pltpu.VMEM((DEPTH, STEP, LEV_DEV * PART, NT), BF16),
            pltpu.VMEM((DEPTH, STEP, half, NT), BF16),
            pltpu.VMEM((groups * 2 * half, SQ * PART), F32),
            pltpu.VMEM((groups * 2 * half, SQ * PART), F32),
            pltpu.VMEM((2, 256), jnp.int32),
            pltpu.SMEM((2, 256), jnp.int32),
            pltpu.SemaphoreType.DMA,
            pltpu.SemaphoreType.DMA((DEPTH, 2)),
        ],
        compiler_params=pltpu.CompilerParams(vmem_limit_bytes=48 * MIB),
        cost_estimate=pl.CostEstimate(flops=2 * slots * 2 * half * 48 * NT, bytes_accessed=slots * NT * 2 * (48 + half), transcendentals=0),
        name="legendre_sums",
    )(*[pltpu.with_memory_space_constraint(x, pltpu.HBM) for x in (brackets, lev_weight, map_rows, spectral, legendre)])


def unit_circle(product, points, inverse):
    big = 12582912.0
    turn = (product * inverse + big) - big
    x = (product - turn * points) * (math.pi * inverse)
    x2 = x * x
    sine = 0.0
    cosine = 0.0
    for power in (11, 9, 7, 5, 3, 1):
        sine = sine * x2 + (-1) ** (power // 2) / math.factorial(power)
    for power in (12, 10, 8, 6, 4, 2, 0):
        cosine = cosine * x2 + (-1) ** (power // 2) / math.factorial(power)
    sine = sine * x
    twice = sine + sine
    return 1.0 - twice * sine, twice * cosine


def own_points(points_ref, r2):
    wave = lax.axis_index("wave")
    lev = lax.axis_index("lev")
    row = 2 * (wave * lax.axis_size("lev") + lev) + r2
    return points_ref[row % points_ref.shape[0]]


def table_kernel(points_ref, map_ref, hi_ref, lo_ref, sorted_ref):
    r2 = pl.program_id(0)
    kb = pl.program_id(1)
    rows = hi_ref.shape[1]
    points = own_points(points_ref, r2).astype(F32)
    inverse = 1.0 / points

    @pl.when((r2 == 0) & (kb == 0))
    def _():
        waves, slots = sorted_ref.shape
        for wave in range(waves):
            rank, down = ranks_of(waves_of(map_ref, wave, slots))
            whole = jnp.floor((rank + 0.5) * (1.0 / SQ))
            place = (rank - whole * SQ) * (slots // SQ) + whole
            hit = (place == iota((256, 256), 1).astype(F32)) & (rank < slots)
            row = jnp.sum(jnp.where(hit, down, 0.0), axis=0, keepdims=True)
            sorted_ref[wave : wave + 1, :] = row[:, :slots].astype(jnp.int32)

    lane = iota((32, 128), 1).astype(F32)

    def chunk_body(i, carry):
        chunk = pl.multiple_of(i * 32, 32)

        def put(tile, value):
            lanes = slice(tile * 128, tile * 128 + 128)
            hi = value.astype(BF16)
            hi_ref[0, pl.ds(chunk, 32), lanes] = hi
            lo_ref[0, pl.ds(chunk, 32), lanes] = ((value - hi.astype(F32)) * REST_SCALE).astype(FP8)

        k = (kb * rows + chunk + iota((32, 128), 0)).astype(F32)
        c, s = unit_circle(2.0 * lane * k, points, inverse)
        c1, s1 = unit_circle(k, points, inverse)
        ct, st = unit_circle(256.0 * k, points, inverse)
        co = c * c1 - s * s1
        so = s * c1 + c * s1
        for t in range(HALF_M // 128):
            if t:
                c, s = c * ct - s * st, s * ct + c * st
                co, so = co * ct - so * st, so * ct + co * st
            put(t, c)
            put(5 + t, s)
            put(10 + t, co)
            put(15 + t, so)
        return carry

    lax.fori_loop(0, rows // 32, chunk_body, 0, unroll=True)


def tables(row_points, map_rows):
    waves = lax.axis_size("wave")
    rows = KPTS // TABLE_STEPS
    table = pltpu.HBM((2, KPTS, 2 * M), BF16)
    table_spec = pl.BlockSpec((1, rows, 2 * M), lambda r, k: (r, k, 0))
    return pl.pallas_call(
        table_kernel,
        out_shape=[table, pltpu.HBM((2, KPTS, 2 * M), FP8), jax.ShapeDtypeStruct((waves, M // waves), jnp.int32)],
        grid=(2, TABLE_STEPS),
        in_specs=[pl.BlockSpec(memory_space=pltpu.SMEM), pl.BlockSpec(memory_space=pltpu.VMEM)],
        out_specs=[table_spec, table_spec, pl.BlockSpec(memory_space=pltpu.VMEM)],
        compiler_params=pltpu.CompilerParams(vmem_limit_bytes=48 * MIB),
        cost_estimate=pl.CostEstimate(flops=2 * KPTS * 2 * M * 12, bytes_accessed=2 * KPTS * 2 * M * 4, transcendentals=0),
        name="fourier_tables",
    )(*[pltpu.with_memory_space_constraint(x, pltpu.HBM) for x in (row_points, map_rows)])


def pick_tables(plev):
    wide = plev * 2 * PART
    out = np.zeros((2, 4, 2 * wide, 2 * wide), np.float32)
    plans = (
        ((0, 1), (0, 1), (0, 1), (0, 1)),
        ((1, -1), (1, 1), (1, -1), (1, 1)),
        ((0, 1), (0, 1), (1, -1), (1, -1)),
        ((1, -1), (1, 1), (0, -1), (0, 1)),
    )
    for r2 in range(2):
        for kind, plan in enumerate(plans):
            for image, (part, sgn) in enumerate(plan):
                for hl in range(2):
                    for p in range(plev):
                        for q in range(FS):
                            src = hl * wide + p * 2 * PART + r2 * PART + q * 2 + part
                            dst = hl * wide + image * plev * FS + p * FS + q
                            out[r2, kind, src, dst] = sgn
    return out.astype(jnp.bfloat16)


def mean_table(plev):
    wide = plev * FS * 4
    out = np.zeros((2 * 4 * plev, 2 * wide), np.float32)
    for quarter in range(4):
        for p in range(plev):
            for part in range(2):
                image_quarter = (quarter + part) % 4
                start = (image_quarter * 2 + part) * plev * FS + p * FS
                out[part * 4 * plev + quarter * plev + p, start : start + FS] = 0.5 / STEPS
    return out.astype(jnp.bfloat16)


def flip_table():
    return np.fliplr(np.eye(KBLK, dtype=np.float32)).astype(jnp.bfloat16)


def split(x):
    hi = x.astype(BF16)
    return hi, (x - hi.astype(F32)).astype(BF16)


def nt_dot(a, b):
    return lax.dot_general(a, b, (((1,), (1,)), ((), ())), preferred_element_type=F32)


def nn_dot(a, b):
    return jnp.dot(a, b, preferred_element_type=F32)


def synth_kernel(points_ref, *refs):
    moved_ref, map_ref, pick_ref, mean_ref, flip_ref, hi_hbm, lo_hbm, out_ref = refs[:8]
    perm_ref, hi_ref, lo_ref, mixed, coef, coef8, flat, mirror, line, sems = refs[8:]
    table_copies = []
    for r2 in range(2):
        table_copies.append([])
        for i, (src, dst) in enumerate(((hi_hbm, hi_ref), (lo_hbm, lo_ref))):
            for c in range(TABLE_CUTS):
                rows = pl.ds(c * (KPTS // TABLE_CUTS), KPTS // TABLE_CUTS)
                table_copies[r2].append(pltpu.make_async_copy(src.at[r2, rows], dst.at[r2, rows], sems.at[r2, i, c]))
    for copy in table_copies[0] + table_copies[1]:
        copy.start()

    slot_waves = jnp.broadcast_to(map_ref[...], (16, M)).astype(jnp.int16)

    def perm_body(i, carry):
        row = pl.multiple_of(i * 16, 16)
        order = row + iota((16, M), 0)
        wanted = jnp.where(row < HALF_M, 2 * order, 2 * (order - HALF_M) + 1).astype(jnp.int16)
        perm_ref[pl.ds(row, 16), :] = jnp.where(slot_waves == wanted, 1.0, 0.0).astype(BF16)
        return carry

    lax.fori_loop(0, M // 16, perm_body, 0, unroll=4)
    waves, plev, _, _ = moved_ref.shape
    wide = plev * 2 * PART
    part_rows = M // SQ
    for base in range(0, plev * 2, 8):
        cur = []
        for g in range(base, base + 8):
            sub = moved_ref.shape[2] // 2
            pieces = [moved_ref[w, g // 2, (g % 2) * sub : (g % 2 + 1) * sub, :] for w in range(waves)]
            cur.append(jnp.concatenate(pieces, axis=0))
        group = iota((part_rows, 128), 1) // PART
        for bit in (1, 2, 4):
            unset = (group & bit) == 0
            nxt = list(cur)
            for g in range(8):
                if g & bit == 0:
                    a, b = cur[g], cur[g + bit]
                    nxt[g] = jnp.where(unset, a, pltpu.roll(b, bit * PART, 1))
                    nxt[g + bit] = jnp.where(unset, pltpu.roll(a, 128 - bit * PART, 1), b)
            cur = nxt
        for sq in range(SQ):
            hi, lo = split(cur[sq])
            lane = base * PART
            mixed[sq * part_rows : (sq + 1) * part_rows, lane : lane + 128] = hi
            mixed[sq * part_rows : (sq + 1) * part_rows, wide + lane : wide + lane + 128] = lo

    lane_row = (iota((1, 2 * wide), 1) // PART) % 2
    limit0 = (own_points(points_ref, 0) - 1) // 2
    limit1 = (own_points(points_ref, 1) - 1) // 2
    limit = jnp.where(lane_row == 0, limit0, limit1)
    place = iota((HALF_M, 1), 0)
    turned = (iota((1, 2 * wide), 1) % wide) // (plev * FS) >= 2
    flip_sign = jnp.where(turned & (place % 2 == 1), -1.0, 1.0).astype(BF16)
    for odd in range(2):
        ordered = nn_dot(perm_ref[odd * HALF_M : (odd + 1) * HALF_M, :], mixed[...])
        wave = 2 * place + odd
        factor = jnp.where(wave <= limit, jnp.where(wave == 0, 1.0, 2.0), 0.0)
        ordered = (ordered * factor).astype(BF16)
        for row in range(2):
            for part in range(2):
                picked = nn_dot(ordered, pick_ref[row, odd * 2 + part]).astype(BF16)
                picked = picked * flip_sign
                coef[row, odd, part * HALF_M : (part + 1) * HALF_M, :] = picked
                coef8[row, odd, part * HALF_M : (part + 1) * HALF_M, :] = picked[:, :wide].astype(F32).astype(FP8)
    flat[...] = jnp.zeros_like(flat)
    mirror[...] = jnp.zeros_like(mirror)

    row_sums = []
    for r2 in range(2):
        for copy in table_copies[r2]:
            copy.wait()

        def contraction(odd):
            lanes = slice(odd * M, (odd + 1) * M)
            both = nn_dot(hi_ref[r2, :, lanes], coef[r2, odd])
            rest = nn_dot(lo_ref[r2, :, lanes], coef8[r2, odd])
            return both[:, :wide] + (both[:, wide:] + rest * (1.0 / REST_SCALE))

        row_sums.append((contraction(0), contraction(1)))

    for r2 in range(2):
        even_sum, odd_sum = row_sums[r2]
        plus = even_sum + odd_sum
        minus = even_sum - odd_sum
        squares = jnp.concatenate([plus * plus, minus * minus], axis=1)
        sq_hi, sq_lo = split(squares)
        energy = nt_dot(mean_ref[...], sq_hi) + nt_dot(mean_ref[...], sq_lo)
        rows = 4 * plev
        flat[:, :KPTS] = energy
        en_hi, en_lo = split(flat[rows:, :KPAD])
        for t in range(KPAD // KBLK):
            lanes = slice(t * KBLK, (t + 1) * KBLK)
            back = KPAD - (t + 1) * KBLK
            mirror[:, back : back + KBLK] = nn_dot(en_hi[:, lanes], flip_ref[...]) + nn_dot(en_lo[:, lanes], flip_ref[...])

        quarter = own_points(points_ref, r2) // 4
        lane = iota((rows, BUF), 1)
        shift = (quarter + (BUF - (KPAD - 1))) % BUF
        flat[:rows, :] = jnp.where(lane <= quarter // 2, flat[:rows, :], pltpu.roll(mirror[...], shift, 1))
        line[...] = jnp.zeros_like(line)
        lane = iota((plev, BUF), 1)
        for b in range(4):
            start = quarter * b
            inner = start % 128
            base = pl.multiple_of(start - inner, 128)
            piece = pltpu.roll(flat[b * plev : (b + 1) * plev, :], inner, 1)
            old = line[:, pl.ds(base, BUF)]
            line[:, pl.ds(base, BUF)] = jnp.where((lane >= inner) & (lane < inner + quarter), piece, old)
        out_ref[:, pl.ds(r2, 1), :] = line[:, :ROWPAD].reshape(plev, 1, ROWPAD)


def synthesis(moved, slot_map, table_hi, table_lo, row_points):
    plev = moved.shape[1]
    wide = plev * 2 * PART
    vmem = pl.BlockSpec(memory_space=pltpu.VMEM)
    return pl.pallas_call(
        synth_kernel,
        out_shape=jax.ShapeDtypeStruct((plev, 2, ROWPAD), F32),
        in_specs=[pl.BlockSpec(memory_space=pltpu.SMEM)] + [vmem] * 5 + [pl.BlockSpec(memory_space=pltpu.HBM)] * 2,
        out_specs=vmem,
        scratch_shapes=[
            pltpu.VMEM((M, M), BF16),
            pltpu.VMEM((2, KPTS, 2 * M), BF16),
            pltpu.VMEM((2, KPTS, 2 * M), FP8),
            pltpu.VMEM((M, 2 * wide), BF16),
            pltpu.VMEM((2, 2, M, 2 * wide), BF16),
            pltpu.VMEM((2, 2, M, wide), FP8),
            pltpu.VMEM((8 * plev, BUF), F32),
            pltpu.VMEM((4 * plev, BUF), F32),
            pltpu.VMEM((plev, 3 * 1280 + BUF), F32),
            pltpu.SemaphoreType.DMA((2, 2, TABLE_CUTS)),
        ],
        compiler_params=pltpu.CompilerParams(vmem_limit_bytes=44 * MIB),
        cost_estimate=pl.CostEstimate(flops=2 * 2 * KPTS * 2 * M * 384, bytes_accessed=2 * KPTS * 2 * M * 4 + M * M * 2, transcendentals=0),
        name="synthesis",
    )(
        pltpu.with_memory_space_constraint(row_points, pltpu.HBM),
        pltpu.with_memory_space_constraint(moved, pltpu.VMEM), slot_map,
        pick_tables(plev), mean_table(plev), flip_table(),
        *[pltpu.with_memory_space_constraint(x, pltpu.HBM) for x in (table_hi, table_lo)],
    )


def join_kernel(*refs):
    parts = (len(refs) - 1) // 2
    at = 0
    for own_ref, other_ref in zip(refs[:parts], refs[parts:-1]):
        rows = own_ref.shape[1]
        refs[-1][:, at : at + rows, :] = own_ref[...] + other_ref[...]
        at += rows


def join(owns, others):
    rows = sum(x.shape[1] for x in owns)
    vmem = pl.BlockSpec(memory_space=pltpu.VMEM)
    return pl.pallas_call(
        join_kernel,
        out_shape=jax.ShapeDtypeStruct((owns[0].shape[0], rows, SQ * PART), F32),
        in_specs=[vmem] * (2 * len(owns)),
        out_specs=vmem,
        compiler_params=pltpu.CompilerParams(vmem_limit_bytes=32 * MIB),
        name="join",
    )(*[pltpu.with_memory_space_constraint(x, pltpu.VMEM) for x in owns + others])


def local(spectral, legendre, wave_map, row_points, brackets, lev_weight, climatology):
    slots = spectral.shape[0]
    half = legendre.shape[1]
    groups = slots // SQ
    wave_count = lax.axis_size("wave")
    lev_count = lax.axis_size("lev")
    rows_dev = 2 * half // (wave_count * lev_count)
    pairs = [(d, d - 1) for d in range(1, lev_count)]
    map_rows = wave_map.reshape(M // 128, 128)
    own, prev, between = legendre_sums(spectral, legendre, map_rows, brackets, lev_weight)
    sent = lax.switch(
        between[0],
        [
            lambda mine, theirs: join([mine], [lax.ppermute(theirs, "lev", pairs[::2])]),
            lambda mine, theirs: join([mine], [lax.ppermute(theirs, "lev", pairs)]),
        ],
        own,
        prev,
    )
    moved = lax.all_to_all(sent, ("wave", "lev"), split_axis=0, concat_axis=0, tiled=True)
    moved = moved.reshape(wave_count, lev_count, rows_dev * groups, SQ * PART)
    table_points, _ = lax.optimization_barrier((row_points, sent))
    table_hi, table_lo, sorted_map = tables(table_points, map_rows)
    slot_map = jnp.transpose(sorted_map.reshape(wave_count, SQ, groups), (1, 0, 2)).reshape(1, M)
    energy = synthesis(moved, slot_map, table_hi, table_lo, row_points)
    result = lax.all_to_all(energy, "lev", split_axis=0, concat_axis=0, tiled=True)
    result = result.reshape(1, rows_dev * lev_count, ROWPAD)
    points_all = jnp.concatenate([row_points, row_points])
    band_rows = rows_dev * lev_count
    out_points = lax.dynamic_slice_in_dim(points_all, lax.axis_index("wave") * band_rows, band_rows, 0)
    places = jnp.arange(ROWPAD, dtype=jnp.int32)
    inside = places[None, None, :] < out_points[None, :, None]
    return jnp.where(inside, result - climatology, 0.0)


def solution(mesh):
    placed = (
        P("wave", "lev", None),
        P("wave", None, None),
        P(),
        P(),
        P(),
        P(),
        P("lev", "wave", None),
    )
    return jax.shard_map(
        local, mesh=mesh, in_specs=placed, out_specs=P("lev", "wave", None), check_vma=False
    )
```

```python
import functools
import math

import jax
import jax.numpy as jnp
import numpy as np
from jax import lax
from jax.experimental import pallas as pl
from jax.experimental.pallas import tpu as pltpu
from jax.sharding import PartitionSpec as P

M = 1280
NT = 1280
LEV_DEV = 4
STEPS = 4
FIELDS = 2
ROWPAD = 5248

FS = FIELDS * STEPS
PART = 2 * FS
SQ = 8
STEP = 16
CHUNK = 256
DEPTH = 3
HALF_M = M // 2
KPTS = 672
KPAD = 768
KBLK = 256
TABLE_STEPS = 7
TABLE_CUTS = 3
BUF = 1536
MIB = 1024 * 1024
F32 = jnp.float32
BF16 = jnp.bfloat16
FP8 = jnp.float8_e4m3fn
REST_SCALE = 256.0


def iota(shape, dim):
    return lax.broadcasted_iota(jnp.int32, shape, dim)


def waves_of(map_ref, wave, slots):
    start = wave * slots
    row = start // 128
    last = map_ref.shape[0] - 1
    pair = jnp.concatenate([map_ref[pl.ds(row, 1), :], map_ref[pl.ds(jnp.minimum(row + 1, last), 1), :]], axis=1)
    pair = jnp.broadcast_to(pair, (8, 256)).astype(F32)
    turned = pltpu.roll(pair, (256 - start % 128) % 256, 1)
    return jnp.where(iota((8, 256), 1) < slots, turned, 4096.0)[:1]


def ranks_of(waves):
    lane = iota((1, 256), 1)
    keys = jnp.where(lane < STEP, (lane - STEP).astype(F32), waves)
    across = jnp.broadcast_to(keys, (256, 256))
    rank = jnp.sum(jnp.where(across < across.T, 1.0, 0.0), axis=1, keepdims=True)
    return rank, jnp.broadcast_to(waves, (256, 256)).T


def legendre_kernel(
    brackets, weight_ref, map_ref, spec_hbm, leg_hbm, own_ref, prev_ref, between_ref,
    spec_buf, leg_buf, own_rows, prev_rows, order_vmem, order, order_sem, sems,
):
    slots, half, _ = leg_hbm.shape
    groups = slots // SQ
    steps = slots // STEP
    wave = lax.axis_index("wave")
    lev = lax.axis_index("lev")
    lower = brackets[lev] - lev * LEV_DEV
    has_upper = lower < LEV_DEV - 1
    w = weight_ref[lev]
    upper_w = jnp.where(has_upper, 1.0 - w, 0.0)
    low_rows = pl.ds(pl.multiple_of(lower * PART, PART), PART)
    up_rows = pl.ds(pl.multiple_of(jnp.minimum(lower + 1, LEV_DEV - 1) * PART, PART), PART)
    before = jnp.maximum(lev - 1, 0)
    crosses = (lev > 0) & (brackets[before] == lev * LEV_DEV - 1)
    first_w = jnp.where(crosses, 1.0 - weight_ref[before], 0.0)
    degree = iota((16, NT), 1).astype(jnp.int16)
    sign = (1 - 2 * (iota((16, NT), 1) % 2)).astype(F32).astype(BF16)
    lane_group = iota((1, 192), 1) % 64 // PART
    left = iota((1, SQ * PART), 1) < 64
    south = iota((2 * half, 1), 0) >= half

    def buffers(slot, c):
        lanes = pl.ds(c * CHUNK, NT - c * CHUNK)
        return [
            (leg_hbm.at[:, :, lanes], leg_buf.at[slot, :, :, lanes], sems.at[slot, 0]),
            (spec_hbm.at[:, :, lanes], spec_buf.at[slot, :, :, lanes], sems.at[slot, 1]),
        ]

    for src, dst, sem in buffers(0, 0):
        pltpu.make_async_copy(src.at[pl.ds(0, STEP)], dst, sem).start()

    rank, down = ranks_of(waves_of(map_ref, wave, slots))
    hit = rank == iota((256, 256), 1).astype(F32)
    slot_at = jnp.sum(jnp.where(hit, iota((256, 256), 0).astype(F32), 0.0), axis=0, keepdims=True)
    wave_at = jnp.sum(jnp.where(hit, down, 0.0), axis=0, keepdims=True)
    order_vmem[0:1, :] = slot_at.astype(jnp.int32)
    order_vmem[1:2, :] = wave_at.astype(jnp.int32)
    to_smem = pltpu.make_async_copy(order_vmem, order, order_sem)
    to_smem.start()
    to_smem.wait()

    def wave_chunk(step):
        return jnp.where(step == 0, 0, order[1, step * STEP] // CHUNK)

    def fetch(step):
        chunk = wave_chunk(step)
        for c in range(NT // CHUNK):

            @pl.when(chunk == c)
            def _():
                for i in range(STEP):
                    at = order[0, step * STEP + i]
                    for src, dst, sem in buffers(step % DEPTH, c):
                        pltpu.make_async_copy(src.at[at], dst.at[i], sem).start()

    for step in range(1, DEPTH - 1):
        fetch(step)
    between = jnp.int32(0)
    for p in range(1, brackets.shape[0] - 1, 2):
        between = between | (brackets[p] == (p + 1) * LEV_DEV - 1).astype(jnp.int32)
    between_ref[0] = between

    def multiply(step, c):
        slot = step % DEPTH
        lanes = slice(c * CHUNK, NT)
        for src, dst, sem in buffers(slot, c):
            pltpu.make_async_copy(src.at[pl.ds(0, STEP)], dst, sem).wait()
        for b in range(STEP // SQ):
            owns, firsts = [], []
            for quad in range(2):
                values, factors, columns = [], [], [[], [], []]
                for i in range(b * SQ + 4 * quad, b * SQ + 4 * quad + 4):
                    m = order[1, step * STEP + i]
                    kept = degree[:, lanes] >= m.astype(jnp.int16)
                    plain = [jnp.where(kept, leg_buf[slot, i, r : r + 16, lanes], 0) for r in range(0, half, 16)]
                    values += plain + [x * sign[:, lanes] for x in plain]
                    factors.append(jnp.where(south, (1 - 2 * (m % 2)).astype(F32), 1.0))
                    columns[quad].append(spec_buf[slot, i, low_rows, lanes])
                    columns[1 - quad].append(spec_buf[slot, i, up_rows, lanes])
                    columns[2].append(spec_buf[slot, i, :PART, lanes])
                sums = nt_dot(jnp.concatenate(values, axis=0), jnp.concatenate(columns[0] + columns[1] + columns[2], axis=0))
                kept_sums = sums[: 2 * half] * factors[0]
                for a in range(1, 4):
                    block = sums[2 * half * a : 2 * half * (a + 1)] * factors[a]
                    kept_sums = jnp.where(lane_group == a, block, kept_sums)
                both = kept_sums[:, :128]
                owns.append(both * w + pltpu.roll(both, 64, 1) * upper_w)
                firsts.append(jnp.concatenate([kept_sums[:, 128:]] * 2, axis=1))
            at = pl.multiple_of((step * (STEP // SQ) + b) * 2 * half, 2 * half)
            own_rows[pl.ds(at, 2 * half), :] = jnp.where(left, owns[0], owns[1])
            prev_rows[pl.ds(at, 2 * half), :] = jnp.where(left, firsts[0], firsts[1]) * first_w

    def step_body(step, carry):
        @pl.when(step + DEPTH - 1 < steps)
        def _():
            fetch(step + DEPTH - 1)

        chunk = wave_chunk(step)
        for c in range(NT // CHUNK):
            pl.when(chunk == c)(functools.partial(multiply, step, c))
        return carry

    lax.fori_loop(0, steps, step_body, 0)
    rows = 2 * half
    for rows_ref, ref in ((own_rows, own_ref), (prev_rows, prev_ref)):
        rows_dev = ref.shape[1] // groups
        for r in range(rows):
            at = (r % rows_dev) * groups
            ref[r // rows_dev, at : at + groups, :] = rows_ref[pl.ds(r, groups, stride=rows), :]


def legendre_sums(spectral, legendre, map_rows, brackets, lev_weight):
    slots = spectral.shape[0]
    half = legendre.shape[1]
    groups = slots // SQ
    devices = lax.axis_size("wave") * lax.axis_size("lev")
    out = pltpu.VMEM((devices, 2 * half // devices * groups, SQ * PART), F32)
    smem = pl.BlockSpec(memory_space=pltpu.SMEM)
    vmem = pl.BlockSpec(memory_space=pltpu.VMEM)
    hbm = pl.BlockSpec(memory_space=pltpu.HBM)
    return pl.pallas_call(
        legendre_kernel,
        out_shape=[out, out, jax.ShapeDtypeStruct((1,), jnp.int32)],
        in_specs=[smem, smem, vmem, hbm, hbm],
        out_specs=[vmem, vmem, smem],
        scratch_shapes=[
            pltpu.VMEM((DEPTH, STEP, LEV_DEV * PART, NT), BF16),
            pltpu.VMEM((DEPTH, STEP, half, NT), BF16),
            pltpu.VMEM((groups * 2 * half, SQ * PART), F32),
            pltpu.VMEM((groups * 2 * half, SQ * PART), F32),
            pltpu.VMEM((2, 256), jnp.int32),
            pltpu.SMEM((2, 256), jnp.int32),
            pltpu.SemaphoreType.DMA,
            pltpu.SemaphoreType.DMA((DEPTH, 2)),
        ],
        compiler_params=pltpu.CompilerParams(vmem_limit_bytes=48 * MIB),
        cost_estimate=pl.CostEstimate(flops=2 * slots * 2 * half * 48 * NT, bytes_accessed=slots * NT * 2 * (48 + half), transcendentals=0),
        name="legendre_sums",
    )(*[pltpu.with_memory_space_constraint(x, pltpu.HBM) for x in (brackets, lev_weight, map_rows, spectral, legendre)])


def unit_circle(product, points, inverse):
    big = 12582912.0
    turn = (product * inverse + big) - big
    x = (product - turn * points) * (math.pi * inverse)
    x2 = x * x
    sine = 0.0
    cosine = 0.0
    for power in (11, 9, 7, 5, 3, 1):
        sine = sine * x2 + (-1) ** (power // 2) / math.factorial(power)
    for power in (12, 10, 8, 6, 4, 2, 0):
        cosine = cosine * x2 + (-1) ** (power // 2) / math.factorial(power)
    sine = sine * x
    twice = sine + sine
    return 1.0 - twice * sine, twice * cosine


def own_points(points_ref, r2):
    wave = lax.axis_index("wave")
    lev = lax.axis_index("lev")
    row = 2 * (wave * lax.axis_size("lev") + lev) + r2
    return points_ref[row % points_ref.shape[0]]


def table_kernel(points_ref, map_ref, hi_ref, lo_ref, sorted_ref):
    r2 = pl.program_id(0)
    kb = pl.program_id(1)
    rows = hi_ref.shape[1]
    points = own_points(points_ref, r2).astype(F32)
    inverse = 1.0 / points

    @pl.when((r2 == 0) & (kb == 0))
    def _():
        waves, slots = sorted_ref.shape
        for wave in range(waves):
            rank, down = ranks_of(waves_of(map_ref, wave, slots))
            whole = jnp.floor((rank + 0.5) * (1.0 / SQ))
            place = (rank - whole * SQ) * (slots // SQ) + whole
            hit = (place == iota((256, 256), 1).astype(F32)) & (rank < slots)
            row = jnp.sum(jnp.where(hit, down, 0.0), axis=0, keepdims=True)
            sorted_ref[wave : wave + 1, :] = row[:, :slots].astype(jnp.int32)

    lane = iota((32, 128), 1).astype(F32)

    def chunk_body(i, carry):
        chunk = pl.multiple_of(i * 32, 32)

        def put(tile, value):
            lanes = slice(tile * 128, tile * 128 + 128)
            hi = value.astype(BF16)
            hi_ref[0, pl.ds(chunk, 32), lanes] = hi
            lo_ref[0, pl.ds(chunk, 32), lanes] = ((value - hi.astype(F32)) * REST_SCALE).astype(FP8)

        k = (kb * rows + chunk + iota((32, 128), 0)).astype(F32)
        c, s = unit_circle(2.0 * lane * k, points, inverse)
        c1, s1 = unit_circle(k, points, inverse)
        ct, st = unit_circle(256.0 * k, points, inverse)
        co = c * c1 - s * s1
        so = s * c1 + c * s1
        for t in range(HALF_M // 128):
            if t:
                c, s = c * ct - s * st, s * ct + c * st
                co, so = co * ct - so * st, so * ct + co * st
            put(t, c)
            put(5 + t, s)
            put(10 + t, co)
            put(15 + t, so)
        return carry

    lax.fori_loop(0, rows // 32, chunk_body, 0, unroll=True)


def tables(row_points, map_rows):
    waves = lax.axis_size("wave")
    rows = KPTS // TABLE_STEPS
    table = pltpu.HBM((2, KPTS, 2 * M), BF16)
    table_spec = pl.BlockSpec((1, rows, 2 * M), lambda r, k: (r, k, 0))
    return pl.pallas_call(
        table_kernel,
        out_shape=[table, pltpu.HBM((2, KPTS, 2 * M), FP8), jax.ShapeDtypeStruct((waves, M // waves), jnp.int32)],
        grid=(2, TABLE_STEPS),
        in_specs=[pl.BlockSpec(memory_space=pltpu.SMEM), pl.BlockSpec(memory_space=pltpu.VMEM)],
        out_specs=[table_spec, table_spec, pl.BlockSpec(memory_space=pltpu.VMEM)],
        compiler_params=pltpu.CompilerParams(vmem_limit_bytes=48 * MIB),
        cost_estimate=pl.CostEstimate(flops=2 * KPTS * 2 * M * 12, bytes_accessed=2 * KPTS * 2 * M * 4, transcendentals=0),
        name="fourier_tables",
    )(*[pltpu.with_memory_space_constraint(x, pltpu.HBM) for x in (row_points, map_rows)])


def pick_tables(plev):
    wide = plev * 2 * PART
    out = np.zeros((2, 4, 2 * wide, 2 * wide), np.float32)
    plans = (
        ((0, 1), (0, 1), (0, 1), (0, 1)),
        ((1, -1), (1, 1), (1, -1), (1, 1)),
        ((0, 1), (0, 1), (1, -1), (1, -1)),
        ((1, -1), (1, 1), (0, -1), (0, 1)),
    )
    for r2 in range(2):
        for kind, plan in enumerate(plans):
            for image, (part, sgn) in enumerate(plan):
                for hl in range(2):
                    for p in range(plev):
                        for q in range(FS):
                            src = hl * wide + p * 2 * PART + r2 * PART + q * 2 + part
                            dst = hl * wide + image * plev * FS + p * FS + q
                            out[r2, kind, src, dst] = sgn
    return out.astype(jnp.bfloat16)


def mean_table(plev):
    wide = plev * FS * 4
    out = np.zeros((2 * 4 * plev, 2 * wide), np.float32)
    for quarter in range(4):
        for p in range(plev):
            for part in range(2):
                image_quarter = (quarter + part) % 4
                start = (image_quarter * 2 + part) * plev * FS + p * FS
                out[part * 4 * plev + quarter * plev + p, start : start + FS] = 0.5 / STEPS
    return out.astype(jnp.bfloat16)


def flip_table():
    return np.fliplr(np.eye(KBLK, dtype=np.float32)).astype(jnp.bfloat16)


def split(x):
    hi = x.astype(BF16)
    return hi, (x - hi.astype(F32)).astype(BF16)


def nt_dot(a, b):
    return lax.dot_general(a, b, (((1,), (1,)), ((), ())), preferred_element_type=F32)


def nn_dot(a, b):
    return jnp.dot(a, b, preferred_element_type=F32)


def synth_kernel(points_ref, *refs):
    moved_ref, map_ref, pick_ref, mean_ref, flip_ref, hi_hbm, lo_hbm, out_ref = refs[:8]
    perm_ref, hi_ref, lo_ref, mixed, coef, coef8, flat, mirror, line, sems = refs[8:]
    table_copies = []
    for r2 in range(2):
        table_copies.append([])
        for i, (src, dst) in enumerate(((hi_hbm, hi_ref), (lo_hbm, lo_ref))):
            for c in range(TABLE_CUTS):
                rows = pl.ds(c * (KPTS // TABLE_CUTS), KPTS // TABLE_CUTS)
                table_copies[r2].append(pltpu.make_async_copy(src.at[r2, rows], dst.at[r2, rows], sems.at[r2, i, c]))
    for copy in table_copies[0] + table_copies[1]:
        copy.start()

    slot_waves = jnp.broadcast_to(map_ref[...], (16, M)).astype(jnp.int16)

    def perm_body(i, carry):
        row = pl.multiple_of(i * 16, 16)
        order = row + iota((16, M), 0)
        wanted = jnp.where(row < HALF_M, 2 * order, 2 * (order - HALF_M) + 1).astype(jnp.int16)
        perm_ref[pl.ds(row, 16), :] = jnp.where(slot_waves == wanted, 1.0, 0.0).astype(BF16)
        return carry

    lax.fori_loop(0, M // 16, perm_body, 0, unroll=4)
    waves, plev, _, _ = moved_ref.shape
    wide = plev * 2 * PART
    part_rows = M // SQ
    for base in range(0, plev * 2, 8):
        cur = []
        for g in range(base, base + 8):
            sub = moved_ref.shape[2] // 2
            pieces = [moved_ref[w, g // 2, (g % 2) * sub : (g % 2 + 1) * sub, :] for w in range(waves)]
            cur.append(jnp.concatenate(pieces, axis=0))
        group = iota((part_rows, 128), 1) // PART
        for bit in (1, 2, 4):
            unset = (group & bit) == 0
            nxt = list(cur)
            for g in range(8):
                if g & bit == 0:
                    a, b = cur[g], cur[g + bit]
                    nxt[g] = jnp.where(unset, a, pltpu.roll(b, bit * PART, 1))
                    nxt[g + bit] = jnp.where(unset, pltpu.roll(a, 128 - bit * PART, 1), b)
            cur = nxt
        for sq in range(SQ):
            hi, lo = split(cur[sq])
            lane = base * PART
            mixed[sq * part_rows : (sq + 1) * part_rows, lane : lane + 128] = hi
            mixed[sq * part_rows : (sq + 1) * part_rows, wide + lane : wide + lane + 128] = lo

    lane_row = (iota((1, 2 * wide), 1) // PART) % 2
    limit0 = (own_points(points_ref, 0) - 1) // 2
    limit1 = (own_points(points_ref, 1) - 1) // 2
    limit = jnp.where(lane_row == 0, limit0, limit1)
    place = iota((HALF_M, 1), 0)
    turned = (iota((1, 2 * wide), 1) % wide) // (plev * FS) >= 2
    flip_sign = jnp.where(turned & (place % 2 == 1), -1.0, 1.0).astype(BF16)
    for odd in range(2):
        ordered = nn_dot(perm_ref[odd * HALF_M : (odd + 1) * HALF_M, :], mixed[...])
        wave = 2 * place + odd
        factor = jnp.where(wave <= limit, jnp.where(wave == 0, 1.0, 2.0), 0.0)
        ordered = (ordered * factor).astype(BF16)
        for row in range(2):
            for part in range(2):
                picked = nn_dot(ordered, pick_ref[row, odd * 2 + part]).astype(BF16)
                picked = picked * flip_sign
                coef[row, odd, part * HALF_M : (part + 1) * HALF_M, :] = picked
                coef8[row, odd, part * HALF_M : (part + 1) * HALF_M, :] = picked[:, :wide].astype(F32).astype(FP8)
    flat[...] = jnp.zeros_like(flat)
    mirror[...] = jnp.zeros_like(mirror)

    row_sums = []
    for r2 in range(2):
        for copy in table_copies[r2]:
            copy.wait()

        def contraction(odd):
            lanes = slice(odd * M, (odd + 1) * M)
            both = nn_dot(hi_ref[r2, :, lanes], coef[r2, odd])
            rest = nn_dot(lo_ref[r2, :, lanes], coef8[r2, odd])
            return both[:, :wide] + (both[:, wide:] + rest * (1.0 / REST_SCALE))

        row_sums.append((contraction(0), contraction(1)))

    for r2 in range(2):
        even_sum, odd_sum = row_sums[r2]
        plus = even_sum + odd_sum
        minus = even_sum - odd_sum
        squares = jnp.concatenate([plus * plus, minus * minus], axis=1)
        sq_hi, sq_lo = split(squares)
        energy = nt_dot(mean_ref[...], sq_hi) + nt_dot(mean_ref[...], sq_lo)
        rows = 4 * plev
        flat[:, :KPTS] = energy
        en_hi, en_lo = split(flat[rows:, :KPAD])
        for t in range(KPAD // KBLK):
            lanes = slice(t * KBLK, (t + 1) * KBLK)
            back = KPAD - (t + 1) * KBLK
            mirror[:, back : back + KBLK] = nn_dot(en_hi[:, lanes], flip_ref[...]) + nn_dot(en_lo[:, lanes], flip_ref[...])

        quarter = own_points(points_ref, r2) // 4
        lane = iota((rows, BUF), 1)
        shift = (quarter + (BUF - (KPAD - 1))) % BUF
        flat[:rows, :] = jnp.where(lane <= quarter // 2, flat[:rows, :], pltpu.roll(mirror[...], shift, 1))
        line[...] = jnp.zeros_like(line)
        lane = iota((plev, BUF), 1)
        for b in range(4):
            start = quarter * b
            inner = start % 128
            base = pl.multiple_of(start - inner, 128)
            piece = pltpu.roll(flat[b * plev : (b + 1) * plev, :], inner, 1)
            old = line[:, pl.ds(base, BUF)]
            line[:, pl.ds(base, BUF)] = jnp.where((lane >= inner) & (lane < inner + quarter), piece, old)
        out_ref[:, pl.ds(r2, 1), :] = line[:, :ROWPAD].reshape(plev, 1, ROWPAD)


def synthesis(moved, slot_map, table_hi, table_lo, row_points):
    plev = moved.shape[1]
    wide = plev * 2 * PART
    vmem = pl.BlockSpec(memory_space=pltpu.VMEM)
    return pl.pallas_call(
        synth_kernel,
        out_shape=jax.ShapeDtypeStruct((plev, 2, ROWPAD), F32),
        in_specs=[pl.BlockSpec(memory_space=pltpu.SMEM)] + [vmem] * 5 + [pl.BlockSpec(memory_space=pltpu.HBM)] * 2,
        out_specs=vmem,
        scratch_shapes=[
            pltpu.VMEM((M, M), BF16),
            pltpu.VMEM((2, KPTS, 2 * M), BF16),
            pltpu.VMEM((2, KPTS, 2 * M), FP8),
            pltpu.VMEM((M, 2 * wide), BF16),
            pltpu.VMEM((2, 2, M, 2 * wide), BF16),
            pltpu.VMEM((2, 2, M, wide), FP8),
            pltpu.VMEM((8 * plev, BUF), F32),
            pltpu.VMEM((4 * plev, BUF), F32),
            pltpu.VMEM((plev, 3 * 1280 + BUF), F32),
            pltpu.SemaphoreType.DMA((2, 2, TABLE_CUTS)),
        ],
        compiler_params=pltpu.CompilerParams(vmem_limit_bytes=44 * MIB),
        cost_estimate=pl.CostEstimate(flops=2 * 2 * KPTS * 2 * M * 384, bytes_accessed=2 * KPTS * 2 * M * 4 + M * M * 2, transcendentals=0),
        name="synthesis",
    )(
        pltpu.with_memory_space_constraint(row_points, pltpu.HBM),
        pltpu.with_memory_space_constraint(moved, pltpu.VMEM), slot_map,
        pick_tables(plev), mean_table(plev), flip_table(),
        *[pltpu.with_memory_space_constraint(x, pltpu.HBM) for x in (table_hi, table_lo)],
    )


def join_kernel(*refs):
    parts = (len(refs) - 1) // 2
    at = 0
    for own_ref, other_ref in zip(refs[:parts], refs[parts:-1]):
        rows = own_ref.shape[1]
        refs[-1][:, at : at + rows, :] = own_ref[...] + other_ref[...]
        at += rows


def join(owns, others):
    rows = sum(x.shape[1] for x in owns)
    vmem = pl.BlockSpec(memory_space=pltpu.VMEM)
    return pl.pallas_call(
        join_kernel,
        out_shape=jax.ShapeDtypeStruct((owns[0].shape[0], rows, SQ * PART), F32),
        in_specs=[vmem] * (2 * len(owns)),
        out_specs=vmem,
        compiler_params=pltpu.CompilerParams(vmem_limit_bytes=32 * MIB),
        name="join",
    )(*[pltpu.with_memory_space_constraint(x, pltpu.VMEM) for x in owns + others])


def local(spectral, legendre, wave_map, row_points, brackets, lev_weight, climatology):
    slots = spectral.shape[0]
    half = legendre.shape[1]
    groups = slots // SQ
    wave_count = lax.axis_size("wave")
    lev_count = lax.axis_size("lev")
    rows_dev = 2 * half // (wave_count * lev_count)
    pairs = [(d, d - 1) for d in range(1, lev_count)]
    map_rows = wave_map.reshape(M // 128, 128)
    own, prev, between = legendre_sums(spectral, legendre, map_rows, brackets, lev_weight)
    sent = lax.switch(
        between[0],
        [
            lambda mine, theirs: join([mine], [lax.ppermute(theirs, "lev", pairs[::2])]),
            lambda mine, theirs: join([mine], [lax.ppermute(theirs, "lev", pairs)]),
        ],
        own,
        prev,
    )
    moved = lax.all_to_all(sent, ("wave", "lev"), split_axis=0, concat_axis=0, tiled=True)
    moved = moved.reshape(wave_count, lev_count, rows_dev * groups, SQ * PART)
    table_points, _ = lax.optimization_barrier((row_points, sent))
    table_hi, table_lo, sorted_map = tables(table_points, map_rows)
    slot_map = jnp.transpose(sorted_map.reshape(wave_count, SQ, groups), (1, 0, 2)).reshape(1, M)
    energy = synthesis(moved, slot_map, table_hi, table_lo, row_points)
    result = lax.all_to_all(energy, "lev", split_axis=0, concat_axis=0, tiled=True)
    result = result.reshape(1, rows_dev * lev_count, ROWPAD)
    points_all = jnp.concatenate([row_points, row_points])
    band_rows = rows_dev * lev_count
    out_points = lax.dynamic_slice_in_dim(points_all, lax.axis_index("wave") * band_rows, band_rows, 0)
    places = jnp.arange(ROWPAD, dtype=jnp.int32)
    inside = places[None, None, :] < out_points[None, :, None]
    return jnp.where(inside, result - climatology, 0.0)


def solution(mesh):
    placed = (
        P("wave", "lev", None),
        P("wave", None, None),
        P(),
        P(),
        P(),
        P(),
        P("lev", "wave", None),
    )
    return jax.shard_map(
        local, mesh=mesh, in_specs=placed, out_specs=P("lev", "wave", None), check_vma=False
    )
```

```python
import functools
import math

import jax
import jax.numpy as jnp
import numpy as np
from jax import lax
from jax.experimental import pallas as pl
from jax.experimental.pallas import tpu as pltpu
from jax.sharding import PartitionSpec as P

M = 1280
NT = 1280
LEV_DEV = 4
STEPS = 4
FIELDS = 2
ROWPAD = 5248

FS = FIELDS * STEPS
PART = 2 * FS
SQ = 8
STEP = 16
CHUNK = 256
DEPTH = 4
HALF_M = M // 2
KPTS = 672
KPAD = 768
KBLK = 256
TABLE_STEPS = 7
TABLE_CUTS = 3
BUF = 1536
MIB = 1024 * 1024
F32 = jnp.float32
BF16 = jnp.bfloat16
FP8 = jnp.float8_e4m3fn
REST_SCALE = 256.0


def iota(shape, dim):
    return lax.broadcasted_iota(jnp.int32, shape, dim)


def waves_of(map_ref, wave, slots):
    start = wave * slots
    row = start // 128
    last = map_ref.shape[0] - 1
    pair = jnp.concatenate([map_ref[pl.ds(row, 1), :], map_ref[pl.ds(jnp.minimum(row + 1, last), 1), :]], axis=1)
    pair = jnp.broadcast_to(pair, (8, 256)).astype(F32)
    turned = pltpu.roll(pair, (256 - start % 128) % 256, 1)
    return jnp.where(iota((8, 256), 1) < slots, turned, 4096.0)[:1]


def ranks_of(waves):
    lane = iota((1, 256), 1)
    keys = jnp.where(lane < STEP, (lane - STEP).astype(F32), waves)
    across = jnp.broadcast_to(keys, (256, 256))
    rank = jnp.sum(jnp.where(across < across.T, 1.0, 0.0), axis=1, keepdims=True)
    return rank, jnp.broadcast_to(waves, (256, 256)).T


def legendre_kernel(
    brackets, weight_ref, map_ref, spec_hbm, leg_hbm, own_ref, prev_ref, between_ref,
    spec_buf, leg_buf, own_rows, prev_rows, order_vmem, order, order_sem, sems,
):
    slots, half, _ = leg_hbm.shape
    groups = slots // SQ
    steps = slots // STEP
    wave = lax.axis_index("wave")
    lev = lax.axis_index("lev")
    lower = brackets[lev] - lev * LEV_DEV
    has_upper = lower < LEV_DEV - 1
    w = weight_ref[lev]
    upper_w = jnp.where(has_upper, 1.0 - w, 0.0)
    low_rows = pl.ds(pl.multiple_of(lower * PART, PART), PART)
    up_rows = pl.ds(pl.multiple_of(jnp.minimum(lower + 1, LEV_DEV - 1) * PART, PART), PART)
    before = jnp.maximum(lev - 1, 0)
    crosses = (lev > 0) & (brackets[before] == lev * LEV_DEV - 1)
    first_w = jnp.where(crosses, 1.0 - weight_ref[before], 0.0)
    degree = iota((16, NT), 1).astype(jnp.int16)
    sign = (1 - 2 * (iota((16, NT), 1) % 2)).astype(F32).astype(BF16)
    lane_group = iota((1, 192), 1) % 64 // PART
    left = iota((1, SQ * PART), 1) < 64
    south = iota((2 * half, 1), 0) >= half

    def buffers(slot, c):
        lanes = pl.ds(c * CHUNK, NT - c * CHUNK)
        return [
            (leg_hbm.at[:, :, lanes], leg_buf.at[slot, :, :, lanes], sems.at[slot, 0]),
            (spec_hbm.at[:, :, lanes], spec_buf.at[slot, :, :, lanes], sems.at[slot, 1]),
        ]

    for src, dst, sem in buffers(0, 0):
        pltpu.make_async_copy(src.at[pl.ds(0, STEP)], dst, sem).start()

    rank, down = ranks_of(waves_of(map_ref, wave, slots))
    hit = rank == iota((256, 256), 1).astype(F32)
    slot_at = jnp.sum(jnp.where(hit, iota((256, 256), 0).astype(F32), 0.0), axis=0, keepdims=True)
    wave_at = jnp.sum(jnp.where(hit, down, 0.0), axis=0, keepdims=True)
    order_vmem[0:1, :] = slot_at.astype(jnp.int32)
    order_vmem[1:2, :] = wave_at.astype(jnp.int32)
    to_smem = pltpu.make_async_copy(order_vmem, order, order_sem)
    to_smem.start()
    to_smem.wait()

    def wave_chunk(step):
        return jnp.where(step == 0, 0, order[1, step * STEP] // CHUNK)

    def fetch(step):
        chunk = wave_chunk(step)
        for c in range(NT // CHUNK):

            @pl.when(chunk == c)
            def _():
                for i in range(STEP):
                    at = order[0, step * STEP + i]
                    for src, dst, sem in buffers(step % DEPTH, c):
                        pltpu.make_async_copy(src.at[at], dst.at[i], sem).start()

    def early_fetch(step, carry):
        fetch(step)
        return carry

    lax.fori_loop(1, DEPTH - 1, early_fetch, 0)
    between = jnp.int32(0)
    for p in range(1, brackets.shape[0] - 1, 2):
        between = between | (brackets[p] == (p + 1) * LEV_DEV - 1).astype(jnp.int32)
    between_ref[0] = between

    def multiply(step, c):
        slot = step % DEPTH
        lanes = slice(c * CHUNK, NT)
        for src, dst, sem in buffers(slot, c):
            pltpu.make_async_copy(src.at[pl.ds(0, STEP)], dst, sem).wait()
        for b in range(STEP // SQ):
            owns, firsts = [], []
            for quad in range(2):
                values, factors, columns = [], [], [[], [], []]
                for i in range(b * SQ + 4 * quad, b * SQ + 4 * quad + 4):
                    m = order[1, step * STEP + i]
                    kept = degree[:, lanes] >= m.astype(jnp.int16)
                    plain = [jnp.where(kept, leg_buf[slot, i, r : r + 16, lanes], 0) for r in range(0, half, 16)]
                    values += plain + [x * sign[:, lanes] for x in plain]
                    factors.append(jnp.where(south, (1 - 2 * (m % 2)).astype(F32), 1.0))
                    columns[quad].append(spec_buf[slot, i, low_rows, lanes])
                    columns[1 - quad].append(spec_buf[slot, i, up_rows, lanes])
                    columns[2].append(spec_buf[slot, i, :PART, lanes])
                sums = nt_dot(jnp.concatenate(values, axis=0), jnp.concatenate(columns[0] + columns[1] + columns[2], axis=0))
                kept_sums = sums[: 2 * half] * factors[0]
                for a in range(1, 4):
                    block = sums[2 * half * a : 2 * half * (a + 1)] * factors[a]
                    kept_sums = jnp.where(lane_group == a, block, kept_sums)
                both = kept_sums[:, :128]
                owns.append(both * w + pltpu.roll(both, 64, 1) * upper_w)
                firsts.append(jnp.concatenate([kept_sums[:, 128:]] * 2, axis=1))
            at = pl.multiple_of((step * (STEP // SQ) + b) * 2 * half, 2 * half)
            own_rows[pl.ds(at, 2 * half), :] = jnp.where(left, owns[0], owns[1])
            prev_rows[pl.ds(at, 2 * half), :] = jnp.where(left, firsts[0], firsts[1]) * first_w

    def step_body(step, carry):
        @pl.when(step + DEPTH - 1 < steps)
        def _():
            fetch(step + DEPTH - 1)

        chunk = wave_chunk(step)
        for c in range(NT // CHUNK):
            pl.when(chunk == c)(functools.partial(multiply, step, c))
        return carry

    lax.fori_loop(0, steps, step_body, 0)
    rows = 2 * half
    for rows_ref, ref in ((own_rows, own_ref), (prev_rows, prev_ref)):
        rows_dev = ref.shape[1] // groups
        for r in range(rows):
            at = (r % rows_dev) * groups
            ref[r // rows_dev, at : at + groups, :] = rows_ref[pl.ds(r, groups, stride=rows), :]


def legendre_sums(spectral, legendre, map_rows, brackets, lev_weight):
    slots = spectral.shape[0]
    half = legendre.shape[1]
    groups = slots // SQ
    devices = lax.axis_size("wave") * lax.axis_size("lev")
    out = pltpu.VMEM((devices, 2 * half // devices * groups, SQ * PART), F32)
    smem = pl.BlockSpec(memory_space=pltpu.SMEM)
    vmem = pl.BlockSpec(memory_space=pltpu.VMEM)
    hbm = pl.BlockSpec(memory_space=pltpu.HBM)
    return pl.pallas_call(
        legendre_kernel,
        out_shape=[out, out, jax.ShapeDtypeStruct((1,), jnp.int32)],
        in_specs=[smem, smem, vmem, hbm, hbm],
        out_specs=[vmem, vmem, smem],
        scratch_shapes=[
            pltpu.VMEM((DEPTH, STEP, LEV_DEV * PART, NT), BF16),
            pltpu.VMEM((DEPTH, STEP, half, NT), BF16),
            pltpu.VMEM((groups * 2 * half, SQ * PART), F32),
            pltpu.VMEM((groups * 2 * half, SQ * PART), F32),
            pltpu.VMEM((2, 256), jnp.int32),
            pltpu.SMEM((2, 256), jnp.int32),
            pltpu.SemaphoreType.DMA,
            pltpu.SemaphoreType.DMA((DEPTH, 2)),
        ],
        compiler_params=pltpu.CompilerParams(vmem_limit_bytes=48 * MIB),
        cost_estimate=pl.CostEstimate(flops=2 * slots * 2 * half * 48 * NT, bytes_accessed=slots * NT * 2 * (48 + half), transcendentals=0),
        name="legendre_sums",
    )(*[pltpu.with_memory_space_constraint(x, pltpu.HBM) for x in (brackets, lev_weight, map_rows, spectral, legendre)])


def unit_circle(product, points, inverse):
    big = 12582912.0
    turn = (product * inverse + big) - big
    x = (product - turn * points) * (math.pi * inverse)
    x2 = x * x
    sine = 0.0
    cosine = 0.0
    for power in (11, 9, 7, 5, 3, 1):
        sine = sine * x2 + (-1) ** (power // 2) / math.factorial(power)
    for power in (12, 10, 8, 6, 4, 2, 0):
        cosine = cosine * x2 + (-1) ** (power // 2) / math.factorial(power)
    sine = sine * x
    twice = sine + sine
    return 1.0 - twice * sine, twice * cosine


def own_points(points_ref, r2):
    wave = lax.axis_index("wave")
    lev = lax.axis_index("lev")
    row = 2 * (wave * lax.axis_size("lev") + lev) + r2
    return points_ref[row % points_ref.shape[0]]


def table_kernel(points_ref, map_ref, hi_ref, lo_ref, sorted_ref):
    r2 = pl.program_id(0)
    kb = pl.program_id(1)
    rows = hi_ref.shape[1]
    points = own_points(points_ref, r2).astype(F32)
    inverse = 1.0 / points

    @pl.when((r2 == 0) & (kb == 0))
    def _():
        waves, slots = sorted_ref.shape
        for wave in range(waves):
            rank, down = ranks_of(waves_of(map_ref, wave, slots))
            whole = jnp.floor((rank + 0.5) * (1.0 / SQ))
            place = (rank - whole * SQ) * (slots // SQ) + whole
            hit = (place == iota((256, 256), 1).astype(F32)) & (rank < slots)
            row = jnp.sum(jnp.where(hit, down, 0.0), axis=0, keepdims=True)
            sorted_ref[wave : wave + 1, :] = row[:, :slots].astype(jnp.int32)

    lane = iota((32, 128), 1).astype(F32)

    def chunk_body(i, carry):
        chunk = pl.multiple_of(i * 32, 32)

        def put(tile, value):
            lanes = slice(tile * 128, tile * 128 + 128)
            hi = value.astype(BF16)
            hi_ref[0, pl.ds(chunk, 32), lanes] = hi
            lo_ref[0, pl.ds(chunk, 32), lanes] = ((value - hi.astype(F32)) * REST_SCALE).astype(FP8)

        k = (kb * rows + chunk + iota((32, 128), 0)).astype(F32)
        c, s = unit_circle(2.0 * lane * k, points, inverse)
        c1, s1 = unit_circle(k, points, inverse)
        ct, st = unit_circle(256.0 * k, points, inverse)
        co = c * c1 - s * s1
        so = s * c1 + c * s1
        for t in range(HALF_M // 128):
            if t:
                c, s = c * ct - s * st, s * ct + c * st
                co, so = co * ct - so * st, so * ct + co * st
            put(t, c)
            put(5 + t, s)
            put(10 + t, co)
            put(15 + t, so)
        return carry

    lax.fori_loop(0, rows // 32, chunk_body, 0, unroll=True)


def tables(row_points, map_rows):
    waves = lax.axis_size("wave")
    rows = KPTS // TABLE_STEPS
    table = pltpu.HBM((2, KPTS, 2 * M), BF16)
    table_spec = pl.BlockSpec((1, rows, 2 * M), lambda r, k: (r, k, 0))
    return pl.pallas_call(
        table_kernel,
        out_shape=[table, pltpu.HBM((2, KPTS, 2 * M), FP8), jax.ShapeDtypeStruct((waves, M // waves), jnp.int32)],
        grid=(2, TABLE_STEPS),
        in_specs=[pl.BlockSpec(memory_space=pltpu.SMEM), pl.BlockSpec(memory_space=pltpu.VMEM)],
        out_specs=[table_spec, table_spec, pl.BlockSpec(memory_space=pltpu.VMEM)],
        compiler_params=pltpu.CompilerParams(vmem_limit_bytes=48 * MIB),
        cost_estimate=pl.CostEstimate(flops=2 * KPTS * 2 * M * 12, bytes_accessed=2 * KPTS * 2 * M * 4, transcendentals=0),
        name="fourier_tables",
    )(*[pltpu.with_memory_space_constraint(x, pltpu.HBM) for x in (row_points, map_rows)])


def pick_tables(plev):
    wide = plev * 2 * PART
    out = np.zeros((2, 4, 2 * wide, 2 * wide), np.float32)
    plans = (
        ((0, 1), (0, 1), (0, 1), (0, 1)),
        ((1, -1), (1, 1), (1, -1), (1, 1)),
        ((0, 1), (0, 1), (1, -1), (1, -1)),
        ((1, -1), (1, 1), (0, -1), (0, 1)),
    )
    for r2 in range(2):
        for kind, plan in enumerate(plans):
            for image, (part, sgn) in enumerate(plan):
                for hl in range(2):
                    for p in range(plev):
                        for q in range(FS):
                            src = hl * wide + p * 2 * PART + r2 * PART + q * 2 + part
                            dst = hl * wide + image * plev * FS + p * FS + q
                            out[r2, kind, src, dst] = sgn
    return out.astype(jnp.bfloat16)


def mean_table(plev):
    wide = plev * FS * 4
    out = np.zeros((2 * 4 * plev, 2 * wide), np.float32)
    for quarter in range(4):
        for p in range(plev):
            for part in range(2):
                image_quarter = (quarter + part) % 4
                start = (image_quarter * 2 + part) * plev * FS + p * FS
                out[part * 4 * plev + quarter * plev + p, start : start + FS] = 0.5 / STEPS
    return out.astype(jnp.bfloat16)


def flip_table():
    return np.fliplr(np.eye(KBLK, dtype=np.float32)).astype(jnp.bfloat16)


def split(x):
    hi = x.astype(BF16)
    return hi, (x - hi.astype(F32)).astype(BF16)


def nt_dot(a, b):
    return lax.dot_general(a, b, (((1,), (1,)), ((), ())), preferred_element_type=F32)


def nn_dot(a, b):
    return jnp.dot(a, b, preferred_element_type=F32)


def synth_kernel(points_ref, *refs):
    moved_ref, map_ref, pick_ref, mean_ref, flip_ref, hi_hbm, lo_hbm, out_ref = refs[:8]
    perm_ref, hi_ref, lo_ref, mixed, coef, coef8, flat, mirror, line, sems = refs[8:]
    table_copies = []
    for r2 in range(2):
        table_copies.append([])
        for i, (src, dst) in enumerate(((hi_hbm, hi_ref), (lo_hbm, lo_ref))):
            for c in range(TABLE_CUTS):
                rows = pl.ds(c * (KPTS // TABLE_CUTS), KPTS // TABLE_CUTS)
                table_copies[r2].append(pltpu.make_async_copy(src.at[r2, rows], dst.at[r2, rows], sems.at[r2, i, c]))
    for copy in table_copies[0] + table_copies[1]:
        copy.start()

    slot_waves = jnp.broadcast_to(map_ref[...], (16, M)).astype(jnp.int16)

    def perm_body(i, carry):
        row = pl.multiple_of(i * 16, 16)
        order = row + iota((16, M), 0)
        wanted = jnp.where(row < HALF_M, 2 * order, 2 * (order - HALF_M) + 1).astype(jnp.int16)
        perm_ref[pl.ds(row, 16), :] = jnp.where(slot_waves == wanted, 1.0, 0.0).astype(BF16)
        return carry

    lax.fori_loop(0, M // 16, perm_body, 0, unroll=4)
    waves, plev, _, _ = moved_ref.shape
    wide = plev * 2 * PART
    part_rows = M // SQ
    for base in range(0, plev * 2, 8):
        cur = []
        for g in range(base, base + 8):
            sub = moved_ref.shape[2] // 2
            pieces = [moved_ref[w, g // 2, (g % 2) * sub : (g % 2 + 1) * sub, :] for w in range(waves)]
            cur.append(jnp.concatenate(pieces, axis=0))
        group = iota((part_rows, 128), 1) // PART
        for bit in (1, 2, 4):
            unset = (group & bit) == 0
            nxt = list(cur)
            for g in range(8):
                if g & bit == 0:
                    a, b = cur[g], cur[g + bit]
                    nxt[g] = jnp.where(unset, a, pltpu.roll(b, bit * PART, 1))
                    nxt[g + bit] = jnp.where(unset, pltpu.roll(a, 128 - bit * PART, 1), b)
            cur = nxt
        for sq in range(SQ):
            hi, lo = split(cur[sq])
            lane = base * PART
            mixed[sq * part_rows : (sq + 1) * part_rows, lane : lane + 128] = hi
            mixed[sq * part_rows : (sq + 1) * part_rows, wide + lane : wide + lane + 128] = lo

    lane_row = (iota((1, 2 * wide), 1) // PART) % 2
    limit0 = (own_points(points_ref, 0) - 1) // 2
    limit1 = (own_points(points_ref, 1) - 1) // 2
    limit = jnp.where(lane_row == 0, limit0, limit1)
    place = iota((HALF_M, 1), 0)
    turned = (iota((1, 2 * wide), 1) % wide) // (plev * FS) >= 2
    flip_sign = jnp.where(turned & (place % 2 == 1), -1.0, 1.0).astype(BF16)
    for odd in range(2):
        ordered = nn_dot(perm_ref[odd * HALF_M : (odd + 1) * HALF_M, :], mixed[...])
        wave = 2 * place + odd
        factor = jnp.where(wave <= limit, jnp.where(wave == 0, 1.0, 2.0), 0.0)
        ordered = (ordered * factor).astype(BF16)
        for row in range(2):
            for part in range(2):
                picked = nn_dot(ordered, pick_ref[row, odd * 2 + part]).astype(BF16)
                picked = picked * flip_sign
                coef[row, odd, part * HALF_M : (part + 1) * HALF_M, :] = picked
                coef8[row, odd, part * HALF_M : (part + 1) * HALF_M, :] = picked[:, :wide].astype(F32).astype(FP8)
    flat[...] = jnp.zeros_like(flat)
    mirror[...] = jnp.zeros_like(mirror)

    row_sums = []
    for r2 in range(2):
        for copy in table_copies[r2]:
            copy.wait()

        def contraction(odd):
            lanes = slice(odd * M, (odd + 1) * M)
            both = nn_dot(hi_ref[r2, :, lanes], coef[r2, odd])
            rest = nn_dot(lo_ref[r2, :, lanes], coef8[r2, odd])
            return both[:, :wide] + (both[:, wide:] + rest * (1.0 / REST_SCALE))

        row_sums.append((contraction(0), contraction(1)))

    for r2 in range(2):
        even_sum, odd_sum = row_sums[r2]
        plus = even_sum + odd_sum
        minus = even_sum - odd_sum
        squares = jnp.concatenate([plus * plus, minus * minus], axis=1)
        sq_hi, sq_lo = split(squares)
        energy = nt_dot(mean_ref[...], sq_hi) + nt_dot(mean_ref[...], sq_lo)
        rows = 4 * plev
        flat[:, :KPTS] = energy
        en_hi, en_lo = split(flat[rows:, :KPAD])
        for t in range(KPAD // KBLK):
            lanes = slice(t * KBLK, (t + 1) * KBLK)
            back = KPAD - (t + 1) * KBLK
            mirror[:, back : back + KBLK] = nn_dot(en_hi[:, lanes], flip_ref[...]) + nn_dot(en_lo[:, lanes], flip_ref[...])

        quarter = own_points(points_ref, r2) // 4
        lane = iota((rows, BUF), 1)
        shift = (quarter + (BUF - (KPAD - 1))) % BUF
        flat[:rows, :] = jnp.where(lane <= quarter // 2, flat[:rows, :], pltpu.roll(mirror[...], shift, 1))
        line[...] = jnp.zeros_like(line)
        lane = iota((plev, BUF), 1)
        for b in range(4):
            start = quarter * b
            inner = start % 128
            base = pl.multiple_of(start - inner, 128)
            piece = pltpu.roll(flat[b * plev : (b + 1) * plev, :], inner, 1)
            old = line[:, pl.ds(base, BUF)]
            line[:, pl.ds(base, BUF)] = jnp.where((lane >= inner) & (lane < inner + quarter), piece, old)
        out_ref[:, pl.ds(r2, 1), :] = line[:, :ROWPAD].reshape(plev, 1, ROWPAD)


def synthesis(moved, slot_map, table_hi, table_lo, row_points):
    plev = moved.shape[1]
    wide = plev * 2 * PART
    vmem = pl.BlockSpec(memory_space=pltpu.VMEM)
    return pl.pallas_call(
        synth_kernel,
        out_shape=jax.ShapeDtypeStruct((plev, 2, ROWPAD), F32),
        in_specs=[pl.BlockSpec(memory_space=pltpu.SMEM)] + [vmem] * 5 + [pl.BlockSpec(memory_space=pltpu.HBM)] * 2,
        out_specs=vmem,
        scratch_shapes=[
            pltpu.VMEM((M, M), BF16),
            pltpu.VMEM((2, KPTS, 2 * M), BF16),
            pltpu.VMEM((2, KPTS, 2 * M), FP8),
            pltpu.VMEM((M, 2 * wide), BF16),
            pltpu.VMEM((2, 2, M, 2 * wide), BF16),
            pltpu.VMEM((2, 2, M, wide), FP8),
            pltpu.VMEM((8 * plev, BUF), F32),
            pltpu.VMEM((4 * plev, BUF), F32),
            pltpu.VMEM((plev, 3 * 1280 + BUF), F32),
            pltpu.SemaphoreType.DMA((2, 2, TABLE_CUTS)),
        ],
        compiler_params=pltpu.CompilerParams(vmem_limit_bytes=44 * MIB),
        cost_estimate=pl.CostEstimate(flops=2 * 2 * KPTS * 2 * M * 384, bytes_accessed=2 * KPTS * 2 * M * 4 + M * M * 2, transcendentals=0),
        name="synthesis",
    )(
        pltpu.with_memory_space_constraint(row_points, pltpu.HBM),
        pltpu.with_memory_space_constraint(moved, pltpu.VMEM), slot_map,
        pick_tables(plev), mean_table(plev), flip_table(),
        *[pltpu.with_memory_space_constraint(x, pltpu.HBM) for x in (table_hi, table_lo)],
    )


def join_kernel(*refs):
    parts = (len(refs) - 1) // 2
    at = 0
    for own_ref, other_ref in zip(refs[:parts], refs[parts:-1]):
        rows = own_ref.shape[1]
        refs[-1][:, at : at + rows, :] = own_ref[...] + other_ref[...]
        at += rows


def join(owns, others):
    rows = sum(x.shape[1] for x in owns)
    vmem = pl.BlockSpec(memory_space=pltpu.VMEM)
    return pl.pallas_call(
        join_kernel,
        out_shape=jax.ShapeDtypeStruct((owns[0].shape[0], rows, SQ * PART), F32),
        in_specs=[vmem] * (2 * len(owns)),
        out_specs=vmem,
        compiler_params=pltpu.CompilerParams(vmem_limit_bytes=32 * MIB),
        name="join",
    )(*[pltpu.with_memory_space_constraint(x, pltpu.VMEM) for x in owns + others])


def local(spectral, legendre, wave_map, row_points, brackets, lev_weight, climatology):
    slots = spectral.shape[0]
    half = legendre.shape[1]
    groups = slots // SQ
    wave_count = lax.axis_size("wave")
    lev_count = lax.axis_size("lev")
    rows_dev = 2 * half // (wave_count * lev_count)
    pairs = [(d, d - 1) for d in range(1, lev_count)]
    map_rows = wave_map.reshape(M // 128, 128)
    own, prev, between = legendre_sums(spectral, legendre, map_rows, brackets, lev_weight)
    sent = lax.switch(
        between[0],
        [
            lambda mine, theirs: join([mine], [lax.ppermute(theirs, "lev", pairs[::2])]),
            lambda mine, theirs: join([mine], [lax.ppermute(theirs, "lev", pairs)]),
        ],
        own,
        prev,
    )
    moved = lax.all_to_all(sent, ("wave", "lev"), split_axis=0, concat_axis=0, tiled=True)
    moved = moved.reshape(wave_count, lev_count, rows_dev * groups, SQ * PART)
    table_points, _ = lax.optimization_barrier((row_points, sent))
    table_hi, table_lo, sorted_map = tables(table_points, map_rows)
    slot_map = jnp.transpose(sorted_map.reshape(wave_count, SQ, groups), (1, 0, 2)).reshape(1, M)
    energy = synthesis(moved, slot_map, table_hi, table_lo, row_points)
    result = lax.all_to_all(energy, "lev", split_axis=0, concat_axis=0, tiled=True)
    result = result.reshape(1, rows_dev * lev_count, ROWPAD)
    points_all = jnp.concatenate([row_points, row_points])
    band_rows = rows_dev * lev_count
    out_points = lax.dynamic_slice_in_dim(points_all, lax.axis_index("wave") * band_rows, band_rows, 0)
    places = jnp.arange(ROWPAD, dtype=jnp.int32)
    inside = places[None, None, :] < out_points[None, :, None]
    return jnp.where(inside, result - climatology, 0.0)


def solution(mesh):
    placed = (
        P("wave", "lev", None),
        P("wave", None, None),
        P(),
        P(),
        P(),
        P(),
        P("lev", "wave", None),
    )
    return jax.shard_map(
        local, mesh=mesh, in_specs=placed, out_specs=P("lev", "wave", None), check_vma=False
    )
```

```python
import functools
import math

import jax
import jax.numpy as jnp
import numpy as np
from jax import lax
from jax.experimental import pallas as pl
from jax.experimental.pallas import tpu as pltpu
from jax.sharding import PartitionSpec as P

M = 1280
NT = 1280
LEV_DEV = 4
STEPS = 4
FIELDS = 2
ROWPAD = 5248

FS = FIELDS * STEPS
PART = 2 * FS
SQ = 8
STEP = 16
CHUNK = 256
DEPTH = 3
HALF_M = M // 2
KPTS = 672
KPAD = 768
KBLK = 256
TABLE_STEPS = 7
TABLE_CUTS = 3
BUF = 1536
MIB = 1024 * 1024
F32 = jnp.float32
BF16 = jnp.bfloat16
FP8 = jnp.float8_e4m3fn
REST_SCALE = 256.0


def iota(shape, dim):
    return lax.broadcasted_iota(jnp.int32, shape, dim)


def waves_of(map_ref, wave, slots):
    start = wave * slots
    row = start // 128
    last = map_ref.shape[0] - 1
    pair = jnp.concatenate([map_ref[pl.ds(row, 1), :], map_ref[pl.ds(jnp.minimum(row + 1, last), 1), :]], axis=1)
    pair = jnp.broadcast_to(pair, (8, 256)).astype(F32)
    turned = pltpu.roll(pair, (256 - start % 128) % 256, 1)
    return jnp.where(iota((8, 256), 1) < slots, turned, 4096.0)[:1]


def ranks_of(waves):
    lane = iota((1, 256), 1)
    keys = jnp.where(lane < STEP, (lane - STEP).astype(F32), waves)
    across = jnp.broadcast_to(keys, (256, 256))
    rank = jnp.sum(jnp.where(across < across.T, 1.0, 0.0), axis=1, keepdims=True)
    return rank, jnp.broadcast_to(waves, (256, 256)).T


def legendre_kernel(
    brackets, weight_ref, map_ref, spec_hbm, leg_hbm, own_ref, prev_ref, between_ref,
    spec_buf, leg_buf, own_rows, prev_rows, order_vmem, order, order_sem, sems,
):
    slots, half, _ = leg_hbm.shape
    groups = slots // SQ
    steps = slots // STEP
    wave = lax.axis_index("wave")
    lev = lax.axis_index("lev")
    lower = brackets[lev] - lev * LEV_DEV
    has_upper = lower < LEV_DEV - 1
    w = weight_ref[lev]
    upper_w = jnp.where(has_upper, 1.0 - w, 0.0)
    low_rows = pl.ds(pl.multiple_of(lower * PART, PART), PART)
    up_rows = pl.ds(pl.multiple_of(jnp.minimum(lower + 1, LEV_DEV - 1) * PART, PART), PART)
    before = jnp.maximum(lev - 1, 0)
    crosses = (lev > 0) & (brackets[before] == lev * LEV_DEV - 1)
    first_w = jnp.where(crosses, 1.0 - weight_ref[before], 0.0)
    degree = iota((16, NT), 1).astype(jnp.int16)
    sign = (1 - 2 * (iota((16, NT), 1) % 2)).astype(F32).astype(BF16)
    lane_group = iota((1, 192), 1) % 64 // PART
    left = iota((1, SQ * PART), 1) < 64
    south = iota((2 * half, 1), 0) >= half

    def buffers(slot, c):
        lanes = pl.ds(c * CHUNK, NT - c * CHUNK)
        return [
            (leg_hbm.at[:, :, lanes], leg_buf.at[slot, :, :, lanes], sems.at[slot, 0]),
            (spec_hbm.at[:, :, lanes], spec_buf.at[slot, :, :, lanes], sems.at[slot, 1]),
        ]

    for src, dst, sem in buffers(0, 0):
        pltpu.make_async_copy(src.at[pl.ds(0, STEP)], dst, sem).start()

    rank, down = ranks_of(waves_of(map_ref, wave, slots))
    hit = rank == iota((256, 256), 1).astype(F32)
    slot_at = jnp.sum(jnp.where(hit, iota((256, 256), 0).astype(F32), 0.0), axis=0, keepdims=True)
    wave_at = jnp.sum(jnp.where(hit, down, 0.0), axis=0, keepdims=True)
    order_vmem[0:1, :] = slot_at.astype(jnp.int32)
    order_vmem[1:2, :] = wave_at.astype(jnp.int32)
    to_smem = pltpu.make_async_copy(order_vmem, order, order_sem)
    to_smem.start()
    to_smem.wait()

    def wave_chunk(step):
        return jnp.where(step == 0, 0, order[1, step * STEP] // CHUNK)

    def fetch(step):
        chunk = wave_chunk(step)
        for c in range(NT // CHUNK):

            @pl.when(chunk == c)
            def _():
                for i in range(STEP):
                    at = order[0, step * STEP + i]
                    for src, dst, sem in buffers(step % DEPTH, c):
                        pltpu.make_async_copy(src.at[at], dst.at[i], sem).start()

    for step in range(1, DEPTH - 1):
        fetch(step)
    between = jnp.int32(0)
    for p in range(1, brackets.shape[0] - 1, 2):
        between = between | (brackets[p] == (p + 1) * LEV_DEV - 1).astype(jnp.int32)
    between_ref[0] = between

    def multiply(step, c):
        slot = step % DEPTH
        lanes = slice(c * CHUNK, NT)
        for src, dst, sem in buffers(slot, c):
            pltpu.make_async_copy(src.at[pl.ds(0, STEP)], dst, sem).wait()
        for b in range(STEP // SQ):
            owns, firsts = [], []
            for quad in range(2):
                values, factors, columns = [], [], [[], [], []]
                for i in range(b * SQ + 4 * quad, b * SQ + 4 * quad + 4):
                    m = order[1, step * STEP + i]
                    kept = degree[:, lanes] >= m.astype(jnp.int16)
                    plain = [jnp.where(kept, leg_buf[slot, i, r : r + 16, lanes], 0) for r in range(0, half, 16)]
                    values += plain + [x * sign[:, lanes] for x in plain]
                    factors.append(jnp.where(south, (1 - 2 * (m % 2)).astype(F32), 1.0))
                    columns[quad].append(spec_buf[slot, i, low_rows, lanes])
                    columns[1 - quad].append(spec_buf[slot, i, up_rows, lanes])
                    columns[2].append(spec_buf[slot, i, :PART, lanes])
                sums = nt_dot(jnp.concatenate(values, axis=0), jnp.concatenate(columns[0] + columns[1] + columns[2], axis=0))
                kept_sums = sums[: 2 * half] * factors[0]
                for a in range(1, 4):
                    block = sums[2 * half * a : 2 * half * (a + 1)] * factors[a]
                    kept_sums = jnp.where(lane_group == a, block, kept_sums)
                both = kept_sums[:, :128]
                owns.append(both * w + pltpu.roll(both, 64, 1) * upper_w)
                firsts.append(jnp.concatenate([kept_sums[:, 128:]] * 2, axis=1))
            at = pl.multiple_of((step * (STEP // SQ) + b) * 2 * half, 2 * half)
            own_rows[pl.ds(at, 2 * half), :] = jnp.where(left, owns[0], owns[1])
            prev_rows[pl.ds(at, 2 * half), :] = jnp.where(left, firsts[0], firsts[1]) * first_w

    def step_body(step, carry):
        @pl.when(step + DEPTH - 1 < steps)
        def _():
            fetch(step + DEPTH - 1)

        chunk = wave_chunk(step)
        for c in range(NT // CHUNK):
            pl.when(chunk == c)(functools.partial(multiply, step, c))
        return carry

    lax.fori_loop(0, steps, step_body, 0)
    rows = 2 * half
    for rows_ref, ref in ((own_rows, own_ref), (prev_rows, prev_ref)):
        rows_dev = ref.shape[1] // groups
        for r in range(rows):
            at = (r % rows_dev) * groups
            ref[r // rows_dev, at : at + groups, :] = rows_ref[pl.ds(r, groups, stride=rows), :]


def legendre_sums(spectral, legendre, map_rows, brackets, lev_weight):
    slots = spectral.shape[0]
    half = legendre.shape[1]
    groups = slots // SQ
    devices = lax.axis_size("wave") * lax.axis_size("lev")
    out = pltpu.VMEM((devices, 2 * half // devices * groups, SQ * PART), F32)
    smem = pl.BlockSpec(memory_space=pltpu.SMEM)
    vmem = pl.BlockSpec(memory_space=pltpu.VMEM)
    hbm = pl.BlockSpec(memory_space=pltpu.HBM)
    return pl.pallas_call(
        legendre_kernel,
        out_shape=[out, out, jax.ShapeDtypeStruct((1,), jnp.int32)],
        in_specs=[smem, smem, vmem, hbm, hbm],
        out_specs=[vmem, vmem, smem],
        scratch_shapes=[
            pltpu.VMEM((DEPTH, STEP, LEV_DEV * PART, NT), BF16),
            pltpu.VMEM((DEPTH, STEP, half, NT), BF16),
            pltpu.VMEM((groups * 2 * half, SQ * PART), F32),
            pltpu.VMEM((groups * 2 * half, SQ * PART), F32),
            pltpu.VMEM((2, 256), jnp.int32),
            pltpu.SMEM((2, 256), jnp.int32),
            pltpu.SemaphoreType.DMA,
            pltpu.SemaphoreType.DMA((DEPTH, 2)),
        ],
        compiler_params=pltpu.CompilerParams(vmem_limit_bytes=48 * MIB),
        cost_estimate=pl.CostEstimate(flops=2 * slots * 2 * half * 48 * NT, bytes_accessed=slots * NT * 2 * (48 + half), transcendentals=0),
        name="legendre_sums",
    )(*[pltpu.with_memory_space_constraint(x, pltpu.HBM) for x in (brackets, lev_weight, map_rows, spectral, legendre)])


def unit_circle(product, points, inverse):
    big = 12582912.0
    turn = (product * inverse + big) - big
    x = (product - turn * points) * (math.pi * inverse)
    x2 = x * x
    sine = 0.0
    cosine = 0.0
    for power in (11, 9, 7, 5, 3, 1):
        sine = sine * x2 + (-1) ** (power // 2) / math.factorial(power)
    for power in (12, 10, 8, 6, 4, 2, 0):
        cosine = cosine * x2 + (-1) ** (power // 2) / math.factorial(power)
    sine = sine * x
    twice = sine + sine
    return 1.0 - twice * sine, twice * cosine


def own_points(points_ref, r2):
    wave = lax.axis_index("wave")
    lev = lax.axis_index("lev")
    row = 2 * (wave * lax.axis_size("lev") + lev) + r2
    return points_ref[row % points_ref.shape[0]]


def table_kernel(points_ref, map_ref, hi_ref, lo_ref, sorted_ref):
    r2 = pl.program_id(0)
    kb = pl.program_id(1)
    rows = hi_ref.shape[1]
    points = own_points(points_ref, r2).astype(F32)
    inverse = 1.0 / points

    @pl.when((r2 == 0) & (kb == 0))
    def _():
        waves, slots = sorted_ref.shape
        for wave in range(waves):
            rank, down = ranks_of(waves_of(map_ref, wave, slots))
            whole = jnp.floor((rank + 0.5) * (1.0 / SQ))
            place = (rank - whole * SQ) * (slots // SQ) + whole
            hit = (place == iota((256, 256), 1).astype(F32)) & (rank < slots)
            row = jnp.sum(jnp.where(hit, down, 0.0), axis=0, keepdims=True)
            sorted_ref[wave : wave + 1, :] = row[:, :slots].astype(jnp.int32)

    lane = iota((32, 128), 1).astype(F32)

    def chunk_body(i, carry):
        chunk = pl.multiple_of(i * 32, 32)

        def put(tile, value):
            lanes = slice(tile * 128, tile * 128 + 128)
            hi = value.astype(BF16)
            hi_ref[0, pl.ds(chunk, 32), lanes] = hi
            lo_ref[0, pl.ds(chunk, 32), lanes] = ((value - hi.astype(F32)) * REST_SCALE).astype(FP8)

        k = (kb * rows + chunk + iota((32, 128), 0)).astype(F32)
        c, s = unit_circle(2.0 * lane * k, points, inverse)
        c1, s1 = unit_circle(k, points, inverse)
        ct, st = unit_circle(256.0 * k, points, inverse)
        co = c * c1 - s * s1
        so = s * c1 + c * s1
        for t in range(HALF_M // 128):
            if t:
                c, s = c * ct - s * st, s * ct + c * st
                co, so = co * ct - so * st, so * ct + co * st
            put(t, c)
            put(5 + t, s)
            put(10 + t, co)
            put(15 + t, so)
        return carry

    lax.fori_loop(0, rows // 32, chunk_body, 0, unroll=True)


def tables(row_points, map_rows):
    waves = lax.axis_size("wave")
    rows = KPTS // TABLE_STEPS
    table = pltpu.HBM((2, KPTS, 2 * M), BF16)
    table_spec = pl.BlockSpec((1, rows, 2 * M), lambda r, k: (r, k, 0))
    return pl.pallas_call(
        table_kernel,
        out_shape=[table, pltpu.HBM((2, KPTS, 2 * M), FP8), jax.ShapeDtypeStruct((waves, M // waves), jnp.int32)],
        grid=(2, TABLE_STEPS),
        in_specs=[pl.BlockSpec(memory_space=pltpu.SMEM), pl.BlockSpec(memory_space=pltpu.VMEM)],
        out_specs=[table_spec, table_spec, pl.BlockSpec(memory_space=pltpu.VMEM)],
        compiler_params=pltpu.CompilerParams(vmem_limit_bytes=48 * MIB),
        cost_estimate=pl.CostEstimate(flops=2 * KPTS * 2 * M * 12, bytes_accessed=2 * KPTS * 2 * M * 4, transcendentals=0),
        name="fourier_tables",
    )(*[pltpu.with_memory_space_constraint(x, pltpu.HBM) for x in (row_points, map_rows)])


def pick_tables(plev):
    wide = plev * 2 * PART
    out = np.zeros((2, 4, 2 * wide, 2 * wide), np.float32)
    plans = (
        ((0, 1), (0, 1), (0, 1), (0, 1)),
        ((1, -1), (1, 1), (1, -1), (1, 1)),
        ((0, 1), (0, 1), (1, -1), (1, -1)),
        ((1, -1), (1, 1), (0, -1), (0, 1)),
    )
    for r2 in range(2):
        for kind, plan in enumerate(plans):
            for image, (part, sgn) in enumerate(plan):
                for hl in range(2):
                    for p in range(plev):
                        for q in range(FS):
                            src = hl * wide + p * 2 * PART + r2 * PART + q * 2 + part
                            dst = hl * wide + image * plev * FS + p * FS + q
                            out[r2, kind, src, dst] = sgn
    return out.astype(jnp.bfloat16)


def mean_table(plev):
    wide = plev * FS * 4
    out = np.zeros((2 * 4 * plev, 2 * wide), np.float32)
    for quarter in range(4):
        for p in range(plev):
            for part in range(2):
                image_quarter = (quarter + part) % 4
                start = (image_quarter * 2 + part) * plev * FS + p * FS
                out[part * 4 * plev + quarter * plev + p, start : start + FS] = 0.5 / STEPS
    return out.astype(jnp.bfloat16)


def flip_table():
    return np.fliplr(np.eye(KBLK, dtype=np.float32)).astype(jnp.bfloat16)


def split(x):
    hi = x.astype(BF16)
    return hi, (x - hi.astype(F32)).astype(BF16)


def nt_dot(a, b):
    return lax.dot_general(a, b, (((1,), (1,)), ((), ())), preferred_element_type=F32)


def nn_dot(a, b):
    return jnp.dot(a, b, preferred_element_type=F32)


def synth_kernel(points_ref, *refs):
    moved_ref, map_ref, pick_ref, mean_ref, flip_ref, hi_hbm, lo_hbm, out_ref = refs[:8]
    perm_ref, hi_ref, lo_ref, mixed, coef, coef8, flat, mirror, line, sems = refs[8:]
    table_copies = []
    for r2 in range(2):
        table_copies.append([])
        for i, (src, dst) in enumerate(((hi_hbm, hi_ref), (lo_hbm, lo_ref))):
            for c in range(TABLE_CUTS):
                rows = pl.ds(c * (KPTS // TABLE_CUTS), KPTS // TABLE_CUTS)
                table_copies[r2].append(pltpu.make_async_copy(src.at[r2, rows], dst.at[r2, rows], sems.at[r2, i, c]))
    for copy in table_copies[0] + table_copies[1]:
        copy.start()

    slot_waves = jnp.broadcast_to(map_ref[...], (16, M)).astype(jnp.int16)

    def perm_body(i, carry):
        row = pl.multiple_of(i * 16, 16)
        order = row + iota((16, M), 0)
        wanted = jnp.where(row < HALF_M, 2 * order, 2 * (order - HALF_M) + 1).astype(jnp.int16)
        perm_ref[pl.ds(row, 16), :] = jnp.where(slot_waves == wanted, 1.0, 0.0).astype(BF16)
        return carry

    lax.fori_loop(0, M // 16, perm_body, 0, unroll=4)
    waves, plev, _, _ = moved_ref.shape
    wide = plev * 2 * PART
    part_rows = M // SQ
    for base in range(0, plev * 2, 8):
        cur = []
        for g in range(base, base + 8):
            sub = moved_ref.shape[2] // 2
            pieces = [moved_ref[w, g // 2, (g % 2) * sub : (g % 2 + 1) * sub, :] for w in range(waves)]
            cur.append(jnp.concatenate(pieces, axis=0))
        group = iota((part_rows, 128), 1) // PART
        for bit in (1, 2, 4):
            unset = (group & bit) == 0
            nxt = list(cur)
            for g in range(8):
                if g & bit == 0:
                    a, b = cur[g], cur[g + bit]
                    nxt[g] = jnp.where(unset, a, pltpu.roll(b, bit * PART, 1))
                    nxt[g + bit] = jnp.where(unset, pltpu.roll(a, 128 - bit * PART, 1), b)
            cur = nxt
        for sq in range(SQ):
            hi, lo = split(cur[sq])
            lane = base * PART
            mixed[sq * part_rows : (sq + 1) * part_rows, lane : lane + 128] = hi
            mixed[sq * part_rows : (sq + 1) * part_rows, wide + lane : wide + lane + 128] = lo

    lane_row = (iota((1, 2 * wide), 1) // PART) % 2
    limit0 = (own_points(points_ref, 0) - 1) // 2
    limit1 = (own_points(points_ref, 1) - 1) // 2
    limit = jnp.where(lane_row == 0, limit0, limit1)
    place = iota((HALF_M, 1), 0)
    turned = (iota((1, 2 * wide), 1) % wide) // (plev * FS) >= 2
    flip_sign = jnp.where(turned & (place % 2 == 1), -1.0, 1.0).astype(BF16)
    for odd in range(2):
        ordered = nn_dot(perm_ref[odd * HALF_M : (odd + 1) * HALF_M, :], mixed[...])
        wave = 2 * place + odd
        factor = jnp.where(wave <= limit, jnp.where(wave == 0, 1.0, 2.0), 0.0)
        ordered = (ordered * factor).astype(BF16)
        for row in range(2):
            for part in range(2):
                picked = nn_dot(ordered, pick_ref[row, odd * 2 + part]).astype(BF16)
                picked = picked * flip_sign
                coef[row, odd, part * HALF_M : (part + 1) * HALF_M, :] = picked
                coef8[row, odd, part * HALF_M : (part + 1) * HALF_M, :] = picked[:, :wide].astype(F32).astype(FP8)
    flat[...] = jnp.zeros_like(flat)
    mirror[...] = jnp.zeros_like(mirror)

    for r2 in range(2):
        for copy in table_copies[r2]:
            copy.wait()

        def contraction(odd):
            lanes = slice(odd * M, (odd + 1) * M)
            both = nn_dot(hi_ref[r2, :, lanes], coef[r2, odd])
            rest = nn_dot(lo_ref[r2, :, lanes], coef8[r2, odd])
            return both[:, :wide] + (both[:, wide:] + rest * (1.0 / REST_SCALE))

        even_sum = contraction(0)
        odd_sum = contraction(1)
        plus = even_sum + odd_sum
        minus = even_sum - odd_sum
        squares = jnp.concatenate([plus * plus, minus * minus], axis=1)
        sq_hi, sq_lo = split(squares)
        energy = nt_dot(mean_ref[...], sq_hi) + nt_dot(mean_ref[...], sq_lo)
        rows = 4 * plev
        flat[:, :KPTS] = energy
        en_hi, en_lo = split(flat[rows:, :KPAD])
        for t in range(KPAD // KBLK):
            lanes = slice(t * KBLK, (t + 1) * KBLK)
            back = KPAD - (t + 1) * KBLK
            mirror[:, back : back + KBLK] = nn_dot(en_hi[:, lanes], flip_ref[...]) + nn_dot(en_lo[:, lanes], flip_ref[...])

        quarter = own_points(points_ref, r2) // 4
        lane = iota((rows, BUF), 1)
        shift = (quarter + (BUF - (KPAD - 1))) % BUF
        flat[:rows, :] = jnp.where(lane <= quarter // 2, flat[:rows, :], pltpu.roll(mirror[...], shift, 1))
        line[...] = jnp.zeros_like(line)
        lane = iota((plev, BUF), 1)
        for b in range(4):
            start = quarter * b
            inner = start % 128
            base = pl.multiple_of(start - inner, 128)
            piece = pltpu.roll(flat[b * plev : (b + 1) * plev, :], inner, 1)
            old = line[:, pl.ds(base, BUF)]
            line[:, pl.ds(base, BUF)] = jnp.where((lane >= inner) & (lane < inner + quarter), piece, old)
        out_ref[:, pl.ds(r2, 1), :] = line[:, :ROWPAD].reshape(plev, 1, ROWPAD)


def synthesis(moved, slot_map, table_hi, table_lo, row_points):
    plev = moved.shape[1]
    wide = plev * 2 * PART
    vmem = pl.BlockSpec(memory_space=pltpu.VMEM)
    return pl.pallas_call(
        synth_kernel,
        out_shape=jax.ShapeDtypeStruct((plev, 2, ROWPAD), F32),
        in_specs=[pl.BlockSpec(memory_space=pltpu.SMEM)] + [vmem] * 5 + [pl.BlockSpec(memory_space=pltpu.HBM)] * 2,
        out_specs=vmem,
        scratch_shapes=[
            pltpu.VMEM((M, M), BF16),
            pltpu.VMEM((2, KPTS, 2 * M), BF16),
            pltpu.VMEM((2, KPTS, 2 * M), FP8),
            pltpu.VMEM((M, 2 * wide), BF16),
            pltpu.VMEM((2, 2, M, 2 * wide), BF16),
            pltpu.VMEM((2, 2, M, wide), FP8),
            pltpu.VMEM((8 * plev, BUF), F32),
            pltpu.VMEM((4 * plev, BUF), F32),
            pltpu.VMEM((plev, 3 * 1280 + BUF), F32),
            pltpu.SemaphoreType.DMA((2, 2, TABLE_CUTS)),
        ],
        compiler_params=pltpu.CompilerParams(vmem_limit_bytes=44 * MIB),
        cost_estimate=pl.CostEstimate(flops=2 * 2 * KPTS * 2 * M * 384, bytes_accessed=2 * KPTS * 2 * M * 4 + M * M * 2, transcendentals=0),
        name="synthesis",
    )(
        pltpu.with_memory_space_constraint(row_points, pltpu.HBM),
        pltpu.with_memory_space_constraint(moved, pltpu.VMEM), slot_map,
        pick_tables(plev), mean_table(plev), flip_table(),
        *[pltpu.with_memory_space_constraint(x, pltpu.HBM) for x in (table_hi, table_lo)],
    )


def join_kernel(*refs):
    parts = (len(refs) - 1) // 2
    at = 0
    for own_ref, other_ref in zip(refs[:parts], refs[parts:-1]):
        rows = own_ref.shape[1]
        refs[-1][:, at : at + rows, :] = own_ref[...] + other_ref[...]
        at += rows


def join(owns, others):
    rows = sum(x.shape[1] for x in owns)
    vmem = pl.BlockSpec(memory_space=pltpu.VMEM)
    return pl.pallas_call(
        join_kernel,
        out_shape=jax.ShapeDtypeStruct((owns[0].shape[0], rows, SQ * PART), F32),
        in_specs=[vmem] * (2 * len(owns)),
        out_specs=vmem,
        compiler_params=pltpu.CompilerParams(vmem_limit_bytes=32 * MIB),
        name="join",
    )(*[pltpu.with_memory_space_constraint(x, pltpu.VMEM) for x in owns + others])


def local(spectral, legendre, wave_map, row_points, brackets, lev_weight, climatology):
    slots = spectral.shape[0]
    half = legendre.shape[1]
    groups = slots // SQ
    wave_count = lax.axis_size("wave")
    lev_count = lax.axis_size("lev")
    rows_dev = 2 * half // (wave_count * lev_count)
    pairs = [(d, d - 1) for d in range(1, lev_count)]
    map_rows = wave_map.reshape(M // 128, 128)
    own, prev, between = legendre_sums(spectral, legendre, map_rows, brackets, lev_weight)
    sent = lax.switch(
        between[0],
        [
            lambda mine, theirs: join([mine], [lax.ppermute(theirs, "lev", pairs[::2])]),
            lambda mine, theirs: join([mine], [lax.ppermute(theirs, "lev", pairs)]),
        ],
        own,
        prev,
    )
    moved = lax.all_to_all(sent, ("wave", "lev"), split_axis=0, concat_axis=0, tiled=True)
    moved = moved.reshape(wave_count, lev_count, rows_dev * groups, SQ * PART)
    table_points, _ = lax.optimization_barrier((row_points, sent))
    table_hi, table_lo, sorted_map = tables(table_points, map_rows)
    slot_map = jnp.transpose(sorted_map.reshape(wave_count, SQ, groups), (1, 0, 2)).reshape(1, M)
    energy = synthesis(moved, slot_map, table_hi, table_lo, row_points)
    result = lax.all_to_all(energy, "lev", split_axis=0, concat_axis=0, tiled=True)
    result = result.reshape(1, rows_dev * lev_count, ROWPAD)
    points_all = jnp.concatenate([row_points, row_points])
    band_rows = rows_dev * lev_count
    out_points = lax.dynamic_slice_in_dim(points_all, lax.axis_index("wave") * band_rows, band_rows, 0)
    places = jnp.arange(ROWPAD, dtype=jnp.int32)
    inside = places[None, None, :] < out_points[None, :, None]
    return jnp.where(inside, result - climatology, 0.0)


def solution(mesh):
    placed = (
        P("wave", "lev", None),
        P("wave", None, None),
        P(),
        P(),
        P(),
        P(),
        P("lev", "wave", None),
    )
    return jax.shard_map(
        local, mesh=mesh, in_specs=placed, out_specs=P("lev", "wave", None), check_vma=False
    )
```

```python
import functools
import math

import jax
import jax.numpy as jnp
import numpy as np
from jax import lax
from jax.experimental import pallas as pl
from jax.experimental.pallas import tpu as pltpu
from jax.sharding import PartitionSpec as P

M = 1280
NT = 1280
LEV_DEV = 4
STEPS = 4
FIELDS = 2
ROWPAD = 5248

FS = FIELDS * STEPS
PART = 2 * FS
SQ = 8
STEP = 16
CHUNK = 256
DEPTH = 3
HALF_M = M // 2
KPTS = 672
KPAD = 768
KBLK = 256
TABLE_STEPS = 7
TABLE_CUTS = 3
BUF = 1536
MIB = 1024 * 1024
F32 = jnp.float32
BF16 = jnp.bfloat16
FP8 = jnp.float8_e4m3fn
REST_SCALE = 256.0


def iota(shape, dim):
    return lax.broadcasted_iota(jnp.int32, shape, dim)


def waves_of(map_ref, wave, slots):
    start = wave * slots
    row = start // 128
    last = map_ref.shape[0] - 1
    pair = jnp.concatenate([map_ref[pl.ds(row, 1), :], map_ref[pl.ds(jnp.minimum(row + 1, last), 1), :]], axis=1)
    pair = jnp.broadcast_to(pair, (8, 256)).astype(F32)
    turned = pltpu.roll(pair, (256 - start % 128) % 256, 1)
    return jnp.where(iota((8, 256), 1) < slots, turned, 4096.0)[:1]


def ranks_of(waves):
    lane = iota((1, 256), 1)
    keys = jnp.where(lane < STEP, (lane - STEP).astype(F32), waves)
    across = jnp.broadcast_to(keys, (256, 256))
    rank = jnp.sum(jnp.where(across < across.T, 1.0, 0.0), axis=1, keepdims=True)
    return rank, jnp.broadcast_to(waves, (256, 256)).T


def legendre_kernel(
    brackets, weight_ref, map_ref, spec_hbm, leg_hbm, own_ref, prev_ref, between_ref,
    spec_buf, leg_buf, own_rows, prev_rows, order_vmem, order, order_sem, sems,
):
    slots, half, _ = leg_hbm.shape
    groups = slots // SQ
    steps = slots // STEP
    wave = lax.axis_index("wave")
    lev = lax.axis_index("lev")
    lower = brackets[lev] - lev * LEV_DEV
    has_upper = lower < LEV_DEV - 1
    w = weight_ref[lev]
    upper_w = jnp.where(has_upper, 1.0 - w, 0.0)
    low_rows = pl.ds(pl.multiple_of(lower * PART, PART), PART)
    up_rows = pl.ds(pl.multiple_of(jnp.minimum(lower + 1, LEV_DEV - 1) * PART, PART), PART)
    before = jnp.maximum(lev - 1, 0)
    crosses = (lev > 0) & (brackets[before] == lev * LEV_DEV - 1)
    first_w = jnp.where(crosses, 1.0 - weight_ref[before], 0.0)
    degree = iota((16, NT), 1).astype(jnp.int16)
    sign = (1 - 2 * (iota((16, NT), 1) % 2)).astype(F32).astype(BF16)
    lane_group = iota((1, 192), 1) % 64 // PART
    left = iota((1, SQ * PART), 1) < 64
    south = iota((2 * half, 1), 0) >= half

    def buffers(slot, c):
        lanes = pl.ds(c * CHUNK, NT - c * CHUNK)
        return [
            (leg_hbm.at[:, :, lanes], leg_buf.at[slot, :, :, lanes], sems.at[slot, 0]),
            (spec_hbm.at[:, :, lanes], spec_buf.at[slot, :, :, lanes], sems.at[slot, 1]),
        ]

    for src, dst, sem in buffers(0, 0):
        pltpu.make_async_copy(src.at[pl.ds(0, STEP)], dst, sem).start()

    rank, down = ranks_of(waves_of(map_ref, wave, slots))
    hit = rank == iota((256, 256), 1).astype(F32)
    slot_at = jnp.sum(jnp.where(hit, iota((256, 256), 0).astype(F32), 0.0), axis=0, keepdims=True)
    wave_at = jnp.sum(jnp.where(hit, down, 0.0), axis=0, keepdims=True)
    order_vmem[0:1, :] = slot_at.astype(jnp.int32)
    order_vmem[1:2, :] = wave_at.astype(jnp.int32)
    to_smem = pltpu.make_async_copy(order_vmem, order, order_sem)
    to_smem.start()
    to_smem.wait()

    def wave_chunk(step):
        return jnp.where(step == 0, 0, order[1, step * STEP] // CHUNK)

    def fetch(step):
        chunk = wave_chunk(step)
        for c in range(NT // CHUNK):

            @pl.when(chunk == c)
            def _():
                for i in range(STEP):
                    at = order[0, step * STEP + i]
                    for src, dst, sem in buffers(step % DEPTH, c):
                        pltpu.make_async_copy(src.at[at], dst.at[i], sem).start()

    for step in range(1, DEPTH - 1):
        fetch(step)
    between = jnp.int32(0)
    for p in range(1, brackets.shape[0] - 1, 2):
        between = between | (brackets[p] == (p + 1) * LEV_DEV - 1).astype(jnp.int32)
    between_ref[0] = between

    def multiply(step, c):
        slot = step % DEPTH
        lanes = slice(c * CHUNK, NT)
        for src, dst, sem in buffers(slot, c):
            pltpu.make_async_copy(src.at[pl.ds(0, STEP)], dst, sem).wait()
        for b in range(STEP // SQ):
            owns, firsts = [], []
            for quad in range(2):
                values, factors, columns = [], [], [[], [], []]
                for i in range(b * SQ + 4 * quad, b * SQ + 4 * quad + 4):
                    m = order[1, step * STEP + i]
                    kept = degree[:, lanes] >= m.astype(jnp.int16)
                    plain = [jnp.where(kept, leg_buf[slot, i, r : r + 16, lanes], 0) for r in range(0, half, 16)]
                    values += plain + [x * sign[:, lanes] for x in plain]
                    factors.append(jnp.where(south, (1 - 2 * (m % 2)).astype(F32), 1.0))
                    columns[quad].append(spec_buf[slot, i, low_rows, lanes])
                    columns[1 - quad].append(spec_buf[slot, i, up_rows, lanes])
                    columns[2].append(spec_buf[slot, i, :PART, lanes])
                sums = nt_dot(jnp.concatenate(values, axis=0), jnp.concatenate(columns[0] + columns[1] + columns[2], axis=0))
                kept_sums = sums[: 2 * half] * factors[0]
                for a in range(1, 4):
                    block = sums[2 * half * a : 2 * half * (a + 1)] * factors[a]
                    kept_sums = jnp.where(lane_group == a, block, kept_sums)
                both = kept_sums[:, :128]
                owns.append(both * w + pltpu.roll(both, 64, 1) * upper_w)
                firsts.append(jnp.concatenate([kept_sums[:, 128:]] * 2, axis=1))
            at = pl.multiple_of((step * (STEP // SQ) + b) * 2 * half, 2 * half)
            own_rows[pl.ds(at, 2 * half), :] = jnp.where(left, owns[0], owns[1])
            prev_rows[pl.ds(at, 2 * half), :] = jnp.where(left, firsts[0], firsts[1]) * first_w

    def step_body(step, carry):
        @pl.when(step + DEPTH - 1 < steps)
        def _():
            fetch(step + DEPTH - 1)

        chunk = wave_chunk(step)
        for c in range(NT // CHUNK):
            pl.when(chunk == c)(functools.partial(multiply, step, c))
        return carry

    lax.fori_loop(0, steps, step_body, 0)
    rows = 2 * half
    for rows_ref, ref in ((own_rows, own_ref), (prev_rows, prev_ref)):
        rows_dev = ref.shape[1] // groups
        for r in range(rows):
            at = (r % rows_dev) * groups
            ref[r // rows_dev, at : at + groups, :] = rows_ref[pl.ds(r, groups, stride=rows), :]


def legendre_sums(spectral, legendre, map_rows, brackets, lev_weight):
    slots = spectral.shape[0]
    half = legendre.shape[1]
    groups = slots // SQ
    devices = lax.axis_size("wave") * lax.axis_size("lev")
    out = pltpu.VMEM((devices, 2 * half // devices * groups, SQ * PART), F32)
    smem = pl.BlockSpec(memory_space=pltpu.SMEM)
    vmem = pl.BlockSpec(memory_space=pltpu.VMEM)
    hbm = pl.BlockSpec(memory_space=pltpu.HBM)
    return pl.pallas_call(
        legendre_kernel,
        out_shape=[out, out, jax.ShapeDtypeStruct((1,), jnp.int32)],
        in_specs=[smem, smem, vmem, hbm, hbm],
        out_specs=[vmem, vmem, smem],
        scratch_shapes=[
            pltpu.VMEM((DEPTH, STEP, LEV_DEV * PART, NT), BF16),
            pltpu.VMEM((DEPTH, STEP, half, NT), BF16),
            pltpu.VMEM((groups * 2 * half, SQ * PART), F32),
            pltpu.VMEM((groups * 2 * half, SQ * PART), F32),
            pltpu.VMEM((2, 256), jnp.int32),
            pltpu.SMEM((2, 256), jnp.int32),
            pltpu.SemaphoreType.DMA,
            pltpu.SemaphoreType.DMA((DEPTH, 2)),
        ],
        compiler_params=pltpu.CompilerParams(vmem_limit_bytes=48 * MIB),
        cost_estimate=pl.CostEstimate(flops=2 * slots * 2 * half * 48 * NT, bytes_accessed=slots * NT * 2 * (48 + half), transcendentals=0),
        name="legendre_sums",
    )(*[pltpu.with_memory_space_constraint(x, pltpu.HBM) for x in (brackets, lev_weight, map_rows, spectral, legendre)])


def unit_circle(product, points, inverse):
    big = 12582912.0
    turn = (product * inverse + big) - big
    x = (product - turn * points) * (math.pi * inverse)
    x2 = x * x
    sine = 0.0
    cosine = 0.0
    for power in (11, 9, 7, 5, 3, 1):
        sine = sine * x2 + (-1) ** (power // 2) / math.factorial(power)
    for power in (12, 10, 8, 6, 4, 2, 0):
        cosine = cosine * x2 + (-1) ** (power // 2) / math.factorial(power)
    sine = sine * x
    twice = sine + sine
    return 1.0 - twice * sine, twice * cosine


def own_points(points_ref, r2):
    wave = lax.axis_index("wave")
    lev = lax.axis_index("lev")
    row = 2 * (wave * lax.axis_size("lev") + lev) + r2
    return points_ref[row % points_ref.shape[0]]


def table_kernel(points_ref, map_ref, hi_ref, lo_ref, sorted_ref):
    r2 = pl.program_id(0)
    kb = pl.program_id(1)
    rows = hi_ref.shape[1]
    points = own_points(points_ref, r2).astype(F32)
    inverse = 1.0 / points

    @pl.when((r2 == 0) & (kb == 0))
    def _():
        waves, slots = sorted_ref.shape
        for wave in range(waves):
            rank, down = ranks_of(waves_of(map_ref, wave, slots))
            whole = jnp.floor((rank + 0.5) * (1.0 / SQ))
            place = (rank - whole * SQ) * (slots // SQ) + whole
            hit = (place == iota((256, 256), 1).astype(F32)) & (rank < slots)
            row = jnp.sum(jnp.where(hit, down, 0.0), axis=0, keepdims=True)
            sorted_ref[wave : wave + 1, :] = row[:, :slots].astype(jnp.int32)

    lane = iota((32, 128), 1).astype(F32)

    def chunk_body(i, carry):
        chunk = pl.multiple_of(i * 32, 32)

        def put(tile, value):
            lanes = slice(tile * 128, tile * 128 + 128)
            hi = value.astype(BF16)
            hi_ref[0, pl.ds(chunk, 32), lanes] = hi
            lo_ref[0, pl.ds(chunk, 32), lanes] = ((value - hi.astype(F32)) * REST_SCALE).astype(FP8)

        k = (kb * rows + chunk + iota((32, 128), 0)).astype(F32)
        c, s = unit_circle(2.0 * lane * k, points, inverse)
        c1, s1 = unit_circle(k, points, inverse)
        ct, st = unit_circle(256.0 * k, points, inverse)
        co = c * c1 - s * s1
        so = s * c1 + c * s1
        for t in range(HALF_M // 128):
            if t:
                c, s = c * ct - s * st, s * ct + c * st
                co, so = co * ct - so * st, so * ct + co * st
            put(t, c)
            put(5 + t, s)
            put(10 + t, co)
            put(15 + t, so)
        return carry

    lax.fori_loop(0, rows // 32, chunk_body, 0, unroll=True)


def tables(row_points, map_rows):
    waves = lax.axis_size("wave")
    rows = KPTS // TABLE_STEPS
    table = pltpu.HBM((2, KPTS, 2 * M), BF16)
    table_spec = pl.BlockSpec((1, rows, 2 * M), lambda r, k: (r, k, 0))
    return pl.pallas_call(
        table_kernel,
        out_shape=[table, pltpu.HBM((2, KPTS, 2 * M), FP8), jax.ShapeDtypeStruct((waves, M // waves), jnp.int32)],
        grid=(2, TABLE_STEPS),
        in_specs=[pl.BlockSpec(memory_space=pltpu.SMEM), pl.BlockSpec(memory_space=pltpu.VMEM)],
        out_specs=[table_spec, table_spec, pl.BlockSpec(memory_space=pltpu.VMEM)],
        compiler_params=pltpu.CompilerParams(vmem_limit_bytes=48 * MIB),
        cost_estimate=pl.CostEstimate(flops=2 * KPTS * 2 * M * 12, bytes_accessed=2 * KPTS * 2 * M * 4, transcendentals=0),
        name="fourier_tables",
    )(*[pltpu.with_memory_space_constraint(x, pltpu.HBM) for x in (row_points, map_rows)])


def pick_tables(plev):
    wide = plev * 2 * PART
    out = np.zeros((2, 4, 2 * wide, 2 * wide), np.float32)
    plans = (
        ((0, 1), (0, 1), (0, 1), (0, 1)),
        ((1, -1), (1, 1), (1, -1), (1, 1)),
        ((0, 1), (0, 1), (1, -1), (1, -1)),
        ((1, -1), (1, 1), (0, -1), (0, 1)),
    )
    for r2 in range(2):
        for kind, plan in enumerate(plans):
            for image, (part, sgn) in enumerate(plan):
                for hl in range(2):
                    for p in range(plev):
                        for q in range(FS):
                            src = hl * wide + p * 2 * PART + r2 * PART + q * 2 + part
                            dst = hl * wide + image * plev * FS + p * FS + q
                            out[r2, kind, src, dst] = sgn
    return out.astype(jnp.bfloat16)


def mean_table(plev):
    wide = plev * FS * 4
    out = np.zeros((2 * 4 * plev, 2 * wide), np.float32)
    for quarter in range(4):
        for p in range(plev):
            for part in range(2):
                image_quarter = (quarter + part) % 4
                start = (image_quarter * 2 + part) * plev * FS + p * FS
                out[part * 4 * plev + quarter * plev + p, start : start + FS] = 0.5 / STEPS
    return out.astype(jnp.bfloat16)


def flip_table():
    return np.fliplr(np.eye(KBLK, dtype=np.float32)).astype(jnp.bfloat16)


def split(x):
    hi = x.astype(BF16)
    return hi, (x - hi.astype(F32)).astype(BF16)


def nt_dot(a, b):
    return lax.dot_general(a, b, (((1,), (1,)), ((), ())), preferred_element_type=F32)


def nn_dot(a, b):
    return jnp.dot(a, b, preferred_element_type=F32)


def synth_kernel(points_ref, *refs):
    moved_ref, map_ref, pick_ref, mean_ref, flip_ref, hi_hbm, lo_hbm, out_ref = refs[:8]
    perm_ref, hi_ref, lo_ref, mixed, coef, coef8, flat, mirror, line, sems = refs[8:]
    table_copies = []
    for r2 in range(2):
        table_copies.append([])
        for i, (src, dst) in enumerate(((hi_hbm, hi_ref), (lo_hbm, lo_ref))):
            for c in range(TABLE_CUTS):
                rows = pl.ds(c * (KPTS // TABLE_CUTS), KPTS // TABLE_CUTS)
                table_copies[r2].append(pltpu.make_async_copy(src.at[r2, rows], dst.at[r2, rows], sems.at[r2, i, c]))
    for copy in table_copies[0] + table_copies[1]:
        copy.start()

    slot_waves = jnp.broadcast_to(map_ref[...], (16, M)).astype(jnp.int16)
    doubled = (2 * iota((16, M), 0)).astype(jnp.int16)
    ones, zeros = jnp.ones((16, M), BF16), jnp.zeros((16, M), BF16)

    def perm_body(i, carry):
        row = pl.multiple_of(i * 16, 16)
        first = jnp.where(row < HALF_M, 2 * row, 2 * (row - HALF_M) + 1).astype(jnp.int16)
        perm_ref[pl.ds(row, 16), :] = jnp.where(slot_waves == doubled + first, ones, zeros)
        return carry

    lax.fori_loop(0, M // 16, perm_body, 0, unroll=4)
    waves, plev, _, _ = moved_ref.shape
    wide = plev * 2 * PART
    part_rows = M // SQ
    for base in range(0, plev * 2, 8):
        cur = []
        for g in range(base, base + 8):
            sub = moved_ref.shape[2] // 2
            pieces = [moved_ref[w, g // 2, (g % 2) * sub : (g % 2 + 1) * sub, :] for w in range(waves)]
            cur.append(jnp.concatenate(pieces, axis=0))
        group = iota((part_rows, 128), 1) // PART
        for bit in (1, 2, 4):
            unset = (group & bit) == 0
            nxt = list(cur)
            for g in range(8):
                if g & bit == 0:
                    a, b = cur[g], cur[g + bit]
                    nxt[g] = jnp.where(unset, a, pltpu.roll(b, bit * PART, 1))
                    nxt[g + bit] = jnp.where(unset, pltpu.roll(a, 128 - bit * PART, 1), b)
            cur = nxt
        for sq in range(SQ):
            hi, lo = split(cur[sq])
            lane = base * PART
            mixed[sq * part_rows : (sq + 1) * part_rows, lane : lane + 128] = hi
            mixed[sq * part_rows : (sq + 1) * part_rows, wide + lane : wide + lane + 128] = lo

    lane_row = (iota((1, 2 * wide), 1) // PART) % 2
    limit0 = (own_points(points_ref, 0) - 1) // 2
    limit1 = (own_points(points_ref, 1) - 1) // 2
    limit = jnp.where(lane_row == 0, limit0, limit1)
    place = iota((HALF_M, 1), 0)
    turned = (iota((1, 2 * wide), 1) % wide) // (plev * FS) >= 2
    flip_sign = jnp.where(turned & (place % 2 == 1), -1.0, 1.0).astype(BF16)
    for odd in range(2):
        ordered = nn_dot(perm_ref[odd * HALF_M : (odd + 1) * HALF_M, :], mixed[...])
        wave = 2 * place + odd
        factor = jnp.where(wave <= limit, jnp.where(wave == 0, 1.0, 2.0), 0.0)
        ordered = (ordered * factor).astype(BF16)
        for row in range(2):
            for part in range(2):
                picked = nn_dot(ordered, pick_ref[row, odd * 2 + part]).astype(BF16)
                picked = picked * flip_sign
                coef[row, odd, part * HALF_M : (part + 1) * HALF_M, :] = picked
                coef8[row, odd, part * HALF_M : (part + 1) * HALF_M, :] = picked[:, :wide].astype(F32).astype(FP8)
    flat[...] = jnp.zeros_like(flat)
    mirror[...] = jnp.zeros_like(mirror)

    row_sums = []
    for r2 in range(2):
        for copy in table_copies[r2]:
            copy.wait()

        def contraction(odd):
            lanes = slice(odd * M, (odd + 1) * M)
            both = nn_dot(hi_ref[r2, :, lanes], coef[r2, odd])
            rest = nn_dot(lo_ref[r2, :, lanes], coef8[r2, odd])
            return both[:, :wide] + (both[:, wide:] + rest * (1.0 / REST_SCALE))

        row_sums.append((contraction(0), contraction(1)))

    for r2 in range(2):
        even_sum, odd_sum = row_sums[r2]
        plus = even_sum + odd_sum
        minus = even_sum - odd_sum
        squares = jnp.concatenate([plus * plus, minus * minus], axis=1)
        sq_hi, sq_lo = split(squares)
        energy = nt_dot(mean_ref[...], sq_hi) + nt_dot(mean_ref[...], sq_lo)
        rows = 4 * plev
        flat[:, :KPTS] = energy
        en_hi, en_lo = split(flat[rows:, :KPAD])
        for t in range(KPAD // KBLK):
            lanes = slice(t * KBLK, (t + 1) * KBLK)
            back = KPAD - (t + 1) * KBLK
            mirror[:, back : back + KBLK] = nn_dot(en_hi[:, lanes], flip_ref[...]) + nn_dot(en_lo[:, lanes], flip_ref[...])

        quarter = own_points(points_ref, r2) // 4
        lane = iota((rows, BUF), 1)
        shift = (quarter + (BUF - (KPAD - 1))) % BUF
        flat[:rows, :] = jnp.where(lane <= quarter // 2, flat[:rows, :], pltpu.roll(mirror[...], shift, 1))
        line[...] = jnp.zeros_like(line)
        lane = iota((plev, BUF), 1)
        for b in range(4):
            start = quarter * b
            inner = start % 128
            base = pl.multiple_of(start - inner, 128)
            piece = pltpu.roll(flat[b * plev : (b + 1) * plev, :], inner, 1)
            old = line[:, pl.ds(base, BUF)]
            line[:, pl.ds(base, BUF)] = jnp.where((lane >= inner) & (lane < inner + quarter), piece, old)
        out_ref[:, pl.ds(r2, 1), :] = line[:, :ROWPAD].reshape(plev, 1, ROWPAD)


def synthesis(moved, slot_map, table_hi, table_lo, row_points):
    plev = moved.shape[1]
    wide = plev * 2 * PART
    vmem = pl.BlockSpec(memory_space=pltpu.VMEM)
    return pl.pallas_call(
        synth_kernel,
        out_shape=jax.ShapeDtypeStruct((plev, 2, ROWPAD), F32),
        in_specs=[pl.BlockSpec(memory_space=pltpu.SMEM)] + [vmem] * 5 + [pl.BlockSpec(memory_space=pltpu.HBM)] * 2,
        out_specs=vmem,
        scratch_shapes=[
            pltpu.VMEM((M, M), BF16),
            pltpu.VMEM((2, KPTS, 2 * M), BF16),
            pltpu.VMEM((2, KPTS, 2 * M), FP8),
            pltpu.VMEM((M, 2 * wide), BF16),
            pltpu.VMEM((2, 2, M, 2 * wide), BF16),
            pltpu.VMEM((2, 2, M, wide), FP8),
            pltpu.VMEM((8 * plev, BUF), F32),
            pltpu.VMEM((4 * plev, BUF), F32),
            pltpu.VMEM((plev, 3 * 1280 + BUF), F32),
            pltpu.SemaphoreType.DMA((2, 2, TABLE_CUTS)),
        ],
        compiler_params=pltpu.CompilerParams(vmem_limit_bytes=44 * MIB),
        cost_estimate=pl.CostEstimate(flops=2 * 2 * KPTS * 2 * M * 384, bytes_accessed=2 * KPTS * 2 * M * 4 + M * M * 2, transcendentals=0),
        name="synthesis",
    )(
        pltpu.with_memory_space_constraint(row_points, pltpu.HBM),
        pltpu.with_memory_space_constraint(moved, pltpu.VMEM), slot_map,
        pick_tables(plev), mean_table(plev), flip_table(),
        *[pltpu.with_memory_space_constraint(x, pltpu.HBM) for x in (table_hi, table_lo)],
    )


def join_kernel(*refs):
    parts = (len(refs) - 1) // 2
    at = 0
    for own_ref, other_ref in zip(refs[:parts], refs[parts:-1]):
        rows = own_ref.shape[1]
        refs[-1][:, at : at + rows, :] = own_ref[...] + other_ref[...]
        at += rows


def join(owns, others):
    rows = sum(x.shape[1] for x in owns)
    vmem = pl.BlockSpec(memory_space=pltpu.VMEM)
    return pl.pallas_call(
        join_kernel,
        out_shape=jax.ShapeDtypeStruct((owns[0].shape[0], rows, SQ * PART), F32),
        in_specs=[vmem] * (2 * len(owns)),
        out_specs=vmem,
        compiler_params=pltpu.CompilerParams(vmem_limit_bytes=32 * MIB),
        name="join",
    )(*[pltpu.with_memory_space_constraint(x, pltpu.VMEM) for x in owns + others])


def local(spectral, legendre, wave_map, row_points, brackets, lev_weight, climatology):
    slots = spectral.shape[0]
    half = legendre.shape[1]
    groups = slots // SQ
    wave_count = lax.axis_size("wave")
    lev_count = lax.axis_size("lev")
    rows_dev = 2 * half // (wave_count * lev_count)
    pairs = [(d, d - 1) for d in range(1, lev_count)]
    map_rows = wave_map.reshape(M // 128, 128)
    own, prev, between = legendre_sums(spectral, legendre, map_rows, brackets, lev_weight)
    sent = lax.switch(
        between[0],
        [
            lambda mine, theirs: join([mine], [lax.ppermute(theirs, "lev", pairs[::2])]),
            lambda mine, theirs: join([mine], [lax.ppermute(theirs, "lev", pairs)]),
        ],
        own,
        prev,
    )
    moved = lax.all_to_all(sent, ("wave", "lev"), split_axis=0, concat_axis=0, tiled=True)
    moved = moved.reshape(wave_count, lev_count, rows_dev * groups, SQ * PART)
    table_points, _ = lax.optimization_barrier((row_points, sent))
    table_hi, table_lo, sorted_map = tables(table_points, map_rows)
    slot_map = jnp.transpose(sorted_map.reshape(wave_count, SQ, groups), (1, 0, 2)).reshape(1, M)
    energy = synthesis(moved, slot_map, table_hi, table_lo, row_points)
    result = lax.all_to_all(energy, "lev", split_axis=0, concat_axis=0, tiled=True)
    result = result.reshape(1, rows_dev * lev_count, ROWPAD)
    points_all = jnp.concatenate([row_points, row_points])
    band_rows = rows_dev * lev_count
    out_points = lax.dynamic_slice_in_dim(points_all, lax.axis_index("wave") * band_rows, band_rows, 0)
    places = jnp.arange(ROWPAD, dtype=jnp.int32)
    inside = places[None, None, :] < out_points[None, :, None]
    return jnp.where(inside, result - climatology, 0.0)


def solution(mesh):
    placed = (
        P("wave", "lev", None),
        P("wave", None, None),
        P(),
        P(),
        P(),
        P(),
        P("lev", "wave", None),
    )
    return jax.shard_map(
        local, mesh=mesh, in_specs=placed, out_specs=P("lev", "wave", None), check_vma=False
    )
```
